32 devices in a mesh: clip: 4 (over z), tok: 4 (over x, core), head: 2 (over y).
Axes of the slice: x: 2, y: 2, z: 4, core: 2. Of those that a mesh axis runs over, the one named last changes fastest.
Arguments:
- clips_in: bfloat16 [4, 4, 16, 196, 384], P('clip', None, 'tok'), may hold values from -6 to 6
- resets: int32 [4, 4], P('clip'), may hold values from 0 to 1, as said below
- assign: int32 [4, 4], P('clip'), may hold values from 0 to 3, as said below
- w_qkv_a: bfloat16 [384, 3, 384], P('tok', None, 'head'), may hold values from -0.625 to 0.625
- w_out_a: bfloat16 [384, 384], P('tok', 'head'), may hold values from -0.15625 to 0.15625
- w_up_a: bfloat16 [384, 1536], P('tok', 'head'), may hold values from -0.3125 to 0.3125
- w_down_a: bfloat16 [384, 1536], P('tok', 'head'), may hold values from -0.15625 to 0.15625
- w_qkv_b: bfloat16 [384, 3, 768], P('tok', None, 'head'), may hold values from -0.625 to 0.625
- w_out_b: bfloat16 [768, 768], P('tok', 'head'), may hold values from -0.109375 to 0.109375
- w_skip_b: bfloat16 [768, 384], P('tok', 'head'), may hold values from -0.3125 to 0.3125
- w_up_b: bfloat16 [768, 3072], P('tok', 'head'), may hold values from -0.21875 to 0.21875
- w_down_b: bfloat16 [768, 3072], P('tok', 'head'), may hold values from -0.109375 to 0.109375
- gains_a: float32 [3, 384], replicated, may hold values from 0.25 to 1.75
- gains_b: float32 [768], replicated, may hold values from 0.25 to 1.75
- shifts_a: float32 [5, 384], replicated, may hold values from -1.2 to 1.2
- shifts_b: float32 [3, 768], replicated, may hold values from -1.2 to 1.2
- qv_bias_a: float32 [2, 384], P(None, 'head'), may hold values from -1.2 to 1.2
- qv_bias_b: float32 [2, 768], P(None, 'head'), may hold values from -1.2 to 1.2
- up_bias_a: float32 [1536], P('head'), may hold values from -1.2 to 1.2
- up_bias_b: float32 [3072], P('head'), may hold values from -1.2 to 1.2
- cotangent: bfloat16 [4, 4, 16, 49, 768], P('clip', None, 'tok'), may hold values from -6 to 6
Outputs:
- mixed: bfloat16 [4, 4, 16, 49, 768], P('clip', None, 'tok')
- grad_clips_in: float32 [4, 4, 16, 196, 384], P('clip', None, 'tok')
- grad_w_qkv_a: float32 [384, 3, 384], P('tok', None, 'head')
- grad_w_out_a: float32 [384, 384], P('tok', 'head')
- grad_w_up_a: float32 [384, 1536], P('tok', 'head')
- grad_w_down_a: float32 [384, 1536], P('tok', 'head')
- grad_w_qkv_b: float32 [384, 3, 768], P('tok', None, 'head')
- grad_w_out_b: float32 [768, 768], P('tok', 'head')
- grad_w_skip_b: float32 [768, 384], P('tok', 'head')
- grad_w_up_b: float32 [768, 3072], P('tok', 'head')
- grad_w_down_b: float32 [768, 3072], P('tok', 'head')
- grad_gains_a: float32 [3, 384], replicated
- grad_gains_b: float32 [768], replicated
- grad_shifts_a: float32 [5, 384], replicated
- grad_shifts_b: float32 [3, 768], replicated
- grad_qv_bias_a: float32 [2, 384], P(None, 'head')
- grad_qv_bias_b: float32 [2, 768], P(None, 'head')
- grad_up_bias_a: float32 [1536], P('head')
- grad_up_bias_b: float32 [3072], P('head')
The draws below stay inside these ranges and needn't reach their ends.
Inputs may be any that keep to these rules, and one draw needn't show every extreme that they name: `resets`: 1 marks a clip that starts a new video; every micro-batch is marked at clip 0; following assign back from some micro-batch of the last clip reaches clip 0 through unmarked clips. `assign`: each row is a permutation of the 4 micro-batches.
All inputs are finite; a program needn't handle non-finite values.
Results may differ from the reference program's by a relative error of at most 0.023.
Values may be sent and summed in bfloat16 or wider, within the bound.
A program may use at most 448 MiB of HBM per device.

```python
import jax
import jax.numpy as jnp
from jax import lax

D1 = 384
HEADS_A = 4
FF1 = 1536
D2 = 768
HEADS_B = 8
FF2 = 3072
GRID = 14
MICRO = 4
PATCH = 196
POOLED = 49
FRAMES = 16
CLIPS = 4


def draw_links(key):
    row_list = []
    for clip_index in range(CLIPS):
        row_list.append(jax.random.permutation(jax.random.fold_in(key, clip_index), MICRO))
    orders = jnp.stack(row_list).astype(jnp.int32)
    reset_flags = (jax.random.randint(jax.random.fold_in(key, 1000), (CLIPS, MICRO), 0, 3) == 0).astype(jnp.int32)
    reset_flags = reset_flags.at[0].set(1)
    chain_slot = jax.random.randint(jax.random.fold_in(key, 2000), (), 0, MICRO)
    for clip_index in range(CLIPS - 1, 0, -1):
        reset_flags = reset_flags.at[clip_index, chain_slot].set(0)
        chain_slot = orders[clip_index, chain_slot]
    return (orders, reset_flags)


def draw_resets(key, part):
    return draw_links(key)[1]


def draw_assign(key, part):
    return draw_links(key)[0]


def scene_tokens(key, noise, clip_scale, frame_scale):
    clip_key, frame_key = jax.random.split(key, 2)
    clip_part = clip_scale * jax.random.normal(clip_key, (CLIPS, MICRO, 1, 1, D1), jnp.float32)
    frame_part = frame_scale * jax.random.normal(frame_key, (CLIPS, MICRO, FRAMES, 1, D1), jnp.float32)
    return jnp.clip(noise + clip_part + frame_part, -6.0, 6.0)


def draw_clips_in(key, part):
    key = jax.random.fold_in(key, 31337)
    noise_key, scene_key = jax.random.split(key, 2)
    extent = (CLIPS, MICRO, FRAMES, PATCH, D1)
    noise = jax.random.normal(noise_key, extent, jnp.float32)
    tokens = scene_tokens(scene_key, noise, 0.6, 0.4)
    return tokens.astype(jnp.bfloat16)


def levels(stream_key, dims, cuts, low, top_value):
    gain = 1.0
    for position, shards_of in cuts:
        heights = jax.random.uniform(jax.random.fold_in(jax.random.fold_in(stream_key, 6), position), (shards_of,), jnp.float32, low / len(cuts), top_value / len(cuts))
        gain = gain * jnp.repeat(jnp.exp(heights), dims[position] // shards_of).reshape((-1,) + (1,) * (len(dims) - 1 - position))
    return gain


def gaussian(stream_key, shape, scale, reach, shards=(), held_as=jnp.bfloat16):
    values = scale * jax.random.normal(stream_key, shape, jnp.float32)
    if shards:
        values = values * levels(stream_key, shape, shards, -0.22, 0.18)
    return jnp.clip(values, -reach, reach).astype(held_as)


def setup_inputs(seed: int = 0) -> dict:
    arg_keys = jax.random.split(jax.random.key(seed), 22)
    clips_in = draw_clips_in(jax.random.fold_in(arg_keys[21], 71), 0)
    resets = draw_resets(jax.random.fold_in(arg_keys[21], 71), 0)
    assign = draw_assign(jax.random.fold_in(arg_keys[21], 71), 0)
    w_qkv_a = gaussian(arg_keys[3], (D1, 3, D1), (D1 // 4) ** -0.5, 0.625, ((0, 4), (2, 2)))
    w_out_a = gaussian(arg_keys[4], (D1, D1), (4 * D1) ** -0.5, 0.15625, ((0, 4), (1, 2)))
    w_up_a = gaussian(arg_keys[5], (D1, FF1), D1 ** -0.5, 0.3125, ((0, 4), (1, 2)))
    w_down_a = gaussian(arg_keys[6], (D1, FF1), FF1 ** -0.5, 0.15625, ((0, 4), (1, 2)))
    w_qkv_b = gaussian(arg_keys[7], (D1, 3, D2), (D1 // 4) ** -0.5, 0.625, ((0, 4), (2, 2)))
    w_out_b = gaussian(arg_keys[8], (D2, D2), (4 * D2) ** -0.5, 0.109375, ((0, 4), (1, 2)))
    w_skip_b = gaussian(arg_keys[9], (D2, D1), D1 ** -0.5, 0.3125, ((0, 4), (1, 2)))
    w_up_b = gaussian(arg_keys[10], (D2, FF2), D2 ** -0.5, 0.21875, ((0, 4), (1, 2)))
    w_down_b = gaussian(arg_keys[11], (D2, FF2), FF2 ** -0.5, 0.109375, ((0, 4), (1, 2)))
    gains_a = jnp.clip(1.0 + 0.15 * jax.random.normal(arg_keys[12], (3, D1), jnp.float32), 0.25, 1.75)
    gains_b = jnp.clip(1.0 + 0.15 * jax.random.normal(arg_keys[13], (D2,), jnp.float32), 0.25, 1.75)
    shifts_a = gaussian(arg_keys[14], (5, D1), 0.3, 1.2, (), jnp.float32)
    shifts_b = gaussian(arg_keys[15], (3, D2), 0.3, 1.2, (), jnp.float32)
    qv_bias_a = gaussian(arg_keys[16], (2, D1), 0.3, 1.2, ((1, 2),), jnp.float32)
    qv_bias_b = gaussian(arg_keys[17], (2, D2), 0.3, 1.2, ((1, 2),), jnp.float32)
    up_bias_a = gaussian(arg_keys[18], (FF1,), 0.3, 1.2, ((0, 2),), jnp.float32)
    up_bias_b = gaussian(arg_keys[19], (FF2,), 0.3, 1.2, ((0, 2),), jnp.float32)
    cotangent = gaussian(arg_keys[20], (CLIPS, MICRO, FRAMES, POOLED, D2), 1.0, 6.0, ((0, 4), (2, 4)))
    return dict(clips_in=clips_in, resets=resets, assign=assign, w_qkv_a=w_qkv_a, w_out_a=w_out_a, w_up_a=w_up_a, w_down_a=w_down_a, w_qkv_b=w_qkv_b, w_out_b=w_out_b, w_skip_b=w_skip_b, w_up_b=w_up_b, w_down_b=w_down_b, gains_a=gains_a, gains_b=gains_b, shifts_a=shifts_a, shifts_b=shifts_b, qv_bias_a=qv_bias_a, qv_bias_b=qv_bias_b, up_bias_a=up_bias_a, up_bias_b=up_bias_b, cotangent=cotangent)


eps = 1e-06
precise = lax.Precision.HIGHEST

@jax.custom_vjp
def low(v):
    return lax.optimization_barrier(v.astype(jnp.bfloat16)).astype(jnp.float32)

@jax.custom_vjp
def low_back(v):
    return v

def low_keep(v):
    return (low(v), None)

def low_pass(kept, grad):
    return (grad,)

def back_keep(v):
    return (v, None)

def back_low(kept, grad):
    return (low(grad),)
low.defvjp(low_keep, low_pass)
low_back.defvjp(back_keep, back_low)

def layer_norm(tensor, gain_row, shift_row):
    average = lax.optimization_barrier(jnp.mean(tensor, axis=-1, keepdims=True))
    centred = tensor - average
    variance = lax.optimization_barrier(jnp.mean(centred * centred, axis=-1, keepdims=True))
    return centred * lax.rsqrt(variance + eps) * gain_row + shift_row

def pool_grid(tensor):
    extent = tensor.shape
    half_grid = GRID // 2
    grid_view = tensor.reshape(extent[:-2] + (half_grid, 2, half_grid, 2, extent[-1]))
    return lax.optimization_barrier(jnp.mean(grid_view, axis=(-4, -2))).reshape(extent[:-2] + (half_grid * half_grid, extent[-1]))

def to_heads(tensor, count):
    return tensor.reshape(tensor.shape[:-1] + (count, tensor.shape[-1] // count))

def attend_clip(queries, clip_keys, clip_values, mem_keys, mem_values, has_memory):
    scaling = queries.shape[-1] ** (-0.5)
    all_keys = jnp.concatenate([clip_keys, mem_keys], axis=1)
    all_values = jnp.concatenate([clip_values, mem_values], axis=1)
    scores = low_back(jnp.einsum('mqhe,mkhe->mhqk', queries, all_keys, precision=precise) * scaling)
    column = jnp.arange(all_keys.shape[1])
    keep_mask = (column[None, :] < clip_keys.shape[1]) | (has_memory[:, None] > 0.5)
    scores = jnp.where(keep_mask[:, None, None, :], scores, -1e+30)
    highest = lax.optimization_barrier(jnp.max(scores, axis=-1, keepdims=True))
    exponent = jnp.exp(scores - highest)
    weights_low = low(exponent / lax.optimization_barrier(jnp.sum(exponent, axis=-1, keepdims=True)))
    return jnp.einsum('mhqk,mkhe->mqhe', weights_low, all_values, precision=precise)

def carry_memory(pooled, chooser):
    clips, batches, frames = (pooled.shape[0], pooled.shape[1], pooled.shape[2])
    frame_pairs = pooled.reshape((clips, batches, frames // 2, 2) + pooled.shape[3:])
    memory = low(lax.optimization_barrier(jnp.mean(frame_pairs, axis=3)))
    memory = memory.reshape((clips, batches, -1) + pooled.shape[4:])
    earlier = jnp.concatenate([jnp.zeros_like(memory[:1]), memory[:-1]], axis=0)
    return jnp.einsum('cms,csjhe->cmjhe', chooser, earlier, precision=precise)

def flatten_keys(tensor):
    return tensor.reshape(tensor.shape[:2] + (-1,) + tensor.shape[4:])

def clip_attention(queries, pooled_keys, pooled_values, has_memory, chooser):
    mem_keys = carry_memory(pooled_keys, chooser)
    mem_values = carry_memory(pooled_values, chooser)
    attend_step = jax.checkpoint(attend_clip)
    return lax.map(lambda pieces: attend_step(*pieces), (queries, flatten_keys(pooled_keys), flatten_keys(pooled_values), mem_keys, mem_values, has_memory))

def block_first(stream, has_memory, chooser, w_qkv, w_out, w_up, w_down, gain_rows, shifts, qv_bias, up_bias):
    clips, batches, frames, patches, width = stream.shape
    normed = low(layer_norm(stream, gain_rows[0], shifts[0]))
    projected = low_back(jnp.einsum('cmfpd,dke->cmfpke', normed, w_qkv, precision=precise))
    queries = low(projected[..., 0, :] + qv_bias[0])
    pooled_keys = low(pool_grid(projected[..., 1, :]))
    pooled_values = low(pool_grid(projected[..., 2, :] + qv_bias[1]))
    query_heads = to_heads(queries, HEADS_A).reshape(clips, batches, frames * patches, HEADS_A, -1)
    attended = clip_attention(query_heads, to_heads(pooled_keys, HEADS_A), to_heads(pooled_values, HEADS_A), has_memory, chooser)
    combined = low(low_back(attended + query_heads)).reshape(clips, batches, frames, patches, width)
    residual = stream + low_back(jnp.einsum('cmfpi,oi->cmfpo', combined, w_out, precision=precise)) + shifts[1]
    normed_mlp = low(layer_norm(residual, gain_rows[1], shifts[2]))
    pre_act = low_back(jnp.einsum('cmfpd,dh->cmfph', normed_mlp, w_up, precision=precise)) + up_bias
    hidden = low(jax.nn.gelu(pre_act, approximate=True))
    return residual + low_back(jnp.einsum('cmfph,oh->cmfpo', hidden, w_down, precision=precise)) + shifts[3]

def block_second(stream, has_memory, chooser, w_qkv, w_out, w_skip, w_up, w_down, gain_in, shift_in, gain_mlp, shifts, qv_bias, up_bias):
    clips, batches, frames, patches, width = stream.shape
    wide = w_qkv.shape[-1]
    normed_full = layer_norm(stream, gain_in, shift_in)
    projected = low_back(jnp.einsum('cmfpd,dke->cmfpke', low(normed_full), w_qkv, precision=precise))
    queries = low(pool_grid(projected[..., 0, :] + qv_bias[0]))
    pooled_keys = low(pool_grid(projected[..., 1, :]))
    pooled_values = low(pool_grid(projected[..., 2, :] + qv_bias[1]))
    query_heads = to_heads(queries, HEADS_B).reshape(clips, batches, frames * POOLED, HEADS_B, -1)
    attended = clip_attention(query_heads, to_heads(pooled_keys, HEADS_B), to_heads(pooled_values, HEADS_B), has_memory, chooser)
    combined = low(low_back(attended + query_heads)).reshape(clips, batches, frames, POOLED, wide)
    skip_in = low(pool_grid(normed_full))
    residual = low_back(jnp.einsum('cmfpi,oi->cmfpo', combined, w_out, precision=precise) + jnp.einsum('cmfpi,oi->cmfpo', skip_in, w_skip, precision=precise)) + shifts[0]
    normed_mlp = low(layer_norm(residual, gain_mlp, shifts[1]))
    pre_act = low_back(jnp.einsum('cmfpd,dh->cmfph', normed_mlp, w_up, precision=precise)) + up_bias
    hidden = low(jax.nn.gelu(pre_act, approximate=True))
    return residual + low_back(jnp.einsum('cmfph,oh->cmfpo', hidden, w_down, precision=precise)) + shifts[2]

def reference(clips_in, resets, assign, w_qkv_a, w_out_a, w_up_a, w_down_a, w_qkv_b, w_out_b, w_skip_b, w_up_b, w_down_b, gains_a, gains_b, shifts_a, shifts_b, qv_bias_a, qv_bias_b, up_bias_a, up_bias_b, cotangent):
    clip_ids = jnp.arange(CLIPS)
    has_memory = ((resets == 0) & (clip_ids[:, None] > 0)).astype(jnp.float32)
    chooser = (assign[:, :, None] == jnp.arange(MICRO)[None, None, :]).astype(jnp.float32)
    floats = tuple((tensor.astype(jnp.float32) for tensor in (clips_in, w_qkv_a, w_out_a, w_up_a, w_down_a, w_qkv_b, w_out_b, w_skip_b, w_up_b, w_down_b, gains_a, gains_b, shifts_a, shifts_b, qv_bias_a, qv_bias_b, up_bias_a, up_bias_b)))

    def forward_pass(stream, qkv_a, out_a, up_a, down_a, qkv_b, out_b, skip_b, up_b, down_b, gain_one, gain_two, shift_one, shift_two, qv_one, qv_two, upb_one, upb_two):
        middle = block_first(stream, has_memory, chooser, qkv_a, out_a, up_a, down_a, gain_one, shift_one, qv_one, upb_one)
        return block_second(middle, has_memory, chooser, qkv_b, out_b, skip_b, up_b, down_b, gain_one[2], shift_one[4], gain_two, shift_two, qv_two, upb_two)
    primal, pullback = jax.vjp(forward_pass, *floats)
    gradients = pullback(cotangent.astype(jnp.float32))
    return (primal.astype(jnp.bfloat16), gradients[0], gradients[1], gradients[2], gradients[3], gradients[4], gradients[5], gradients[6], gradients[7], gradients[8], gradients[9], gradients[10], gradients[11], gradients[12], gradients[13], gradients[14], gradients[15], gradients[16], gradients[17])
```

```python
import functools
import math
import jax
import jax.numpy as jnp
import numpy as np
from jax import lax
from jax.experimental import pallas as pl
from jax.experimental.pallas import tpu as pltpu
from jax.sharding import PartitionSpec as P
HD = 96
NEG = -1e30
VMEM_CAP = 60 * 2**20

def window(head):
    low = HD * head
    start = low // 128 * 128
    stop = -(-(low + HD) // 128) * 128
    return low, start, stop

def head_mask(head):
    low, start, stop = window(head)
    lane = lax.broadcasted_iota(jnp.int32, (1, stop - start), 1) + start
    return (lane >= low) & (lane < low + HD)

def attend_kernel(scaling, chunk, q_ref, kv_ref, mem_ref, bias_ref, out_ref, lse_ref, k_s, v_s, s_s, p_s):
    width = q_ref.shape[2]
    heads = width // HD
    nq = q_ref.shape[1]
    row = 0
    for ref in (kv_ref, mem_ref):
        rows = ref.shape[2]
        for t in range(ref.shape[0]):
            k_s[row:row + rows, :] = ref[t, 0, :, :width]
            v_s[row:row + rows, :] = ref[t, 0, :, width:]
            row += rows
    factor = scaling * math.log2(math.e)
    lane8 = lax.broadcasted_iota(jnp.int32, (chunk, 128), 1)
    for tile in range(width // 384):
        acc = q_ref[0, :, 384 * tile:384 * tile + 384].astype(jnp.float32)
        parts = [acc[:, :128], acc[:, 128:256], acc[:, 256:384]]
        for head in range(4 * tile, 4 * tile + 4):
            low, start, stop = window(head)
            mask = head_mask(head)
            qm = jnp.where(mask, q_ref[0, :, start:stop], jnp.bfloat16(0))
            s_s[...] = lax.dot_general(qm, k_s[:, start:stop], (((1,), (1,)), ((), ())), preferred_element_type=jnp.float32)

            def body(i, carry, head=head):
                rows = pl.ds(pl.multiple_of(i * chunk, chunk), chunk)
                s = s_s[rows, :] * factor + bias_ref[0]
                top = jnp.max(s, axis=1, keepdims=True)
                e = jnp.exp2(s - top)
                total = jnp.sum(e, axis=1, keepdims=True)
                p_s[rows, :] = (e * (1.0 / total)).astype(jnp.bfloat16)
                stat = top + jnp.log2(total)
                lse_ref[0, rows, :] = jnp.where(lane8 == head, stat, lse_ref[0, rows, :])
                return carry
            lax.fori_loop(0, nq // chunk, body, 0, unroll=nq // chunk)
            o = lax.dot_general(p_s[...], v_s[:, start:stop], (((1,), (0,)), ((), ())), preferred_element_type=jnp.float32)
            o = jnp.where(mask, o, 0.0)
            for w in range((stop - start) // 128):
                k = start // 128 - 3 * tile + w
                parts[k] = parts[k] + o[:, 128 * w:128 * w + 128]
        out_ref[0, :, 384 * tile:384 * tile + 384] = jnp.concatenate(parts, axis=1).astype(jnp.bfloat16)

def attend(q, kv, mem, bias):
    batches, nq, width = q.shape
    keys = kv.shape[0] * kv.shape[2] + mem.shape[0] * mem.shape[2]
    scaling = HD ** -0.5
    chunk = 112 if nq % 112 == 0 else 16
    return pl.pallas_call(
        functools.partial(attend_kernel, scaling, chunk),
        grid=(batches,),
        in_specs=[
            pl.BlockSpec((1, nq, width), lambda m: (m, 0, 0)),
            pl.BlockSpec((kv.shape[0], 1) + kv.shape[2:], lambda m: (0, m, 0, 0)),
            pl.BlockSpec((mem.shape[0], 1) + mem.shape[2:], lambda m: (0, m, 0, 0)),
            pl.BlockSpec((1, 1, keys), lambda m: (m, 0, 0)),
        ],
        out_specs=[
            pl.BlockSpec((1, nq, width), lambda m: (m, 0, 0)),
            pl.BlockSpec((1, nq, 128), lambda m: (m, 0, 0)),
        ],
        out_shape=[
            jax.ShapeDtypeStruct((batches, nq, width), jnp.bfloat16),
            jax.ShapeDtypeStruct((batches, nq, 128), jnp.float32),
        ],
        scratch_shapes=[
            pltpu.VMEM((keys, width), jnp.bfloat16),
            pltpu.VMEM((keys, width), jnp.bfloat16),
            pltpu.VMEM((nq, keys), jnp.float32),
            pltpu.VMEM((nq, keys), jnp.bfloat16),
        ],
        compiler_params=pltpu.CompilerParams(vmem_limit_bytes=VMEM_CAP),
        name="attend",
    )(q, kv, mem, bias)

def attend_back_kernel(scaling, chunk, q_ref, g_ref, kv_ref, mem_ref, bias_ref, lse_ref, dq_ref, dkv_ref, dmem_ref,
                       k_s, v_s, s_s, dp_s, p_s, ds_s, dkt_s, dvt_s):
    width = q_ref.shape[2]
    heads = width // HD
    nq = q_ref.shape[1]
    row = 0
    for ref in (kv_ref, mem_ref):
        rows = ref.shape[2]
        for t in range(ref.shape[0]):
            k_s[row:row + rows, :] = ref[t, 0, :, :width]
            v_s[row:row + rows, :] = ref[t, 0, :, width:]
            row += rows
    factor = scaling * math.log2(math.e)
    lane8 = lax.broadcasted_iota(jnp.int32, (chunk, 128), 1)
    nt = (((1,), (1,)), ((), ()))
    nn = (((1,), (0,)), ((), ()))
    for tile in range(width // 384):
        group = slice(384 * tile, 384 * tile + 384)
        qt = q_ref[0, :, group].astype(jnp.float32).T.astype(jnp.bfloat16)
        gt = g_ref[0, :, group].astype(jnp.float32).T.astype(jnp.bfloat16)
        parts = [None] * 3
        for head in range(4 * tile, 4 * tile + 4):
            low, start, stop = window(head)
            mask = head_mask(head)
            qm = jnp.where(mask, q_ref[0, :, start:stop], jnp.bfloat16(0))
            gm = jnp.where(mask, g_ref[0, :, start:stop], jnp.bfloat16(0))
            s_s[...] = lax.dot_general(qm, k_s[:, start:stop], nt, preferred_element_type=jnp.float32)
            dp_s[...] = lax.dot_general(gm, v_s[:, start:stop], nt, preferred_element_type=jnp.float32)

            def body(i, carry, head=head):
                rows = pl.ds(pl.multiple_of(i * chunk, chunk), chunk)
                lse = jnp.sum(jnp.where(lane8 == head, lse_ref[0, rows, :], 0.0), axis=1, keepdims=True)
                p = jnp.exp2(s_s[rows, :] * factor + bias_ref[0] - lse)
                dp = dp_s[rows, :]
                inner = jnp.sum(p * dp, axis=1, keepdims=True)
                p_s[rows, :] = p.astype(jnp.bfloat16)
                ds_s[rows, :] = (p * (dp - inner)).astype(jnp.bfloat16)
                return carry
            lax.fori_loop(0, nq // chunk, body, 0, unroll=nq // chunk)
            r = HD * (head - 4 * tile)
            dvt_s[r:r + HD, :] = lax.dot_general(gt[r:r + HD], p_s[...], nn, preferred_element_type=jnp.float32)
            dkt_s[r:r + HD, :] = lax.dot_general(qt[r:r + HD], ds_s[...], nn, preferred_element_type=jnp.float32) * scaling
            dq = lax.dot_general(ds_s[...], k_s[:, start:stop], nn, preferred_element_type=jnp.float32) * scaling
            dq = jnp.where(mask, dq, 0.0)
            for w in range((stop - start) // 128):
                k = start // 128 - 3 * tile + w
                part = dq[:, 128 * w:128 * w + 128]
                parts[k] = part if parts[k] is None else parts[k] + part
        dq_ref[0, :, group] = jnp.concatenate(parts, axis=1) + g_ref[0, :, group].astype(jnp.float32)
        for base, src in ((0, dkt_s), (width, dvt_s)):
            total = src[...].T.astype(jnp.bfloat16)
            lanes = slice(base + 384 * tile, base + 384 * tile + 384)
            row = 0
            for ref in (dkv_ref, dmem_ref):
                rows = ref.shape[2]
                for t in range(ref.shape[0]):
                    ref[t, 0, :, lanes] = total[row:row + rows]
                    row += rows

def attend_back(q, grad, kv, mem, bias, lse):
    batches, nq, width = q.shape
    keys = kv.shape[0] * kv.shape[2] + mem.shape[0] * mem.shape[2]
    scaling = HD ** -0.5
    chunk = 112 if nq % 112 == 0 else 16
    rows_spec = pl.BlockSpec((1, nq, width), lambda m: (m, 0, 0))
    kv_spec = pl.BlockSpec((kv.shape[0], 1) + kv.shape[2:], lambda m: (0, m, 0, 0))
    mem_spec = pl.BlockSpec((mem.shape[0], 1) + mem.shape[2:], lambda m: (0, m, 0, 0))
    return pl.pallas_call(
        functools.partial(attend_back_kernel, scaling, chunk),
        grid=(batches,),
        in_specs=[rows_spec, rows_spec, kv_spec, mem_spec,
            pl.BlockSpec((1, 1, keys), lambda m: (m, 0, 0)),
            pl.BlockSpec((1, nq, 128), lambda m: (m, 0, 0)),
        ],
        out_specs=[rows_spec, kv_spec, mem_spec],
        out_shape=[
            jax.ShapeDtypeStruct((batches, nq, width), jnp.float32),
            jax.ShapeDtypeStruct(kv.shape, jnp.bfloat16),
            jax.ShapeDtypeStruct(mem.shape, jnp.bfloat16),
        ],
        scratch_shapes=[
            pltpu.VMEM((keys, width), jnp.bfloat16),
            pltpu.VMEM((keys, width), jnp.bfloat16),
            pltpu.VMEM((nq, keys), jnp.float32),
            pltpu.VMEM((nq, keys), jnp.float32),
            pltpu.VMEM((nq, keys), jnp.bfloat16),
            pltpu.VMEM((nq, keys), jnp.bfloat16),
            pltpu.VMEM((384, keys), jnp.float32),
            pltpu.VMEM((384, keys), jnp.float32),
        ],
        compiler_params=pltpu.CompilerParams(vmem_limit_bytes=VMEM_CAP),
        name="attend_back",
    )(q, grad, kv, mem, bias, lse)


GRID = 14
PATCH = GRID * GRID
POOLED = PATCH // 4
eps = 1e-06
f32, bf16 = jnp.float32, jnp.bfloat16


def up16(n):
    return -(-n // 16) * 16


def dot(a, b, dims=((1,), (0,))):
    return lax.dot_general(a, b, (dims, ((), ())), preferred_element_type=f32)


def tokens_dot(a, b):
    return jnp.einsum("mnd,de->mne", a, b, preferred_element_type=f32)


def tokens_dot_t(a, b):
    return jnp.einsum("mne,de->mnd", a, b, preferred_element_type=f32)


def weight_grad(a, g):
    return jnp.einsum("mnd,mne->de", a, g, preferred_element_type=f32)


def pool_matrix(frames):
    rows, cols = up16(frames * POOLED), frames * PATCH
    out = np.zeros((rows, cols), np.float32)
    half = GRID // 2
    for f in range(frames):
        for p in range(PATCH):
            r, c = divmod(p, GRID)
            out[f * POOLED + (r // 2) * half + c // 2, f * PATCH + p] = 0.25
    return out


def pair_matrix(frames):
    rows, cols = up16(frames // 2 * POOLED), up16(frames * POOLED)
    out = np.zeros((rows, cols), np.float32)
    for j in range(frames // 2):
        for p in range(POOLED):
            out[j * POOLED + p, 2 * j * POOLED + p] = 0.5
            out[j * POOLED + p, (2 * j + 1) * POOLED + p] = 0.5
    return out


def pool(matrix, tensor):
    return jnp.einsum("pt,mtd->mpd", matrix, tensor, precision=lax.Precision.HIGHEST)


def unpool(matrix, tensor):
    return jnp.einsum("pt,mpd->mtd", matrix, tensor, precision=lax.Precision.HIGHEST)


def layer_norm(tensor, gain_row, shift_row):
    average = jnp.mean(tensor, axis=-1, keepdims=True)
    centred = tensor - average
    variance = jnp.mean(centred * centred, axis=-1, keepdims=True)
    return centred * lax.rsqrt(variance + eps) * gain_row + shift_row


def norm_back(tensor, gain_row, gradient):
    average = jnp.mean(tensor, axis=-1, keepdims=True)
    centred = tensor - average
    variance = jnp.mean(centred * centred, axis=-1, keepdims=True)
    inverse = lax.rsqrt(variance + eps)
    unit = centred * inverse
    scaled = gradient * gain_row
    back = inverse * (
        scaled
        - jnp.mean(scaled, axis=-1, keepdims=True)
        - unit * jnp.mean(scaled * unit, axis=-1, keepdims=True)
    )
    return back, jnp.sum(gradient * unit, axis=(0, 1)), jnp.sum(gradient, axis=(0, 1))


def gelu_back(pre_act, gradient):
    primal, pullback = jax.vjp(lambda v: jax.nn.gelu(v, approximate=True), pre_act)
    return pullback(gradient)[0]


def gelu(pre_act):
    return jax.nn.gelu(pre_act, approximate=True)


def grouped(pairs_of):
    clips, heads = lax.axis_size("clip"), lax.axis_size("head")
    return [
        (c * heads + h, c2 * heads + h2)
        for c in range(clips)
        for h in range(heads)
        for c2, h2 in [pairs_of(c, h)]
        if 0 <= c2 < clips
    ]


def send_memory(memory, by, heads):
    return [
        lax.ppermute(
            memory if not isinstance(memory, list) else memory[d],
            ("clip", "head"),
            grouped(lambda c, h, d=d: (c + by, (h + d) % heads)),
        )
        for d in range(heads)
    ]


def share_keys(kv, memory, slots, heads):
    received = send_memory(memory, 1, heads)
    own = lax.all_gather(kv, "tok")
    flat = jnp.stack(received).reshape((-1,) + memory.shape[1:])
    chosen = jnp.stack([lax.dynamic_index_in_dim(flat, slot, 0, keepdims=False) for slot in slots])
    return own, lax.all_gather(chosen, "tok")


def halve_over_tok(partial):
    size = lax.axis_size("tok")
    index = lax.axis_index("tok")
    bit = 1
    while bit < size:
        mine = (index // bit) % 2
        paired = partial.reshape((partial.shape[0] // 2, 2) + partial.shape[1:])
        keep = lax.dynamic_index_in_dim(paired, mine, 1, keepdims=False)
        give = lax.dynamic_index_in_dim(paired, 1 - mine, 1, keepdims=False)
        got = lax.ppermute(give, "tok", [(i, i ^ bit) for i in range(size)])
        partial = (keep.astype(f32) + got.astype(f32)).astype(bf16)
        bit *= 2
    return partial[0]


def return_keys(own_grad, mem_grad, slots, heads, pairing):
    mem = halve_over_tok(mem_grad)
    own = halve_over_tok(own_grad)
    routed = jnp.zeros((heads * mem.shape[0],) + mem.shape[1:], bf16)
    for m, slot in enumerate(slots):
        routed = lax.dynamic_update_index_in_dim(routed, mem[m], slot, 0)
    routed = routed.reshape((heads,) + mem.shape)
    back = send_memory([routed[(heads - d) % heads] for d in range(heads)], -1, heads)
    total = sum(piece.astype(f32) for piece in back)
    spread = jnp.einsum("jf,mjd->mfd", pairing, total, precision=lax.Precision.HIGHEST)
    return own.astype(f32) + spread


def padded(tensor, rows):
    return jnp.pad(tensor, ((0, 0), (0, rows - tensor.shape[1]), (0, 0)))


def local(
    clips_in, resets, assign, w_qkv_a, w_out_a, w_up_a, w_down_a, w_qkv_b, w_out_b, w_skip_b, w_up_b, w_down_b,
    gains_a, gains_b, shifts_a, shifts_b, qv_bias_a, qv_bias_b, up_bias_a, up_bias_b, cotangent,
):
    heads, toks = lax.axis_size("head"), lax.axis_size("tok")
    head = lax.axis_index("head")
    micro, frames = clips_in.shape[1], clips_in.shape[2]
    d1, d2 = clips_in.shape[-1], cotangent.shape[-1]
    share = micro // heads
    first = head * share
    pooling = jnp.asarray(pool_matrix(frames))
    pairing = jnp.asarray(pair_matrix(frames))
    own_rows, mem_rows = up16(frames * POOLED), up16(frames // 2 * POOLED)

    stream = lax.dynamic_slice_in_dim(clips_in[0], first, share, 0)
    stream = stream.reshape(share, frames * PATCH, d1).astype(f32)
    cot = lax.dynamic_slice_in_dim(cotangent[0], first, share, 0)
    cot = padded(cot.reshape(share, frames * POOLED, d2), own_rows)

    slots = []
    masks = []
    row_own = jnp.where(jnp.arange(own_rows) < frames * POOLED, 0.0, NEG)
    row_mem = jnp.arange(mem_rows) < frames // 2 * POOLED
    for m in range(share):
        source = lax.dynamic_index_in_dim(assign[0], first + m, 0, keepdims=False)
        flag = lax.dynamic_index_in_dim(resets[0], first + m, 0, keepdims=False)
        slots.append(((head - source // share + heads) % heads) * share + source % share)
        has = (flag == 0) & (lax.axis_index("clip") > 0)
        masks.append(jnp.concatenate([jnp.tile(row_own, toks), jnp.tile(jnp.where(row_mem & has, 0.0, NEG), toks)]))
    bias = jnp.stack(masks)[:, None, :].astype(f32)

    pack_a = jnp.concatenate([w_up_a, w_down_a, w_qkv_a.reshape(w_qkv_a.shape[0], -1), w_out_a], axis=1)
    pack_q = w_qkv_b.reshape(w_qkv_b.shape[0], -1)
    pack_b = jnp.concatenate([w_up_b, w_down_b, w_out_b, w_skip_b], axis=1)
    group = ("head", "tok")
    all_a = lax.all_gather(pack_a, group).reshape(heads, d1, -1)
    all_q = lax.all_gather(pack_q, group).reshape(heads, d1, -1)
    all_b = lax.all_gather(pack_b, group).reshape(heads, d2, -1)

    def lanes(pack, low, width):
        return jnp.concatenate([pack[h, :, low:low + width] for h in range(heads)], axis=1)

    fa, ha = w_up_a.shape[1], w_out_a.shape[1]
    fb, hb, hs = w_up_b.shape[1], w_out_b.shape[1], w_skip_b.shape[1]
    up_a, down_a = lanes(all_a, 0, fa), lanes(all_a, fa, fa)
    q_a, k_a, v_a = (lanes(all_a, 2 * fa + i * ha, ha) for i in range(3))
    kv_a = jnp.concatenate([k_a, v_a], axis=1)
    out_a = lanes(all_a, 2 * fa + 3 * ha, ha)
    qkv_b = jnp.concatenate([lanes(all_q, i * hb, hb) for i in range(3)], axis=1)
    up_b, down_b = lanes(all_b, 0, fb), lanes(all_b, fb, fb)
    out_b, skip_b = lanes(all_b, 2 * fb, hb), lanes(all_b, 2 * fb + hb, hs)

    bias_qv_a, bias_qv_b = (lax.all_gather(b, "head", axis=1, tiled=True) for b in (qv_bias_a, qv_bias_b))
    bias_up_a, bias_up_b = (lax.all_gather(b, "head", axis=0, tiled=True) for b in (up_bias_a, up_bias_b))

    normed1 = layer_norm(stream, gains_a[0], shifts_a[0])
    low1 = normed1.astype(bf16)
    pooled1 = pool(pooling, normed1).astype(bf16)
    zero1 = jnp.zeros((d1,), f32)
    kv1 = (tokens_dot(pooled1, kv_a) + jnp.concatenate([zero1, bias_qv_a[1]])).astype(bf16)
    q1 = (tokens_dot(low1, q_a) + bias_qv_a[0]).astype(bf16)
    mem1 = jnp.einsum("jf,mfd->mjd", pairing.astype(bf16), kv1, preferred_element_type=f32).astype(bf16)
    own_kv1, mem_kv1 = share_keys(kv1, mem1, slots, heads)
    comb1, lse1 = attend(q1, own_kv1, mem_kv1, bias)
    after1 = stream + tokens_dot_t(comb1, out_a) + shifts_a[1]
    normed2 = layer_norm(after1, gains_a[1], shifts_a[2]).astype(bf16)
    pre1 = tokens_dot(normed2, up_a) + bias_up_a
    hidden1 = gelu(pre1).astype(bf16)
    middle = after1 + tokens_dot_t(hidden1, down_a) + shifts_a[3]

    normed3 = layer_norm(middle, gains_a[2], shifts_a[4])
    pooled3 = pool(pooling, normed3).astype(bf16)
    zero2 = jnp.zeros((d2,), f32)
    proj2 = (tokens_dot(pooled3, qkv_b) + jnp.concatenate([bias_qv_b[0], zero2, bias_qv_b[1]])).astype(bf16)
    q2, kv2 = proj2[..., :d2], proj2[..., d2:]
    mem2 = jnp.einsum("jf,mfd->mjd", pairing.astype(bf16), kv2, preferred_element_type=f32).astype(bf16)
    own_kv2, mem_kv2 = share_keys(kv2, mem2, slots, heads)
    comb2, lse2 = attend(q2, own_kv2, mem_kv2, bias)
    after2 = tokens_dot_t(comb2, out_b) + tokens_dot_t(pooled3, skip_b) + shifts_b[0]
    normed4 = layer_norm(after2, gains_b, shifts_b[1]).astype(bf16)
    pre2 = tokens_dot(normed4, up_b) + bias_up_b
    hidden2 = gelu(pre2).astype(bf16)
    mixed = (after2 + tokens_dot_t(hidden2, down_b) + shifts_b[2]).astype(bf16)

    cot32 = cot.astype(f32)
    g_down_b = weight_grad(cot, hidden2)
    pre_grad = gelu_back(pre2, tokens_dot(cot, down_b))
    g_bias_up_b = jnp.sum(pre_grad, axis=(0, 1))
    pre_low = pre_grad.astype(bf16)
    g_up_b = weight_grad(normed4, pre_low)
    back, g_gain_b, g_shift_b1 = norm_back(after2, gains_b, tokens_dot_t(pre_low, up_b))
    res2 = back + cot32
    res2_low = res2.astype(bf16)
    g_out_b = weight_grad(res2_low, comb2)
    g_skip_b = weight_grad(res2_low, pooled3)
    g_shifts_b = jnp.stack([jnp.sum(res2, axis=(0, 1)), g_shift_b1, jnp.sum(cot32, axis=(0, 1))])
    comb2_grad = tokens_dot(res2_low, out_b).astype(bf16)
    skip_grad = tokens_dot(res2_low, skip_b)
    dq2, dkv2, dmem2 = attend_back(q2, comb2_grad, own_kv2, mem_kv2, bias, lse2)
    kv2_grad = return_keys(dkv2, dmem2, slots, heads, pairing)
    g_qv_b = jnp.stack([jnp.sum(dq2, axis=(0, 1)), jnp.sum(kv2_grad[..., d2:], axis=(0, 1))])
    proj2_low = jnp.concatenate([dq2.astype(bf16), kv2_grad.astype(bf16)], axis=-1)
    g_qkv_b = weight_grad(pooled3, proj2_low)
    normed3_grad = unpool(pooling, tokens_dot_t(proj2_low, qkv_b) + skip_grad)
    middle_grad, g_gain_a2, g_shift_a4 = norm_back(middle, gains_a[2], normed3_grad)

    mid_low = middle_grad.astype(bf16)
    g_down_a = weight_grad(mid_low, hidden1)
    pre_grad = gelu_back(pre1, tokens_dot(mid_low, down_a))
    g_bias_up_a = jnp.sum(pre_grad, axis=(0, 1))
    pre_low = pre_grad.astype(bf16)
    g_up_a = weight_grad(normed2, pre_low)
    back, g_gain_a1, g_shift_a2 = norm_back(after1, gains_a[1], tokens_dot_t(pre_low, up_a))
    res1 = back + middle_grad
    res1_low = res1.astype(bf16)
    g_out_a = weight_grad(res1_low, comb1)
    comb1_grad = tokens_dot(res1_low, out_a).astype(bf16)
    dq1, dkv1, dmem1 = attend_back(q1, comb1_grad, own_kv1, mem_kv1, bias, lse1)
    kv1_grad = return_keys(dkv1, dmem1, slots, heads, pairing)
    g_qv_a = jnp.stack([jnp.sum(dq1, axis=(0, 1)), jnp.sum(kv1_grad[..., d1:], axis=(0, 1))])
    dq1_low, kv1_low = dq1.astype(bf16), kv1_grad.astype(bf16)
    g_q_a = weight_grad(low1, dq1_low)
    g_kv_a = weight_grad(pooled1, kv1_low)
    normed1_grad = tokens_dot_t(dq1_low, q_a) + unpool(pooling, tokens_dot_t(kv1_low, kv_a))
    back, g_gain_a0, g_shift_a0 = norm_back(stream, gains_a[0], normed1_grad)
    stream_grad = (back + res1).astype(bf16)

    def by_head(grad, width):
        return grad.reshape(grad.shape[0], heads, width).transpose(1, 0, 2)

    grad_a = jnp.concatenate(
        [by_head(g_up_a, fa), by_head(g_down_a, fa), by_head(g_q_a, ha), by_head(g_kv_a[:, :d1], ha),
         by_head(g_kv_a[:, d1:], ha), by_head(g_out_a, ha)], axis=2).astype(bf16)
    grad_q = jnp.concatenate([by_head(g_qkv_b[:, i * d2:(i + 1) * d2], hb) for i in range(3)], axis=2).astype(bf16)
    grad_b = jnp.concatenate(
        [by_head(g_up_b, fb), by_head(g_down_b, fb), by_head(g_out_b, hb), by_head(g_skip_b, hs)], axis=2).astype(bf16)

    def reduce_grads(grad):
        blocks = grad.reshape((heads * toks, -1) + grad.shape[2:])
        shard = lax.psum_scatter(blocks, group, scatter_dimension=0, tiled=False)
        return lax.psum(shard, "clip").astype(f32)

    sum_b, sum_q, sum_a = reduce_grads(grad_b), reduce_grads(grad_q), reduce_grads(grad_a)

    small = [
        jnp.stack([g_gain_a0, g_gain_a1, g_gain_a2]), g_gain_b,
        jnp.stack([g_shift_a0, jnp.sum(res1, axis=(0, 1)), g_shift_a2, jnp.sum(middle_grad, axis=(0, 1)), g_shift_a4]),
        g_shifts_b, g_qv_a, g_qv_b, g_bias_up_a, g_bias_up_b,
    ]
    flat = lax.psum(jnp.concatenate([piece.reshape(-1) for piece in small]), ("clip", "tok", "head"))
    pieces, at = [], 0
    for piece in small:
        pieces.append(flat[at:at + piece.size].reshape(piece.shape))
        at += piece.size

    def mine(piece, axis):
        width = piece.shape[axis] // heads
        return lax.dynamic_slice_in_dim(piece, head * width, width, axis)

    mixed_all = lax.all_gather(mixed[:, :frames * POOLED], "head", axis=0, tiled=True)
    stream_all = lax.all_gather(stream_grad, "head", axis=0, tiled=True)
    return (
        mixed_all.reshape(cotangent.shape),
        stream_all.astype(f32).reshape(clips_in.shape),
        sum_a[:, 2 * fa:2 * fa + 3 * ha].reshape(w_qkv_a.shape),
        sum_a[:, 2 * fa + 3 * ha:],
        sum_a[:, :fa],
        sum_a[:, fa:2 * fa],
        sum_q.reshape(w_qkv_b.shape),
        sum_b[:, 2 * fb:2 * fb + hb],
        sum_b[:, 2 * fb + hb:],
        sum_b[:, :fb],
        sum_b[:, fb:2 * fb],
        pieces[0], pieces[1], pieces[2], pieces[3],
        mine(pieces[4], 1), mine(pieces[5], 1), mine(pieces[6], 0), mine(pieces[7], 0),
    )


def solution(mesh):
    in_specs = (
        P("clip", None, "tok", None, None),
        P("clip", None),
        P("clip", None),
        P("tok", None, "head"),
        P("tok", "head"),
        P("tok", "head"),
        P("tok", "head"),
        P("tok", None, "head"),
        P("tok", "head"),
        P("tok", "head"),
        P("tok", "head"),
        P("tok", "head"),
        P(),
        P(),
        P(),
        P(),
        P(None, "head"),
        P(None, "head"),
        P("head"),
        P("head"),
        P("clip", None, "tok", None, None),
    )
    out_specs = (
        P("clip", None, "tok", None, None),
        P("clip", None, "tok", None, None),
        P("tok", None, "head"),
        P("tok", "head"),
        P("tok", "head"),
        P("tok", "head"),
        P("tok", None, "head"),
        P("tok", "head"),
        P("tok", "head"),
        P("tok", "head"),
        P("tok", "head"),
        P(),
        P(),
        P(),
        P(),
        P(None, "head"),
        P(None, "head"),
        P("head"),
        P("head"),
    )
    return jax.shard_map(local, mesh=mesh, in_specs=in_specs, out_specs=out_specs, check_vma=False)
```

```python
import functools
import math

import jax
import jax.numpy as jnp
import numpy as np
from jax import lax
from jax.experimental import pallas as pl
from jax.experimental.pallas import tpu as pltpu
from jax.sharding import PartitionSpec as P

GRID = 14
PATCH = GRID * GRID
POOLED = PATCH // 4
HD = 96
NEG = -1e30
VMEM_CAP = 62 * 2**20
eps = 1e-06
f32, bf16 = jnp.float32, jnp.bfloat16
NN, NT, TN = ((1,), (0,)), ((1,), (1,)), ((0,), (0,))


def up16(n):
    return -(-n // 16) * 16


def pool_matrix(frames):
    rows, cols = up16(frames * POOLED), frames * PATCH
    out = np.zeros((rows, cols), np.float32)
    half = GRID // 2
    for f in range(frames):
        for p in range(PATCH):
            r, c = divmod(p, GRID)
            out[f * POOLED + (r // 2) * half + c // 2, f * PATCH + p] = 0.25
    return out


def pair_matrix(frames):
    rows, cols = up16(frames // 2 * POOLED), up16(frames * POOLED)
    out = np.zeros((rows, cols), np.float32)
    for j in range(frames // 2):
        for p in range(POOLED):
            out[j * POOLED + p, 2 * j * POOLED + p] = 0.5
            out[j * POOLED + p, (2 * j + 1) * POOLED + p] = 0.5
    return out


def dot(a, b, dims=NN):
    return lax.dot_general(a, b, (dims, ((), ())), preferred_element_type=f32)


def exact_dot(matrix, tensor):
    high = tensor.astype(bf16)
    low = (tensor - high.astype(f32)).astype(bf16)
    return dot(matrix, high) + dot(matrix, low)


def norm(x):
    average = jnp.mean(x, axis=-1, keepdims=True)
    centred = x - average
    inverse = lax.rsqrt(jnp.mean(centred * centred, axis=-1, keepdims=True) + eps)
    return centred * inverse, inverse


def norm_back(unit, inverse, gain, gradient):
    scaled = gradient * gain
    return inverse * (
        scaled
        - jnp.mean(scaled, axis=-1, keepdims=True)
        - unit * jnp.mean(scaled * unit, axis=-1, keepdims=True)
    )


GELU_A, GELU_B = math.sqrt(2.0 / math.pi), 0.044715


def gelu(x):
    t = jnp.tanh(GELU_A * (x + GELU_B * (x * x * x)))
    return 0.5 * x * (1.0 + t)


def gelu_both(x):
    square = x * x
    t = jnp.tanh(GELU_A * x * (1.0 + GELU_B * square))
    value = 0.5 * x * (1.0 + t)
    slope = 0.5 * (1.0 + t) + 0.5 * x * (1.0 - t * t) * (GELU_A * (1.0 + 3.0 * GELU_B * square))
    return value, slope


def sum_rows(x):
    return jnp.sum(x, axis=0, keepdims=True)


def add_rows(ref, rows):
    step = pl.program_id(0)

    @pl.when(step == 0)
    def _():
        ref[...] = jnp.zeros_like(ref)

    for i, row in enumerate(rows):
        ref[i:i + 1, :] += row


def transposed(x):
    return x.astype(f32).T.astype(bf16)


def window(head):
    low = HD * head
    return low // 128 * 128, -(-(low + HD) // 128) * 128


def head_mask(head):
    start, stop = window(head)
    lane = lax.broadcasted_iota(jnp.int32, (1, stop - start), 1) + start
    return (lane >= HD * head) & (lane < HD * head + HD)


def key_rows(own_ref, mem_ref):
    row = 0
    for ref in (own_ref, mem_ref):
        for t in range(ref.shape[0]):
            yield ref, t, slice(row, row + ref.shape[2])
            row += ref.shape[2]


def project_keys(own_ref, mem_ref, w_ref, bias_ref, x_s, k_s, v_s):
    for ref, t, rows in key_rows(own_ref, mem_ref):
        x_s[rows, :] = ref[t, 0]
    width = k_s.shape[1]
    for low in range(0, width, 384):
        k_s[:, low:low + 384] = dot(x_s[...], w_ref[:, width + low:width + low + 384]).astype(bf16)
    for low in range(0, width, 384):
        value = dot(x_s[...], w_ref[:, 2 * width + low:2 * width + low + 384])
        v_s[:, low:low + 384] = (value + bias_ref[1:2, low:low + 384]).astype(bf16)


def project_queries(x_ref, w_ref, bias_ref, q_s):
    width = q_s.shape[1]
    for low in range(0, width, 384):
        value = dot(x_ref[0], w_ref[:, low:low + 384])
        q_s[:, low:low + 384] = (value + bias_ref[0:1, low:low + 384]).astype(bf16)


def norm_pool_kernel(x_ref, vec_ref, pool_ref, pair_ref, low_ref, pooled_ref, mean_ref):
    unit, _ = norm(x_ref[0].astype(f32))
    normed = unit * vec_ref[0:1, :] + vec_ref[1:2, :]
    low_ref[0] = normed.astype(bf16)
    pooled = exact_dot(pool_ref[...], normed)
    pooled_ref[0] = pooled.astype(bf16)
    mean_ref[0] = exact_dot(pair_ref[...], pooled).astype(bf16)


def attend_kernel(chunk, x_ref, own_ref, mem_ref, w_ref, qv_ref, mask_ref, out_ref, lse_ref, x_s, q_s, k_s, v_s, s_s, p_s):
    nq, width = q_s.shape
    project_queries(x_ref, w_ref, qv_ref, q_s)
    project_keys(own_ref, mem_ref, w_ref, qv_ref, x_s, k_s, v_s)
    factor = HD**-0.5 * math.log2(math.e)
    lanes = lax.broadcasted_iota(jnp.int32, (chunk, 128), 1)
    for tile in range(width // 384):
        group = slice(384 * tile, 384 * tile + 384)
        base = q_s[:, group].astype(f32)
        parts = [base[:, :128], base[:, 128:256], base[:, 256:384]]
        for head in range(4 * tile, 4 * tile + 4):
            start, stop = window(head)
            mask = head_mask(head)
            query = jnp.where(mask, q_s[:, start:stop], jnp.zeros((), bf16))
            s_s[...] = dot(query, k_s[:, start:stop], NT)

            def body(i, carry, head=head):
                rows = pl.ds(pl.multiple_of(i * chunk, chunk), chunk)
                score = s_s[rows, :] * factor + mask_ref[0]
                top = jnp.max(score, axis=1, keepdims=True)
                power = jnp.exp2(score - top)
                total = jnp.sum(power, axis=1, keepdims=True)
                p_s[rows, :] = (power * (1.0 / total)).astype(bf16)
                lse_ref[0, rows, :] = jnp.where(lanes == head, top + jnp.log2(total), lse_ref[0, rows, :])
                return carry

            lax.fori_loop(0, nq // chunk, body, 0, unroll=nq // chunk)
            out = jnp.where(mask, dot(p_s[...], v_s[:, start:stop]), 0.0)
            for w in range((stop - start) // 128):
                k = start // 128 - 3 * tile + w
                parts[k] = parts[k] + out[:, 128 * w:128 * w + 128]
        out_ref[0, :, group] = jnp.concatenate(parts, axis=1).astype(bf16)


def attend_back_kernel(
    chunk, x_ref, g_ref, own_ref, mem_ref, w_ref, qv_ref, mask_ref, lse_ref,
    dx_ref, dpool_ref, gw_ref, row_ref,
    x_s, q_s, k_s, v_s, s_s, dp_s, p_s, ds_s, dk_s, dv_s, dq_s, gw_s,
):
    nq, width = q_s.shape
    step = pl.program_id(0)
    project_queries(x_ref, w_ref, qv_ref, q_s)
    project_keys(own_ref, mem_ref, w_ref, qv_ref, x_s, k_s, v_s)
    scaling = HD**-0.5
    factor = scaling * math.log2(math.e)
    lanes = lax.broadcasted_iota(jnp.int32, (chunk, 128), 1)

    @pl.when(step == 0)
    def _():
        gw_s[...] = jnp.zeros_like(gw_s)

    xt = transposed(x_ref[0])
    keys_t = transposed(x_s[...])
    dx = None
    dpool = None
    row_q, row_v = [], []
    for tile in range(width // 384):
        group = slice(384 * tile, 384 * tile + 384)
        qt = transposed(q_s[:, group])
        gt = transposed(g_ref[0, :, group])
        parts = [None] * 3
        for head in range(4 * tile, 4 * tile + 4):
            start, stop = window(head)
            mask = head_mask(head)
            query = jnp.where(mask, q_s[:, start:stop], jnp.zeros((), bf16))
            grad = jnp.where(mask, g_ref[0, :, start:stop], jnp.zeros((), bf16))
            s_s[...] = dot(query, k_s[:, start:stop], NT)
            dp_s[...] = dot(grad, v_s[:, start:stop], NT)

            def body(i, carry, head=head):
                rows = pl.ds(pl.multiple_of(i * chunk, chunk), chunk)
                lse = jnp.sum(jnp.where(lanes == head, lse_ref[0, rows, :], 0.0), axis=1, keepdims=True)
                p = jnp.exp2(s_s[rows, :] * factor + mask_ref[0] - lse)
                dp = dp_s[rows, :]
                inner = jnp.sum(p * dp, axis=1, keepdims=True)
                p_s[rows, :] = p.astype(bf16)
                ds_s[rows, :] = (p * (dp - inner)).astype(bf16)
                return carry

            lax.fori_loop(0, nq // chunk, body, 0, unroll=nq // chunk)
            r = slice(HD * (head - 4 * tile), HD * (head - 4 * tile) + HD)
            dv_s[r, :] = dot(gt[r], p_s[...])
            dk_s[r, :] = dot(qt[r], ds_s[...]) * scaling
            dq = jnp.where(mask, dot(ds_s[...], k_s[:, start:stop]) * scaling, 0.0)
            for w in range((stop - start) // 128):
                k = start // 128 - 3 * tile + w
                part = dq[:, 128 * w:128 * w + 128]
                parts[k] = part if parts[k] is None else parts[k] + part
        total = jnp.concatenate(parts, axis=1) + g_ref[0, :, group].astype(f32)
        row_q.append(sum_rows(total))
        low = total.astype(bf16)
        gw_s[:, group] += dot(xt, low)
        add = dot(low, w_ref[:, group], NT)
        dx = add if dx is None else dx + add
        for base, src in ((width, dk_s), (2 * width, dv_s)):
            grad = src[...].T
            if base == 2 * width:
                row_v.append(sum_rows(grad))
            low = grad.astype(bf16)
            here = slice(base + 384 * tile, base + 384 * tile + 384)
            gw_s[:, here] += dot(keys_t, low)
            add = dot(low, w_ref[:, here], NT)
            dpool = add if dpool is None else dpool + add
    dx_ref[0] = dx
    row = 0
    own, mem = own_ref.shape[2], mem_ref.shape[2]
    toks = own_ref.shape[0]
    for t in range(toks):
        dpool_ref[t, 0, :own, :] = dpool[t * own:(t + 1) * own].astype(bf16)
        dpool_ref[t, 0, own:, :] = dpool[toks * own + t * mem:toks * own + (t + 1) * mem].astype(bf16)
    add_rows(row_ref, [jnp.concatenate(row_q, axis=1), jnp.concatenate(row_v, axis=1)])

    @pl.when(step == pl.num_programs(0) - 1)
    def _():
        gw_ref[...] = gw_s[...].astype(bf16)


def first_mlp_kernel(x_ref, comb_ref, out_ref, up_ref, down_ref, ub_ref, vec_ref, pool_ref, pair_ref,
                     after_ref, middle_ref, pooled_ref, mean_ref):
    after = x_ref[0].astype(f32) + dot(comb_ref[0], out_ref[...], NT) + vec_ref[0:1, :]
    after_ref[0] = after
    unit, _ = norm(after)
    low = (unit * vec_ref[1:2, :] + vec_ref[2:3, :]).astype(bf16)
    total = after + vec_ref[3:4, :]
    for h in range(up_ref.shape[0]):
        hidden = gelu(dot(low, up_ref[h]) + ub_ref[h]).astype(bf16)
        total = total + dot(hidden, down_ref[h], NT)
    middle_ref[0] = total
    unit, _ = norm(total)
    pooled = exact_dot(pool_ref[...], unit * vec_ref[4:5, :] + vec_ref[5:6, :])
    pooled_ref[0] = pooled.astype(bf16)
    mean_ref[0] = exact_dot(pair_ref[...], pooled).astype(bf16)


def second_mlp_kernel(
    comb_ref, pooled_ref, cot_ref, out_ref, skip_ref, up_ref, down_ref, ub_ref, vec_ref,
    mixed_ref, dcomb_ref, dskip_ref, gup_ref, gdown_ref, gout_ref, gskip_ref, gub_ref, row_ref,
    after_s, low_s, lowt_s, cott_s, sum_s, dlow_s,
):
    step = pl.program_id(0)

    @pl.when(step == 0)
    def _():
        after = dot(comb_ref[...], out_ref[...], NT) + dot(pooled_ref[...], skip_ref[...], NT) + vec_ref[0:1, :]
        after_s[...] = after
        unit, _ = norm(after)
        low = (unit * vec_ref[1:2, :] + vec_ref[2:3, :]).astype(bf16)
        low_s[...] = low
        lowt_s[...] = transposed(low)
        cott_s[...] = transposed(cot_ref[...])
        sum_s[...] = after + vec_ref[3:4, :]
        dlow_s[...] = jnp.zeros_like(dlow_s)

    pre = dot(low_s[...], up_ref[0]) + ub_ref[...]
    hidden, slope = gelu_both(pre)
    hidden = hidden.astype(bf16)
    dpre = dot(cot_ref[...], down_ref[0]) * slope
    gub_ref[...] = sum_rows(dpre)
    dpre = dpre.astype(bf16)
    sum_s[...] += dot(hidden, down_ref[0], NT)
    dlow_s[...] += dot(dpre, up_ref[0], NT)
    gup_ref[0] = dot(lowt_s[...], dpre).astype(bf16)
    gdown_ref[0] = dot(cott_s[...], hidden).astype(bf16)

    @pl.when(step == pl.num_programs(0) - 1)
    def _():
        mixed_ref[...] = sum_s[...].astype(bf16)
        unit, inverse = norm(after_s[...])
        dlow = dlow_s[...]
        cot = cot_ref[...].astype(f32)
        res = norm_back(unit, inverse, vec_ref[1:2, :], dlow) + cot
        row_ref[...] = jnp.zeros_like(row_ref)
        for i, row in enumerate((res, dlow, cot, dlow * unit)):
            row_ref[i:i + 1, :] = sum_rows(row)
        res = res.astype(bf16)
        dcomb_ref[...] = dot(res, out_ref[...]).astype(bf16)
        dskip_ref[...] = dot(res, skip_ref[...])
        rest = transposed(res)
        gout_ref[...] = dot(rest, comb_ref[...]).astype(bf16)
        gskip_ref[...] = dot(rest, pooled_ref[...]).astype(bf16)


def first_back_kernel(
    middle_ref, after_ref, comb_ref, dskip_ref, dq_ref, own_ref, mem_ref, out_ref, up_ref, down_ref, ub_ref, vec_ref,
    unpool_ref, unpair_ref,
    res_ref, dcomb_ref, gup_ref, gdown_ref, gout_ref, gub_ref, row_ref,
    gup_s, gdown_s, gout_s,
):
    step = pl.program_id(0)

    @pl.when(step == 0)
    def _():
        gup_s[...] = jnp.zeros_like(gup_s)
        gdown_s[...] = jnp.zeros_like(gdown_s)
        gout_s[...] = jnp.zeros_like(gout_s)
        gub_ref[...] = jnp.zeros_like(gub_ref)

    memory = mem_ref[0, 0].astype(f32)
    for d in range(1, mem_ref.shape[0]):
        memory = memory + mem_ref[d, 0].astype(f32)
    dpool = dskip_ref[0] + dq_ref[0] + own_ref[0].astype(f32) + exact_dot(unpair_ref[...], memory)
    dnorm = exact_dot(unpool_ref[...], dpool)
    unit, inverse = norm(middle_ref[0])
    grad = norm_back(unit, inverse, vec_ref[2:3, :], dnorm)
    rows = [sum_rows(dnorm * unit), sum_rows(dnorm), sum_rows(grad)]
    low = grad.astype(bf16)
    lowt = transposed(low)
    unit, inverse = norm(after_ref[0])
    normed = (unit * vec_ref[0:1, :] + vec_ref[1:2, :]).astype(bf16)
    normedt = transposed(normed)
    dnormed = None
    for h in range(up_ref.shape[0]):
        hidden, slope = gelu_both(dot(normed, up_ref[h]) + ub_ref[h])
        hidden = hidden.astype(bf16)
        dpre = dot(low, down_ref[h]) * slope
        gub_ref[h] += sum_rows(dpre)
        dpre = dpre.astype(bf16)
        gdown_s[h] += dot(lowt, hidden)
        gup_s[h] += dot(normedt, dpre)
        add = dot(dpre, up_ref[h], NT)
        dnormed = add if dnormed is None else dnormed + add
    res = norm_back(unit, inverse, vec_ref[0:1, :], dnormed) + grad
    rows += [sum_rows(dnormed * unit), sum_rows(dnormed), sum_rows(res)]
    res_ref[0] = res
    res = res.astype(bf16)
    dcomb_ref[0] = dot(res, out_ref[...]).astype(bf16)
    gout_s[...] += dot(transposed(res), comb_ref[0])
    add_rows(row_ref, rows)

    @pl.when(step == pl.num_programs(0) - 1)
    def _():
        gup_ref[...] = gup_s[...].astype(bf16)
        gdown_ref[...] = gdown_s[...].astype(bf16)
        gout_ref[...] = gout_s[...].astype(bf16)


def last_back_kernel(x_ref, res_ref, dx_ref, own_ref, mem_ref, vec_ref, unpool_ref, unpair_ref, grad_ref, row_ref):
    memory = mem_ref[0, 0].astype(f32)
    for d in range(1, mem_ref.shape[0]):
        memory = memory + mem_ref[d, 0].astype(f32)
    dpool = own_ref[0].astype(f32) + exact_dot(unpair_ref[...], memory)
    dnorm = dx_ref[0] + exact_dot(unpool_ref[...], dpool)
    unit, inverse = norm(x_ref[0].astype(f32))
    grad_ref[0] = (norm_back(unit, inverse, vec_ref[0:1, :], dnorm) + res_ref[0]).astype(bf16)
    add_rows(row_ref, [sum_rows(dnorm * unit), sum_rows(dnorm)])


def whole(array):
    return pl.BlockSpec(array.shape, lambda i: (0,) * array.ndim)


def by_micro(array, axis=0):
    block = array.shape[:axis] + (1,) + array.shape[axis + 1:]
    return pl.BlockSpec(block, lambda i: (0,) * axis + (i,) + (0,) * (array.ndim - axis - 1))


def shape(dims, dtype):
    return jax.ShapeDtypeStruct(dims, dtype)


def call(kernel, steps, args, outs, scratch=(), name=None):
    def spec(array, how):
        if how is None:
            return whole(array)
        return by_micro(array, how) if isinstance(how, int) else how

    return pl.pallas_call(
        kernel,
        grid=(steps,),
        in_specs=[spec(a, how) for a, how in args],
        out_specs=[spec(a, how) for a, how in outs],
        out_shape=[a for a, _ in outs],
        scratch_shapes=[pltpu.VMEM(dims, dtype) for dims, dtype in scratch],
        compiler_params=pltpu.CompilerParams(vmem_limit_bytes=VMEM_CAP),
        name=name,
    )(*[a for a, _ in args])


def chunk_of(nq):
    return 112 if nq % 112 == 0 else 16


def attend(x, own, mem, w, qv, mask, width):
    batches, nq, d = x.shape
    keys = own.shape[0] * own.shape[2] + mem.shape[0] * mem.shape[2]
    return call(
        functools.partial(attend_kernel, chunk_of(nq)), batches,
        [(x, 0), (own, 1), (mem, 1), (w, None), (qv, None), (mask, 0)],
        [(shape((batches, nq, width), bf16), 0), (shape((batches, nq, 128), f32), 0)],
        [((keys, d), bf16), ((nq, width), bf16), ((keys, width), bf16), ((keys, width), bf16), ((nq, keys), f32), ((nq, keys), bf16)],
        name="attend",
    )


def attend_back(x, grad, own, mem, w, qv, mask, lse):
    batches, nq, d = x.shape
    width = grad.shape[2]
    keys = own.shape[0] * own.shape[2] + mem.shape[0] * mem.shape[2]
    both = (own.shape[0], batches, own.shape[2] + mem.shape[2], d)
    return call(
        functools.partial(attend_back_kernel, chunk_of(nq)), batches,
        [(x, 0), (grad, 0), (own, 1), (mem, 1), (w, None), (qv, None), (mask, 0), (lse, 0)],
        [(shape((batches, nq, d), f32), 0), (shape(both, bf16), 1), (shape(w.shape, bf16), None), (shape((8, width), f32), None)],
        [((keys, d), bf16), ((nq, width), bf16), ((keys, width), bf16), ((keys, width), bf16),
         ((nq, keys), f32), ((nq, keys), f32), ((nq, keys), bf16), ((nq, keys), bf16),
         ((384, keys), f32), ((384, keys), f32), ((8, 128), f32), (w.shape, f32)],
        name="attend_back",
    )


def grouped(pairs_of):
    clips, heads = lax.axis_size("clip"), lax.axis_size("head")
    return [
        (c * heads + h, c2 * heads + h2)
        for c in range(clips)
        for h in range(heads)
        for c2, h2 in [pairs_of(c, h)]
        if 0 <= c2 < clips
    ]


def to_clip(pieces, by, heads):
    return [
        lax.ppermute(pieces[d], ("clip", "head"), grouped(lambda c, h, d=d: (c + by, (h + d) % heads)))
        for d in range(heads)
    ]


def share_pooled(pooled, mean, slots, heads):
    received = to_clip([mean] * heads, 1, heads)
    own = lax.all_gather(pooled, "tok")
    flat = jnp.stack(received).reshape((-1,) + mean.shape[1:])
    chosen = jnp.stack([lax.dynamic_index_in_dim(flat, slot, 0, keepdims=False) for slot in slots])
    return own, lax.all_gather(chosen, "tok")


def halve_over_tok(partial):
    size = lax.axis_size("tok")
    index = lax.axis_index("tok")
    bit = 1
    while bit < size:
        mine = (index // bit) % 2
        paired = partial.reshape((partial.shape[0] // 2, 2) + partial.shape[1:])
        keep = lax.dynamic_index_in_dim(paired, mine, 1, keepdims=False)
        give = lax.dynamic_index_in_dim(paired, 1 - mine, 1, keepdims=False)
        got = lax.ppermute(give, "tok", [(i, i ^ bit) for i in range(size)])
        partial = (keep.astype(f32) + got.astype(f32)).astype(bf16)
        bit *= 2
    return partial[0]


def return_pooled(dpool, own_rows, slots, heads):
    total = halve_over_tok(dpool)
    own, mem = total[:, :own_rows], total[:, own_rows:]
    routed = jnp.zeros((heads * mem.shape[0],) + mem.shape[1:], bf16)
    for m, slot in enumerate(slots):
        routed = lax.dynamic_update_index_in_dim(routed, mem[m], slot, 0)
    routed = routed.reshape((heads,) + mem.shape)
    return own, jnp.stack(to_clip([routed[(heads - d) % heads] for d in range(heads)], -1, heads))


def padded_rows(*rows):
    return jnp.concatenate([jnp.stack(rows), jnp.zeros((-len(rows) % 8, rows[0].shape[0]), f32)])


def local(
    clips_in, resets, assign, w_qkv_a, w_out_a, w_up_a, w_down_a, w_qkv_b, w_out_b, w_skip_b, w_up_b, w_down_b,
    gains_a, gains_b, shifts_a, shifts_b, qv_bias_a, qv_bias_b, up_bias_a, up_bias_b, cotangent,
):
    heads, toks = lax.axis_size("head"), lax.axis_size("tok")
    head = lax.axis_index("head")
    micro, frames = clips_in.shape[1], clips_in.shape[2]
    d1, d2 = clips_in.shape[-1], cotangent.shape[-1]
    share = micro // heads
    first = head * share
    pool_np, pair_np = pool_matrix(frames), pair_matrix(frames)
    pooling, pairing = jnp.asarray(pool_np, bf16), jnp.asarray(pair_np, bf16)
    unpooling, unpairing = jnp.asarray(pool_np.T, bf16), jnp.asarray(pair_np.T, bf16)
    tokens, pooled_tokens = frames * PATCH, frames * POOLED
    own_rows, mem_rows = up16(pooled_tokens), up16(frames // 2 * POOLED)
    rows2 = share * own_rows

    stream = lax.dynamic_slice_in_dim(clips_in[0], first, share, 0).reshape(share, tokens, d1)
    cot = lax.dynamic_slice_in_dim(cotangent[0], first, share, 0).reshape(share, pooled_tokens, d2)
    cot = jnp.pad(cot, ((0, 0), (0, own_rows - pooled_tokens), (0, 0))).reshape(rows2, d2)

    slots, masks = [], []
    row_own = jnp.where(jnp.arange(own_rows) < pooled_tokens, 0.0, NEG)
    row_mem = jnp.arange(mem_rows) < frames // 2 * POOLED
    for m in range(share):
        source = lax.dynamic_index_in_dim(assign[0], first + m, 0, keepdims=False)
        flag = lax.dynamic_index_in_dim(resets[0], first + m, 0, keepdims=False)
        slots.append(((head - source // share + heads) % heads) * share + source % share)
        has = (flag == 0) & (lax.axis_index("clip") > 0)
        masks.append(jnp.concatenate([jnp.tile(row_own, toks), jnp.tile(jnp.where(row_mem & has, 0.0, NEG), toks)]))
    mask = jnp.stack(masks)[:, None, :].astype(f32)

    group = ("head", "tok")
    fa, ha = w_up_a.shape[1], w_out_a.shape[1]
    fb, hb, hs = w_up_b.shape[1], w_out_b.shape[1], w_skip_b.shape[1]
    pack_a = jnp.concatenate([w_up_a, w_down_a, w_qkv_a.reshape(w_qkv_a.shape[0], -1), w_out_a], axis=1)
    all_a = lax.all_gather(pack_a, group).reshape(heads, d1, -1)
    all_q = lax.all_gather(w_qkv_b.reshape(w_qkv_b.shape[0], -1), group).reshape(heads, d1, -1)
    all_o = lax.all_gather(jnp.concatenate([w_out_b, w_skip_b], axis=1), group).reshape(heads, d2, -1)
    all_b = lax.all_gather(jnp.concatenate([w_up_b, w_down_b], axis=1), group).reshape(heads, d2, -1)
    flat = jnp.concatenate([qv_bias_a.reshape(-1), qv_bias_b.reshape(-1), up_bias_a, up_bias_b])
    flat = lax.all_gather(flat, "head")
    qv_a = flat[:, :2 * ha].reshape(heads, 2, ha).transpose(1, 0, 2).reshape(2, d1)
    qv_b = flat[:, 2 * ha:2 * ha + 2 * hb].reshape(heads, 2, hb).transpose(1, 0, 2).reshape(2, d2)
    ub_a = flat[:, 2 * (ha + hb):2 * (ha + hb) + fa].reshape(heads, 1, fa)
    ub_b = flat[:, 2 * (ha + hb) + fa:].reshape(1, heads * fb)

    def lanes(pack, low, width):
        return jnp.concatenate([pack[h, :, low:low + width] for h in range(heads)], axis=1)

    up_a, down_a = all_a[:, :, :fa], all_a[:, :, fa:2 * fa]
    qkv_a = jnp.concatenate([lanes(all_a, 2 * fa + i * ha, ha) for i in range(3)], axis=1)
    out_a = lanes(all_a, 2 * fa + 3 * ha, ha)
    qkv_b = jnp.concatenate([lanes(all_q, i * hb, hb) for i in range(3)], axis=1)
    out_b, skip_b = lanes(all_o, 0, hb), lanes(all_o, hb, hs)

    low1, pooled1, mean1 = call(
        norm_pool_kernel, share,
        [(stream, 0), (padded_rows(gains_a[0], shifts_a[0]), None), (pooling, None), (pairing, None)],
        [(shape((share, tokens, d1), bf16), 0), (shape((share, own_rows, d1), bf16), 0), (shape((share, mem_rows, d1), bf16), 0)],
        name="norm_pool",
    )
    own1, mem1 = share_pooled(pooled1, mean1, slots, heads)
    comb1, lse1 = attend(low1, own1, mem1, qkv_a, qv_a, mask, d1)
    after1, middle, pooled3, mean3 = call(
        first_mlp_kernel, share,
        [(stream, 0), (comb1, 0), (out_a, None), (up_a, None), (down_a, None), (ub_a, None),
         (padded_rows(shifts_a[1], gains_a[1], shifts_a[2], shifts_a[3], gains_a[2], shifts_a[4]), None),
         (pooling, None), (pairing, None)],
        [(shape((share, tokens, d1), f32), 0), (shape((share, tokens, d1), f32), 0),
         (shape((share, own_rows, d1), bf16), 0), (shape((share, mem_rows, d1), bf16), 0)],
        name="first_mlp",
    )

    own2, mem2 = share_pooled(pooled3, mean3, slots, heads)
    comb2, lse2 = attend(pooled3, own2, mem2, qkv_b, qv_b, mask, d2)
    chunk = 768
    per_head = fb // chunk
    steps = heads * per_head
    rows_spec = pl.BlockSpec((1, d2, chunk), lambda j: (j // per_head, 0, j % per_head))
    mixed, dcomb2, dskip, g_up_b, g_down_b, g_out_b, g_skip_b, g_ub_b, rows_b = call(
        second_mlp_kernel, steps,
        [(comb2.reshape(rows2, d2), None), (pooled3.reshape(rows2, d1), None), (cot, None), (out_b, None), (skip_b, None),
         (all_b, rows_spec),
         (all_b, pl.BlockSpec((1, d2, chunk), lambda j: (j // per_head, 0, per_head + j % per_head))),
         (ub_b, pl.BlockSpec((1, chunk), lambda j: (0, j))),
         (padded_rows(shifts_b[0], gains_b, shifts_b[1], shifts_b[2]), None)],
        [(shape((rows2, d2), bf16), None), (shape((rows2, d2), bf16), None), (shape((rows2, d1), f32), None),
         (shape((heads, d2, fb), bf16), rows_spec), (shape((heads, d2, fb), bf16), rows_spec),
         (shape((d2, d2), bf16), None), (shape((d2, d1), bf16), None),
         (shape((1, heads * fb), f32), pl.BlockSpec((1, chunk), lambda j: (0, j))), (shape((8, d2), f32), None)],
        [((rows2, d2), f32), ((rows2, d2), bf16), ((d2, rows2), bf16), ((d2, rows2), bf16), ((rows2, d2), f32), ((rows2, d2), f32)],
        name="second_mlp",
    )

    def reduce_grad(blocks):
        blocks = blocks.reshape((heads * toks, -1) + blocks.shape[2:])
        shard = lax.psum_scatter(blocks, group, scatter_dimension=0, tiled=False)
        return lax.psum(shard, "clip").astype(f32)

    def by_head(grad, width):
        return grad.reshape(grad.shape[0], heads, width).transpose(1, 0, 2)

    dcomb2 = dcomb2.reshape(share, own_rows, d2)
    dq2, dpool2, g_qkv_b, rows_qv_b = attend_back(pooled3, dcomb2, own2, mem2, qkv_b, qv_b, mask, lse2)
    own_back2, mem_back2 = return_pooled(dpool2, own_rows, slots, heads)

    res1, dcomb1, g_up_a, g_down_a, g_out_a, g_ub_a, rows_a = call(
        first_back_kernel, share,
        [(middle, 0), (after1, 0), (comb1, 0), (dskip.reshape(share, own_rows, d1), 0), (dq2, 0), (own_back2, 0), (mem_back2, 1),
         (out_a, None), (up_a, None), (down_a, None), (ub_a, None),
         (padded_rows(gains_a[1], shifts_a[2], gains_a[2]), None), (unpooling, None), (unpairing, None)],
        [(shape((share, tokens, d1), f32), 0), (shape((share, tokens, d1), bf16), 0),
         (shape((heads, d1, fa), bf16), None), (shape((heads, d1, fa), bf16), None), (shape((d1, d1), bf16), None),
         (shape((heads, 1, fa), f32), None), (shape((8, d1), f32), None)],
        [((heads, d1, fa), f32), ((heads, d1, fa), f32), ((d1, d1), f32)],
        name="first_back",
    )
    dx1, dpool1, g_qkv_a, rows_qv_a = attend_back(low1, dcomb1, own1, mem1, qkv_a, qv_a, mask, lse1)
    own_back1, mem_back1 = return_pooled(dpool1, own_rows, slots, heads)
    stream_grad, rows_last = call(
        last_back_kernel, share,
        [(stream, 0), (res1, 0), (dx1, 0), (own_back1, 0), (mem_back1, 1), (padded_rows(gains_a[0]), None),
         (unpooling, None), (unpairing, None)],
        [(shape((share, tokens, d1), bf16), 0), (shape((8, d1), f32), None)],
        name="last_back",
    )

    sum_up_b, sum_down_b = reduce_grad(g_up_b), reduce_grad(g_down_b)
    grad_q = jnp.concatenate([by_head(g_qkv_b[:, i * d2:(i + 1) * d2], hb) for i in range(3)], axis=2)
    grad_o = jnp.concatenate([by_head(g_out_b, hb), by_head(g_skip_b, hs)], axis=2)
    sum_q, sum_o = reduce_grad(grad_q), reduce_grad(grad_o)
    grad_a = jnp.concatenate(
        [g_up_a, g_down_a] + [by_head(g_qkv_a[:, i * d1:(i + 1) * d1], ha) for i in range(3)] + [by_head(g_out_a, ha)], axis=2)
    sum_a = reduce_grad(grad_a)

    small = [
        jnp.stack([rows_last[0], rows_a[3], rows_a[0]]), rows_b[3],
        jnp.stack([rows_last[1], rows_a[5], rows_a[4], rows_a[2], rows_a[1]]),
        rows_b[:3], rows_qv_a[:2], rows_qv_b[:2], g_ub_a, g_ub_b,
    ]
    flat = lax.all_gather(jnp.concatenate([piece.reshape(-1) for piece in small]), ("clip", "tok", "head")).sum(axis=0)
    pieces, at = [], 0
    for piece in small:
        pieces.append(flat[at:at + piece.size].reshape(piece.shape))
        at += piece.size

    def mine(piece, axis):
        width = piece.shape[axis] // heads
        return lax.dynamic_slice_in_dim(piece, head * width, width, axis)

    mixed = mixed.reshape(share, own_rows, d2)[:, :pooled_tokens]
    mixed_all = lax.all_gather(mixed, "head", axis=0, tiled=True)
    stream_all = lax.all_gather(stream_grad, "head", axis=0, tiled=True)
    return (
        mixed_all.reshape(cotangent.shape),
        stream_all.astype(f32).reshape(clips_in.shape),
        sum_a[:, 2 * fa:2 * fa + 3 * ha].reshape(w_qkv_a.shape),
        sum_a[:, 2 * fa + 3 * ha:],
        sum_a[:, :fa],
        sum_a[:, fa:2 * fa],
        sum_q.reshape(w_qkv_b.shape),
        sum_o[:, :hb],
        sum_o[:, hb:],
        sum_up_b,
        sum_down_b,
        pieces[0], pieces[1], pieces[2], pieces[3],
        mine(pieces[4], 1), mine(pieces[5], 1), mine(pieces[6].reshape(-1), 0), mine(pieces[7].reshape(-1), 0),
    )


def solution(mesh):
    in_specs = (
        P("clip", None, "tok", None, None),
        P("clip", None),
        P("clip", None),
        P("tok", None, "head"),
        P("tok", "head"),
        P("tok", "head"),
        P("tok", "head"),
        P("tok", None, "head"),
        P("tok", "head"),
        P("tok", "head"),
        P("tok", "head"),
        P("tok", "head"),
        P(),
        P(),
        P(),
        P(),
        P(None, "head"),
        P(None, "head"),
        P("head"),
        P("head"),
        P("clip", None, "tok", None, None),
    )
    out_specs = (
        P("clip", None, "tok", None, None),
        P("clip", None, "tok", None, None),
        P("tok", None, "head"),
        P("tok", "head"),
        P("tok", "head"),
        P("tok", "head"),
        P("tok", None, "head"),
        P("tok", "head"),
        P("tok", "head"),
        P("tok", "head"),
        P("tok", "head"),
        P(),
        P(),
        P(),
        P(),
        P(None, "head"),
        P(None, "head"),
        P("head"),
        P("head"),
    )
    return jax.shard_map(local, mesh=mesh, in_specs=in_specs, out_specs=out_specs, check_vma=False)
```

```python
import functools
import math

import jax
import jax.numpy as jnp
import numpy as np
from jax import lax
from jax.experimental import pallas as pl
from jax.experimental.pallas import tpu as pltpu
from jax.sharding import PartitionSpec as P

GRID = 14
PATCH = GRID * GRID
POOLED = PATCH // 4
HD = 96
NEG = -1e30
VMEM_CAP = 62 * 2**20
eps = 1e-06
f32, bf16 = jnp.float32, jnp.bfloat16
NN, NT, TN = ((1,), (0,)), ((1,), (1,)), ((0,), (0,))


def up16(n):
    return -(-n // 16) * 16


def pool_matrix(frames):
    rows, cols = up16(frames * POOLED), frames * PATCH
    out = np.zeros((rows, cols), np.float32)
    half = GRID // 2
    for f in range(frames):
        for p in range(PATCH):
            r, c = divmod(p, GRID)
            out[f * POOLED + (r // 2) * half + c // 2, f * PATCH + p] = 0.25
    return out


def pair_matrix(frames):
    rows, cols = up16(frames // 2 * POOLED), up16(frames * POOLED)
    out = np.zeros((rows, cols), np.float32)
    for j in range(frames // 2):
        for p in range(POOLED):
            out[j * POOLED + p, 2 * j * POOLED + p] = 0.5
            out[j * POOLED + p, (2 * j + 1) * POOLED + p] = 0.5
    return out


def dot(a, b, dims=NN):
    return lax.dot_general(a, b, (dims, ((), ())), preferred_element_type=f32)


def exact_dot(matrix, tensor):
    high = tensor.astype(bf16)
    low = (tensor - high.astype(f32)).astype(bf16)
    return dot(matrix, high) + dot(matrix, low)


def norm(x):
    average = jnp.mean(x, axis=-1, keepdims=True)
    centred = x - average
    inverse = lax.rsqrt(jnp.mean(centred * centred, axis=-1, keepdims=True) + eps)
    return centred * inverse, inverse


def norm_back(unit, inverse, gain, gradient):
    scaled = gradient * gain
    return inverse * (
        scaled
        - jnp.mean(scaled, axis=-1, keepdims=True)
        - unit * jnp.mean(scaled * unit, axis=-1, keepdims=True)
    )


GELU_A, GELU_B = math.sqrt(2.0 / math.pi), 0.044715


def gelu(x):
    t = jnp.tanh(GELU_A * (x + GELU_B * (x * x * x)))
    return 0.5 * x * (1.0 + t)


def gelu_both(x):
    square = x * x
    t = jnp.tanh(GELU_A * x * (1.0 + GELU_B * square))
    value = 0.5 * x * (1.0 + t)
    slope = 0.5 * (1.0 + t) + 0.5 * x * (1.0 - t * t) * (GELU_A * (1.0 + 3.0 * GELU_B * square))
    return value, slope


def sum_rows(x):
    return jnp.sum(x, axis=0, keepdims=True)


def add_rows(ref, rows):
    step = pl.program_id(0)

    @pl.when(step == 0)
    def _():
        ref[...] = jnp.zeros_like(ref)

    for i, row in enumerate(rows):
        ref[i:i + 1, :] += row


def transposed(x):
    return x.astype(f32).T.astype(bf16)


def window(head):
    low = HD * head
    return low // 128 * 128, -(-(low + HD) // 128) * 128


def head_mask(head):
    start, stop = window(head)
    lane = lax.broadcasted_iota(jnp.int32, (1, stop - start), 1) + start
    return (lane >= HD * head) & (lane < HD * head + HD)


def key_rows(own_ref, mem_ref):
    row = 0
    for ref in (own_ref, mem_ref):
        for t in range(ref.shape[0]):
            yield ref, t, slice(row, row + ref.shape[2])
            row += ref.shape[2]


def project_keys(own_ref, mem_ref, w_ref, bias_ref, x_s, k_s, v_s):
    for ref, t, rows in key_rows(own_ref, mem_ref):
        x_s[rows, :] = ref[t, 0]
    width = k_s.shape[1]
    for low in range(0, width, 384):
        k_s[:, low:low + 384] = dot(x_s[...], w_ref[:, width + low:width + low + 384]).astype(bf16)
    for low in range(0, width, 384):
        value = dot(x_s[...], w_ref[:, 2 * width + low:2 * width + low + 384])
        v_s[:, low:low + 384] = (value + bias_ref[1:2, low:low + 384]).astype(bf16)


def project_queries(x_ref, w_ref, bias_ref, q_s):
    width = q_s.shape[1]
    for low in range(0, width, 384):
        value = dot(x_ref[0], w_ref[:, low:low + 384])
        q_s[:, low:low + 384] = (value + bias_ref[0:1, low:low + 384]).astype(bf16)


def norm_pool_kernel(x_ref, vec_ref, pool_ref, pair_ref, low_ref, pooled_ref, mean_ref):
    unit, _ = norm(x_ref[0].astype(f32))
    normed = unit * vec_ref[0:1, :] + vec_ref[1:2, :]
    low_ref[0] = normed.astype(bf16)
    pooled = exact_dot(pool_ref[...], normed)
    pooled_ref[0] = pooled.astype(bf16)
    mean_ref[0] = exact_dot(pair_ref[...], pooled).astype(bf16)


def attend_kernel(chunk, x_ref, own_ref, mem_ref, w_ref, qv_ref, mask_ref, out_ref, lse_ref, x_s, q_s, k_s, v_s, s_s, p_s):
    nq, width = q_s.shape
    project_queries(x_ref, w_ref, qv_ref, q_s)
    project_keys(own_ref, mem_ref, w_ref, qv_ref, x_s, k_s, v_s)
    factor = HD**-0.5 * math.log2(math.e)
    lanes = lax.broadcasted_iota(jnp.int32, (chunk, 128), 1)
    for tile in range(width // 384):
        group = slice(384 * tile, 384 * tile + 384)
        base = q_s[:, group].astype(f32)
        parts = [base[:, :128], base[:, 128:256], base[:, 256:384]]
        for head in range(4 * tile, 4 * tile + 4):
            start, stop = window(head)
            mask = head_mask(head)
            query = jnp.where(mask, q_s[:, start:stop], jnp.zeros((), bf16))
            s_s[...] = dot(query, k_s[:, start:stop], NT)

            def body(i, carry, head=head):
                rows = pl.ds(pl.multiple_of(i * chunk, chunk), chunk)
                score = s_s[rows, :] * factor + mask_ref[0]
                top = jnp.max(score, axis=1, keepdims=True)
                power = jnp.exp2(score - top)
                total = jnp.sum(power, axis=1, keepdims=True)
                p_s[rows, :] = (power * (1.0 / total)).astype(bf16)
                lse_ref[0, rows, :] = jnp.where(lanes == head, top + jnp.log2(total), lse_ref[0, rows, :])
                return carry

            lax.fori_loop(0, nq // chunk, body, 0, unroll=nq // chunk)
            out = jnp.where(mask, dot(p_s[...], v_s[:, start:stop]), 0.0)
            for w in range((stop - start) // 128):
                k = start // 128 - 3 * tile + w
                parts[k] = parts[k] + out[:, 128 * w:128 * w + 128]
        out_ref[0, :, group] = jnp.concatenate(parts, axis=1).astype(bf16)


def attend_back_kernel(
    chunk, x_ref, g_ref, own_ref, mem_ref, w_ref, qv_ref, mask_ref, lse_ref,
    dx_ref, dpool_ref, gw_ref, row_ref,
    x_s, q_s, k_s, v_s, s_s, dp_s, p_s, ds_s, dk_s, dv_s, dq_s, gw_s,
):
    nq, width = q_s.shape
    step = pl.program_id(0)
    project_queries(x_ref, w_ref, qv_ref, q_s)
    project_keys(own_ref, mem_ref, w_ref, qv_ref, x_s, k_s, v_s)
    scaling = HD**-0.5
    factor = scaling * math.log2(math.e)
    lanes = lax.broadcasted_iota(jnp.int32, (chunk, 128), 1)

    @pl.when(step == 0)
    def _():
        gw_s[...] = jnp.zeros_like(gw_s)

    xt = transposed(x_ref[0])
    keys_t = transposed(x_s[...])
    dx = None
    dpool = None
    row_q, row_v = [], []
    for tile in range(width // 384):
        group = slice(384 * tile, 384 * tile + 384)
        qt = transposed(q_s[:, group])
        gt = transposed(g_ref[0, :, group])
        parts = [None] * 3
        for head in range(4 * tile, 4 * tile + 4):
            start, stop = window(head)
            mask = head_mask(head)
            query = jnp.where(mask, q_s[:, start:stop], jnp.zeros((), bf16))
            grad = jnp.where(mask, g_ref[0, :, start:stop], jnp.zeros((), bf16))
            s_s[...] = dot(query, k_s[:, start:stop], NT)
            dp_s[...] = dot(grad, v_s[:, start:stop], NT)

            def body(i, carry, head=head):
                rows = pl.ds(pl.multiple_of(i * chunk, chunk), chunk)
                lse = jnp.sum(jnp.where(lanes == head, lse_ref[0, rows, :], 0.0), axis=1, keepdims=True)
                p = jnp.exp2(s_s[rows, :] * factor + mask_ref[0] - lse)
                dp = dp_s[rows, :]
                inner = jnp.sum(p * dp, axis=1, keepdims=True)
                p_s[rows, :] = p.astype(bf16)
                ds_s[rows, :] = (p * (dp - inner)).astype(bf16)
                return carry

            lax.fori_loop(0, nq // chunk, body, 0, unroll=nq // chunk)
            r = slice(HD * (head - 4 * tile), HD * (head - 4 * tile) + HD)
            dv_s[r, :] = dot(gt[r], p_s[...])
            dk_s[r, :] = dot(qt[r], ds_s[...]) * scaling
            dq = jnp.where(mask, dot(ds_s[...], k_s[:, start:stop]) * scaling, 0.0)
            for w in range((stop - start) // 128):
                k = start // 128 - 3 * tile + w
                part = dq[:, 128 * w:128 * w + 128]
                parts[k] = part if parts[k] is None else parts[k] + part
        total = jnp.concatenate(parts, axis=1) + g_ref[0, :, group].astype(f32)
        row_q.append(sum_rows(total))
        low = total.astype(bf16)
        gw_s[:, group] += dot(xt, low)
        add = dot(low, w_ref[:, group], NT)
        dx = add if dx is None else dx + add
        for base, src in ((width, dk_s), (2 * width, dv_s)):
            grad = src[...].T
            if base == 2 * width:
                row_v.append(sum_rows(grad))
            low = grad.astype(bf16)
            here = slice(base + 384 * tile, base + 384 * tile + 384)
            gw_s[:, here] += dot(keys_t, low)
            add = dot(low, w_ref[:, here], NT)
            dpool = add if dpool is None else dpool + add
    dx_ref[0] = dx
    row = 0
    own, mem = own_ref.shape[2], mem_ref.shape[2]
    toks = own_ref.shape[0]
    for t in range(toks):
        dpool_ref[t, 0, :own, :] = dpool[t * own:(t + 1) * own].astype(bf16)
        dpool_ref[t, 0, own:, :] = dpool[toks * own + t * mem:toks * own + (t + 1) * mem].astype(bf16)
    add_rows(row_ref, [jnp.concatenate(row_q, axis=1), jnp.concatenate(row_v, axis=1)])

    @pl.when(step == pl.num_programs(0) - 1)
    def _():
        gw_ref[...] = gw_s[...].astype(bf16)


def first_mlp_kernel(x_ref, comb_ref, out_ref, up_ref, down_ref, ub_ref, vec_ref, pool_ref, pair_ref,
                     after_ref, middle_ref, pooled_ref, mean_ref):
    after = x_ref[0].astype(f32) + dot(comb_ref[0], out_ref[...], NT) + vec_ref[0:1, :]
    after_ref[0] = after
    unit, _ = norm(after)
    low = (unit * vec_ref[1:2, :] + vec_ref[2:3, :]).astype(bf16)
    total = after + vec_ref[3:4, :]
    for h in range(up_ref.shape[0]):
        hidden = gelu(dot(low, up_ref[h]) + ub_ref[h]).astype(bf16)
        total = total + dot(hidden, down_ref[h], NT)
    middle_ref[0] = total
    unit, _ = norm(total)
    pooled = exact_dot(pool_ref[...], unit * vec_ref[4:5, :] + vec_ref[5:6, :])
    pooled_ref[0] = pooled.astype(bf16)
    mean_ref[0] = exact_dot(pair_ref[...], pooled).astype(bf16)


def second_mlp_kernel(
    comb_ref, pooled_ref, cot_ref, out_ref, skip_ref, up_ref, down_ref, ub_ref, vec_ref,
    mixed_ref, dcomb_ref, dskip_ref, gmlp_ref, gout_ref, gskip_ref, gub_ref, row_ref,
    after_s, low_s, lowt_s, cott_s, sum_s, dlow_s,
):
    step = pl.program_id(0)

    @pl.when(step == 0)
    def _():
        after = dot(comb_ref[...], out_ref[...], NT) + dot(pooled_ref[...], skip_ref[...], NT) + vec_ref[0:1, :]
        after_s[...] = after
        unit, _ = norm(after)
        low = (unit * vec_ref[1:2, :] + vec_ref[2:3, :]).astype(bf16)
        low_s[...] = low
        lowt_s[...] = transposed(low)
        cott_s[...] = transposed(cot_ref[...])
        sum_s[...] = after + vec_ref[3:4, :]
        dlow_s[...] = jnp.zeros_like(dlow_s)

    pre = dot(low_s[...], up_ref[0]) + ub_ref[...]
    hidden, slope = gelu_both(pre)
    hidden = hidden.astype(bf16)
    dpre = dot(cot_ref[...], down_ref[0]) * slope
    gub_ref[...] = sum_rows(dpre)
    dpre = dpre.astype(bf16)
    sum_s[...] += dot(hidden, down_ref[0], NT)
    dlow_s[...] += dot(dpre, up_ref[0], NT)
    for n, grad in enumerate((dot(lowt_s[...], dpre), dot(cott_s[...], hidden))):
        rows = gmlp_ref.shape[3]
        for t in range(gmlp_ref.shape[1]):
            gmlp_ref[0, t, n] = grad[t * rows:(t + 1) * rows].astype(bf16)

    @pl.when(step == pl.num_programs(0) - 1)
    def _():
        mixed_ref[...] = sum_s[...].astype(bf16)
        unit, inverse = norm(after_s[...])
        dlow = dlow_s[...]
        cot = cot_ref[...].astype(f32)
        res = norm_back(unit, inverse, vec_ref[1:2, :], dlow) + cot
        row_ref[...] = jnp.zeros_like(row_ref)
        for i, row in enumerate((res, dlow, cot, dlow * unit)):
            row_ref[i:i + 1, :] = sum_rows(row)
        res = res.astype(bf16)
        dcomb_ref[...] = dot(res, out_ref[...]).astype(bf16)
        dskip_ref[...] = dot(res, skip_ref[...])
        rest = transposed(res)
        gout_ref[...] = dot(rest, comb_ref[...]).astype(bf16)
        gskip_ref[...] = dot(rest, pooled_ref[...]).astype(bf16)


def first_back_kernel(
    middle_ref, after_ref, comb_ref, dskip_ref, dq_ref, own_ref, mem_ref, out_ref, up_ref, down_ref, ub_ref, vec_ref,
    unpool_ref, unpair_ref,
    res_ref, dcomb_ref, gup_ref, gdown_ref, gout_ref, gub_ref, row_ref,
    gup_s, gdown_s, gout_s,
):
    step = pl.program_id(0)

    @pl.when(step == 0)
    def _():
        gup_s[...] = jnp.zeros_like(gup_s)
        gdown_s[...] = jnp.zeros_like(gdown_s)
        gout_s[...] = jnp.zeros_like(gout_s)
        gub_ref[...] = jnp.zeros_like(gub_ref)

    dpool = dskip_ref[0] + dq_ref[0] + own_ref[0] + exact_dot(unpair_ref[...], mem_ref[0])
    dnorm = exact_dot(unpool_ref[...], dpool)
    unit, inverse = norm(middle_ref[0])
    grad = norm_back(unit, inverse, vec_ref[2:3, :], dnorm)
    rows = [sum_rows(dnorm * unit), sum_rows(dnorm), sum_rows(grad)]
    low = grad.astype(bf16)
    lowt = transposed(low)
    unit, inverse = norm(after_ref[0])
    normed = (unit * vec_ref[0:1, :] + vec_ref[1:2, :]).astype(bf16)
    normedt = transposed(normed)
    dnormed = None
    for h in range(up_ref.shape[0]):
        hidden, slope = gelu_both(dot(normed, up_ref[h]) + ub_ref[h])
        hidden = hidden.astype(bf16)
        dpre = dot(low, down_ref[h]) * slope
        gub_ref[h] += sum_rows(dpre)
        dpre = dpre.astype(bf16)
        gdown_s[h] += dot(lowt, hidden)
        gup_s[h] += dot(normedt, dpre)
        add = dot(dpre, up_ref[h], NT)
        dnormed = add if dnormed is None else dnormed + add
    res = norm_back(unit, inverse, vec_ref[0:1, :], dnormed) + grad
    rows += [sum_rows(dnormed * unit), sum_rows(dnormed), sum_rows(res)]
    res_ref[0] = res
    res = res.astype(bf16)
    dcomb_ref[0] = dot(res, out_ref[...]).astype(bf16)
    gout_s[...] += dot(transposed(res), comb_ref[0])
    add_rows(row_ref, rows)

    @pl.when(step == pl.num_programs(0) - 1)
    def _():
        gup_ref[...] = gup_s[...].astype(bf16)
        gdown_ref[...] = gdown_s[...].astype(bf16)
        gout_ref[...] = gout_s[...].astype(bf16)


def last_back_kernel(x_ref, res_ref, dx_ref, own_ref, mem_ref, vec_ref, unpool_ref, unpair_ref, grad_ref, row_ref):
    dpool = own_ref[0] + exact_dot(unpair_ref[...], mem_ref[0])
    dnorm = dx_ref[0] + exact_dot(unpool_ref[...], dpool)
    unit, inverse = norm(x_ref[0].astype(f32))
    grad_ref[0] = (norm_back(unit, inverse, vec_ref[0:1, :], dnorm) + res_ref[0]).astype(bf16)
    add_rows(row_ref, [sum_rows(dnorm * unit), sum_rows(dnorm)])


def whole(array):
    return pl.BlockSpec(array.shape, lambda i: (0,) * array.ndim)


def by_micro(array, axis=0):
    block = array.shape[:axis] + (1,) + array.shape[axis + 1:]
    return pl.BlockSpec(block, lambda i: (0,) * axis + (i,) + (0,) * (array.ndim - axis - 1))


def shape(dims, dtype):
    return jax.ShapeDtypeStruct(dims, dtype)


def call(kernel, steps, args, outs, scratch=(), name=None):
    def spec(array, how):
        if how is None:
            return whole(array)
        return by_micro(array, how) if isinstance(how, int) else how

    return pl.pallas_call(
        kernel,
        grid=(steps,),
        in_specs=[spec(a, how) for a, how in args],
        out_specs=[spec(a, how) for a, how in outs],
        out_shape=[a for a, _ in outs],
        scratch_shapes=[pltpu.VMEM(dims, dtype) for dims, dtype in scratch],
        compiler_params=pltpu.CompilerParams(vmem_limit_bytes=VMEM_CAP),
        name=name,
    )(*[a for a, _ in args])


def chunk_of(nq):
    return 112 if nq % 112 == 0 else 16


def attend(x, own, mem, w, qv, mask, width):
    batches, nq, d = x.shape
    keys = own.shape[0] * own.shape[2] + mem.shape[0] * mem.shape[2]
    return call(
        functools.partial(attend_kernel, chunk_of(nq)), batches,
        [(x, 0), (own, 1), (mem, 1), (w, None), (qv, None), (mask, 0)],
        [(shape((batches, nq, width), bf16), 0), (shape((batches, nq, 128), f32), 0)],
        [((keys, d), bf16), ((nq, width), bf16), ((keys, width), bf16), ((keys, width), bf16), ((nq, keys), f32), ((nq, keys), bf16)],
        name="attend",
    )


def attend_back(x, grad, own, mem, w, qv, mask, lse):
    batches, nq, d = x.shape
    width = grad.shape[2]
    keys = own.shape[0] * own.shape[2] + mem.shape[0] * mem.shape[2]
    both = (own.shape[0], batches, own.shape[2] + mem.shape[2], d)
    return call(
        functools.partial(attend_back_kernel, chunk_of(nq)), batches,
        [(x, 0), (grad, 0), (own, 1), (mem, 1), (w, None), (qv, None), (mask, 0), (lse, 0)],
        [(shape((batches, nq, d), f32), 0), (shape(both, bf16), 1), (shape(w.shape, bf16), None), (shape((8, width), f32), None)],
        [((keys, d), bf16), ((nq, width), bf16), ((keys, width), bf16), ((keys, width), bf16),
         ((nq, keys), f32), ((nq, keys), f32), ((nq, keys), bf16), ((nq, keys), bf16),
         ((384, keys), f32), ((384, keys), f32), ((8, 128), f32), (w.shape, f32)],
        name="attend_back",
    )


MESH = pl.DeviceIdType.MESH


def places():
    tok, toks = lax.axis_index("tok"), lax.axis_size("tok")
    return lax.axis_index("clip"), lax.axis_index("head"), tok // 2, tok % 2, toks // 2


def greet(copies_to_me, i_copy_to):
    barrier = pltpu.get_barrier_semaphore()
    for device, condition in copies_to_me:
        if condition is None:
            pl.semaphore_signal(barrier, inc=1, device_id=device, device_id_type=MESH)
        else:
            @pl.when(condition)
            def _():
                pl.semaphore_signal(barrier, inc=1, device_id=device, device_id_type=MESH)
    count = 0
    for _, condition in i_copy_to:
        count = count + (1 if condition is None else jnp.where(condition, 1, 0))
    pl.semaphore_wait(barrier, count)


def remote(src, dst, send, recv, device):
    return pltpu.make_async_remote_copy(
        src_ref=src, dst_ref=dst, send_sem=send, recv_sem=recv, device_id=device, device_id_type=MESH
    )


def rem(a, n):
    return lax.rem(a + n, n)


def share_kernel(pooled_ref, mean_ref, pick_ref, own_ref, mem_ref, got_s, pick_s, local_sem, own_send, own_recv, mem_send, mem_recv,
                 pass_send, pass_recv, clip_send, clip_recv):
    clip, head, chip, core, chips = places()
    clips, heads = lax.axis_size("clip"), lax.axis_size("head")
    share = pooled_ref.shape[0]
    here = 2 * chip + core
    partner = {"tok": 2 * chip + 1 - core}
    across = [{"tok": 2 * rem(chip + k, chips) + core} for k in range(1, chips)]
    heads_of = lambda by, sign: [{"clip": clip + by, "head": rem(head + sign * d, heads)} for d in range(heads)]
    last, begun = clip < clips - 1, clip > 0
    to = [(partner, None)] + [(d, None) for d in across] + [(d, last) for d in heads_of(1, 1)]
    fro = [(partner, None)] + [(d, None) for d in across] + [(d, begun) for d in heads_of(-1, -1)]
    greet(fro, to)

    def spread(src, out, send, recv):
        copies = [remote(src, out.at[here], send.at[0], recv.at[0], partner)]
        copies += [remote(src, out.at[here], send.at[k + 1], recv.at[k + 1], across[k]) for k in range(chips - 1)]
        return copies

    def passed(out, k, row):
        block = 2 * rem(chip - k, chips) + core
        return remote(out.at[block], out.at[block], pass_send.at[row, k - 1], pass_recv.at[row, k - 1], partner)

    clip_copies = [remote(mean_ref, got_s.at[d], clip_send.at[d], clip_recv.at[d], device) for d, device in enumerate(heads_of(1, 1))]

    @pl.when(last)
    def _():
        for copy in clip_copies:
            copy.start()

    own_copies = spread(pooled_ref, own_ref, own_send, own_recv)
    for copy in own_copies[1:] + own_copies[:1]:
        copy.start()
    own_local = pltpu.make_async_copy(pooled_ref, own_ref.at[here], local_sem.at[0])
    own_local.start()

    @pl.when(begun)
    def _():
        for copy in clip_copies:
            copy.wait_recv()
        for m in range(share):
            total = None
            for d in range(heads):
                for s in range(share):
                    piece = got_s[d, s].astype(f32) * pick_ref[m, d * share + s]
                    total = piece if total is None else total + piece
            pick_s[m] = total.astype(bf16)

    @pl.when(jnp.logical_not(begun))
    def _():
        pick_s[...] = jnp.zeros_like(pick_s)

    mem_copies = spread(pick_s, mem_ref, mem_send, mem_recv)
    for copy in mem_copies[1:] + mem_copies[:1]:
        copy.start()
    mem_local = pltpu.make_async_copy(pick_s, mem_ref.at[here], local_sem.at[1])
    mem_local.start()
    forwards = []
    for row, (copies, out) in enumerate(((own_copies, own_ref), (mem_copies, mem_ref))):
        for k in range(1, chips):
            copies[k].wait_recv()
            forwards.append(passed(out, k, row))
            forwards[-1].start()
    own_copies[0].wait_recv()
    mem_copies[0].wait_recv()
    for copy in forwards:
        copy.wait_recv()
    for copy in own_copies + mem_copies + forwards:
        copy.wait_send()
    own_local.wait()
    mem_local.wait()

    @pl.when(last)
    def _():
        for copy in clip_copies:
            copy.wait_send()


ANY = pl.BlockSpec(memory_space=pl.ANY)
INVMEM = pl.BlockSpec(memory_space=pltpu.VMEM)
INSMEM = pl.BlockSpec(memory_space=pltpu.SMEM)


def dma(*dims):
    return pltpu.SemaphoreType.DMA(dims)


def share_pooled(pooled, mean, pick, number):
    toks, heads = lax.axis_size("tok"), lax.axis_size("head")
    chips = toks // 2
    return pl.pallas_call(
        share_kernel,
        in_specs=[INVMEM, INVMEM, INSMEM],
        out_specs=[ANY, ANY],
        out_shape=[shape((toks,) + pooled.shape, bf16), shape((toks,) + mean.shape, bf16)],
        scratch_shapes=[
            pltpu.VMEM((heads,) + mean.shape, bf16), pltpu.VMEM(mean.shape, bf16), dma(2),
            dma(chips), dma(chips), dma(chips), dma(chips),
            dma(2, max(chips - 1, 1)), dma(2, max(chips - 1, 1)), dma(heads), dma(heads),
        ],
        compiler_params=pltpu.CompilerParams(collective_id=number, has_side_effects=True, vmem_limit_bytes=VMEM_CAP),
        name="share_pooled",
    )(pooled, mean, pick)


def give_back_kernel(part_ref, pick_ref, own_ref, back_ref, mine_s, core_s, sum_s, chip_s, route_s, got_s,
                     local_sem, core_send, core_recv, mem_send, mem_recv, own_send, own_recv, clip_send, clip_recv):
    clip, head, chip, core, chips = places()
    clips, heads = lax.axis_size("clip"), lax.axis_size("head")
    share, rows = own_ref.shape[0], own_ref.shape[1]
    partner = {"tok": 2 * chip + 1 - core}
    across = [{"tok": 2 * rem(chip + k, chips) + core} for k in range(1, chips)]
    heads_of = lambda by, sign: [{"clip": clip + by, "head": rem(head + sign * d, heads)} for d in range(heads)]
    last, begun = clip < clips - 1, clip > 0
    to = [(partner, None)] + [(d, None) for d in across] + [(d, begun) for d in heads_of(-1, -1)]
    fro = [(partner, None)] + [(d, None) for d in across] + [(d, last) for d in heads_of(1, 1)]
    greet(fro, to)

    order = [rem(chip + k, chips) for k in list(range(1, chips)) + [0]]
    core_copies, local_copies = [], []
    for n, other in enumerate(order):
        core_copies.append(remote(part_ref.at[2 * other + 1 - core], core_s.at[n], core_send.at[n], core_recv.at[n], partner))
        core_copies[-1].start()
    for n, other in enumerate(order):
        local_copies.append(pltpu.make_async_copy(part_ref.at[2 * other + core], mine_s.at[n], local_sem.at[n]))
        local_copies[-1].start()
    mem_copies, own_copies = [], []
    for n in range(chips):
        local_copies[n].wait()
        core_copies[n].wait_recv()
        if n == chips - 1:
            break
        sum_s[n] = (mine_s[n].astype(f32) + core_s[n].astype(f32)).astype(bf16)
        low, high = pl.ds(0, rows), pl.ds(rows, sum_s.shape[2] - rows)
        mem_copies.append(remote(sum_s.at[n, :, high, :], chip_s.at[n, :, high, :], mem_send.at[n], mem_recv.at[n], across[n]))
        mem_copies[-1].start()
        own_copies.append(remote(sum_s.at[n, :, low, :], chip_s.at[n, :, low, :], own_send.at[n], own_recv.at[n], across[n]))
        own_copies[-1].start()
    base = chips - 1
    for copy in mem_copies:
        copy.wait_recv()
    memory = []
    for m in range(share):
        total = mine_s[base, m, rows:].astype(f32) + core_s[base, m, rows:].astype(f32)
        for n in range(chips - 1):
            total = total + chip_s[n, m, rows:].astype(f32)
        memory.append(total)
    clip_copies = [
        remote(route_s.at[d], got_s.at[d], clip_send.at[d], clip_recv.at[d], device) for d, device in enumerate(heads_of(-1, -1))
    ]

    @pl.when(begun)
    def _():
        for d in range(heads):
            for s in range(share):
                total = None
                for m in range(share):
                    piece = memory[m] * pick_ref[m, d * share + s]
                    total = piece if total is None else total + piece
                route_s[d, s] = total.astype(bf16)
            clip_copies[d].start()

    for copy in own_copies:
        copy.wait_recv()
    for m in range(share):
        total = mine_s[base, m, :rows].astype(f32) + core_s[base, m, :rows].astype(f32)
        for n in range(chips - 1):
            total = total + chip_s[n, m, :rows].astype(f32)
        own_ref[m] = total

    @pl.when(last)
    def _():
        for copy in clip_copies:
            copy.wait_recv()
        total = got_s[0].astype(f32)
        for d in range(1, heads):
            total = total + got_s[d].astype(f32)
        back_ref[...] = total

    @pl.when(jnp.logical_not(last))
    def _():
        back_ref[...] = jnp.zeros_like(back_ref)

    for copy in core_copies + mem_copies + own_copies:
        copy.wait_send()

    @pl.when(begun)
    def _():
        for copy in clip_copies:
            copy.wait_send()


def give_back(part, pick, own_rows, number):
    toks, heads = lax.axis_size("tok"), lax.axis_size("head")
    chips, few = toks // 2, max(toks // 2 - 1, 1)
    share, rows, d = part.shape[1:]
    return pl.pallas_call(
        give_back_kernel,
        in_specs=[ANY, INSMEM],
        out_specs=[INVMEM, INVMEM],
        out_shape=[shape((share, own_rows, d), f32), shape((share, rows - own_rows, d), f32)],
        scratch_shapes=[
            pltpu.VMEM((chips,) + part.shape[1:], bf16), pltpu.VMEM((chips,) + part.shape[1:], bf16),
            pltpu.VMEM((few,) + part.shape[1:], bf16), pltpu.VMEM((few,) + part.shape[1:], bf16),
            pltpu.VMEM((heads, share, rows - own_rows, d), bf16), pltpu.VMEM((heads, share, rows - own_rows, d), bf16),
            dma(chips), dma(chips), dma(chips), dma(few), dma(few), dma(few), dma(few), dma(heads), dma(heads),
        ],
        compiler_params=pltpu.CompilerParams(collective_id=number, has_side_effects=True, vmem_limit_bytes=VMEM_CAP),
        name="give_back",
    )(part, pick)


def finish_kernel(half_ref, small_ref, all_ref, total_ref, sum_s, core_s, chip_s, head_s, clip_s,
                  local_sem, half_send, half_recv, core_send, core_recv, chip_send, chip_recv, head_send, head_recv, clip_send, clip_recv):
    clip, head, chip, core, chips = places()
    clips, heads = lax.axis_size("clip"), lax.axis_size("head")
    partner = {"tok": 2 * chip + 1 - core}
    across = [{"tok": 2 * rem(chip + k, chips) + core} for k in range(1, chips)]
    beside = [{"head": rem(head + k, heads)} for k in range(1, heads)]
    along = [{"clip": rem(clip + k, clips)} for k in range(1, clips)]
    peers = [(d, None) for d in [partner] + across + beside + along]
    greet(peers, peers)
    halves = [remote(half_ref, all_ref.at[head], half_send.at[k], half_recv.at[k], d) for k, d in enumerate(beside)]
    for copy in halves:
        copy.start()
    local_half = pltpu.make_async_copy(half_ref, all_ref.at[head], local_sem.at[0])
    local_half.start()
    first = remote(small_ref, core_s, core_send.at[0], core_recv.at[0], partner)
    first.start()
    first.wait_recv()
    sum_s[0] = small_ref[...] + core_s[...]
    waits = [first]
    stages = ((across, chip, chips, chip_s, chip_send, chip_recv), (beside, head, heads, head_s, head_send, head_recv),
              (along, clip, clips, clip_s, clip_send, clip_recv))
    for n, (devices, index, size, slots, send, recv) in enumerate(stages):
        copies = [remote(sum_s.at[n], slots.at[k], send.at[k], recv.at[k], d) for k, d in enumerate(devices)]
        for copy in copies:
            copy.start()
        for copy in copies:
            copy.wait_recv()
        total = None
        for i in range(size):
            piece = jnp.zeros_like(sum_s[n])
            piece = jnp.where(index == i, sum_s[n], piece)
            for k in range(size - 1):
                piece = jnp.where(rem(index - k - 1, size) == i, slots[k], piece)
            total = piece if total is None else total + piece
        if n + 1 < len(stages):
            sum_s[n + 1] = total
        else:
            total_ref[...] = total
        waits += copies
    for copy in halves:
        copy.wait_recv()
    for copy in waits + halves:
        copy.wait_send()
    local_half.wait()


def finish(half, small, number):
    toks, heads, clips = lax.axis_size("tok"), lax.axis_size("head"), lax.axis_size("clip")
    counts = [max(n, 1) for n in (toks // 2 - 1, heads - 1, clips - 1)]
    return pl.pallas_call(
        finish_kernel,
        in_specs=[ANY, INVMEM],
        out_specs=[ANY, INVMEM],
        out_shape=[shape((heads,) + half.shape, half.dtype), shape(small.shape, f32)],
        scratch_shapes=[pltpu.VMEM((3,) + small.shape, f32), pltpu.VMEM(small.shape, f32)]
        + [pltpu.VMEM((n,) + small.shape, f32) for n in counts]
        + [dma(1), dma(counts[1]), dma(counts[1]), dma(1), dma(1)] + [dma(n) for n in counts for _ in range(2)],
        compiler_params=pltpu.CompilerParams(collective_id=number, has_side_effects=True, vmem_limit_bytes=VMEM_CAP),
        name="finish",
    )(half, small)


def from_heads(piece, heads):
    head = lax.axis_index("head")
    out = jnp.zeros((heads,) + piece.shape, piece.dtype)
    out = lax.dynamic_update_index_in_dim(out, piece, head, 0)
    for d in range(1, heads):
        got = lax.ppermute(piece, "head", [(i, (i + d) % heads) for i in range(heads)])
        out = lax.dynamic_update_index_in_dim(out, got, (head - d + heads) % heads, 0)
    return out.reshape((-1,) + piece.shape[1:])


def padded_rows(*rows):
    return jnp.concatenate([jnp.stack(rows), jnp.zeros((-len(rows) % 8, rows[0].shape[0]), f32)])


def local(
    clips_in, resets, assign, w_qkv_a, w_out_a, w_up_a, w_down_a, w_qkv_b, w_out_b, w_skip_b, w_up_b, w_down_b,
    gains_a, gains_b, shifts_a, shifts_b, qv_bias_a, qv_bias_b, up_bias_a, up_bias_b, cotangent,
):
    heads, toks = lax.axis_size("head"), lax.axis_size("tok")
    head = lax.axis_index("head")
    micro, frames = clips_in.shape[1], clips_in.shape[2]
    d1, d2 = clips_in.shape[-1], cotangent.shape[-1]
    share = micro // heads
    first = head * share
    pool_np, pair_np = pool_matrix(frames), pair_matrix(frames)
    pooling, pairing = jnp.asarray(pool_np, bf16), jnp.asarray(pair_np, bf16)
    unpooling, unpairing = jnp.asarray(pool_np.T, bf16), jnp.asarray(pair_np.T, bf16)
    tokens, pooled_tokens = frames * PATCH, frames * POOLED
    own_rows, mem_rows = up16(pooled_tokens), up16(frames // 2 * POOLED)
    rows2 = share * own_rows

    stream = lax.dynamic_slice_in_dim(clips_in[0], first, share, 0).reshape(share, tokens, d1)
    cot = lax.dynamic_slice_in_dim(cotangent[0], first, share, 0).reshape(share, pooled_tokens, d2)
    cot = jnp.pad(cot, ((0, 0), (0, own_rows - pooled_tokens), (0, 0))).reshape(rows2, d2)

    picks, masks = [], []
    row_own = jnp.where(jnp.arange(own_rows) < pooled_tokens, 0.0, NEG)
    row_mem = jnp.arange(mem_rows) < frames // 2 * POOLED
    for m in range(share):
        source = lax.dynamic_index_in_dim(assign[0], first + m, 0, keepdims=False)
        flag = lax.dynamic_index_in_dim(resets[0], first + m, 0, keepdims=False)
        slot = ((head - source // share + heads) % heads) * share + source % share
        picks.append((jnp.arange(heads * share) == slot).astype(f32))
        has = (flag == 0) & (lax.axis_index("clip") > 0)
        masks.append(jnp.concatenate([jnp.tile(row_own, toks), jnp.tile(jnp.where(row_mem & has, 0.0, NEG), toks)]))
    mask = jnp.stack(masks)[:, None, :].astype(f32)
    pick = jnp.stack(picks)

    group = ("head", "tok")
    fa, ha = w_up_a.shape[1], w_out_a.shape[1]
    fb, hb, hs = w_up_b.shape[1], w_out_b.shape[1], w_skip_b.shape[1]
    pack_a = jnp.concatenate([w_up_a, w_down_a, w_qkv_a.reshape(w_qkv_a.shape[0], -1), w_out_a], axis=1)
    all_a = lax.all_gather(pack_a, group).reshape(heads, d1, -1)
    all_q = lax.all_gather(w_qkv_b.reshape(w_qkv_b.shape[0], -1), group).reshape(heads, d1, -1)
    all_b = lax.all_gather(jnp.concatenate([w_up_b, w_down_b, w_out_b, w_skip_b], axis=1), group).reshape(heads, d2, -1)
    flat = jnp.concatenate([qv_bias_a.reshape(-1), qv_bias_b.reshape(-1), up_bias_a, up_bias_b])
    flat = lax.all_gather(flat, "head")
    qv_a = flat[:, :2 * ha].reshape(heads, 2, ha).transpose(1, 0, 2).reshape(2, d1)
    qv_b = flat[:, 2 * ha:2 * ha + 2 * hb].reshape(heads, 2, hb).transpose(1, 0, 2).reshape(2, d2)
    ub_a = flat[:, 2 * (ha + hb):2 * (ha + hb) + fa].reshape(heads, 1, fa)
    ub_b = flat[:, 2 * (ha + hb) + fa:].reshape(1, heads * fb)

    def lanes(pack, low, width):
        return jnp.concatenate([pack[h, :, low:low + width] for h in range(heads)], axis=1)

    up_a, down_a = all_a[:, :, :fa], all_a[:, :, fa:2 * fa]
    qkv_a = jnp.concatenate([lanes(all_a, 2 * fa + i * ha, ha) for i in range(3)], axis=1)
    out_a = lanes(all_a, 2 * fa + 3 * ha, ha)
    qkv_b = jnp.concatenate([lanes(all_q, i * hb, hb) for i in range(3)], axis=1)
    out_b, skip_b = lanes(all_b, 2 * fb, hb), lanes(all_b, 2 * fb + hb, hs)

    low1, pooled1, mean1 = call(
        norm_pool_kernel, share,
        [(stream, 0), (padded_rows(gains_a[0], shifts_a[0]), None), (pooling, None), (pairing, None)],
        [(shape((share, tokens, d1), bf16), 0), (shape((share, own_rows, d1), bf16), 0), (shape((share, mem_rows, d1), bf16), 0)],
        name="norm_pool",
    )
    own1, mem1 = share_pooled(pooled1, mean1, pick, 0)
    comb1, lse1 = attend(low1, own1, mem1, qkv_a, qv_a, mask, d1)
    after1, middle, pooled3, mean3 = call(
        first_mlp_kernel, share,
        [(stream, 0), (comb1, 0), (out_a, None), (up_a, None), (down_a, None), (ub_a, None),
         (padded_rows(shifts_a[1], gains_a[1], shifts_a[2], shifts_a[3], gains_a[2], shifts_a[4]), None),
         (pooling, None), (pairing, None)],
        [(shape((share, tokens, d1), f32), 0), (shape((share, tokens, d1), f32), 0),
         (shape((share, own_rows, d1), bf16), 0), (shape((share, mem_rows, d1), bf16), 0)],
        name="first_mlp",
    )

    own2, mem2 = share_pooled(pooled3, mean3, pick, 1)
    comb2, lse2 = attend(pooled3, own2, mem2, qkv_b, qv_b, mask, d2)
    chunk = 768
    per_head = fb // chunk
    steps = heads * per_head
    rows_spec = pl.BlockSpec((1, d2, chunk), lambda j: (j // per_head, 0, j % per_head))
    mixed, dcomb2, dskip, g_mlp_b, g_out_b, g_skip_b, g_ub_b, rows_b = call(
        second_mlp_kernel, steps,
        [(comb2.reshape(rows2, d2), None), (pooled3.reshape(rows2, d1), None), (cot, None), (out_b, None), (skip_b, None),
         (all_b, rows_spec),
         (all_b, pl.BlockSpec((1, d2, chunk), lambda j: (j // per_head, 0, per_head + j % per_head))),
         (ub_b, pl.BlockSpec((1, chunk), lambda j: (0, j))),
         (padded_rows(shifts_b[0], gains_b, shifts_b[1], shifts_b[2]), None)],
        [(shape((rows2, d2), bf16), None), (shape((rows2, d2), bf16), None), (shape((rows2, d1), f32), None),
         (shape((heads, toks, 2, d2 // toks, fb), bf16),
          pl.BlockSpec((1, toks, 2, d2 // toks, chunk), lambda j: (j // per_head, 0, 0, 0, j % per_head))),
         (shape((d2, d2), bf16), None), (shape((d2, d1), bf16), None),
         (shape((1, heads * fb), f32), pl.BlockSpec((1, chunk), lambda j: (0, j))), (shape((8, d2), f32), None)],
        [((rows2, d2), f32), ((rows2, d2), bf16), ((d2, rows2), bf16), ((d2, rows2), bf16), ((rows2, d2), f32), ((rows2, d2), f32)],
        name="second_mlp",
    )

    def reduce_grad(blocks):
        return lax.psum(lax.psum_scatter(blocks, group, scatter_dimension=0, tiled=False), "clip")

    sum_mlp_b = reduce_grad(g_mlp_b.reshape((heads * toks,) + g_mlp_b.shape[2:]))

    def by_head(grad, width):
        return grad.reshape(grad.shape[0], heads, width).transpose(1, 0, 2)

    dcomb2 = dcomb2.reshape(share, own_rows, d2)
    dq2, dpool2, g_qkv_b, rows_qv_b = attend_back(pooled3, dcomb2, own2, mem2, qkv_b, qv_b, mask, lse2)
    own_back2, mem_back2 = give_back(dpool2, pick, own_rows, 2)

    res1, dcomb1, g_up_a, g_down_a, g_out_a, g_ub_a, rows_a = call(
        first_back_kernel, share,
        [(middle, 0), (after1, 0), (comb1, 0), (dskip.reshape(share, own_rows, d1), 0), (dq2, 0), (own_back2, 0), (mem_back2, 0),
         (out_a, None), (up_a, None), (down_a, None), (ub_a, None),
         (padded_rows(gains_a[1], shifts_a[2], gains_a[2]), None), (unpooling, None), (unpairing, None)],
        [(shape((share, tokens, d1), f32), 0), (shape((share, tokens, d1), bf16), 0),
         (shape((heads, d1, fa), bf16), None), (shape((heads, d1, fa), bf16), None), (shape((d1, d1), bf16), None),
         (shape((heads, 1, fa), f32), None), (shape((8, d1), f32), None)],
        [((heads, d1, fa), f32), ((heads, d1, fa), f32), ((d1, d1), f32)],
        name="first_back",
    )
    dx1, dpool1, g_qkv_a, rows_qv_a = attend_back(low1, dcomb1, own1, mem1, qkv_a, qv_a, mask, lse1)
    own_back1, mem_back1 = give_back(dpool1, pick, own_rows, 3)
    stream_grad, rows_last = call(
        last_back_kernel, share,
        [(stream, 0), (res1, 0), (dx1, 0), (own_back1, 0), (mem_back1, 0), (padded_rows(gains_a[0]), None),
         (unpooling, None), (unpairing, None)],
        [(shape((share, tokens, d1), bf16), 0), (shape((8, d1), f32), None)],
        name="last_back",
    )

    def by_owner(grad):
        return grad.reshape((heads * toks, -1) + grad.shape[2:])

    grad_q = by_owner(jnp.concatenate([by_head(g_qkv_b[:, i * d2:(i + 1) * d2], hb) for i in range(3)], axis=2))
    grad_o = by_owner(jnp.concatenate([by_head(g_out_b, hb), by_head(g_skip_b, hs)], axis=2))
    grad_a = by_owner(jnp.concatenate(
        [g_up_a, g_down_a] + [by_head(g_qkv_a[:, i * d1:(i + 1) * d1], ha) for i in range(3)] + [by_head(g_out_a, ha)], axis=2))
    rest = jnp.concatenate([grad_a, grad_q], axis=2)
    rest, grad_o, sum_mlp_b = lax.optimization_barrier((rest, grad_o, sum_mlp_b))
    sum_rest, sum_o = reduce_grad(rest).astype(f32), reduce_grad(grad_o).astype(f32)
    sum_mlp_b = sum_mlp_b.astype(f32)
    sum_a, sum_q = sum_rest[:, :grad_a.shape[2]], sum_rest[:, grad_a.shape[2]:]

    small = [
        jnp.stack([rows_last[0], rows_a[3], rows_a[0]]), rows_b[3],
        jnp.stack([rows_last[1], rows_a[5], rows_a[4], rows_a[2], rows_a[1]]),
        rows_b[:3], rows_qv_a[:2], rows_qv_b[:2], g_ub_a, g_ub_b,
    ]
    flat = jnp.concatenate([piece.reshape(-1) for piece in small])
    flat = jnp.pad(flat, (0, -flat.size % 1024)).reshape(-1, 128)
    stream_all, flat = finish(stream_grad, flat, 4)
    flat = flat.reshape(-1)
    pieces, at = [], 0
    for piece in small:
        pieces.append(flat[at:at + piece.size].reshape(piece.shape))
        at += piece.size

    def mine(piece, axis):
        width = piece.shape[axis] // heads
        return lax.dynamic_slice_in_dim(piece, head * width, width, axis)

    mixed = mixed.reshape(share, own_rows, d2)[:, :pooled_tokens]
    mixed_all = from_heads(mixed, heads)
    return (
        mixed_all.reshape(cotangent.shape),
        stream_all.astype(f32).reshape(clips_in.shape),
        sum_a[:, 2 * fa:2 * fa + 3 * ha].reshape(w_qkv_a.shape),
        sum_a[:, 2 * fa + 3 * ha:],
        sum_a[:, :fa],
        sum_a[:, fa:2 * fa],
        sum_q.reshape(w_qkv_b.shape),
        sum_o[:, :hb],
        sum_o[:, hb:],
        sum_mlp_b[0],
        sum_mlp_b[1],
        pieces[0], pieces[1], pieces[2], pieces[3],
        mine(pieces[4], 1), mine(pieces[5], 1), mine(pieces[6].reshape(-1), 0), mine(pieces[7].reshape(-1), 0),
    )


def solution(mesh):
    in_specs = (
        P("clip", None, "tok", None, None),
        P("clip", None),
        P("clip", None),
        P("tok", None, "head"),
        P("tok", "head"),
        P("tok", "head"),
        P("tok", "head"),
        P("tok", None, "head"),
        P("tok", "head"),
        P("tok", "head"),
        P("tok", "head"),
        P("tok", "head"),
        P(),
        P(),
        P(),
        P(),
        P(None, "head"),
        P(None, "head"),
        P("head"),
        P("head"),
        P("clip", None, "tok", None, None),
    )
    out_specs = (
        P("clip", None, "tok", None, None),
        P("clip", None, "tok", None, None),
        P("tok", None, "head"),
        P("tok", "head"),
        P("tok", "head"),
        P("tok", "head"),
        P("tok", None, "head"),
        P("tok", "head"),
        P("tok", "head"),
        P("tok", "head"),
        P("tok", "head"),
        P(),
        P(),
        P(),
        P(),
        P(None, "head"),
        P(None, "head"),
        P("head"),
        P("head"),
    )
    return jax.shard_map(local, mesh=mesh, in_specs=in_specs, out_specs=out_specs, check_vma=False)
```

```python
import functools
import math

import jax
import jax.numpy as jnp
import numpy as np
from jax import lax
from jax.experimental import pallas as pl
from jax.experimental.pallas import tpu as pltpu
from jax.sharding import PartitionSpec as P

GRID = 14
PATCH = GRID * GRID
POOLED = PATCH // 4
HD = 96
NEG = -1e30
VMEM_CAP = 62 * 2**20
eps = 1e-06
f32, bf16 = jnp.float32, jnp.bfloat16
NN, NT, TN = ((1,), (0,)), ((1,), (1,)), ((0,), (0,))


def up16(n):
    return -(-n // 16) * 16


def pool_matrix(frames):
    rows, cols = up16(frames * POOLED), frames * PATCH
    out = np.zeros((rows, cols), np.float32)
    half = GRID // 2
    for f in range(frames):
        for p in range(PATCH):
            r, c = divmod(p, GRID)
            out[f * POOLED + (r // 2) * half + c // 2, f * PATCH + p] = 0.25
    return out


def pair_matrix(frames):
    rows, cols = up16(frames // 2 * POOLED), up16(frames * POOLED)
    out = np.zeros((rows, cols), np.float32)
    for j in range(frames // 2):
        for p in range(POOLED):
            out[j * POOLED + p, 2 * j * POOLED + p] = 0.5
            out[j * POOLED + p, (2 * j + 1) * POOLED + p] = 0.5
    return out


def dot(a, b, dims=NN):
    return lax.dot_general(a, b, (dims, ((), ())), preferred_element_type=f32)


def exact_dot(matrix, tensor):
    high = tensor.astype(bf16)
    low = (tensor - high.astype(f32)).astype(bf16)
    return dot(matrix, high) + dot(matrix, low)


def norm(x):
    average = jnp.mean(x, axis=-1, keepdims=True)
    centred = x - average
    inverse = lax.rsqrt(jnp.mean(centred * centred, axis=-1, keepdims=True) + eps)
    return centred * inverse, inverse


def norm_back(unit, inverse, gain, gradient):
    scaled = gradient * gain
    return inverse * (
        scaled
        - jnp.mean(scaled, axis=-1, keepdims=True)
        - unit * jnp.mean(scaled * unit, axis=-1, keepdims=True)
    )


GELU_A, GELU_B = math.sqrt(2.0 / math.pi), 0.044715


def gelu(x):
    t = jnp.tanh(GELU_A * (x + GELU_B * (x * x * x)))
    return 0.5 * x * (1.0 + t)


def gelu_both(x):
    square = x * x
    t = jnp.tanh(GELU_A * x * (1.0 + GELU_B * square))
    value = 0.5 * x * (1.0 + t)
    slope = 0.5 * (1.0 + t) + 0.5 * x * (1.0 - t * t) * (GELU_A * (1.0 + 3.0 * GELU_B * square))
    return value, slope


def sum_rows(x):
    return jnp.sum(x, axis=0, keepdims=True)


def add_rows(ref, rows):
    step = pl.program_id(0)

    @pl.when(step == 0)
    def _():
        ref[...] = jnp.zeros_like(ref)

    for i, row in enumerate(rows):
        ref[i:i + 1, :] += row


def transposed(x):
    return x.astype(f32).T.astype(bf16)


def window(head):
    low = HD * head
    return low // 128 * 128, -(-(low + HD) // 128) * 128


def head_mask(head):
    start, stop = window(head)
    lane = lax.broadcasted_iota(jnp.int32, (1, stop - start), 1) + start
    return (lane >= HD * head) & (lane < HD * head + HD)


def key_rows(own_ref, mem_ref):
    row = 0
    for ref in (own_ref, mem_ref):
        for t in range(ref.shape[0]):
            yield ref, t, slice(row, row + ref.shape[2])
            row += ref.shape[2]


def project_keys(own_ref, mem_ref, w_ref, bias_ref, x_s, k_s, v_s):
    for ref, t, rows in key_rows(own_ref, mem_ref):
        x_s[rows, :] = ref[t, 0]
    width = k_s.shape[1]
    for low in range(0, width, 384):
        k_s[:, low:low + 384] = dot(x_s[...], w_ref[low // 384, :, 384:768]).astype(bf16)
    for low in range(0, width, 384):
        value = dot(x_s[...], w_ref[low // 384, :, 768:])
        v_s[:, low:low + 384] = (value + bias_ref[1:2, low:low + 384]).astype(bf16)


def project_queries(x_ref, w_ref, bias_ref, q_s):
    width = q_s.shape[1]
    for low in range(0, width, 384):
        value = dot(x_ref[0], w_ref[low // 384, :, :384])
        q_s[:, low:low + 384] = (value + bias_ref[0:1, low:low + 384]).astype(bf16)


def norm_pool_kernel(x_ref, vec_ref, pool_ref, pair_ref, low_ref, pooled_ref, mean_ref):
    unit, _ = norm(x_ref[0].astype(f32))
    normed = unit * vec_ref[0:1, :] + vec_ref[1:2, :]
    low_ref[0] = normed.astype(bf16)
    pooled = exact_dot(pool_ref[...], normed)
    pooled_ref[0] = pooled.astype(bf16)
    mean_ref[0] = exact_dot(pair_ref[...], pooled).astype(bf16)


def write_shares(gw_ref, h, gw_s):
    wide = gw_ref.shape[2] // 3
    for part in range(3):
        low = wide * h
        columns = gw_s[low // 384, :, 384 * part:384 * part + 384][:, low % 384:low % 384 + wide]
        gw_ref[h, :, wide * part:wide * part + wide] = columns.astype(bf16)


def attend_kernel(chunk, x_ref, own_ref, mem_ref, w_ref, qv_ref, mask_ref, out_ref, lse_ref, x_s, q_s, k_s, v_s, s_s, p_s):
    nq, width = q_s.shape
    project_queries(x_ref, w_ref, qv_ref, q_s)
    project_keys(own_ref, mem_ref, w_ref, qv_ref, x_s, k_s, v_s)
    factor = HD**-0.5 * math.log2(math.e)
    lanes = lax.broadcasted_iota(jnp.int32, (chunk, 128), 1)
    for tile in range(width // 384):
        group = slice(384 * tile, 384 * tile + 384)
        base = q_s[:, group].astype(f32)
        parts = [base[:, :128], base[:, 128:256], base[:, 256:384]]
        for head in range(4 * tile, 4 * tile + 4):
            start, stop = window(head)
            mask = head_mask(head)
            query = jnp.where(mask, q_s[:, start:stop], jnp.zeros((), bf16))
            s_s[...] = dot(query, k_s[:, start:stop], NT)

            def body(i, carry, head=head):
                rows = pl.ds(pl.multiple_of(i * chunk, chunk), chunk)
                score = s_s[rows, :] * factor + mask_ref[0]
                top = jnp.max(score, axis=1, keepdims=True)
                power = jnp.exp2(score - top)
                total = jnp.sum(power, axis=1, keepdims=True)
                p_s[rows, :] = (power * (1.0 / total)).astype(bf16)
                lse_ref[0, rows, :] = jnp.where(lanes == head, top + jnp.log2(total), lse_ref[0, rows, :])
                return carry

            lax.fori_loop(0, nq // chunk, body, 0, unroll=nq // chunk)
            out = jnp.where(mask, dot(p_s[...], v_s[:, start:stop]), 0.0)
            for w in range((stop - start) // 128):
                k = start // 128 - 3 * tile + w
                parts[k] = parts[k] + out[:, 128 * w:128 * w + 128]
        out_ref[0, :, group] = jnp.concatenate(parts, axis=1).astype(bf16)


def attend_back_kernel(
    chunk, x_ref, g_ref, own_ref, mem_ref, w_ref, qv_ref, mask_ref, lse_ref,
    dx_ref, dpool_ref, gw_ref, row_ref,
    x_s, q_s, k_s, v_s, s_s, dp_s, p_s, ds_s, dk_s, dv_s, dq_s, gw_s,
):
    nq, width = q_s.shape
    step = pl.program_id(0)
    project_queries(x_ref, w_ref, qv_ref, q_s)
    project_keys(own_ref, mem_ref, w_ref, qv_ref, x_s, k_s, v_s)
    scaling = HD**-0.5
    factor = scaling * math.log2(math.e)
    lanes = lax.broadcasted_iota(jnp.int32, (chunk, 128), 1)

    @pl.when(step == 0)
    def _():
        gw_s[...] = jnp.zeros_like(gw_s)

    xt = transposed(x_ref[0])
    keys_t = transposed(x_s[...])
    dx = None
    dpool = None
    row_q, row_v = [], []
    for tile in range(width // 384):
        group = slice(384 * tile, 384 * tile + 384)
        qt = transposed(q_s[:, group])
        gt = transposed(g_ref[0, :, group])
        parts = [None] * 3
        for head in range(4 * tile, 4 * tile + 4):
            start, stop = window(head)
            mask = head_mask(head)
            query = jnp.where(mask, q_s[:, start:stop], jnp.zeros((), bf16))
            grad = jnp.where(mask, g_ref[0, :, start:stop], jnp.zeros((), bf16))
            s_s[...] = dot(query, k_s[:, start:stop], NT)
            dp_s[...] = dot(grad, v_s[:, start:stop], NT)

            def body(i, carry, head=head):
                rows = pl.ds(pl.multiple_of(i * chunk, chunk), chunk)
                lse = jnp.sum(jnp.where(lanes == head, lse_ref[0, rows, :], 0.0), axis=1, keepdims=True)
                p = jnp.exp2(s_s[rows, :] * factor + mask_ref[0] - lse)
                dp = dp_s[rows, :]
                inner = jnp.sum(p * dp, axis=1, keepdims=True)
                p_s[rows, :] = p.astype(bf16)
                ds_s[rows, :] = (p * (dp - inner)).astype(bf16)
                return carry

            lax.fori_loop(0, nq // chunk, body, 0, unroll=nq // chunk)
            r = slice(HD * (head - 4 * tile), HD * (head - 4 * tile) + HD)
            dv_s[r, :] = dot(gt[r], p_s[...])
            dk_s[r, :] = dot(qt[r], ds_s[...]) * scaling
            dq = jnp.where(mask, dot(ds_s[...], k_s[:, start:stop]) * scaling, 0.0)
            for w in range((stop - start) // 128):
                k = start // 128 - 3 * tile + w
                part = dq[:, 128 * w:128 * w + 128]
                parts[k] = part if parts[k] is None else parts[k] + part
        total = jnp.concatenate(parts, axis=1) + g_ref[0, :, group].astype(f32)
        row_q.append(sum_rows(total))
        low = total.astype(bf16)
        gw_s[tile, :, :384] += dot(xt, low)
        add = dot(low, w_ref[tile, :, :384], NT)
        dx = add if dx is None else dx + add
        for part, src in ((1, dk_s), (2, dv_s)):
            grad = src[...].T
            if part == 2:
                row_v.append(sum_rows(grad))
            low = grad.astype(bf16)
            here = slice(384 * part, 384 * part + 384)
            gw_s[tile, :, here] += dot(keys_t, low)
            add = dot(low, w_ref[tile, :, here], NT)
            dpool = add if dpool is None else dpool + add
    dx_ref[0] = dx
    row = 0
    own, mem = own_ref.shape[2], mem_ref.shape[2]
    toks = own_ref.shape[0]
    for t in range(toks):
        dpool_ref[t, 0, :own, :] = dpool[t * own:(t + 1) * own].astype(bf16)
        dpool_ref[t, 0, own:, :] = dpool[toks * own + t * mem:toks * own + (t + 1) * mem].astype(bf16)
    add_rows(row_ref, [jnp.concatenate(row_q, axis=1), jnp.concatenate(row_v, axis=1)])

    @pl.when(step == pl.num_programs(0) - 1)
    def _():
        for h in range(gw_ref.shape[0]):
            write_shares(gw_ref, h, gw_s)


def first_mlp_kernel(x_ref, comb_ref, out_ref, up_ref, down_ref, ub_ref, vec_ref, pool_ref, pair_ref,
                     after_ref, middle_ref, pooled_ref, mean_ref):
    after = x_ref[0].astype(f32) + dot(comb_ref[0], out_ref[...], NT) + vec_ref[0:1, :]
    after_ref[0] = after
    unit, _ = norm(after)
    low = (unit * vec_ref[1:2, :] + vec_ref[2:3, :]).astype(bf16)
    total = after + vec_ref[3:4, :]
    for h in range(up_ref.shape[0]):
        hidden = gelu(dot(low, up_ref[h]) + ub_ref[h]).astype(bf16)
        total = total + dot(hidden, down_ref[h], NT)
    middle_ref[0] = total
    unit, _ = norm(total)
    pooled = exact_dot(pool_ref[...], unit * vec_ref[4:5, :] + vec_ref[5:6, :])
    pooled_ref[0] = pooled.astype(bf16)
    mean_ref[0] = exact_dot(pair_ref[...], pooled).astype(bf16)


def second_mlp_kernel(
    comb_ref, pooled_ref, cot_ref, out_ref, skip_ref, up_ref, down_ref, ub_ref, vec_ref,
    mixed_ref, dcomb_ref, dskip_ref, gmlp_ref, gout_ref, gskip_ref, gub_ref, row_ref,
    after_s, low_s, lowt_s, cott_s, sum_s, dlow_s,
):
    step = pl.program_id(0)

    @pl.when(step == 0)
    def _():
        after = dot(pooled_ref[...], skip_ref[...], NT) + vec_ref[0:1, :]
        wide = out_ref.shape[2]
        for h in range(out_ref.shape[0]):
            after = after + dot(comb_ref[:, wide * h:wide * h + wide], out_ref[h], NT)
        after_s[...] = after
        unit, _ = norm(after)
        low = (unit * vec_ref[1:2, :] + vec_ref[2:3, :]).astype(bf16)
        low_s[...] = low
        lowt_s[...] = transposed(low)
        cott_s[...] = transposed(cot_ref[...])
        sum_s[...] = after + vec_ref[3:4, :]
        dlow_s[...] = jnp.zeros_like(dlow_s)

    pre = dot(low_s[...], up_ref[0]) + ub_ref[...]
    hidden, slope = gelu_both(pre)
    hidden = hidden.astype(bf16)
    dpre = dot(cot_ref[...], down_ref[0]) * slope
    gub_ref[...] = sum_rows(dpre)
    dpre = dpre.astype(bf16)
    sum_s[...] += dot(hidden, down_ref[0], NT)
    dlow_s[...] += dot(dpre, up_ref[0], NT)
    for n, grad in enumerate((dot(lowt_s[...], dpre), dot(cott_s[...], hidden))):
        rows = gmlp_ref.shape[3]
        for t in range(gmlp_ref.shape[1]):
            gmlp_ref[0, t, n] = grad[t * rows:(t + 1) * rows].astype(bf16)

    @pl.when(step == pl.num_programs(0) - 1)
    def _():
        mixed_ref[...] = sum_s[...].astype(bf16)
        unit, inverse = norm(after_s[...])
        dlow = dlow_s[...]
        cot = cot_ref[...].astype(f32)
        res = norm_back(unit, inverse, vec_ref[1:2, :], dlow) + cot
        row_ref[...] = jnp.zeros_like(row_ref)
        for i, row in enumerate((res, dlow, cot, dlow * unit)):
            row_ref[i:i + 1, :] = sum_rows(row)
        res = res.astype(bf16)
        dskip_ref[...] = dot(res, skip_ref[...])
        rest = transposed(res)
        wide = out_ref.shape[2]
        for h in range(out_ref.shape[0]):
            here = slice(wide * h, wide * h + wide)
            dcomb_ref[:, here] = dot(res, out_ref[h]).astype(bf16)
            gout_ref[h] = dot(rest, comb_ref[:, here]).astype(bf16)
        grad = dot(rest, pooled_ref[...])
        wide = gskip_ref.shape[2]
        for h in range(gskip_ref.shape[0]):
            gskip_ref[h] = grad[:, wide * h:wide * h + wide].astype(bf16)


def first_back_kernel(
    middle_ref, after_ref, comb_ref, dskip_ref, dq_ref, own_ref, mem_ref, out_ref, up_ref, down_ref, ub_ref, vec_ref,
    unpool_ref, unpair_ref,
    res_ref, dcomb_ref, gmlp_ref, gout_ref, gub_ref, row_ref,
    gup_s, gdown_s, gout_s,
):
    step = pl.program_id(0)

    @pl.when(step == 0)
    def _():
        gup_s[...] = jnp.zeros_like(gup_s)
        gdown_s[...] = jnp.zeros_like(gdown_s)
        gout_s[...] = jnp.zeros_like(gout_s)
        gub_ref[...] = jnp.zeros_like(gub_ref)

    dpool = dskip_ref[0] + dq_ref[0] + own_ref[0] + exact_dot(unpair_ref[...], mem_ref[0])
    dnorm = exact_dot(unpool_ref[...], dpool)
    unit, inverse = norm(middle_ref[0])
    grad = norm_back(unit, inverse, vec_ref[2:3, :], dnorm)
    rows = [sum_rows(dnorm * unit), sum_rows(dnorm), sum_rows(grad)]
    low = grad.astype(bf16)
    lowt = transposed(low)
    unit, inverse = norm(after_ref[0])
    normed = (unit * vec_ref[0:1, :] + vec_ref[1:2, :]).astype(bf16)
    normedt = transposed(normed)
    dnormed = None
    for h in range(up_ref.shape[0]):
        hidden, slope = gelu_both(dot(normed, up_ref[h]) + ub_ref[h])
        hidden = hidden.astype(bf16)
        dpre = dot(low, down_ref[h]) * slope
        gub_ref[h] += sum_rows(dpre)
        dpre = dpre.astype(bf16)
        gdown_s[h] += dot(lowt, hidden)
        gup_s[h] += dot(normedt, dpre)
        add = dot(dpre, up_ref[h], NT)
        dnormed = add if dnormed is None else dnormed + add
    res = norm_back(unit, inverse, vec_ref[0:1, :], dnormed) + grad
    rows += [sum_rows(dnormed * unit), sum_rows(dnormed), sum_rows(res)]
    res_ref[0] = res
    res = res.astype(bf16)
    dcomb_ref[0] = dot(res, out_ref[...]).astype(bf16)
    gout_s[...] += dot(transposed(res), comb_ref[0])
    add_rows(row_ref, rows)

    @pl.when(step == pl.num_programs(0) - 1)
    def _():
        fa, ha = gmlp_ref.shape[2] // 2, gout_ref.shape[2]
        for h in range(gmlp_ref.shape[0]):
            gmlp_ref[h, :, :fa] = gup_s[h].astype(bf16)
            gmlp_ref[h, :, fa:] = gdown_s[h].astype(bf16)
            gout_ref[h] = gout_s[:, ha * h:ha * h + ha].astype(bf16)


def last_back_kernel(x_ref, res_ref, dx_ref, own_ref, mem_ref, vec_ref, unpool_ref, unpair_ref, grad_ref, row_ref):
    dpool = own_ref[0] + exact_dot(unpair_ref[...], mem_ref[0])
    dnorm = dx_ref[0] + exact_dot(unpool_ref[...], dpool)
    unit, inverse = norm(x_ref[0].astype(f32))
    grad = norm_back(unit, inverse, vec_ref[0:1, :], dnorm) + res_ref[0]
    for f in range(grad_ref.shape[1]):
        grad_ref[0, f] = grad[PATCH * f:PATCH * f + PATCH].astype(bf16)
    add_rows(row_ref, [sum_rows(dnorm * unit), sum_rows(dnorm)])


def whole(array):
    return pl.BlockSpec(array.shape, lambda i: (0,) * array.ndim)


def by_micro(array, axis=0):
    block = array.shape[:axis] + (1,) + array.shape[axis + 1:]
    return pl.BlockSpec(block, lambda i: (0,) * axis + (i,) + (0,) * (array.ndim - axis - 1))


def shape(dims, dtype):
    return jax.ShapeDtypeStruct(dims, dtype)


def call(kernel, steps, args, outs, scratch=(), name=None):
    def spec(array, how):
        if how is None:
            return whole(array)
        return by_micro(array, how) if isinstance(how, int) else how

    return pl.pallas_call(
        kernel,
        grid=(steps,),
        in_specs=[spec(a, how) for a, how in args],
        out_specs=[spec(a, how) for a, how in outs],
        out_shape=[a for a, _ in outs],
        scratch_shapes=[pltpu.VMEM(dims, dtype) for dims, dtype in scratch],
        compiler_params=pltpu.CompilerParams(vmem_limit_bytes=VMEM_CAP),
        name=name,
    )(*[a for a, _ in args])


def chunk_of(nq):
    return 112 if nq % 112 == 0 else 16


def attend(x, own, mem, w, qv, mask, width):
    batches, nq, d = x.shape
    keys = own.shape[0] * own.shape[2] + mem.shape[0] * mem.shape[2]
    return call(
        functools.partial(attend_kernel, chunk_of(nq)), batches,
        [(x, 0), (own, 1), (mem, 1), (w, None), (qv, None), (mask, 0)],
        [(shape((batches, nq, width), bf16), 0), (shape((batches, nq, 128), f32), 0)],
        [((keys, d), bf16), ((nq, width), bf16), ((keys, width), bf16), ((keys, width), bf16), ((nq, keys), f32), ((nq, keys), bf16)],
        name="attend",
    )


def attend_back(x, grad, own, mem, w, qv, mask, lse, heads):
    batches, nq, d = x.shape
    width = grad.shape[2]
    keys = own.shape[0] * own.shape[2] + mem.shape[0] * mem.shape[2]
    both = (own.shape[0], batches, own.shape[2] + mem.shape[2], d)
    return call(
        functools.partial(attend_back_kernel, chunk_of(nq)), batches,
        [(x, 0), (grad, 0), (own, 1), (mem, 1), (w, None), (qv, None), (mask, 0), (lse, 0)],
        [(shape((batches, nq, d), f32), 0), (shape(both, bf16), 1), (shape((heads, d, 3 * width // heads), bf16), None), (shape((8, width), f32), None)],
        [((keys, d), bf16), ((nq, width), bf16), ((keys, width), bf16), ((keys, width), bf16),
         ((nq, keys), f32), ((nq, keys), f32), ((nq, keys), bf16), ((nq, keys), bf16),
         ((384, keys), f32), ((384, keys), f32), ((8, 128), f32), (w.shape, f32)],
        name="attend_back",
    )


MESH = pl.DeviceIdType.MESH


def places():
    tok, toks = lax.axis_index("tok"), lax.axis_size("tok")
    return lax.axis_index("clip"), lax.axis_index("head"), tok // 2, tok % 2, toks // 2


def greet(copies_to_me, i_copy_to):
    barrier = pltpu.get_barrier_semaphore()
    for device, condition in copies_to_me:
        if condition is None:
            pl.semaphore_signal(barrier, inc=1, device_id=device, device_id_type=MESH)
        else:
            @pl.when(condition)
            def _():
                pl.semaphore_signal(barrier, inc=1, device_id=device, device_id_type=MESH)
    count = 0
    for _, condition in i_copy_to:
        count = count + (1 if condition is None else jnp.where(condition, 1, 0))
    pl.semaphore_wait(barrier, count)


def remote(src, dst, send, recv, device):
    return pltpu.make_async_remote_copy(
        src_ref=src, dst_ref=dst, send_sem=send, recv_sem=recv, device_id=device, device_id_type=MESH
    )


def rem(a, n):
    return lax.rem(a + n, n)


def share_kernel(pooled_ref, mean_ref, pick_ref, own_ref, mem_ref, got_s, pick_s, local_sem, own_send, own_recv, mem_send, mem_recv,
                 pass_send, pass_recv, clip_send, clip_recv):
    clip, head, chip, core, chips = places()
    clips, heads = lax.axis_size("clip"), lax.axis_size("head")
    share = pooled_ref.shape[0]
    here = 2 * chip + core
    partner = {"tok": 2 * chip + 1 - core}
    across = [{"tok": 2 * rem(chip + k, chips) + core} for k in range(1, chips)]
    heads_of = lambda by, sign: [{"clip": clip + by, "head": rem(head + sign * d, heads)} for d in range(heads)]
    last, begun = clip < clips - 1, clip > 0
    to = [(partner, None)] + [(d, None) for d in across] + [(d, last) for d in heads_of(1, 1)]
    fro = [(partner, None)] + [(d, None) for d in across] + [(d, begun) for d in heads_of(-1, -1)]
    greet(fro, to)

    def spread(src, out, send, recv):
        copies = [remote(src, out.at[here], send.at[0], recv.at[0], partner)]
        copies += [remote(src, out.at[here], send.at[k + 1], recv.at[k + 1], across[k]) for k in range(chips - 1)]
        return copies

    def passed(out, k, row):
        block = 2 * rem(chip - k, chips) + core
        return remote(out.at[block], out.at[block], pass_send.at[row, k - 1], pass_recv.at[row, k - 1], partner)

    clip_copies = [remote(mean_ref, got_s.at[d], clip_send.at[d], clip_recv.at[d], device) for d, device in enumerate(heads_of(1, 1))]

    @pl.when(last)
    def _():
        for copy in clip_copies:
            copy.start()

    own_copies = spread(pooled_ref, own_ref, own_send, own_recv)
    for copy in own_copies[1:] + own_copies[:1]:
        copy.start()
    own_local = pltpu.make_async_copy(pooled_ref, own_ref.at[here], local_sem.at[0])
    own_local.start()

    @pl.when(begun)
    def _():
        for copy in clip_copies:
            copy.wait_recv()
        for m in range(share):
            total = None
            for d in range(heads):
                for s in range(share):
                    piece = got_s[d, s].astype(f32) * pick_ref[m, d * share + s]
                    total = piece if total is None else total + piece
            pick_s[m] = total.astype(bf16)

    @pl.when(jnp.logical_not(begun))
    def _():
        pick_s[...] = jnp.zeros_like(pick_s)

    mem_copies = spread(pick_s, mem_ref, mem_send, mem_recv)
    for copy in mem_copies[1:] + mem_copies[:1]:
        copy.start()
    mem_local = pltpu.make_async_copy(pick_s, mem_ref.at[here], local_sem.at[1])
    mem_local.start()
    forwards = []
    for row, (copies, out) in enumerate(((own_copies, own_ref), (mem_copies, mem_ref))):
        for k in range(1, chips):
            copies[k].wait_recv()
            forwards.append(passed(out, k, row))
            forwards[-1].start()
    own_copies[0].wait_recv()
    mem_copies[0].wait_recv()
    for copy in forwards:
        copy.wait_recv()
    for copy in own_copies + mem_copies + forwards:
        copy.wait_send()
    own_local.wait()
    mem_local.wait()

    @pl.when(last)
    def _():
        for copy in clip_copies:
            copy.wait_send()


ANY = pl.BlockSpec(memory_space=pl.ANY)
INVMEM = pl.BlockSpec(memory_space=pltpu.VMEM)
INSMEM = pl.BlockSpec(memory_space=pltpu.SMEM)


def dma(*dims):
    return pltpu.SemaphoreType.DMA(dims)


def share_pooled(pooled, mean, pick, number):
    toks, heads = lax.axis_size("tok"), lax.axis_size("head")
    chips = toks // 2
    return pl.pallas_call(
        share_kernel,
        in_specs=[INVMEM, INVMEM, INSMEM],
        out_specs=[ANY, ANY],
        out_shape=[shape((toks,) + pooled.shape, bf16), shape((toks,) + mean.shape, bf16)],
        scratch_shapes=[
            pltpu.VMEM((heads,) + mean.shape, bf16), pltpu.VMEM(mean.shape, bf16), dma(2),
            dma(chips), dma(chips), dma(chips), dma(chips),
            dma(2, max(chips - 1, 1)), dma(2, max(chips - 1, 1)), dma(heads), dma(heads),
        ],
        compiler_params=pltpu.CompilerParams(collective_id=number, has_side_effects=True, vmem_limit_bytes=VMEM_CAP),
        name="share_pooled",
    )(pooled, mean, pick)


def give_back_kernel(part_ref, pick_ref, own_ref, back_ref, mine_s, core_s, sum_s, chip_s, route_s, got_s,
                     local_sem, core_send, core_recv, mem_send, mem_recv, own_send, own_recv, clip_send, clip_recv):
    clip, head, chip, core, chips = places()
    clips, heads = lax.axis_size("clip"), lax.axis_size("head")
    share, rows = own_ref.shape[0], own_ref.shape[1]
    partner = {"tok": 2 * chip + 1 - core}
    across = [{"tok": 2 * rem(chip + k, chips) + core} for k in range(1, chips)]
    heads_of = lambda by, sign: [{"clip": clip + by, "head": rem(head + sign * d, heads)} for d in range(heads)]
    last, begun = clip < clips - 1, clip > 0
    to = [(partner, None)] + [(d, None) for d in across] + [(d, begun) for d in heads_of(-1, -1)]
    fro = [(partner, None)] + [(d, None) for d in across] + [(d, last) for d in heads_of(1, 1)]
    greet(fro, to)

    order = [rem(chip + k, chips) for k in list(range(1, chips)) + [0]]
    core_copies, local_copies = [], []
    for n, other in enumerate(order):
        core_copies.append(remote(part_ref.at[2 * other + 1 - core], core_s.at[n], core_send.at[n], core_recv.at[n], partner))
        core_copies[-1].start()
    for n, other in enumerate(order):
        local_copies.append(pltpu.make_async_copy(part_ref.at[2 * other + core], mine_s.at[n], local_sem.at[n]))
        local_copies[-1].start()
    mem_copies, own_copies = [], []
    for n in range(chips):
        local_copies[n].wait()
        core_copies[n].wait_recv()
        if n == chips - 1:
            break
        sum_s[n] = (mine_s[n].astype(f32) + core_s[n].astype(f32)).astype(bf16)
        low, high = pl.ds(0, rows), pl.ds(rows, sum_s.shape[2] - rows)
        mem_copies.append(remote(sum_s.at[n, :, high, :], chip_s.at[n, :, high, :], mem_send.at[n], mem_recv.at[n], across[n]))
        mem_copies[-1].start()
        own_copies.append(remote(sum_s.at[n, :, low, :], chip_s.at[n, :, low, :], own_send.at[n], own_recv.at[n], across[n]))
        own_copies[-1].start()
    base = chips - 1
    for copy in mem_copies:
        copy.wait_recv()
    memory = []
    for m in range(share):
        total = mine_s[base, m, rows:].astype(f32) + core_s[base, m, rows:].astype(f32)
        for n in range(chips - 1):
            total = total + chip_s[n, m, rows:].astype(f32)
        memory.append(total)
    clip_copies = [
        remote(route_s.at[d], got_s.at[d], clip_send.at[d], clip_recv.at[d], device) for d, device in enumerate(heads_of(-1, -1))
    ]

    @pl.when(begun)
    def _():
        for d in range(heads):
            for s in range(share):
                total = None
                for m in range(share):
                    piece = memory[m] * pick_ref[m, d * share + s]
                    total = piece if total is None else total + piece
                route_s[d, s] = total.astype(bf16)
            clip_copies[d].start()

    for copy in own_copies:
        copy.wait_recv()
    for m in range(share):
        total = mine_s[base, m, :rows].astype(f32) + core_s[base, m, :rows].astype(f32)
        for n in range(chips - 1):
            total = total + chip_s[n, m, :rows].astype(f32)
        own_ref[m] = total

    @pl.when(last)
    def _():
        for copy in clip_copies:
            copy.wait_recv()
        total = got_s[0].astype(f32)
        for d in range(1, heads):
            total = total + got_s[d].astype(f32)
        back_ref[...] = total

    @pl.when(jnp.logical_not(last))
    def _():
        back_ref[...] = jnp.zeros_like(back_ref)

    for copy in core_copies + mem_copies + own_copies:
        copy.wait_send()

    @pl.when(begun)
    def _():
        for copy in clip_copies:
            copy.wait_send()


def give_back(part, pick, own_rows, number):
    toks, heads = lax.axis_size("tok"), lax.axis_size("head")
    chips, few = toks // 2, max(toks // 2 - 1, 1)
    share, rows, d = part.shape[1:]
    return pl.pallas_call(
        give_back_kernel,
        in_specs=[ANY, INSMEM],
        out_specs=[INVMEM, INVMEM],
        out_shape=[shape((share, own_rows, d), f32), shape((share, rows - own_rows, d), f32)],
        scratch_shapes=[
            pltpu.VMEM((chips,) + part.shape[1:], bf16), pltpu.VMEM((chips,) + part.shape[1:], bf16),
            pltpu.VMEM((few,) + part.shape[1:], bf16), pltpu.VMEM((few,) + part.shape[1:], bf16),
            pltpu.VMEM((heads, share, rows - own_rows, d), bf16), pltpu.VMEM((heads, share, rows - own_rows, d), bf16),
            dma(chips), dma(chips), dma(chips), dma(few), dma(few), dma(few), dma(few), dma(heads), dma(heads),
        ],
        compiler_params=pltpu.CompilerParams(collective_id=number, has_side_effects=True, vmem_limit_bytes=VMEM_CAP),
        name="give_back",
    )(part, pick)


def finish_kernel(half_ref, small_ref, grad_ref, rest_ref, all_ref, total_ref, gtotal_ref, rtotal_ref, *scratch):
    (small_s, small_core, small_chip, small_head, small_clip, part_s, part_core, chip_s, part_chip, head_s, part_head, mine_s, part_clip,
     rest_in, rest_s, local_sem, half_send, half_recv, core_send, core_recv, chip_send, chip_recv, head_send, head_recv,
     clip_send, clip_recv, rest_send, rest_recv, back_send, back_recv) = scratch
    clip, head, chip, core, chips = places()
    clips, heads = lax.axis_size("clip"), lax.axis_size("head")
    share = half_ref.shape[0]
    partner = {"tok": 2 * chip + 1 - core}
    across = [{"tok": 2 * rem(chip + k, chips) + core} for k in range(1, chips)]
    beside = [{"head": rem(head + k, heads)} for k in range(1, heads)]
    along = [{"clip": rem(clip + k, clips)} for k in range(1, clips)]
    peers = [(d, None) for d in [partner] + across + beside + along]
    greet(peers, peers)
    pending = []

    def go(copies):
        for copy in copies:
            copy.start()
        pending.extend(copies)
        return copies

    def arrived(copies):
        for copy in copies:
            copy.wait_recv()

    def in_order(index, size, own, slot):
        total = None
        for i in range(size):
            piece = jnp.where(index == i, own, jnp.zeros_like(own))
            for k in range(size - 1):
                piece = jnp.where(rem(index - k - 1, size) == i, slot(k), piece)
            total = piece if total is None else total + piece
        return total

    first = go([remote(small_ref, small_core, core_send.at[0], core_recv.at[0], partner)])
    for h in range(heads):
        for x in range(chips):
            n = h * chips + x
            first += go([remote(grad_ref.at[2 * n + 1 - core], part_core.at[n], core_send.at[n + 1], core_recv.at[n + 1], partner)])
    gather = go([remote(rest_ref.at[rem(clip + k + 1, clips)], rest_in.at[k], rest_send.at[k], rest_recv.at[k], d) for k, d in enumerate(along)])
    halves = [
        [remote(half_ref.at[s], all_ref.at[head, s], half_send.at[k, s], half_recv.at[k, s], d) for k, d in enumerate(beside)]
        for s in range(share)
    ]
    for s in range(share - 1):
        go(halves[s])
    local_half = pltpu.make_async_copy(half_ref, all_ref.at[head], local_sem.at[0])
    local_half.start()
    arrived(first)
    small_s[0] = small_ref[...] + small_core[...]
    for n in range(heads * chips):
        part_s[n] = (grad_ref[2 * n + core].astype(f32) + part_core[n].astype(f32)).astype(bf16)
    copies = []
    for k, d in enumerate(across):
        copies += go([remote(small_s.at[0], small_chip.at[k], chip_send.at[k, 0], chip_recv.at[k, 0], d)])
        for h in range(heads):
            block = h * chips + rem(chip + k + 1, chips)
            copies += go([remote(part_s.at[block], part_chip.at[k, h], chip_send.at[k, h + 1], chip_recv.at[k, h + 1], d)])
    arrived(copies)
    small_s[1] = in_order(chip, chips, small_s[0], lambda k: small_chip[k])
    for h in range(heads):
        total = part_s[h * chips + chip].astype(f32)
        for k in range(chips - 1):
            total = total + part_chip[k, h].astype(f32)
        chip_s[h] = total.astype(bf16)
    copies = []
    for k, d in enumerate(beside):
        copies += go([remote(small_s.at[1], small_head.at[k], head_send.at[k, 0], head_recv.at[k, 0], d)])
        copies += go([remote(chip_s.at[rem(head + k + 1, heads)], part_head.at[k], head_send.at[k, 1], head_recv.at[k, 1], d)])
    go(halves[share - 1])
    arrived(gather)
    total = rest_ref[clip].astype(f32)
    for k in range(clips - 1):
        total = total + rest_in[k].astype(f32)
    rest_s[clip] = total.astype(bf16)
    spread = go([remote(rest_s.at[clip], rest_s.at[clip], back_send.at[k], back_recv.at[k], d) for k, d in enumerate(along)])
    arrived(copies)
    small_s[2] = in_order(head, heads, small_s[1], lambda k: small_head[k])
    total = chip_s[head].astype(f32)
    for k in range(heads - 1):
        total = total + part_head[k].astype(f32)
    mine_s[...] = total.astype(bf16)
    copies = []
    for k, d in enumerate(along):
        copies += go([remote(small_s.at[2], small_clip.at[k], clip_send.at[k, 0], clip_recv.at[k, 0], d)])
        copies += go([remote(mine_s, part_clip.at[k], clip_send.at[k, 1], clip_recv.at[k, 1], d)])
    arrived(copies)
    total_ref[...] = in_order(clip, clips, small_s[2], lambda k: small_clip[k])
    gtotal_ref[...] = in_order(clip, clips, mine_s[...].astype(f32), lambda k: part_clip[k].astype(f32))
    arrived(spread)
    rtotal_ref[...] = rest_s[...].astype(f32)
    for copies in halves:
        arrived(copies)
    for copy in pending:
        copy.wait_send()
    local_half.wait()


def finish(half, small, grad, rest, number):
    toks, heads, clips = lax.axis_size("tok"), lax.axis_size("head"), lax.axis_size("clip")
    chips = toks // 2
    across, beside, along = (max(n, 1) for n in (chips - 1, heads - 1, clips - 1))
    rows, lanes = rest.shape
    rest = rest.reshape(clips, rows // clips, lanes)
    pad = up16(rows // clips) - rows // clips
    if pad:
        rest = jnp.pad(rest, ((0, 0), (0, pad), (0, 0)))
    block = grad.shape[1:]
    low, full = lambda *dims: pltpu.VMEM(dims, bf16), lambda *dims: pltpu.VMEM(dims + small.shape, f32)
    all_half, total, gtotal, rtotal = pl.pallas_call(
        finish_kernel,
        in_specs=[ANY, INVMEM, INVMEM, INVMEM],
        out_specs=[ANY, INVMEM, INVMEM, INVMEM],
        out_shape=[shape((heads,) + half.shape, half.dtype), shape(small.shape, f32), shape(block, f32), shape(rest.shape, f32)],
        scratch_shapes=[
            full(3), full(), full(across), full(beside), full(along),
            low(heads * chips, *block), low(heads * chips, *block), low(heads, *block), low(across, heads, *block),
            low(heads, *block), low(beside, *block), low(*block), low(along, *block),
            low(along, *rest.shape[1:]), low(*rest.shape),
            dma(1), dma(beside, half.shape[0]), dma(beside, half.shape[0]), dma(heads * chips + 1), dma(heads * chips + 1),
            dma(across, heads + 1), dma(across, heads + 1), dma(beside, 2), dma(beside, 2), dma(along, 2), dma(along, 2),
            dma(along), dma(along), dma(along), dma(along),
        ],
        compiler_params=pltpu.CompilerParams(collective_id=number, has_side_effects=True, vmem_limit_bytes=VMEM_CAP),
        name="finish",
    )(half, small, grad, rest)
    return all_half, total, gtotal, rtotal[:, :rows // clips].reshape(rows, lanes)


def reduce_clips(shard):
    clips, clip = lax.axis_size("clip"), lax.axis_index("clip")
    pieces = shard.reshape(clips, -1, shard.shape[-1])
    total = lax.dynamic_index_in_dim(pieces, clip, 0, keepdims=False).astype(f32)
    for k in range(1, clips):
        give = lax.dynamic_index_in_dim(pieces, (clip + k) % clips, 0, keepdims=False)
        total = total + lax.ppermute(give, "clip", [(i, (i + k) % clips) for i in range(clips)]).astype(f32)
    return total.astype(bf16)


def spread_clips(piece):
    clips, clip = lax.axis_size("clip"), lax.axis_index("clip")
    out = jnp.zeros((clips,) + piece.shape, piece.dtype)
    out = lax.dynamic_update_index_in_dim(out, piece, clip, 0)
    for k in range(1, clips):
        got = lax.ppermute(piece, "clip", [(i, (i + k) % clips) for i in range(clips)])
        out = lax.dynamic_update_index_in_dim(out, got, (clip - k + clips) % clips, 0)
    return out.reshape((-1,) + piece.shape[1:])


def from_heads(piece, heads):
    head = lax.axis_index("head")
    out = jnp.zeros((heads,) + piece.shape, piece.dtype)
    out = lax.dynamic_update_index_in_dim(out, piece, head, 0)
    for d in range(1, heads):
        got = lax.ppermute(piece, "head", [(i, (i + d) % heads) for i in range(heads)])
        out = lax.dynamic_update_index_in_dim(out, got, (head - d + heads) % heads, 0)
    return out.reshape((-1,) + piece.shape[1:])


def padded_rows(*rows):
    return jnp.concatenate([jnp.stack(rows), jnp.zeros((-len(rows) % 8, rows[0].shape[0]), f32)])


def local(
    clips_in, resets, assign, w_qkv_a, w_out_a, w_up_a, w_down_a, w_qkv_b, w_out_b, w_skip_b, w_up_b, w_down_b,
    gains_a, gains_b, shifts_a, shifts_b, qv_bias_a, qv_bias_b, up_bias_a, up_bias_b, cotangent,
):
    heads, toks = lax.axis_size("head"), lax.axis_size("tok")
    head = lax.axis_index("head")
    micro, frames = clips_in.shape[1], clips_in.shape[2]
    d1, d2 = clips_in.shape[-1], cotangent.shape[-1]
    share = micro // heads
    first = head * share
    pool_np, pair_np = pool_matrix(frames), pair_matrix(frames)
    pooling, pairing = jnp.asarray(pool_np, bf16), jnp.asarray(pair_np, bf16)
    unpooling, unpairing = jnp.asarray(pool_np.T, bf16), jnp.asarray(pair_np.T, bf16)
    tokens, pooled_tokens = frames * PATCH, frames * POOLED
    own_rows, mem_rows = up16(pooled_tokens), up16(frames // 2 * POOLED)
    rows2 = share * own_rows

    stream = lax.dynamic_slice_in_dim(clips_in[0], first, share, 0).reshape(share, tokens, d1)
    cot = lax.dynamic_slice_in_dim(cotangent[0], first, share, 0).reshape(share, pooled_tokens, d2)
    cot = jnp.pad(cot, ((0, 0), (0, own_rows - pooled_tokens), (0, 0))).reshape(rows2, d2)

    picks, masks = [], []
    row_own = jnp.where(jnp.arange(own_rows) < pooled_tokens, 0.0, NEG)
    row_mem = jnp.arange(mem_rows) < frames // 2 * POOLED
    for m in range(share):
        source = lax.dynamic_index_in_dim(assign[0], first + m, 0, keepdims=False)
        flag = lax.dynamic_index_in_dim(resets[0], first + m, 0, keepdims=False)
        slot = ((head - source // share + heads) % heads) * share + source % share
        picks.append((jnp.arange(heads * share) == slot).astype(f32))
        has = (flag == 0) & (lax.axis_index("clip") > 0)
        masks.append(jnp.concatenate([jnp.tile(row_own, toks), jnp.tile(jnp.where(row_mem & has, 0.0, NEG), toks)]))
    mask = jnp.stack(masks)[:, None, :].astype(f32)
    pick = jnp.stack(picks)

    group = ("head", "tok")
    fa, ha = w_up_a.shape[1], w_out_a.shape[1]
    fb, hb, hs = w_up_b.shape[1], w_out_b.shape[1], w_skip_b.shape[1]
    pack_a = jnp.concatenate([w_up_a, w_down_a, w_qkv_a.reshape(w_qkv_a.shape[0], -1), w_out_a], axis=1)
    all_a = lax.all_gather(pack_a, group).reshape(heads, d1, -1)

    low1, pooled1, mean1 = call(
        norm_pool_kernel, share,
        [(stream, 0), (padded_rows(gains_a[0], shifts_a[0]), None), (pooling, None), (pairing, None)],
        [(shape((share, tokens, d1), bf16), 0), (shape((share, own_rows, d1), bf16), 0), (shape((share, mem_rows, d1), bf16), 0)],
        name="norm_pool",
    )
    pooled1, pack_q, pack_b, flat, mask = lax.optimization_barrier((
        pooled1, w_qkv_b.reshape(w_qkv_b.shape[0], -1), jnp.concatenate([w_up_b, w_down_b, w_out_b, w_skip_b], axis=1),
        jnp.concatenate([qv_bias_a.reshape(-1), qv_bias_b.reshape(-1), up_bias_a, up_bias_b]), mask))
    own1, mem1 = share_pooled(pooled1, mean1, pick, 0)
    all_q = lax.all_gather(pack_q, group).reshape(heads, d1, -1)
    all_b = lax.all_gather(pack_b, group).reshape(heads, d2, -1)
    flat = from_heads(flat[None], heads)
    qv_a = flat[:, :2 * ha].reshape(heads, 2, ha).transpose(1, 0, 2).reshape(2, d1)
    qv_b = flat[:, 2 * ha:2 * ha + 2 * hb].reshape(heads, 2, hb).transpose(1, 0, 2).reshape(2, d2)
    ub_a = flat[:, 2 * (ha + hb):2 * (ha + hb) + fa].reshape(heads, 1, fa)
    ub_b = flat[:, 2 * (ha + hb) + fa:].reshape(1, heads * fb)

    def lanes(pack, low, width):
        return jnp.concatenate([pack[h, :, low:low + width] for h in range(heads)], axis=1)

    up_spec, down_spec = (pl.BlockSpec((heads, d1, fa), lambda i, n=n: (0, 0, n)) for n in range(2))
    qkv_a = jnp.concatenate([lanes(all_a, 2 * fa + i * ha, ha) for i in range(3)], axis=1)[None]
    out_a = lanes(all_a, 2 * fa + 3 * ha, ha)
    qkv_b = all_q
    if hb != 384:
        parts = [lanes(all_q, i * hb, hb).reshape(d1, -1, 384).transpose(1, 0, 2) for i in range(3)]
        qkv_b = jnp.concatenate(parts, axis=2)
    skip_b = lanes(all_b, 2 * fb + hb, hs)

    comb1, lse1 = attend(low1, own1, mem1, qkv_a, qv_a, mask, d1)
    after1, middle, pooled3, mean3 = call(
        first_mlp_kernel, share,
        [(stream, 0), (comb1, 0), (out_a, None), (all_a, up_spec), (all_a, down_spec), (ub_a, None),
         (padded_rows(shifts_a[1], gains_a[1], shifts_a[2], shifts_a[3], gains_a[2], shifts_a[4]), None),
         (pooling, None), (pairing, None)],
        [(shape((share, tokens, d1), f32), 0), (shape((share, tokens, d1), f32), 0),
         (shape((share, own_rows, d1), bf16), 0), (shape((share, mem_rows, d1), bf16), 0)],
        name="first_mlp",
    )

    own2, mem2 = share_pooled(pooled3, mean3, pick, 1)
    comb2, lse2 = attend(pooled3, own2, mem2, qkv_b, qv_b, mask, d2)
    chunk = 768
    per_head = fb // chunk
    steps = heads * per_head
    out_spec = pl.BlockSpec((heads, d2, hb), lambda j: (0, 0, 2 * fb // hb))
    rows_spec = pl.BlockSpec((1, d2, chunk), lambda j: (j // per_head, 0, j % per_head))
    mixed, dcomb2, dskip, g_mlp_b, g_out_b, g_skip_b, g_ub_b, rows_b = call(
        second_mlp_kernel, steps,
        [(comb2.reshape(rows2, d2), None), (pooled3.reshape(rows2, d1), None), (cot, None), (all_b, out_spec), (skip_b, None),
         (all_b, rows_spec),
         (all_b, pl.BlockSpec((1, d2, chunk), lambda j: (j // per_head, 0, per_head + j % per_head))),
         (ub_b, pl.BlockSpec((1, chunk), lambda j: (0, j))),
         (padded_rows(shifts_b[0], gains_b, shifts_b[1], shifts_b[2]), None)],
        [(shape((rows2, d2), bf16), None), (shape((rows2, d2), bf16), None), (shape((rows2, d1), f32), None),
         (shape((heads, toks, 2, d2 // toks, fb), bf16),
          pl.BlockSpec((1, toks, 2, d2 // toks, chunk), lambda j: (j // per_head, 0, 0, 0, j % per_head))),
         (shape((heads, d2, hb), bf16), None), (shape((heads, d2, hs), bf16), None),
         (shape((1, heads * fb), f32), pl.BlockSpec((1, chunk), lambda j: (0, j))), (shape((8, d2), f32), None)],
        [((rows2, d2), f32), ((rows2, d2), bf16), ((d2, rows2), bf16), ((d2, rows2), bf16), ((rows2, d2), f32), ((rows2, d2), f32)],
        name="second_mlp",
    )

    def by_owner(grad):
        return grad.reshape((heads * toks, -1) + grad.shape[2:])

    def scatter(grad):
        return lax.psum_scatter(grad, group, scatter_dimension=0, tiled=False)

    sum_mlp_b = scatter(g_mlp_b.reshape((heads * toks,) + g_mlp_b.shape[2:]))
    dcomb2 = dcomb2.reshape(share, own_rows, d2)
    dq2, dpool2, g_qkv_b, rows_qv_b = attend_back(pooled3, dcomb2, own2, mem2, qkv_b, qv_b, mask, lse2, heads)
    own_back2, mem_back2 = give_back(dpool2, pick, own_rows, 2)

    res1, dcomb1, g_mlp_a, g_out_a, g_ub_a, rows_a = call(
        first_back_kernel, share,
        [(middle, 0), (after1, 0), (comb1, 0), (dskip.reshape(share, own_rows, d1), 0), (dq2, 0), (own_back2, 0), (mem_back2, 0),
         (out_a, None), (all_a, up_spec), (all_a, down_spec), (ub_a, None),
         (padded_rows(gains_a[1], shifts_a[2], gains_a[2]), None), (unpooling, None), (unpairing, None)],
        [(shape((share, tokens, d1), f32), 0), (shape((share, tokens, d1), bf16), 0),
         (shape((heads, d1, 2 * fa), bf16), None), (shape((heads, d1, ha), bf16), None),
         (shape((heads, 1, fa), f32), None), (shape((8, d1), f32), None)],
        [((heads, d1, fa), f32), ((heads, d1, fa), f32), ((d1, d1), f32)],
        name="first_back",
    )
    g_out_b, g_skip_b = by_owner(g_out_b), by_owner(g_skip_b)
    half = g_out_b.shape[1] // 2
    rest_b = jnp.concatenate(
        [by_owner(g_qkv_b), g_out_b[:, :half], g_out_b[:, half:], g_skip_b[:, :half], g_skip_b[:, half:]], axis=2)
    rest_a = jnp.concatenate([by_owner(g_mlp_a), by_owner(g_out_a)], axis=2)
    dcomb1, sum_mlp_b, rest_b, rest_a = lax.optimization_barrier((dcomb1, sum_mlp_b, rest_b, rest_a))
    sum_rest_b, sum_rest_a = scatter(rest_b), scatter(rest_a)
    sum_mlp_b = reduce_clips(sum_mlp_b)
    dx1, dpool1, g_qkv_a, rows_qv_a = attend_back(low1, dcomb1, own1, mem1, qkv_a, qv_a, mask, lse1, heads)
    own_back1, mem_back1 = give_back(dpool1, pick, own_rows, 3)
    stream_grad, rows_last = call(
        last_back_kernel, share,
        [(stream, 0), (res1, 0), (dx1, 0), (own_back1, 0), (mem_back1, 0), (padded_rows(gains_a[0]), None),
         (unpooling, None), (unpairing, None)],
        [(shape((share, frames, PATCH, d1), bf16), 0), (shape((8, d1), f32), None)],
        name="last_back",
    )

    small = [
        jnp.stack([rows_last[0], rows_a[3], rows_a[0]]), rows_b[3],
        jnp.stack([rows_last[1], rows_a[5], rows_a[4], rows_a[2], rows_a[1]]),
        rows_b[:3], rows_qv_a[:2], rows_qv_b[:2], g_ub_a, g_ub_b,
    ]
    flat = jnp.concatenate([piece.reshape(-1) for piece in small])
    flat = jnp.pad(flat, (0, -flat.size % 1024)).reshape(-1, 128)
    sum_rest_b = reduce_clips(sum_rest_b)
    flat, sum_mlp_b, sum_rest_b = lax.optimization_barrier((flat, sum_mlp_b, sum_rest_b))
    mlp_b, rest_b = spread_clips(sum_mlp_b), spread_clips(sum_rest_b)
    mlp_b = mlp_b.reshape((2, -1, mlp_b.shape[-1])).astype(f32)
    rest_b = rest_b.astype(f32)
    stream_all, flat, grad_qkv_a, rest_a = finish(stream_grad, flat, by_owner(g_qkv_a), sum_rest_a, 4)
    flat = flat.reshape(-1)
    out_lanes = rest_b[:, 3 * hb:5 * hb]
    skip_lanes = rest_b[:, 5 * hb:]
    pieces, at = [], 0
    for piece in small:
        pieces.append(flat[at:at + piece.size].reshape(piece.shape))
        at += piece.size

    def mine(piece, axis):
        width = piece.shape[axis] // heads
        return lax.dynamic_slice_in_dim(piece, head * width, width, axis)

    mixed = mixed.reshape(share, own_rows, d2)[:, :pooled_tokens]
    mixed_all = from_heads(mixed, heads)
    return (
        mixed_all.reshape(cotangent.shape),
        stream_all.astype(f32).reshape(clips_in.shape),
        grad_qkv_a.reshape(w_qkv_a.shape),
        rest_a[:, 2 * fa:],
        rest_a[:, :fa],
        rest_a[:, fa:2 * fa],
        rest_b[:, :3 * hb].reshape(w_qkv_b.shape),
        jnp.concatenate([out_lanes[:, :hb], out_lanes[:, hb:]], axis=0),
        jnp.concatenate([skip_lanes[:, :hs], skip_lanes[:, hs:]], axis=0),
        mlp_b[0],
        mlp_b[1],
        pieces[0], pieces[1], pieces[2], pieces[3],
        mine(pieces[4], 1), mine(pieces[5], 1), mine(pieces[6].reshape(-1), 0), mine(pieces[7].reshape(-1), 0),
    )


def solution(mesh):
    in_specs = (
        P("clip", None, "tok", None, None),
        P("clip", None),
        P("clip", None),
        P("tok", None, "head"),
        P("tok", "head"),
        P("tok", "head"),
        P("tok", "head"),
        P("tok", None, "head"),
        P("tok", "head"),
        P("tok", "head"),
        P("tok", "head"),
        P("tok", "head"),
        P(),
        P(),
        P(),
        P(),
        P(None, "head"),
        P(None, "head"),
        P("head"),
        P("head"),
        P("clip", None, "tok", None, None),
    )
    out_specs = (
        P("clip", None, "tok", None, None),
        P("clip", None, "tok", None, None),
        P("tok", None, "head"),
        P("tok", "head"),
        P("tok", "head"),
        P("tok", "head"),
        P("tok", None, "head"),
        P("tok", "head"),
        P("tok", "head"),
        P("tok", "head"),
        P("tok", "head"),
        P(),
        P(),
        P(),
        P(),
        P(None, "head"),
        P(None, "head"),
        P("head"),
        P("head"),
    )
    return jax.shard_map(local, mesh=mesh, in_specs=in_specs, out_specs=out_specs, check_vma=False)
```

```python
import functools
import math

import jax
import jax.numpy as jnp
import numpy as np
from jax import lax
from jax.experimental import pallas as pl
from jax.experimental.pallas import tpu as pltpu
from jax.sharding import PartitionSpec as P

GRID = 14
PATCH = GRID * GRID
POOLED = PATCH // 4
HD = 96
NEG = -1e30
VMEM_CAP = 62 * 2**20
eps = 1e-06
f32, bf16 = jnp.float32, jnp.bfloat16
NN, NT, TN = ((1,), (0,)), ((1,), (1,)), ((0,), (0,))


def up16(n):
    return -(-n // 16) * 16


def pool_matrix(frames):
    rows, cols = up16(frames * POOLED), frames * PATCH
    out = np.zeros((rows, cols), np.float32)
    half = GRID // 2
    for f in range(frames):
        for p in range(PATCH):
            r, c = divmod(p, GRID)
            out[f * POOLED + (r // 2) * half + c // 2, f * PATCH + p] = 0.25
    return out


def pair_matrix(frames):
    rows, cols = up16(frames // 2 * POOLED), up16(frames * POOLED)
    out = np.zeros((rows, cols), np.float32)
    for j in range(frames // 2):
        for p in range(POOLED):
            out[j * POOLED + p, 2 * j * POOLED + p] = 0.5
            out[j * POOLED + p, (2 * j + 1) * POOLED + p] = 0.5
    return out


def dot(a, b, dims=NN):
    return lax.dot_general(a, b, (dims, ((), ())), preferred_element_type=f32)


def exact_dot(matrix, tensor):
    high = tensor.astype(bf16)
    low = (tensor - high.astype(f32)).astype(bf16)
    return dot(matrix, high) + dot(matrix, low)


def norm(x):
    average = jnp.mean(x, axis=-1, keepdims=True)
    centred = x - average
    inverse = lax.rsqrt(jnp.mean(centred * centred, axis=-1, keepdims=True) + eps)
    return centred * inverse, inverse


def norm_back(unit, inverse, gain, gradient):
    scaled = gradient * gain
    return inverse * (
        scaled
        - jnp.mean(scaled, axis=-1, keepdims=True)
        - unit * jnp.mean(scaled * unit, axis=-1, keepdims=True)
    )


GELU_A, GELU_B = math.sqrt(2.0 / math.pi), 0.044715


def gelu(x):
    t = jnp.tanh(GELU_A * (x + GELU_B * (x * x * x)))
    return 0.5 * x * (1.0 + t)


def gelu_both(x):
    square = x * x
    t = jnp.tanh(GELU_A * x * (1.0 + GELU_B * square))
    value = 0.5 * x * (1.0 + t)
    slope = 0.5 * (1.0 + t) + 0.5 * x * (1.0 - t * t) * (GELU_A * (1.0 + 3.0 * GELU_B * square))
    return value, slope


def sum_rows(x):
    return jnp.sum(x, axis=0, keepdims=True)


def add_rows(ref, rows):
    step = pl.program_id(0)

    @pl.when(step == 0)
    def _():
        ref[...] = jnp.zeros_like(ref)

    for i, row in enumerate(rows):
        ref[i:i + 1, :] += row


def transposed(x):
    return x.astype(f32).T.astype(bf16)


def window(head):
    low = HD * head
    return low // 128 * 128, -(-(low + HD) // 128) * 128


def head_mask(head):
    start, stop = window(head)
    lane = lax.broadcasted_iota(jnp.int32, (1, stop - start), 1) + start
    return (lane >= HD * head) & (lane < HD * head + HD)


def key_rows(own_ref, mem_ref):
    row = 0
    for ref in (own_ref, mem_ref):
        for t in range(ref.shape[0]):
            yield ref, t, slice(row, row + ref.shape[2])
            row += ref.shape[2]


def project_keys(own_ref, mem_ref, w_ref, bias_ref, x_s, k_s, v_s):
    for ref, t, rows in key_rows(own_ref, mem_ref):
        x_s[rows, :] = ref[t, 0]
    width = k_s.shape[1]
    for low in range(0, width, 384):
        k_s[:, low:low + 384] = dot(x_s[...], w_ref[low // 384, :, 384:768]).astype(bf16)
    for low in range(0, width, 384):
        value = dot(x_s[...], w_ref[low // 384, :, 768:])
        v_s[:, low:low + 384] = (value + bias_ref[1:2, low:low + 384]).astype(bf16)


def project_queries(x_ref, w_ref, bias_ref, q_s):
    width = q_s.shape[1]
    for low in range(0, width, 384):
        value = dot(x_ref[0], w_ref[low // 384, :, :384])
        q_s[:, low:low + 384] = (value + bias_ref[0:1, low:low + 384]).astype(bf16)


def norm_pool_kernel(first_ref, clips_ref, vec_ref, pool_ref, pair_ref, x_ref, low_ref, pooled_ref, mean_ref):
    x = jnp.concatenate([clips_ref[0, 0, f].astype(f32) for f in range(clips_ref.shape[2])], axis=0)
    x_ref[0] = x.astype(bf16)
    unit, _ = norm(x)
    normed = unit * vec_ref[0:1, :] + vec_ref[1:2, :]
    low_ref[0] = normed.astype(bf16)
    pooled = exact_dot(pool_ref[...], normed)
    pooled_ref[0] = pooled.astype(bf16)
    mean_ref[0] = exact_dot(pair_ref[...], pooled).astype(bf16)


def write_shares(gw_ref, h, gw_s):
    wide = gw_ref.shape[2] // 3
    for part in range(3):
        low = wide * h
        columns = gw_s[low // 384, :, 384 * part:384 * part + 384][:, low % 384:low % 384 + wide]
        gw_ref[h, :, wide * part:wide * part + wide] = columns.astype(bf16)


def attend_kernel(chunk, x_ref, own_ref, mem_ref, w_ref, qv_ref, mask_ref, out_ref, lse_ref, x_s, q_s, k_s, v_s, s_s, p_s):
    nq, width = q_s.shape
    project_queries(x_ref, w_ref, qv_ref, q_s)
    project_keys(own_ref, mem_ref, w_ref, qv_ref, x_s, k_s, v_s)
    factor = HD**-0.5 * math.log2(math.e)
    lanes = lax.broadcasted_iota(jnp.int32, (chunk, 128), 1)
    for tile in range(width // 384):
        group = slice(384 * tile, 384 * tile + 384)
        base = q_s[:, group].astype(f32)
        parts = [base[:, :128], base[:, 128:256], base[:, 256:384]]
        for head in range(4 * tile, 4 * tile + 4):
            start, stop = window(head)
            mask = head_mask(head)
            query = jnp.where(mask, q_s[:, start:stop], jnp.zeros((), bf16))
            s_s[...] = dot(query, k_s[:, start:stop], NT)

            def body(i, carry, head=head):
                rows = pl.ds(pl.multiple_of(i * chunk, chunk), chunk)
                score = s_s[rows, :] * factor + mask_ref[0]
                top = jnp.max(score, axis=1, keepdims=True)
                power = jnp.exp2(score - top)
                total = jnp.sum(power, axis=1, keepdims=True)
                p_s[rows, :] = (power * (1.0 / total)).astype(bf16)
                lse_ref[0, rows, :] = jnp.where(lanes == head, top + jnp.log2(total), lse_ref[0, rows, :])
                return carry

            lax.fori_loop(0, nq // chunk, body, 0, unroll=nq // chunk)
            out = jnp.where(mask, dot(p_s[...], v_s[:, start:stop]), 0.0)
            for w in range((stop - start) // 128):
                k = start // 128 - 3 * tile + w
                parts[k] = parts[k] + out[:, 128 * w:128 * w + 128]
        out_ref[0, :, group] = jnp.concatenate(parts, axis=1).astype(bf16)


def attend_back_kernel(
    chunk, x_ref, g_ref, own_ref, mem_ref, w_ref, qv_ref, mask_ref, lse_ref,
    dx_ref, dpool_ref, gw_ref, row_ref,
    x_s, q_s, k_s, v_s, s_s, dp_s, p_s, ds_s, dk_s, dv_s, dq_s, gw_s,
):
    nq, width = q_s.shape
    step = pl.program_id(0)
    project_queries(x_ref, w_ref, qv_ref, q_s)
    project_keys(own_ref, mem_ref, w_ref, qv_ref, x_s, k_s, v_s)
    scaling = HD**-0.5
    factor = scaling * math.log2(math.e)
    lanes = lax.broadcasted_iota(jnp.int32, (chunk, 128), 1)

    @pl.when(step == 0)
    def _():
        gw_s[...] = jnp.zeros_like(gw_s)

    xt = transposed(x_ref[0])
    keys_t = transposed(x_s[...])
    dx = None
    dpool = None
    row_q, row_v = [], []
    for tile in range(width // 384):
        group = slice(384 * tile, 384 * tile + 384)
        qt = transposed(q_s[:, group])
        gt = transposed(g_ref[0, :, group])
        parts = [None] * 3
        for head in range(4 * tile, 4 * tile + 4):
            start, stop = window(head)
            mask = head_mask(head)
            query = jnp.where(mask, q_s[:, start:stop], jnp.zeros((), bf16))
            grad = jnp.where(mask, g_ref[0, :, start:stop], jnp.zeros((), bf16))
            s_s[...] = dot(query, k_s[:, start:stop], NT)
            dp_s[...] = dot(grad, v_s[:, start:stop], NT)

            def body(i, carry, head=head):
                rows = pl.ds(pl.multiple_of(i * chunk, chunk), chunk)
                lse = jnp.sum(jnp.where(lanes == head, lse_ref[0, rows, :], 0.0), axis=1, keepdims=True)
                p = jnp.exp2(s_s[rows, :] * factor + mask_ref[0] - lse)
                dp = dp_s[rows, :]
                inner = jnp.sum(p * dp, axis=1, keepdims=True)
                p_s[rows, :] = p.astype(bf16)
                ds_s[rows, :] = (p * (dp - inner)).astype(bf16)
                return carry

            lax.fori_loop(0, nq // chunk, body, 0, unroll=nq // chunk)
            r = slice(HD * (head - 4 * tile), HD * (head - 4 * tile) + HD)
            dv_s[r, :] = dot(gt[r], p_s[...])
            dk_s[r, :] = dot(qt[r], ds_s[...]) * scaling
            dq = jnp.where(mask, dot(ds_s[...], k_s[:, start:stop]) * scaling, 0.0)
            for w in range((stop - start) // 128):
                k = start // 128 - 3 * tile + w
                part = dq[:, 128 * w:128 * w + 128]
                parts[k] = part if parts[k] is None else parts[k] + part
        total = jnp.concatenate(parts, axis=1) + g_ref[0, :, group].astype(f32)
        row_q.append(sum_rows(total))
        low = total.astype(bf16)
        gw_s[tile, :, :384] += dot(xt, low)
        add = dot(low, w_ref[tile, :, :384], NT)
        dx = add if dx is None else dx + add
        for part, src in ((1, dk_s), (2, dv_s)):
            grad = src[...].T
            if part == 2:
                row_v.append(sum_rows(grad))
            low = grad.astype(bf16)
            here = slice(384 * part, 384 * part + 384)
            gw_s[tile, :, here] += dot(keys_t, low)
            add = dot(low, w_ref[tile, :, here], NT)
            dpool = add if dpool is None else dpool + add
    dx_ref[0] = dx
    row = 0
    own, mem = own_ref.shape[2], mem_ref.shape[2]
    toks = own_ref.shape[0]
    for t in range(toks):
        dpool_ref[t, 0, :own, :] = dpool[t * own:(t + 1) * own].astype(bf16)
        dpool_ref[t, 0, own:, :] = dpool[toks * own + t * mem:toks * own + (t + 1) * mem].astype(bf16)
    add_rows(row_ref, [jnp.concatenate(row_q, axis=1), jnp.concatenate(row_v, axis=1)])

    @pl.when(step == pl.num_programs(0) - 1)
    def _():
        for h in range(gw_ref.shape[0]):
            write_shares(gw_ref, h, gw_s)


def first_mlp_kernel(x_ref, comb_ref, out_ref, up_ref, down_ref, ub_ref, vec_ref, pool_ref, pair_ref,
                     after_ref, middle_ref, pooled_ref, mean_ref):
    after = x_ref[0].astype(f32) + dot(comb_ref[0], out_ref[...], NT) + vec_ref[0:1, :]
    after_ref[0] = after
    unit, _ = norm(after)
    low = (unit * vec_ref[1:2, :] + vec_ref[2:3, :]).astype(bf16)
    total = after + vec_ref[3:4, :]
    for h in range(up_ref.shape[0]):
        hidden = gelu(dot(low, up_ref[h]) + ub_ref[h]).astype(bf16)
        total = total + dot(hidden, down_ref[h], NT)
    middle_ref[0] = total
    unit, _ = norm(total)
    pooled = exact_dot(pool_ref[...], unit * vec_ref[4:5, :] + vec_ref[5:6, :])
    pooled_ref[0] = pooled.astype(bf16)
    mean_ref[0] = exact_dot(pair_ref[...], pooled).astype(bf16)


def second_mlp_kernel(
    comb_ref, pooled_ref, cot_ref, out_ref, skip_ref, up_ref, down_ref, ub_ref, vec_ref,
    mixed_ref, dcomb_ref, dskip_ref, gmlp_ref, gout_ref, gskip_ref, gub_ref, row_ref,
    after_s, low_s, lowt_s, cott_s, sum_s, dlow_s,
):
    step = pl.program_id(0)

    @pl.when(step == 0)
    def _():
        after = dot(pooled_ref[...], skip_ref[...], NT) + vec_ref[0:1, :]
        wide = out_ref.shape[2]
        for h in range(out_ref.shape[0]):
            after = after + dot(comb_ref[:, wide * h:wide * h + wide], out_ref[h], NT)
        after_s[...] = after
        unit, _ = norm(after)
        low = (unit * vec_ref[1:2, :] + vec_ref[2:3, :]).astype(bf16)
        low_s[...] = low
        lowt_s[...] = transposed(low)
        cott_s[...] = transposed(cot_ref[...])
        sum_s[...] = after + vec_ref[3:4, :]
        dlow_s[...] = jnp.zeros_like(dlow_s)

    pre = dot(low_s[...], up_ref[0]) + ub_ref[...]
    hidden, slope = gelu_both(pre)
    hidden = hidden.astype(bf16)
    dpre = dot(cot_ref[...], down_ref[0]) * slope
    gub_ref[...] = sum_rows(dpre)
    dpre = dpre.astype(bf16)
    sum_s[...] += dot(hidden, down_ref[0], NT)
    dlow_s[...] += dot(dpre, up_ref[0], NT)
    for n, grad in enumerate((dot(lowt_s[...], dpre), dot(cott_s[...], hidden))):
        rows = gmlp_ref.shape[3]
        for t in range(gmlp_ref.shape[1]):
            gmlp_ref[0, t, n] = grad[t * rows:(t + 1) * rows].astype(bf16)

    @pl.when(step == pl.num_programs(0) - 1)
    def _():
        mixed_ref[...] = sum_s[...].astype(bf16)
        unit, inverse = norm(after_s[...])
        dlow = dlow_s[...]
        cot = cot_ref[...].astype(f32)
        res = norm_back(unit, inverse, vec_ref[1:2, :], dlow) + cot
        row_ref[...] = jnp.zeros_like(row_ref)
        for i, row in enumerate((res, dlow, cot, dlow * unit)):
            row_ref[i:i + 1, :] = sum_rows(row)
        res = res.astype(bf16)
        dskip_ref[...] = dot(res, skip_ref[...])
        rest = transposed(res)
        wide = out_ref.shape[2]
        for h in range(out_ref.shape[0]):
            here = slice(wide * h, wide * h + wide)
            dcomb_ref[:, here] = dot(res, out_ref[h]).astype(bf16)
            grad = dot(rest, comb_ref[:, here])
            half = gout_ref.shape[2]
            for n in range(2 * gout_ref.shape[1]):
                gout_ref[h, n // 2, :, wide * (n % 2):wide * (n % 2) + wide] = grad[half * n:half * n + half].astype(bf16)
        grad = dot(rest, pooled_ref[...])
        wide = gskip_ref.shape[3] // 2
        for h in range(gskip_ref.shape[0]):
            for t in range(gskip_ref.shape[1]):
                low, high = (grad[half * n:half * n + half, wide * h:wide * h + wide] for n in (2 * t, 2 * t + 1))
                gskip_ref[h, t] = jnp.concatenate([low, high], axis=1).astype(bf16)


def first_back_kernel(
    middle_ref, after_ref, comb_ref, dskip_ref, dq_ref, own_ref, mem_ref, out_ref, up_ref, down_ref, ub_ref, vec_ref,
    unpool_ref, unpair_ref,
    res_ref, dcomb_ref, gmlp_ref, gub_ref, row_ref,
    gup_s, gdown_s, gout_s,
):
    step = pl.program_id(0)

    @pl.when(step == 0)
    def _():
        gup_s[...] = jnp.zeros_like(gup_s)
        gdown_s[...] = jnp.zeros_like(gdown_s)
        gout_s[...] = jnp.zeros_like(gout_s)
        gub_ref[...] = jnp.zeros_like(gub_ref)

    dpool = dskip_ref[0] + dq_ref[0] + own_ref[0] + exact_dot(unpair_ref[...], mem_ref[0])
    dnorm = exact_dot(unpool_ref[...], dpool)
    unit, inverse = norm(middle_ref[0])
    grad = norm_back(unit, inverse, vec_ref[2:3, :], dnorm)
    rows = [sum_rows(dnorm * unit), sum_rows(dnorm), sum_rows(grad)]
    low = grad.astype(bf16)
    lowt = transposed(low)
    unit, inverse = norm(after_ref[0])
    normed = (unit * vec_ref[0:1, :] + vec_ref[1:2, :]).astype(bf16)
    normedt = transposed(normed)
    dnormed = None
    for h in range(up_ref.shape[0]):
        hidden, slope = gelu_both(dot(normed, up_ref[h]) + ub_ref[h])
        hidden = hidden.astype(bf16)
        dpre = dot(low, down_ref[h]) * slope
        gub_ref[h] += sum_rows(dpre)
        dpre = dpre.astype(bf16)
        gdown_s[h] += dot(lowt, hidden)
        gup_s[h] += dot(normedt, dpre)
        add = dot(dpre, up_ref[h], NT)
        dnormed = add if dnormed is None else dnormed + add
    res = norm_back(unit, inverse, vec_ref[0:1, :], dnormed) + grad
    rows += [sum_rows(dnormed * unit), sum_rows(dnormed), sum_rows(res)]
    res_ref[0] = res
    res = res.astype(bf16)
    dcomb_ref[0] = dot(res, out_ref[...]).astype(bf16)
    gout_s[...] += dot(transposed(res), comb_ref[0])
    add_rows(row_ref, rows)

    @pl.when(step == pl.num_programs(0) - 1)
    def _():
        fa, ha = gup_s.shape[2], gout_s.shape[1] // gmlp_ref.shape[0]
        for h in range(gmlp_ref.shape[0]):
            gmlp_ref[h, :, :fa] = gup_s[h].astype(bf16)
            gmlp_ref[h, :, fa:2 * fa] = gdown_s[h].astype(bf16)
            rest = gmlp_ref.shape[2] - 2 * fa - ha
            gout = jnp.concatenate([gout_s[:, ha * h:ha * h + ha], jnp.zeros((gout_s.shape[0], rest), f32)], axis=1)
            gmlp_ref[h, :, 2 * fa:] = gout.astype(bf16)


def last_back_kernel(x_ref, res_ref, dx_ref, own_ref, mem_ref, vec_ref, unpool_ref, unpair_ref, grad_ref, row_ref):
    dpool = own_ref[0] + exact_dot(unpair_ref[...], mem_ref[0])
    dnorm = dx_ref[0] + exact_dot(unpool_ref[...], dpool)
    unit, inverse = norm(x_ref[0].astype(f32))
    grad = norm_back(unit, inverse, vec_ref[0:1, :], dnorm) + res_ref[0]
    for f in range(grad_ref.shape[1]):
        grad_ref[0, f] = grad[PATCH * f:PATCH * f + PATCH].astype(bf16)
    add_rows(row_ref, [sum_rows(dnorm * unit), sum_rows(dnorm)])


def whole(array):
    return pl.BlockSpec(array.shape, lambda i: (0,) * array.ndim)


def by_micro(array, axis=0):
    block = array.shape[:axis] + (1,) + array.shape[axis + 1:]
    return pl.BlockSpec(block, lambda i: (0,) * axis + (i,) + (0,) * (array.ndim - axis - 1))


def shape(dims, dtype):
    return jax.ShapeDtypeStruct(dims, dtype)


def call(kernel, steps, args, outs, scratch=(), name=None):
    def spec(array, how):
        if how is None:
            return whole(array)
        return by_micro(array, how) if isinstance(how, int) else how

    return pl.pallas_call(
        kernel,
        grid=(steps,),
        in_specs=[spec(a, how) for a, how in args],
        out_specs=[spec(a, how) for a, how in outs],
        out_shape=[a for a, _ in outs],
        scratch_shapes=[pltpu.VMEM(dims, dtype) for dims, dtype in scratch],
        compiler_params=pltpu.CompilerParams(vmem_limit_bytes=VMEM_CAP),
        name=name,
    )(*[a for a, _ in args])


def chunk_of(nq):
    return 112 if nq % 112 == 0 else 16


def attend(x, own, mem, w, qv, mask, width):
    batches, nq, d = x.shape
    keys = own.shape[0] * own.shape[2] + mem.shape[0] * mem.shape[2]
    return call(
        functools.partial(attend_kernel, chunk_of(nq)), batches,
        [(x, 0), (own, 1), (mem, 1), (w, None), (qv, None), (mask, 0)],
        [(shape((batches, nq, width), bf16), 0), (shape((batches, nq, 128), f32), 0)],
        [((keys, d), bf16), ((nq, width), bf16), ((keys, width), bf16), ((keys, width), bf16), ((nq, keys), f32), ((nq, keys), bf16)],
        name="attend",
    )


def attend_back(x, grad, own, mem, w, qv, mask, lse, heads):
    batches, nq, d = x.shape
    width = grad.shape[2]
    keys = own.shape[0] * own.shape[2] + mem.shape[0] * mem.shape[2]
    both = (own.shape[0], batches, own.shape[2] + mem.shape[2], d)
    return call(
        functools.partial(attend_back_kernel, chunk_of(nq)), batches,
        [(x, 0), (grad, 0), (own, 1), (mem, 1), (w, None), (qv, None), (mask, 0), (lse, 0)],
        [(shape((batches, nq, d), f32), 0), (shape(both, bf16), 1), (shape((heads, d, 3 * width // heads), bf16), None), (shape((8, width), f32), None)],
        [((keys, d), bf16), ((nq, width), bf16), ((keys, width), bf16), ((keys, width), bf16),
         ((nq, keys), f32), ((nq, keys), f32), ((nq, keys), bf16), ((nq, keys), bf16),
         ((384, keys), f32), ((384, keys), f32), ((8, 128), f32), (w.shape, f32)],
        name="attend_back",
    )


MESH = pl.DeviceIdType.MESH


def places():
    tok, toks = lax.axis_index("tok"), lax.axis_size("tok")
    return lax.axis_index("clip"), lax.axis_index("head"), tok // 2, tok % 2, toks // 2


def greet(copies_to_me, i_copy_to):
    barrier = pltpu.get_barrier_semaphore()
    for device, condition in copies_to_me:
        if condition is None:
            pl.semaphore_signal(barrier, inc=1, device_id=device, device_id_type=MESH)
        else:
            @pl.when(condition)
            def _():
                pl.semaphore_signal(barrier, inc=1, device_id=device, device_id_type=MESH)
    count = 0
    for _, condition in i_copy_to:
        count = count + (1 if condition is None else jnp.where(condition, 1, 0))
    pl.semaphore_wait(barrier, count)


def remote(src, dst, send, recv, device):
    return pltpu.make_async_remote_copy(
        src_ref=src, dst_ref=dst, send_sem=send, recv_sem=recv, device_id=device, device_id_type=MESH
    )


def rem(a, n):
    return lax.rem(a + n, n)


def share_kernel(gather, *refs):
    if gather:
        pooled_ref, mean_ref, pick_ref, w_ref, own_ref, mem_ref, all_ref, *refs = refs
    else:
        pooled_ref, mean_ref, pick_ref, own_ref, mem_ref, *refs = refs
    (got_s, pick_s, local_sem, own_send, own_recv, mem_send, mem_recv, pass_send, pass_recv, clip_send, clip_recv, *refs) = refs
    clip, head, chip, core, chips = places()
    clips, heads = lax.axis_size("clip"), lax.axis_size("head")
    share = pooled_ref.shape[0]
    here = 2 * chip + core
    partner = {"tok": 2 * chip + 1 - core}
    across = [{"tok": 2 * rem(chip + k, chips) + core} for k in range(1, chips)]
    beside = [{"head": rem(head + d, heads)} for d in range(1, heads)]
    heads_of = lambda by, sign: [{"clip": clip + by, "head": rem(head + sign * d, heads)} for d in range(heads)]
    last, begun = clip < clips - 1, clip > 0
    near = [(d, None) for d in [partner] + across + (beside if gather else [])]
    greet(near + [(d, begun) for d in heads_of(-1, -1)], near + [(d, last) for d in heads_of(1, 1)])

    def spread(src, out, send, recv):
        copies = [remote(src, out.at[here], send.at[0], recv.at[0], partner)]
        copies += [remote(src, out.at[here], send.at[k + 1], recv.at[k + 1], across[k]) for k in range(chips - 1)]
        return copies

    def passed(out, k, row):
        block = 2 * rem(chip - k, chips) + core
        return remote(out.at[block], out.at[block], pass_send.at[row, k - 1], pass_recv.at[row, k - 1], partner)

    clip_copies = [remote(mean_ref, got_s.at[d], clip_send.at[d], clip_recv.at[d], device) for d, device in enumerate(heads_of(1, 1))]

    @pl.when(last)
    def _():
        for copy in clip_copies:
            copy.start()

    w_first, w_diagonal, w_core = {}, {}, {}
    if gather:
        w_local, w_send, w_recv, d_send, d_recv, c_send, c_recv = refs
        mine = all_ref.at[head, here]
        for k in range(1, chips):
            w_first[k, 0] = remote(w_ref, mine, w_send.at[k - 1], w_recv.at[k - 1], across[k - 1])
        for d in range(1, heads):
            w_first[0, d] = remote(w_ref, mine, w_send.at[chips - 2 + d], w_recv.at[chips - 2 + d], beside[d - 1])
        w_core[0, 0] = remote(w_ref, mine, c_send.at[0, 0], c_recv.at[0, 0], partner)
        for copy in [*w_first.values(), w_core[0, 0]]:
            copy.start()
        w_copy = pltpu.make_async_copy(w_ref, mine, w_local.at[0])
        w_copy.start()

        def forward(k, d):
            block = all_ref.at[rem(head - d, heads), 2 * rem(chip - k, chips) + core]
            w_core[k, d] = remote(block, block, c_send.at[k, d], c_recv.at[k, d], partner)
            w_core[k, d].start()

    own_copies = spread(pooled_ref, own_ref, own_send, own_recv)
    for copy in own_copies[1:] + own_copies[:1]:
        copy.start()
    own_local = pltpu.make_async_copy(pooled_ref, own_ref.at[here], local_sem.at[0])
    own_local.start()
    if gather:
        for k in range(1, chips):
            w_first[k, 0].wait_recv()
            block = all_ref.at[head, 2 * rem(chip - k, chips) + core]
            for d in range(1, heads):
                w_diagonal[k, d] = remote(block, block, d_send.at[k - 1, d - 1], d_recv.at[k - 1, d - 1], beside[d - 1])
                w_diagonal[k, d].start()
            forward(k, 0)

    @pl.when(begun)
    def _():
        for copy in clip_copies:
            copy.wait_recv()
        for m in range(share):
            total = None
            for d in range(heads):
                for s in range(share):
                    piece = got_s[d, s].astype(f32) * pick_ref[m, d * share + s]
                    total = piece if total is None else total + piece
            pick_s[m] = total.astype(bf16)

    @pl.when(jnp.logical_not(begun))
    def _():
        pick_s[...] = jnp.zeros_like(pick_s)

    mem_copies = spread(pick_s, mem_ref, mem_send, mem_recv)
    for copy in mem_copies[1:] + mem_copies[:1]:
        copy.start()
    mem_local = pltpu.make_async_copy(pick_s, mem_ref.at[here], local_sem.at[1])
    mem_local.start()
    forwards = []
    for k in range(1, chips):
        own_copies[k].wait_recv()
        forwards.append(passed(own_ref, k, 0))
        forwards[-1].start()
    if gather:
        for d in range(1, heads):
            w_first[0, d].wait_recv()
            forward(0, d)
    for k in range(1, chips):
        mem_copies[k].wait_recv()
        forwards.append(passed(mem_ref, k, 1))
        forwards[-1].start()
    if gather:
        for k, d in w_diagonal:
            w_diagonal[k, d].wait_recv()
            forward(k, d)
        for copy in w_core.values():
            copy.wait_recv()
    own_copies[0].wait_recv()
    mem_copies[0].wait_recv()
    for copy in forwards:
        copy.wait_recv()
    for copy in own_copies + mem_copies + forwards + [*w_first.values(), *w_diagonal.values(), *w_core.values()]:
        copy.wait_send()
    own_local.wait()
    mem_local.wait()
    if gather:
        w_copy.wait()

    @pl.when(last)
    def _():
        for copy in clip_copies:
            copy.wait_send()


ANY = pl.BlockSpec(memory_space=pl.ANY)
INVMEM = pl.BlockSpec(memory_space=pltpu.VMEM)
INSMEM = pl.BlockSpec(memory_space=pltpu.SMEM)


def dma(*dims):
    return pltpu.SemaphoreType.DMA(dims)


def share_pooled(pooled, mean, pick, number, block=None):
    toks, heads = lax.axis_size("tok"), lax.axis_size("head")
    chips = toks // 2
    few = max(chips - 1, 1)
    args, specs = [pooled, mean, pick], [INVMEM, INVMEM, INSMEM]
    outs = [shape((toks,) + pooled.shape, bf16), shape((toks,) + mean.shape, bf16)]
    scratch = [
        pltpu.VMEM((heads,) + mean.shape, bf16), pltpu.VMEM(mean.shape, bf16), dma(2),
        dma(chips), dma(chips), dma(chips), dma(chips), dma(2, few), dma(2, few), dma(heads), dma(heads),
    ]
    if block is not None:
        args, specs, outs = args + [block], specs + [ANY], outs + [shape((heads, toks) + block.shape, bf16)]
        firsts = max(chips + heads - 2, 1)
        scratch += [dma(1), dma(firsts), dma(firsts), dma(few, max(heads - 1, 1)), dma(few, max(heads - 1, 1)), dma(chips, heads), dma(chips, heads)]
    return pl.pallas_call(
        functools.partial(share_kernel, block is not None),
        in_specs=specs,
        out_specs=[ANY] * len(outs),
        out_shape=outs,
        scratch_shapes=scratch,
        compiler_params=pltpu.CompilerParams(collective_id=number, has_side_effects=True, vmem_limit_bytes=VMEM_CAP),
        name="share_pooled",
    )(*args)


def give_back_kernel(exchange, *refs):
    if exchange:
        part_ref, pick_ref, half_ref, own_ref, back_ref, all_ref, *refs = refs
        *refs, half_local, half_send, half_recv = refs
    else:
        part_ref, pick_ref, own_ref, back_ref, *refs = refs
    (mine_s, core_s, sum_s, chip_s, route_s, got_s,
     local_sem, core_send, core_recv, mem_send, mem_recv, own_send, own_recv, clip_send, clip_recv) = refs
    clip, head, chip, core, chips = places()
    clips, heads = lax.axis_size("clip"), lax.axis_size("head")
    share, rows = own_ref.shape[0], own_ref.shape[1]
    partner = {"tok": 2 * chip + 1 - core}
    across = [{"tok": 2 * rem(chip + k, chips) + core} for k in range(1, chips)]
    beside = [{"head": rem(head + d, heads)} for d in range(1, heads)]
    heads_of = lambda by, sign: [{"clip": clip + by, "head": rem(head + sign * d, heads)} for d in range(heads)]
    last, begun = clip < clips - 1, clip > 0
    near = [(d, None) for d in [partner] + across + (beside if exchange else [])]
    greet(near + [(d, last) for d in heads_of(1, 1)], near + [(d, begun) for d in heads_of(-1, -1)])

    order = [rem(chip + k, chips) for k in list(range(1, chips)) + [0]]
    core_copies, local_copies = [], []
    for n, other in enumerate(order):
        core_copies.append(remote(part_ref.at[2 * other + 1 - core], core_s.at[n], core_send.at[n], core_recv.at[n], partner))
        core_copies[-1].start()
    for n, other in enumerate(order):
        local_copies.append(pltpu.make_async_copy(part_ref.at[2 * other + core], mine_s.at[n], local_sem.at[n]))
        local_copies[-1].start()
    halves = []
    if exchange:
        halves = [remote(half_ref, all_ref.at[head], half_send.at[k], half_recv.at[k], d) for k, d in enumerate(beside)]
        for copy in halves:
            copy.start()
        half_copy = pltpu.make_async_copy(half_ref, all_ref.at[head], half_local.at[0])
        half_copy.start()
    mem_copies, own_copies = [], []
    for n in range(chips):
        local_copies[n].wait()
        core_copies[n].wait_recv()
        if n == chips - 1:
            break
        sum_s[n] = (mine_s[n].astype(f32) + core_s[n].astype(f32)).astype(bf16)
        low, high = pl.ds(0, rows), pl.ds(rows, sum_s.shape[2] - rows)
        mem_copies.append(remote(sum_s.at[n, :, high, :], chip_s.at[n, :, high, :], mem_send.at[n], mem_recv.at[n], across[n]))
        mem_copies[-1].start()
        own_copies.append(remote(sum_s.at[n, :, low, :], chip_s.at[n, :, low, :], own_send.at[n], own_recv.at[n], across[n]))
        own_copies[-1].start()
    base = chips - 1
    for copy in mem_copies:
        copy.wait_recv()
    memory = []
    for m in range(share):
        total = mine_s[base, m, rows:].astype(f32) + core_s[base, m, rows:].astype(f32)
        for n in range(chips - 1):
            total = total + chip_s[n, m, rows:].astype(f32)
        memory.append(total)
    clip_copies = [
        remote(route_s.at[d], got_s.at[d], clip_send.at[d], clip_recv.at[d], device) for d, device in enumerate(heads_of(-1, -1))
    ]

    @pl.when(begun)
    def _():
        for d in range(heads):
            for s in range(share):
                total = None
                for m in range(share):
                    piece = memory[m] * pick_ref[m, d * share + s]
                    total = piece if total is None else total + piece
                route_s[d, s] = total.astype(bf16)
            clip_copies[d].start()

    for copy in own_copies:
        copy.wait_recv()
    for m in range(share):
        total = mine_s[base, m, :rows].astype(f32) + core_s[base, m, :rows].astype(f32)
        for n in range(chips - 1):
            total = total + chip_s[n, m, :rows].astype(f32)
        own_ref[m] = total

    @pl.when(last)
    def _():
        for copy in clip_copies:
            copy.wait_recv()
        total = got_s[0].astype(f32)
        for d in range(1, heads):
            total = total + got_s[d].astype(f32)
        back_ref[...] = total

    @pl.when(jnp.logical_not(last))
    def _():
        back_ref[...] = jnp.zeros_like(back_ref)

    for copy in halves:
        copy.wait_recv()
    for copy in core_copies + mem_copies + own_copies + halves:
        copy.wait_send()
    if exchange:
        half_copy.wait()

    @pl.when(begun)
    def _():
        for copy in clip_copies:
            copy.wait_send()


def give_back(part, pick, own_rows, number, half=None):
    toks, heads = lax.axis_size("tok"), lax.axis_size("head")
    chips, few = toks // 2, max(toks // 2 - 1, 1)
    share, rows, d = part.shape[1:]
    args, specs = [part, pick], [ANY, INSMEM]
    outs, out_specs = [shape((share, own_rows, d), f32), shape((share, rows - own_rows, d), f32)], [INVMEM, INVMEM]
    scratch = [
        pltpu.VMEM((chips,) + part.shape[1:], bf16), pltpu.VMEM((chips,) + part.shape[1:], bf16),
        pltpu.VMEM((few,) + part.shape[1:], bf16), pltpu.VMEM((few,) + part.shape[1:], bf16),
        pltpu.VMEM((heads, share, rows - own_rows, d), bf16), pltpu.VMEM((heads, share, rows - own_rows, d), bf16),
        dma(chips), dma(chips), dma(chips), dma(few), dma(few), dma(few), dma(few), dma(heads), dma(heads),
    ]
    if half is not None:
        args, specs = args + [half], specs + [ANY]
        outs, out_specs = outs + [shape((heads,) + half.shape, half.dtype)], out_specs + [ANY]
        scratch += [dma(1), dma(max(heads - 1, 1)), dma(max(heads - 1, 1))]
    return pl.pallas_call(
        functools.partial(give_back_kernel, half is not None),
        in_specs=specs,
        out_specs=out_specs,
        out_shape=outs,
        scratch_shapes=scratch,
        compiler_params=pltpu.CompilerParams(collective_id=number, has_side_effects=True, vmem_limit_bytes=VMEM_CAP),
        name="give_back",
    )(*args)


def finish_kernel(sizes, half_ref, early_ref, last_ref, qv_ref, grad_ref, rest_ref, all_ref, gains_a_ref, gains_b_ref, shifts_a_ref,
                  shifts_b_ref, qv_a_ref, qv_b_ref, ub_a_ref, ub_b_ref, gtotal_ref, up_ref, down_ref, out_ref, *scratch):
    (small_ref, small_s, small_core, small_chip, small_head, small_clip, part_s, part_core, chip_s, part_chip, head_s, part_head, mine_s, part_clip,
     rest_in, rest_s, local_sem, half_send, half_recv, core_send, core_recv, chip_send, chip_recv, head_send, head_recv,
     clip_send, clip_recv, rest_send, rest_recv, back_send, back_recv) = scratch
    clip, head, chip, core, chips = places()
    clips, heads = lax.axis_size("clip"), lax.axis_size("head")
    share = half_ref.shape[0]
    partner = {"tok": 2 * chip + 1 - core}
    across = [{"tok": 2 * rem(chip + k, chips) + core} for k in range(1, chips)]
    beside = [{"head": rem(head + k, heads)} for k in range(1, heads)]
    along = [{"clip": rem(clip + k, clips)} for k in range(1, clips)]
    peers = [(d, None) for d in [partner] + across + beside + along]
    greet(peers, peers)
    pending = []
    small_ref[...] = early_ref[...]
    small_ref[0:2, :] = last_ref[0:2, :]
    small_ref[2:4, :] = qv_ref[0:2, :]
    wide = rest_ref.shape[1] // clips

    def lanes(c):
        return pl.ds(pl.multiple_of(wide * c, wide), wide)

    def go(copies):
        for copy in copies:
            copy.start()
        pending.extend(copies)
        return copies

    def arrived(copies):
        for copy in copies:
            copy.wait_recv()

    def in_order(index, size, own, slot):
        total = None
        for i in range(size):
            piece = jnp.where(index == i, own, jnp.zeros_like(own))
            for k in range(size - 1):
                piece = jnp.where(rem(index - k - 1, size) == i, slot(k), piece)
            total = piece if total is None else total + piece
        return total

    first = go([remote(small_ref, small_core, core_send.at[0], core_recv.at[0], partner)])
    for h in range(heads):
        for x in range(chips):
            n = h * chips + x
            first += go([remote(grad_ref.at[2 * n + 1 - core], part_core.at[n], core_send.at[n + 1], core_recv.at[n + 1], partner)])
    gather = go([remote(rest_ref.at[:, lanes(rem(clip + k + 1, clips))], rest_in.at[k], rest_send.at[k], rest_recv.at[k], d) for k, d in enumerate(along)])
    halves = [
        [remote(half_ref.at[s], all_ref.at[head, s], half_send.at[k, s], half_recv.at[k, s], d) for k, d in enumerate(beside)]
        for s in range(share)
    ]
    for s in range(share - 1):
        go(halves[s])
    local_half = pltpu.make_async_copy(half_ref, all_ref.at[head], local_sem.at[0])
    local_half.start()
    arrived(first)
    small_s[0] = small_ref[...] + small_core[...]
    for n in range(heads * chips):
        part_s[n] = (grad_ref[2 * n + core].astype(f32) + part_core[n].astype(f32)).astype(bf16)
    copies = []
    for k, d in enumerate(across):
        copies += go([remote(small_s.at[0], small_chip.at[k], chip_send.at[k, 0], chip_recv.at[k, 0], d)])
        for h in range(heads):
            block = h * chips + rem(chip + k + 1, chips)
            copies += go([remote(part_s.at[block], part_chip.at[k, h], chip_send.at[k, h + 1], chip_recv.at[k, h + 1], d)])
    arrived(copies)
    small_s[1] = in_order(chip, chips, small_s[0], lambda k: small_chip[k])
    for h in range(heads):
        total = part_s[h * chips + chip].astype(f32)
        for k in range(chips - 1):
            total = total + part_chip[k, h].astype(f32)
        chip_s[h] = total.astype(bf16)
    copies = []
    for k, d in enumerate(beside):
        copies += go([remote(small_s.at[1], small_head.at[k], head_send.at[k, 0], head_recv.at[k, 0], d)])
        copies += go([remote(chip_s.at[rem(head + k + 1, heads)], part_head.at[k], head_send.at[k, 1], head_recv.at[k, 1], d)])
    go(halves[share - 1])
    arrived(gather)
    total = rest_ref[:, lanes(clip)].astype(f32)
    for k in range(clips - 1):
        total = total + rest_in[k].astype(f32)
    rest_s[:, lanes(clip)] = total.astype(bf16)
    spread = go([remote(rest_s.at[:, lanes(clip)], rest_s.at[:, lanes(clip)], back_send.at[k], back_recv.at[k], d) for k, d in enumerate(along)])
    arrived(copies)
    small_s[2] = in_order(head, heads, small_s[1], lambda k: small_head[k])
    total = chip_s[head].astype(f32)
    for k in range(heads - 1):
        total = total + part_head[k].astype(f32)
    mine_s[...] = total.astype(bf16)
    copies = []
    for k, d in enumerate(along):
        copies += go([remote(small_s.at[2], small_clip.at[k], clip_send.at[k, 0], clip_recv.at[k, 0], d)])
        copies += go([remote(mine_s, part_clip.at[k], clip_send.at[k, 1], clip_recv.at[k, 1], d)])
    arrived(copies)
    total = in_order(clip, clips, small_s[2], lambda k: small_clip[k])
    at = [4]

    def rows(width):
        first = at[0]
        at[0] += width // total.shape[1]
        return jnp.concatenate([total[r:r + 1] for r in range(first, at[0])], axis=1)

    def share_of(row):
        width = row.shape[1] // heads
        piece = row[:, :width]
        for h in range(1, heads):
            piece = jnp.where(head == h, row[:, width * h:width * h + width], piece)
        return piece

    gains_a_ref[0:1, :] = total[0:1]
    gains_a_ref[1:3, :] = total[4:6]
    shifts_a_ref[0:1, :] = total[1:2]
    shifts_a_ref[1:5, :] = total[6:10]
    qv_a_ref[0:1, :] = share_of(total[2:3])
    qv_a_ref[1:2, :] = share_of(total[3:4])
    at[0] = 10
    d2, fa, fb = sizes
    gains_b_ref[...] = rows(d2)
    for i in range(3):
        shifts_b_ref[i:i + 1, :] = rows(d2)
    for i in range(2):
        qv_b_ref[i:i + 1, :] = share_of(rows(d2))
    ub_a_ref[...] = share_of(rows(fa))
    ub_b_ref[...] = share_of(rows(fb))
    gtotal_ref[...] = in_order(clip, clips, mine_s[...].astype(f32), lambda k: part_clip[k].astype(f32))
    arrived(spread)
    wide = up_ref.shape[1]
    up_ref[...] = rest_s[:, :wide].astype(f32)
    down_ref[...] = rest_s[:, wide:2 * wide].astype(f32)
    out_ref[...] = rest_s[:, 2 * wide:2 * wide + out_ref.shape[1]].astype(f32)
    for copies in halves:
        arrived(copies)
    for copy in pending:
        copy.wait_send()
    local_half.wait()


def finish(half, early, last, qv, grad, rest, d2, fa, fb, ha, number):
    toks, heads, clips = lax.axis_size("tok"), lax.axis_size("head"), lax.axis_size("clip")
    chips = toks // 2
    across, beside, along = (max(n, 1) for n in (chips - 1, heads - 1, clips - 1))
    block, rows, d1 = grad.shape[1:], rest.shape[0], early.shape[1]
    low, full = lambda *dims: pltpu.VMEM(dims, bf16), lambda *dims: pltpu.VMEM(dims + early.shape, f32)
    sums = [(3, d1), (1, d2), (5, d1), (3, d2), (2, d1 // heads), (2, d2 // heads), (1, fa // heads), (1, fb // heads),
            block, (rows, fa // heads), (rows, fa // heads), (rows, ha)]
    return pl.pallas_call(
        functools.partial(finish_kernel, (d2, fa, fb)),
        in_specs=[ANY] + [INVMEM] * 5,
        out_specs=[ANY] + [INVMEM] * len(sums),
        out_shape=[shape((heads,) + half.shape, half.dtype)] + [shape(dims, f32) for dims in sums],
        scratch_shapes=[
            full(), full(3), full(), full(across), full(beside), full(along),
            low(heads * chips, *block), low(heads * chips, *block), low(heads, *block), low(across, heads, *block),
            low(heads, *block), low(beside, *block), low(*block), low(along, *block),
            low(along, rows, rest.shape[1] // clips), low(*rest.shape),
            dma(1), dma(beside, half.shape[0]), dma(beside, half.shape[0]), dma(heads * chips + 1), dma(heads * chips + 1),
            dma(across, heads + 1), dma(across, heads + 1), dma(beside, 2), dma(beside, 2), dma(along, 2), dma(along, 2),
            dma(along), dma(along), dma(along), dma(along),
        ],
        compiler_params=pltpu.CompilerParams(collective_id=number, has_side_effects=True, vmem_limit_bytes=VMEM_CAP),
        name="finish",
    )(half, early, last, qv, grad, rest)


def reduce_clips(shard):
    clips, clip = lax.axis_size("clip"), lax.axis_index("clip")
    pieces = shard.reshape(clips, -1, shard.shape[-1])
    total = lax.dynamic_index_in_dim(pieces, clip, 0, keepdims=False).astype(f32)
    for k in range(1, clips):
        give = lax.dynamic_index_in_dim(pieces, (clip + k) % clips, 0, keepdims=False)
        total = total + lax.ppermute(give, "clip", [(i, (i + k) % clips) for i in range(clips)]).astype(f32)
    return total.astype(bf16)


def spread_clips(piece):
    clips, clip = lax.axis_size("clip"), lax.axis_index("clip")
    out = jnp.zeros((clips,) + piece.shape, piece.dtype)
    out = lax.dynamic_update_index_in_dim(out, piece, clip, 0)
    for k in range(1, clips):
        got = lax.ppermute(piece, "clip", [(i, (i + k) % clips) for i in range(clips)])
        out = lax.dynamic_update_index_in_dim(out, got, (clip - k + clips) % clips, 0)
    return out.reshape((-1,) + piece.shape[1:])


def from_heads(piece, heads):
    head = lax.axis_index("head")
    out = jnp.zeros((heads,) + piece.shape, piece.dtype)
    out = lax.dynamic_update_index_in_dim(out, piece, head, 0)
    for d in range(1, heads):
        got = lax.ppermute(piece, "head", [(i, (i + d) % heads) for i in range(heads)])
        out = lax.dynamic_update_index_in_dim(out, got, (head - d + heads) % heads, 0)
    return out.reshape((-1,) + piece.shape[1:])


def padded_rows(*rows):
    return jnp.concatenate([jnp.stack(rows), jnp.zeros((-len(rows) % 8, rows[0].shape[0]), f32)])


def local(
    clips_in, resets, assign, w_qkv_a, w_out_a, w_up_a, w_down_a, w_qkv_b, w_out_b, w_skip_b, w_up_b, w_down_b,
    gains_a, gains_b, shifts_a, shifts_b, qv_bias_a, qv_bias_b, up_bias_a, up_bias_b, cotangent,
):
    heads, toks, clips = lax.axis_size("head"), lax.axis_size("tok"), lax.axis_size("clip")
    head = lax.axis_index("head")
    micro, frames = clips_in.shape[1], clips_in.shape[2]
    d1, d2 = clips_in.shape[-1], cotangent.shape[-1]
    share = micro // heads
    first = head * share
    pool_np, pair_np = pool_matrix(frames), pair_matrix(frames)
    pooling, pairing = jnp.asarray(pool_np, bf16), jnp.asarray(pair_np, bf16)
    unpooling, unpairing = jnp.asarray(pool_np.T, bf16), jnp.asarray(pair_np.T, bf16)
    tokens, pooled_tokens = frames * PATCH, frames * POOLED
    own_rows, mem_rows = up16(pooled_tokens), up16(frames // 2 * POOLED)
    rows2 = share * own_rows

    cot = lax.dynamic_slice_in_dim(cotangent[0], first, share, 0).reshape(share, pooled_tokens, d2)
    cot = jnp.pad(cot, ((0, 0), (0, own_rows - pooled_tokens), (0, 0))).reshape(rows2, d2)

    picks, masks = [], []
    row_own = jnp.where(jnp.arange(own_rows) < pooled_tokens, 0.0, NEG)
    row_mem = jnp.arange(mem_rows) < frames // 2 * POOLED
    for m in range(share):
        source = lax.dynamic_index_in_dim(assign[0], first + m, 0, keepdims=False)
        flag = lax.dynamic_index_in_dim(resets[0], first + m, 0, keepdims=False)
        slot = ((head - source // share + heads) % heads) * share + source % share
        picks.append((jnp.arange(heads * share) == slot).astype(f32))
        has = (flag == 0) & (lax.axis_index("clip") > 0)
        masks.append(jnp.concatenate([jnp.tile(row_own, toks), jnp.tile(jnp.where(row_mem & has, 0.0, NEG), toks)]))
    mask = jnp.stack(masks)[:, None, :].astype(f32)
    pick = jnp.stack(picks)

    group = ("head", "tok")
    fa, ha = w_up_a.shape[1], w_out_a.shape[1]
    fb, hb, hs = w_up_b.shape[1], w_out_b.shape[1], w_skip_b.shape[1]
    pack_a = jnp.concatenate([w_up_a, w_down_a, w_qkv_a.reshape(w_qkv_a.shape[0], -1), w_out_a], axis=1)
    pack_q = w_qkv_b.reshape(w_qkv_b.shape[0], -1)
    pack_b = jnp.concatenate([w_up_b, w_down_b, w_out_b, w_skip_b], axis=1)
    vec1 = padded_rows(gains_a[0], shifts_a[0])
    fixed = lambda *dims: pl.BlockSpec(dims, lambda i, first: (0,) * len(dims))
    micro_spec = lambda rows: pl.BlockSpec((1, rows, d1), lambda i, first: (i, 0, 0))
    stream, low1, pooled1, mean1 = pl.pallas_call(
        norm_pool_kernel,
        grid_spec=pltpu.PrefetchScalarGridSpec(
            num_scalar_prefetch=1,
            grid=(share,),
            in_specs=[pl.BlockSpec((1, 1) + clips_in.shape[2:], lambda i, first: (0, first[0] + i, 0, 0, 0)),
                      fixed(*vec1.shape), fixed(*pooling.shape), fixed(*pairing.shape)],
            out_specs=[micro_spec(rows) for rows in (tokens, tokens, own_rows, mem_rows)],
        ),
        out_shape=[shape((share, rows, d1), bf16) for rows in (tokens, tokens, own_rows, mem_rows)],
        compiler_params=pltpu.CompilerParams(vmem_limit_bytes=VMEM_CAP),
        name="norm_pool",
    )(first.astype(jnp.int32)[None], clips_in, vec1, pooling, pairing)
    own1, mem1, all_a = share_pooled(pooled1, mean1, pick, 0, pack_a)
    all_a = all_a.reshape(heads, d1, -1)
    own1, flat = lax.optimization_barrier((
        own1, jnp.concatenate([qv_bias_a.reshape(-1), qv_bias_b.reshape(-1), up_bias_a, up_bias_b])))
    all_q = lax.all_gather(pack_q, group).reshape(heads, d1, -1)
    all_b = lax.all_gather(pack_b, group).reshape(heads, d2, -1)
    flat = from_heads(flat[None], heads)
    qv_a = flat[:, :2 * ha].reshape(heads, 2, ha).transpose(1, 0, 2).reshape(2, d1)
    qv_b = flat[:, 2 * ha:2 * ha + 2 * hb].reshape(heads, 2, hb).transpose(1, 0, 2).reshape(2, d2)
    ub_a = flat[:, 2 * (ha + hb):2 * (ha + hb) + fa].reshape(heads, 1, fa)
    ub_b = flat[:, 2 * (ha + hb) + fa:].reshape(1, heads * fb)

    def lanes(pack, low, width):
        return jnp.concatenate([pack[h, :, low:low + width] for h in range(heads)], axis=1)

    up_spec, down_spec = (pl.BlockSpec((heads, d1, fa), lambda i, n=n: (0, 0, n)) for n in range(2))
    qkv_a = jnp.concatenate([lanes(all_a, 2 * fa + i * ha, ha) for i in range(3)], axis=1)[None]
    out_a = lanes(all_a, 2 * fa + 3 * ha, ha)
    qkv_b = all_q
    if hb != 384:
        parts = [lanes(all_q, i * hb, hb).reshape(d1, -1, 384).transpose(1, 0, 2) for i in range(3)]
        qkv_b = jnp.concatenate(parts, axis=2)
    skip_b = lanes(all_b, 2 * fb + hb, hs)

    comb1, lse1 = attend(low1, own1, mem1, qkv_a, qv_a, mask, d1)
    after1, middle, pooled3, mean3 = call(
        first_mlp_kernel, share,
        [(stream, 0), (comb1, 0), (out_a, None), (all_a, up_spec), (all_a, down_spec), (ub_a, None),
         (padded_rows(shifts_a[1], gains_a[1], shifts_a[2], shifts_a[3], gains_a[2], shifts_a[4]), None),
         (pooling, None), (pairing, None)],
        [(shape((share, tokens, d1), f32), 0), (shape((share, tokens, d1), f32), 0),
         (shape((share, own_rows, d1), bf16), 0), (shape((share, mem_rows, d1), bf16), 0)],
        name="first_mlp",
    )

    own2, mem2 = share_pooled(pooled3, mean3, pick, 1)
    comb2, lse2 = attend(pooled3, own2, mem2, qkv_b, qv_b, mask, d2)
    chunk = 768
    per_head = fb // chunk
    steps = heads * per_head
    out_spec = pl.BlockSpec((heads, d2, hb), lambda j: (0, 0, 2 * fb // hb))
    rows_spec = pl.BlockSpec((1, d2, chunk), lambda j: (j // per_head, 0, j % per_head))
    mixed, dcomb2, dskip, g_mlp_b, g_out_b, g_skip_b, g_ub_b, rows_b = call(
        second_mlp_kernel, steps,
        [(comb2.reshape(rows2, d2), None), (pooled3.reshape(rows2, d1), None), (cot, None), (all_b, out_spec), (skip_b, None),
         (all_b, rows_spec),
         (all_b, pl.BlockSpec((1, d2, chunk), lambda j: (j // per_head, 0, per_head + j % per_head))),
         (ub_b, pl.BlockSpec((1, chunk), lambda j: (0, j))),
         (padded_rows(shifts_b[0], gains_b, shifts_b[1], shifts_b[2]), None)],
        [(shape((rows2, d2), bf16), None), (shape((rows2, d2), bf16), None), (shape((rows2, d1), f32), None),
         (shape((heads, toks, 2, d2 // toks, fb), bf16),
          pl.BlockSpec((1, toks, 2, d2 // toks, chunk), lambda j: (j // per_head, 0, 0, 0, j % per_head))),
         (shape((heads, toks, d2 // toks // 2, 2 * hb), bf16), None), (shape((heads, toks, d2 // toks // 2, 2 * hs), bf16), None),
         (shape((1, heads * fb), f32), pl.BlockSpec((1, chunk), lambda j: (0, j))), (shape((8, d2), f32), None)],
        [((rows2, d2), f32), ((rows2, d2), bf16), ((d2, rows2), bf16), ((d2, rows2), bf16), ((rows2, d2), f32), ((rows2, d2), f32)],
        name="second_mlp",
    )

    def by_owner(grad):
        return grad.reshape((heads * toks, -1) + grad.shape[2:])

    def scatter(grad):
        return lax.psum_scatter(grad, group, scatter_dimension=0, tiled=False)

    sum_mlp_b = scatter(g_mlp_b.reshape((heads * toks,) + g_mlp_b.shape[2:]))
    dcomb2 = dcomb2.reshape(share, own_rows, d2)
    dq2, dpool2, g_qkv_b, rows_qv_b = attend_back(pooled3, dcomb2, own2, mem2, qkv_b, qv_b, mask, lse2, heads)
    own_back2, mem_back2, mixed_all = give_back(dpool2, pick, own_rows, 2, mixed.reshape(share, own_rows, d2))

    merge = lambda grad: grad.reshape((heads * toks,) + grad.shape[2:])
    sum_rest_b = scatter(jnp.concatenate([by_owner(g_qkv_b), merge(g_out_b), merge(g_skip_b)], axis=2))

    res1, dcomb1, g_mlp_a, g_ub_a, rows_a = call(
        first_back_kernel, share,
        [(middle, 0), (after1, 0), (comb1, 0), (dskip.reshape(share, own_rows, d1), 0), (dq2, 0), (own_back2, 0), (mem_back2, 0),
         (out_a, None), (all_a, up_spec), (all_a, down_spec), (ub_a, None),
         (padded_rows(gains_a[1], shifts_a[2], gains_a[2]), None), (unpooling, None), (unpairing, None)],
        [(shape((share, tokens, d1), f32), 0), (shape((share, tokens, d1), bf16), 0),
         (shape((heads, d1, -(-(2 * fa + ha) // (128 * clips)) * 128 * clips), bf16), None),
         (shape((heads, 1, fa), f32), None), (shape((8, d1), f32), None)],
        [((heads, d1, fa), f32), ((heads, d1, fa), f32), ((d1, d1), f32)],
        name="first_back",
    )
    rest_a = by_owner(g_mlp_a)
    dcomb1, sum_mlp_b, rest_a = lax.optimization_barrier((dcomb1, sum_mlp_b, rest_a))
    sum_rest_a = scatter(rest_a)
    sum_mlp_b = reduce_clips(sum_mlp_b)
    dx1, dpool1, g_qkv_a, rows_qv_a = attend_back(low1, dcomb1, own1, mem1, qkv_a, qv_a, mask, lse1, heads)
    dpool1, sum_mlp_b, sum_rest_b = lax.optimization_barrier((dpool1, sum_mlp_b, sum_rest_b))
    mlp_b = spread_clips(sum_mlp_b)
    sum_rest_b = reduce_clips(sum_rest_b)
    own_back1, mem_back1 = give_back(dpool1, pick, own_rows, 3)
    stream_grad, rows_last = call(
        last_back_kernel, share,
        [(stream, 0), (res1, 0), (dx1, 0), (own_back1, 0), (mem_back1, 0), (padded_rows(gains_a[0]), None),
         (unpooling, None), (unpairing, None)],
        [(shape((share, frames, PATCH, d1), bf16), 0), (shape((8, d1), f32), None)],
        name="last_back",
    )

    zero = jnp.zeros((4, d1), f32)
    early = [
        zero, rows_a[3:4], rows_a[0:1], rows_a[5:6], rows_a[4:5], rows_a[2:3], rows_a[1:2],
        rows_b[3:4], rows_b[:3], rows_qv_b[:2], g_ub_a, g_ub_b,
    ]
    early = jnp.concatenate([piece.reshape(-1, d1) for piece in early])
    early = jnp.pad(early, ((0, -early.shape[0] % 8), (0, 0)))
    rows_last, sum_rest_b, early = lax.optimization_barrier((rows_last, sum_rest_b, early))
    rest_b = spread_clips(sum_rest_b).astype(f32)
    mlp_b = mlp_b.reshape((2, -1, mlp_b.shape[-1])).astype(f32)
    stream_all, *sums = finish(
        stream_grad, early, rows_last, rows_qv_a, by_owner(g_qkv_a), sum_rest_a, d2, heads * fa, heads * fb, ha, 4)
    out_lanes = rest_b[:, 3 * hb:5 * hb]
    skip_lanes = rest_b[:, 5 * hb:]
    mixed_all = mixed_all.reshape(micro, own_rows, d2)[:, :pooled_tokens]
    return (
        mixed_all.reshape(cotangent.shape),
        stream_all.astype(f32).reshape(clips_in.shape),
        sums[8].reshape(w_qkv_a.shape),
        sums[11],
        sums[9],
        sums[10],
        rest_b[:, :3 * hb].reshape(w_qkv_b.shape),
        jnp.concatenate([out_lanes[:, :hb], out_lanes[:, hb:]], axis=0),
        jnp.concatenate([skip_lanes[:, :hs], skip_lanes[:, hs:]], axis=0),
        mlp_b[0],
        mlp_b[1],
        sums[0], sums[1][0], sums[2], sums[3], sums[4], sums[5], sums[6][0], sums[7][0],
    )


def solution(mesh):
    in_specs = (
        P("clip", None, "tok", None, None),
        P("clip", None),
        P("clip", None),
        P("tok", None, "head"),
        P("tok", "head"),
        P("tok", "head"),
        P("tok", "head"),
        P("tok", None, "head"),
        P("tok", "head"),
        P("tok", "head"),
        P("tok", "head"),
        P("tok", "head"),
        P(),
        P(),
        P(),
        P(),
        P(None, "head"),
        P(None, "head"),
        P("head"),
        P("head"),
        P("clip", None, "tok", None, None),
    )
    out_specs = (
        P("clip", None, "tok", None, None),
        P("clip", None, "tok", None, None),
        P("tok", None, "head"),
        P("tok", "head"),
        P("tok", "head"),
        P("tok", "head"),
        P("tok", None, "head"),
        P("tok", "head"),
        P("tok", "head"),
        P("tok", "head"),
        P("tok", "head"),
        P(),
        P(),
        P(),
        P(),
        P(None, "head"),
        P(None, "head"),
        P("head"),
        P("head"),
    )
    return jax.shard_map(local, mesh=mesh, in_specs=in_specs, out_specs=out_specs, check_vma=False)
```

```python
import functools
import math

import jax
import jax.numpy as jnp
import numpy as np
from jax import lax
from jax.experimental import pallas as pl
from jax.experimental.pallas import tpu as pltpu
from jax.sharding import PartitionSpec as P

GRID = 14
PATCH = GRID * GRID
POOLED = PATCH // 4
HD = 96
NEG = -1e30
VMEM_CAP = 62 * 2**20
eps = 1e-06
f32, bf16 = jnp.float32, jnp.bfloat16
NN, NT, TN = ((1,), (0,)), ((1,), (1,)), ((0,), (0,))


def up16(n):
    return -(-n // 16) * 16


def pool_matrix(frames):
    rows, cols = up16(frames * POOLED), frames * PATCH
    out = np.zeros((rows, cols), np.float32)
    half = GRID // 2
    for f in range(frames):
        for p in range(PATCH):
            r, c = divmod(p, GRID)
            out[f * POOLED + (r // 2) * half + c // 2, f * PATCH + p] = 0.25
    return out


def pair_matrix(frames):
    rows, cols = up16(frames // 2 * POOLED), up16(frames * POOLED)
    out = np.zeros((rows, cols), np.float32)
    for j in range(frames // 2):
        for p in range(POOLED):
            out[j * POOLED + p, 2 * j * POOLED + p] = 0.5
            out[j * POOLED + p, (2 * j + 1) * POOLED + p] = 0.5
    return out


def dot(a, b, dims=NN):
    return lax.dot_general(a, b, (dims, ((), ())), preferred_element_type=f32)


def exact_dot(matrix, tensor):
    high = tensor.astype(bf16)
    low = (tensor - high.astype(f32)).astype(bf16)
    return dot(matrix, high) + dot(matrix, low)


def norm(x):
    average = jnp.mean(x, axis=-1, keepdims=True)
    centred = x - average
    inverse = lax.rsqrt(jnp.mean(centred * centred, axis=-1, keepdims=True) + eps)
    return centred * inverse, inverse


def norm_back(unit, inverse, gain, gradient):
    scaled = gradient * gain
    return inverse * (
        scaled
        - jnp.mean(scaled, axis=-1, keepdims=True)
        - unit * jnp.mean(scaled * unit, axis=-1, keepdims=True)
    )


GELU_A, GELU_B = math.sqrt(2.0 / math.pi), 0.044715


def gelu(x):
    t = jnp.tanh(GELU_A * (x + GELU_B * (x * x * x)))
    return 0.5 * x * (1.0 + t)


def gelu_both(x):
    square = x * x
    t = jnp.tanh(GELU_A * x * (1.0 + GELU_B * square))
    value = 0.5 * x * (1.0 + t)
    slope = 0.5 * (1.0 + t) + 0.5 * x * (1.0 - t * t) * (GELU_A * (1.0 + 3.0 * GELU_B * square))
    return value, slope


def sum_rows(x):
    return jnp.sum(x, axis=0, keepdims=True)


def add_rows(ref, rows):
    step = pl.program_id(0)

    @pl.when(step == 0)
    def _():
        ref[...] = jnp.zeros_like(ref)

    for i, row in enumerate(rows):
        ref[i:i + 1, :] += row


def transposed(x):
    return x.astype(f32).T.astype(bf16)


def window(head):
    low = HD * head
    return low // 128 * 128, -(-(low + HD) // 128) * 128


def head_mask(head):
    start, stop = window(head)
    lane = lax.broadcasted_iota(jnp.int32, (1, stop - start), 1) + start
    return (lane >= HD * head) & (lane < HD * head + HD)


def key_rows(own_ref, mem_ref):
    row = 0
    for ref in (own_ref, mem_ref):
        for t in range(ref.shape[0]):
            yield ref, t, slice(row, row + ref.shape[2])
            row += ref.shape[2]


def key_mask(own_ref, mem_ref, valid, has):
    parts = []
    for ref, rows, there in ((own_ref, valid[0], None), (mem_ref, valid[1], has)):
        block = ref.shape[2]
        lane = lax.rem(lax.broadcasted_iota(jnp.int32, (1, ref.shape[0] * block), 1), block)
        limit = rows if there is None else jnp.where(there > 0, rows, 0)
        parts.append(jnp.where(lane < limit, 0.0, NEG))
    return jnp.concatenate(parts, axis=1)


def assemble(w_ref, w_s):
    wide = w_ref.shape[2] // 4
    for part in range(3):
        pieces = [w_ref[h, :, wide * part:wide * part + wide].astype(f32) for h in range(w_ref.shape[0])]
        w_s[0, :, 384 * part:384 * part + 384] = jnp.concatenate(pieces, axis=1).astype(bf16)


def assemble_out(w_ref, out_s):
    wide = w_ref.shape[2] // 4
    pieces = [w_ref[h, :, 3 * wide:].astype(f32) for h in range(w_ref.shape[0])]
    out_s[...] = jnp.concatenate(pieces, axis=1).astype(bf16)


def project_keys(own_ref, mem_ref, w_ref, bias_ref, x_s, k_s, v_s):
    for ref, t, rows in key_rows(own_ref, mem_ref):
        x_s[rows, :] = ref[t, 0]
    width = k_s.shape[1]
    for low in range(0, width, 384):
        k_s[:, low:low + 384] = dot(x_s[...], w_ref[low // 384, :, 384:768]).astype(bf16)
    for low in range(0, width, 384):
        value = dot(x_s[...], w_ref[low // 384, :, 768:])
        v_s[:, low:low + 384] = (value + bias_ref[1:2, low:low + 384]).astype(bf16)


def project_queries(x_ref, w_ref, bias_ref, q_s):
    width = q_s.shape[1]
    for low in range(0, width, 384):
        value = dot(x_ref[0], w_ref[low // 384, :, :384])
        q_s[:, low:low + 384] = (value + bias_ref[0:1, low:low + 384]).astype(bf16)


def norm_pool_kernel(clips_ref, vec_ref, pool_ref, pair_ref, x_ref, low_ref, pooled_ref, mean_ref):
    x = jnp.concatenate([clips_ref[0, f].astype(f32) for f in range(clips_ref.shape[1])], axis=0)
    x_ref[0] = x.astype(bf16)
    unit, _ = norm(x)
    normed = unit * vec_ref[0:1, :] + vec_ref[1:2, :]
    low_ref[0] = normed.astype(bf16)
    pooled = exact_dot(pool_ref[...], normed)
    pooled_ref[0] = pooled.astype(bf16)
    mean_ref[0] = exact_dot(pair_ref[...], pooled).astype(bf16)


def write_shares(gw_ref, h, gw_s):
    wide = gw_ref.shape[2] // 3
    for part in range(3):
        low = wide * h
        columns = gw_s[low // 384, :, 384 * part:384 * part + 384][:, low % 384:low % 384 + wide]
        gw_ref[h, :, wide * part:wide * part + wide] = columns.astype(bf16)


def attend_kernel(chunk, valid, x_ref, own_ref, mem_ref, w_ref, qv_ref, has_ref, out_ref, lse_ref, w_s, x_s, q_s, k_s, v_s, s_s, p_s):
    nq, width = q_s.shape
    columns = key_mask(own_ref, mem_ref, valid, has_ref[pl.program_id(0)])
    if width == 384:
        @pl.when(pl.program_id(0) == 0)
        def _():
            assemble(w_ref, w_s)
        w_ref = w_s
    project_queries(x_ref, w_ref, qv_ref, q_s)
    project_keys(own_ref, mem_ref, w_ref, qv_ref, x_s, k_s, v_s)
    factor = HD**-0.5 * math.log2(math.e)
    lanes = lax.broadcasted_iota(jnp.int32, (chunk, 128), 1)
    for tile in range(width // 384):
        group = slice(384 * tile, 384 * tile + 384)
        base = q_s[:, group].astype(f32)
        parts = [base[:, :128], base[:, 128:256], base[:, 256:384]]
        for head in range(4 * tile, 4 * tile + 4):
            start, stop = window(head)
            mask = head_mask(head)
            query = jnp.where(mask, q_s[:, start:stop], jnp.zeros((), bf16))
            s_s[...] = dot(query, k_s[:, start:stop], NT)

            def body(i, carry, head=head):
                rows = pl.ds(pl.multiple_of(i * chunk, chunk), chunk)
                score = s_s[rows, :] * factor + columns
                top = jnp.max(score, axis=1, keepdims=True)
                power = jnp.exp2(score - top)
                total = jnp.sum(power, axis=1, keepdims=True)
                p_s[rows, :] = (power * (1.0 / total)).astype(bf16)
                lse_ref[0, rows, :] = jnp.where(lanes == head, top + jnp.log2(total), lse_ref[0, rows, :])
                return carry

            lax.fori_loop(0, nq // chunk, body, 0, unroll=nq // chunk)
            out = jnp.where(mask, dot(p_s[...], v_s[:, start:stop]), 0.0)
            for w in range((stop - start) // 128):
                k = start // 128 - 3 * tile + w
                parts[k] = parts[k] + out[:, 128 * w:128 * w + 128]
        out_ref[0, :, group] = jnp.concatenate(parts, axis=1).astype(bf16)


def attend_back_kernel(
    chunk, valid, x_ref, g_ref, own_ref, mem_ref, w_ref, qv_ref, has_ref, lse_ref,
    dx_ref, dpool_ref, gw_ref, row_ref,
    w_s, x_s, q_s, k_s, v_s, s_s, dp_s, p_s, ds_s, dk_s, dv_s, dq_s, gw_s,
):
    nq, width = q_s.shape
    step = pl.program_id(0)
    columns = key_mask(own_ref, mem_ref, valid, has_ref[step])
    if width == 384:
        @pl.when(step == 0)
        def _():
            assemble(w_ref, w_s)
        w_ref = w_s
    project_queries(x_ref, w_ref, qv_ref, q_s)
    project_keys(own_ref, mem_ref, w_ref, qv_ref, x_s, k_s, v_s)
    scaling = HD**-0.5
    factor = scaling * math.log2(math.e)
    lanes = lax.broadcasted_iota(jnp.int32, (chunk, 128), 1)

    @pl.when(step == 0)
    def _():
        gw_s[...] = jnp.zeros_like(gw_s)

    xt = transposed(x_ref[0])
    keys_t = transposed(x_s[...])
    dx = None
    dpool = None
    row_q, row_v = [], []
    for tile in range(width // 384):
        group = slice(384 * tile, 384 * tile + 384)
        qt = transposed(q_s[:, group])
        gt = transposed(g_ref[0, :, group])
        parts = [None] * 3
        for head in range(4 * tile, 4 * tile + 4):
            start, stop = window(head)
            mask = head_mask(head)
            query = jnp.where(mask, q_s[:, start:stop], jnp.zeros((), bf16))
            grad = jnp.where(mask, g_ref[0, :, start:stop], jnp.zeros((), bf16))
            s_s[...] = dot(query, k_s[:, start:stop], NT)
            dp_s[...] = dot(grad, v_s[:, start:stop], NT)

            def body(i, carry, head=head):
                rows = pl.ds(pl.multiple_of(i * chunk, chunk), chunk)
                lse = jnp.sum(jnp.where(lanes == head, lse_ref[0, rows, :], 0.0), axis=1, keepdims=True)
                p = jnp.exp2(s_s[rows, :] * factor + columns - lse)
                dp = dp_s[rows, :]
                inner = jnp.sum(p * dp, axis=1, keepdims=True)
                p_s[rows, :] = p.astype(bf16)
                ds_s[rows, :] = (p * (dp - inner)).astype(bf16)
                return carry

            lax.fori_loop(0, nq // chunk, body, 0, unroll=nq // chunk)
            r = slice(HD * (head - 4 * tile), HD * (head - 4 * tile) + HD)
            dv_s[r, :] = dot(gt[r], p_s[...])
            dk_s[r, :] = dot(qt[r], ds_s[...]) * scaling
            dq = jnp.where(mask, dot(ds_s[...], k_s[:, start:stop]) * scaling, 0.0)
            for w in range((stop - start) // 128):
                k = start // 128 - 3 * tile + w
                part = dq[:, 128 * w:128 * w + 128]
                parts[k] = part if parts[k] is None else parts[k] + part
        total = jnp.concatenate(parts, axis=1) + g_ref[0, :, group].astype(f32)
        row_q.append(sum_rows(total))
        low = total.astype(bf16)
        gw_s[tile, :, :384] += dot(xt, low)
        add = dot(low, w_ref[tile, :, :384], NT)
        dx = add if dx is None else dx + add
        for part, src in ((1, dk_s), (2, dv_s)):
            grad = src[...].T
            if part == 2:
                row_v.append(sum_rows(grad))
            low = grad.astype(bf16)
            here = slice(384 * part, 384 * part + 384)
            gw_s[tile, :, here] += dot(keys_t, low)
            add = dot(low, w_ref[tile, :, here], NT)
            dpool = add if dpool is None else dpool + add
    dx_ref[0] = dx
    row = 0
    own, mem = own_ref.shape[2], mem_ref.shape[2]
    toks = own_ref.shape[0]
    for t in range(toks):
        dpool_ref[t, 0, :own, :] = dpool[t * own:(t + 1) * own].astype(bf16)
        dpool_ref[t, 0, own:, :] = dpool[toks * own + t * mem:toks * own + (t + 1) * mem].astype(bf16)
    add_rows(row_ref, [jnp.concatenate(row_q, axis=1), jnp.concatenate(row_v, axis=1)])

    @pl.when(step == pl.num_programs(0) - 1)
    def _():
        for h in range(gw_ref.shape[0]):
            write_shares(gw_ref, h, gw_s)


def first_mlp_kernel(x_ref, comb_ref, out_ref, up_ref, down_ref, ub_ref, vec_ref, pool_ref, pair_ref,
                     after_ref, middle_ref, pooled_ref, mean_ref, out_s):
    @pl.when(pl.program_id(0) == 0)
    def _():
        assemble_out(out_ref, out_s)

    after = x_ref[0].astype(f32) + dot(comb_ref[0], out_s[...], NT) + vec_ref[0:1, :]
    after_ref[0] = after
    unit, _ = norm(after)
    low = (unit * vec_ref[1:2, :] + vec_ref[2:3, :]).astype(bf16)
    total = after + vec_ref[3:4, :]
    for h in range(up_ref.shape[0]):
        hidden = gelu(dot(low, up_ref[h]) + ub_ref[h]).astype(bf16)
        total = total + dot(hidden, down_ref[h], NT)
    middle_ref[0] = total
    unit, _ = norm(total)
    pooled = exact_dot(pool_ref[...], unit * vec_ref[4:5, :] + vec_ref[5:6, :])
    pooled_ref[0] = pooled.astype(bf16)
    mean_ref[0] = exact_dot(pair_ref[...], pooled).astype(bf16)


def second_mlp_kernel(
    comb_ref, pooled_ref, cot_ref, out_ref, skip_ref, up_ref, down_ref, ub_ref, vec_ref,
    mixed_ref, dcomb_ref, dskip_ref, gmlp_ref, gout_ref, gskip_ref, gub_ref, row_ref,
    after_s, low_s, lowt_s, cott_s, sum_s, dlow_s,
):
    step = pl.program_id(0)

    @pl.when(step == 0)
    def _():
        after = dot(pooled_ref[...], skip_ref[...], NT) + vec_ref[0:1, :]
        wide = out_ref.shape[2]
        for h in range(out_ref.shape[0]):
            after = after + dot(comb_ref[:, wide * h:wide * h + wide], out_ref[h], NT)
        after_s[...] = after
        unit, _ = norm(after)
        low = (unit * vec_ref[1:2, :] + vec_ref[2:3, :]).astype(bf16)
        low_s[...] = low
        lowt_s[...] = transposed(low)
        cott_s[...] = transposed(cot_ref[...])
        sum_s[...] = after + vec_ref[3:4, :]
        dlow_s[...] = jnp.zeros_like(dlow_s)

    pre = dot(low_s[...], up_ref[0]) + ub_ref[...]
    hidden, slope = gelu_both(pre)
    hidden = hidden.astype(bf16)
    dpre = dot(cot_ref[...], down_ref[0]) * slope
    gub_ref[...] = sum_rows(dpre)
    dpre = dpre.astype(bf16)
    sum_s[...] += dot(hidden, down_ref[0], NT)
    dlow_s[...] += dot(dpre, up_ref[0], NT)
    for n, grad in enumerate((dot(lowt_s[...], dpre), dot(cott_s[...], hidden))):
        rows = gmlp_ref.shape[3]
        for t in range(gmlp_ref.shape[1]):
            gmlp_ref[0, t, n] = grad[t * rows:(t + 1) * rows].astype(bf16)

    @pl.when(step == pl.num_programs(0) - 1)
    def _():
        mixed_ref[...] = sum_s[...].astype(bf16)
        unit, inverse = norm(after_s[...])
        dlow = dlow_s[...]
        cot = cot_ref[...].astype(f32)
        res = norm_back(unit, inverse, vec_ref[1:2, :], dlow) + cot
        row_ref[...] = jnp.zeros_like(row_ref)
        for i, row in enumerate((res, dlow, cot, dlow * unit)):
            row_ref[i:i + 1, :] = sum_rows(row)
        res = res.astype(bf16)
        dskip_ref[...] = dot(res, skip_ref[...])
        rest = transposed(res)
        wide = out_ref.shape[2]
        for h in range(out_ref.shape[0]):
            here = slice(wide * h, wide * h + wide)
            dcomb_ref[:, here] = dot(res, out_ref[h]).astype(bf16)
            grad = dot(rest, comb_ref[:, here])
            half = gout_ref.shape[2]
            for n in range(2 * gout_ref.shape[1]):
                gout_ref[h, n // 2, :, wide * (n % 2):wide * (n % 2) + wide] = grad[half * n:half * n + half].astype(bf16)
        grad = dot(rest, pooled_ref[...])
        wide = gskip_ref.shape[3] // 2
        for h in range(gskip_ref.shape[0]):
            for t in range(gskip_ref.shape[1]):
                low, high = (grad[half * n:half * n + half, wide * h:wide * h + wide] for n in (2 * t, 2 * t + 1))
                gskip_ref[h, t] = jnp.concatenate([low, high], axis=1).astype(bf16)


def first_back_kernel(
    middle_ref, after_ref, comb_ref, dskip_ref, dq_ref, own_ref, mem_ref, out_ref, up_ref, down_ref, ub_ref, vec_ref,
    unpool_ref, unpair_ref,
    res_ref, dcomb_ref, gmlp_ref, gub_ref, row_ref,
    gup_s, gdown_s, gout_s, out_s,
):
    step = pl.program_id(0)

    @pl.when(step == 0)
    def _():
        gup_s[...] = jnp.zeros_like(gup_s)
        gdown_s[...] = jnp.zeros_like(gdown_s)
        gout_s[...] = jnp.zeros_like(gout_s)
        gub_ref[...] = jnp.zeros_like(gub_ref)
        assemble_out(out_ref, out_s)

    dpool = dskip_ref[0] + dq_ref[0] + own_ref[0] + exact_dot(unpair_ref[...], mem_ref[0])
    dnorm = exact_dot(unpool_ref[...], dpool)
    unit, inverse = norm(middle_ref[0])
    grad = norm_back(unit, inverse, vec_ref[2:3, :], dnorm)
    rows = [sum_rows(dnorm * unit), sum_rows(dnorm), sum_rows(grad)]
    low = grad.astype(bf16)
    lowt = transposed(low)
    unit, inverse = norm(after_ref[0])
    normed = (unit * vec_ref[0:1, :] + vec_ref[1:2, :]).astype(bf16)
    normedt = transposed(normed)
    dnormed = None
    for h in range(up_ref.shape[0]):
        hidden, slope = gelu_both(dot(normed, up_ref[h]) + ub_ref[h])
        hidden = hidden.astype(bf16)
        dpre = dot(low, down_ref[h]) * slope
        gub_ref[h] += sum_rows(dpre)
        dpre = dpre.astype(bf16)
        gdown_s[h] += dot(lowt, hidden)
        gup_s[h] += dot(normedt, dpre)
        add = dot(dpre, up_ref[h], NT)
        dnormed = add if dnormed is None else dnormed + add
    res = norm_back(unit, inverse, vec_ref[0:1, :], dnormed) + grad
    rows += [sum_rows(dnormed * unit), sum_rows(dnormed), sum_rows(res)]
    res_ref[0] = res
    res = res.astype(bf16)
    dcomb_ref[0] = dot(res, out_s[...]).astype(bf16)
    gout_s[...] += dot(transposed(res), comb_ref[0])
    add_rows(row_ref, rows)

    @pl.when(step == pl.num_programs(0) - 1)
    def _():
        fa, ha = gup_s.shape[2], gout_s.shape[1] // gmlp_ref.shape[0]
        for h in range(gmlp_ref.shape[0]):
            gmlp_ref[h, :, :fa] = gup_s[h].astype(bf16)
            gmlp_ref[h, :, fa:2 * fa] = gdown_s[h].astype(bf16)
            rest = gmlp_ref.shape[2] - 2 * fa - ha
            gout = jnp.concatenate([gout_s[:, ha * h:ha * h + ha], jnp.zeros((gout_s.shape[0], rest), f32)], axis=1)
            gmlp_ref[h, :, 2 * fa:] = gout.astype(bf16)


def last_back_kernel(x_ref, res_ref, dx_ref, own_ref, mem_ref, vec_ref, unpool_ref, unpair_ref, grad_ref, row_ref):
    dpool = own_ref[0] + exact_dot(unpair_ref[...], mem_ref[0])
    dnorm = dx_ref[0] + exact_dot(unpool_ref[...], dpool)
    unit, inverse = norm(x_ref[0].astype(f32))
    grad = norm_back(unit, inverse, vec_ref[0:1, :], dnorm) + res_ref[0]
    for f in range(grad_ref.shape[1]):
        grad_ref[0, f] = grad[PATCH * f:PATCH * f + PATCH].astype(bf16)
    add_rows(row_ref, [sum_rows(dnorm * unit), sum_rows(dnorm)])


def whole(array):
    return pl.BlockSpec(array.shape, lambda i: (0,) * array.ndim)


def by_micro(array, axis=0):
    block = array.shape[:axis] + (1,) + array.shape[axis + 1:]
    return pl.BlockSpec(block, lambda i: (0,) * axis + (i,) + (0,) * (array.ndim - axis - 1))


def shape(dims, dtype):
    return jax.ShapeDtypeStruct(dims, dtype)


def about(us):
    return pl.CostEstimate(flops=int(us * 1e9), bytes_accessed=0, transcendentals=0)


def call(kernel, steps, args, outs, scratch=(), name=None, us=10):
    def spec(array, how):
        if how is None:
            return whole(array)
        return by_micro(array, how) if isinstance(how, int) else how

    return pl.pallas_call(
        kernel,
        grid=(steps,),
        in_specs=[spec(a, how) for a, how in args],
        out_specs=[spec(a, how) for a, how in outs],
        out_shape=[a for a, _ in outs],
        scratch_shapes=[pltpu.VMEM(dims, dtype) for dims, dtype in scratch],
        compiler_params=pltpu.CompilerParams(vmem_limit_bytes=VMEM_CAP),
        cost_estimate=about(us),
        name=name,
    )(*[a for a, _ in args])


def chunk_of(nq):
    return 112 if nq % 112 == 0 else 16


def attend(x, own, mem, w, qv, has, valid, width):
    batches, nq, d = x.shape
    keys = own.shape[0] * own.shape[2] + mem.shape[0] * mem.shape[2]
    return call(
        functools.partial(attend_kernel, chunk_of(nq), valid), batches,
        [(x, 0), (own, 1), (mem, 1), w, (qv, None), (has, pl.BlockSpec(memory_space=pltpu.SMEM))],
        [(shape((batches, nq, width), bf16), 0), (shape((batches, nq, 128), f32), 0)],
        [((1, d, 1152 if width == 384 else 128), bf16),
         ((keys, d), bf16), ((nq, width), bf16), ((keys, width), bf16), ((keys, width), bf16), ((nq, keys), f32), ((nq, keys), bf16)],
        name="attend", us=20,
    )


def attend_back(x, grad, own, mem, w, qv, has, valid, lse, heads):
    batches, nq, d = x.shape
    width = grad.shape[2]
    keys = own.shape[0] * own.shape[2] + mem.shape[0] * mem.shape[2]
    both = (own.shape[0], batches, own.shape[2] + mem.shape[2], d)
    groups = (width // 384, d, 1152)
    return call(
        functools.partial(attend_back_kernel, chunk_of(nq), valid), batches,
        [(x, 0), (grad, 0), (own, 1), (mem, 1), w, (qv, None), (has, pl.BlockSpec(memory_space=pltpu.SMEM)), (lse, 0)],
        [(shape((batches, nq, d), f32), 0), (shape(both, bf16), 1), (shape((heads, d, 3 * width // heads), bf16), None), (shape((8, width), f32), None)],
        [((1, d, 1152 if width == 384 else 128), bf16),
         ((keys, d), bf16), ((nq, width), bf16), ((keys, width), bf16), ((keys, width), bf16),
         ((nq, keys), f32), ((nq, keys), f32), ((nq, keys), bf16), ((nq, keys), bf16),
         ((384, keys), f32), ((384, keys), f32), ((8, 128), f32), (groups, f32)],
        name="attend_back", us=36,
    )


MESH = pl.DeviceIdType.MESH


def places():
    tok, toks = lax.axis_index("tok"), lax.axis_size("tok")
    return lax.axis_index("clip"), lax.axis_index("head"), tok // 2, tok % 2, toks // 2


def greet(copies_to_me, i_copy_to):
    barrier = pltpu.get_barrier_semaphore()
    for device, condition in copies_to_me:
        if condition is None:
            pl.semaphore_signal(barrier, inc=1, device_id=device, device_id_type=MESH)
        else:
            @pl.when(condition)
            def _():
                pl.semaphore_signal(barrier, inc=1, device_id=device, device_id_type=MESH)
    count = 0
    for _, condition in i_copy_to:
        count = count + (1 if condition is None else jnp.where(condition, 1, 0))
    pl.semaphore_wait(barrier, count)


def remote(src, dst, send, recv, device):
    return pltpu.make_async_remote_copy(
        src_ref=src, dst_ref=dst, send_sem=send, recv_sem=recv, device_id=device, device_id_type=MESH
    )


def rem(a, n):
    return lax.rem(a + n, n)


def share_kernel(gather, *refs):
    if gather:
        pooled_ref, mean_ref, pick_ref, w_ref, *refs = refs
        biases, (own_ref, mem_ref, all_ref, *refs) = refs[:4], refs[4:]
        (qv_a_ref, qv_b_ref, ub_a_ref, ub_b_ref), refs = refs[:4], refs[4:]
    else:
        pooled_ref, mean_ref, pick_ref, own_ref, mem_ref, *refs = refs
    (got_s, pick_s, local_sem, own_send, own_recv, mem_send, mem_recv, pass_send, pass_recv, clip_send, clip_recv, *refs) = refs
    clip, head, chip, core, chips = places()
    clips, heads = lax.axis_size("clip"), lax.axis_size("head")
    share = pooled_ref.shape[0]
    here = 2 * chip + core
    partner = {"tok": 2 * chip + 1 - core}
    across = [{"tok": 2 * rem(chip + k, chips) + core} for k in range(1, chips)]
    beside = [{"head": rem(head + d, heads)} for d in range(1, heads)]
    heads_of = lambda by, sign: [{"clip": clip + by, "head": rem(head + sign * d, heads)} for d in range(heads)]
    last, begun = clip < clips - 1, clip > 0
    near = [(d, None) for d in [partner] + across + (beside if gather else [])]
    greet(near + [(d, begun) for d in heads_of(-1, -1)], near + [(d, last) for d in heads_of(1, 1)])

    def spread(src, out, send, recv):
        copies = [remote(src, out.at[here], send.at[0], recv.at[0], partner)]
        copies += [remote(src, out.at[here], send.at[k + 1], recv.at[k + 1], across[k]) for k in range(chips - 1)]
        return copies

    def passed(out, k, row):
        block = 2 * rem(chip - k, chips) + core
        return remote(out.at[block], out.at[block], pass_send.at[row, k - 1], pass_recv.at[row, k - 1], partner)

    clip_copies = [remote(mean_ref, got_s.at[d], clip_send.at[d], clip_recv.at[d], device) for d, device in enumerate(heads_of(1, 1))]

    @pl.when(last)
    def _():
        for copy in clip_copies:
            copy.start()

    w_first, w_diagonal, w_core = {}, {}, {}
    if gather:
        w_local, w_send, w_recv, d_send, d_recv, c_send, c_recv, b_send, b_recv, *bias_got = refs
        bias_copies = [
            remote(ref, got.at[d], b_send.at[d, n], b_recv.at[d, n], device)
            for d, device in enumerate(beside)
            for n, (ref, got) in enumerate(zip(biases, bias_got))
        ]
        for copy in bias_copies:
            copy.start()
        mine = all_ref.at[head, here]
        for k in range(1, chips):
            w_first[k, 0] = remote(w_ref, mine, w_send.at[k - 1], w_recv.at[k - 1], across[k - 1])
        for d in range(1, heads):
            w_first[0, d] = remote(w_ref, mine, w_send.at[chips - 2 + d], w_recv.at[chips - 2 + d], beside[d - 1])
        w_core[0, 0] = remote(w_ref, mine, c_send.at[0, 0], c_recv.at[0, 0], partner)
        for copy in [*w_first.values(), w_core[0, 0]]:
            copy.start()
        w_copy = pltpu.make_async_copy(w_ref, mine, w_local.at[0])
        w_copy.start()

        def forward(k, d):
            block = all_ref.at[rem(head - d, heads), 2 * rem(chip - k, chips) + core]
            w_core[k, d] = remote(block, block, c_send.at[k, d], c_recv.at[k, d], partner)
            w_core[k, d].start()

    own_copies = spread(pooled_ref, own_ref, own_send, own_recv)
    for copy in own_copies[1:] + own_copies[:1]:
        copy.start()
    own_local = pltpu.make_async_copy(pooled_ref, own_ref.at[here], local_sem.at[0])
    own_local.start()
    if gather:
        for k in range(1, chips):
            w_first[k, 0].wait_recv()
            block = all_ref.at[head, 2 * rem(chip - k, chips) + core]
            for d in range(1, heads):
                w_diagonal[k, d] = remote(block, block, d_send.at[k - 1, d - 1], d_recv.at[k - 1, d - 1], beside[d - 1])
                w_diagonal[k, d].start()
            forward(k, 0)

    @pl.when(begun)
    def _():
        for copy in clip_copies:
            copy.wait_recv()
        for m in range(share):
            total = None
            for d in range(heads):
                for s in range(share):
                    piece = got_s[d, s].astype(f32) * pick_ref[m, d * share + s]
                    total = piece if total is None else total + piece
            pick_s[m] = total.astype(bf16)

    @pl.when(jnp.logical_not(begun))
    def _():
        pick_s[...] = jnp.zeros_like(pick_s)

    mem_copies = spread(pick_s, mem_ref, mem_send, mem_recv)
    for copy in mem_copies[1:] + mem_copies[:1]:
        copy.start()
    mem_local = pltpu.make_async_copy(pick_s, mem_ref.at[here], local_sem.at[1])
    mem_local.start()
    forwards = []
    for k in range(1, chips):
        own_copies[k].wait_recv()
        forwards.append(passed(own_ref, k, 0))
        forwards[-1].start()
    if gather:
        for d in range(1, heads):
            w_first[0, d].wait_recv()
            forward(0, d)
    for k in range(1, chips):
        mem_copies[k].wait_recv()
        forwards.append(passed(mem_ref, k, 1))
        forwards[-1].start()
    if gather:
        for k, d in w_diagonal:
            w_diagonal[k, d].wait_recv()
            forward(k, d)
        for copy in w_core.values():
            copy.wait_recv()
        for copy in bias_copies:
            copy.wait_recv()
        by_head = []
        for ref, got in zip(biases, bias_got):
            pieces = []
            for h in range(heads):
                piece = ref[...]
                for d in range(1, heads):
                    piece = jnp.where(rem(head - d, heads) == h, got[d - 1], piece)
                pieces.append(piece)
            by_head.append(pieces)
        qv_a_ref[...] = jnp.concatenate(by_head[0], axis=1)
        qv_b_ref[...] = jnp.concatenate(by_head[1], axis=1)
        for h in range(heads):
            ub_a_ref[h] = by_head[2][h]
        ub_b_ref[...] = jnp.concatenate(by_head[3], axis=1)
        for copy in bias_copies:
            copy.wait_send()
    own_copies[0].wait_recv()
    mem_copies[0].wait_recv()
    for copy in forwards:
        copy.wait_recv()
    for copy in own_copies + mem_copies + forwards + [*w_first.values(), *w_diagonal.values(), *w_core.values()]:
        copy.wait_send()
    own_local.wait()
    mem_local.wait()
    if gather:
        w_copy.wait()

    @pl.when(last)
    def _():
        for copy in clip_copies:
            copy.wait_send()


ANY = pl.BlockSpec(memory_space=pl.ANY)
INVMEM = pl.BlockSpec(memory_space=pltpu.VMEM)
INSMEM = pl.BlockSpec(memory_space=pltpu.SMEM)


def dma(*dims):
    return pltpu.SemaphoreType.DMA(dims)


def share_pooled(pooled, mean, pick, number, block=None, biases=()):
    toks, heads = lax.axis_size("tok"), lax.axis_size("head")
    chips = toks // 2
    few = max(chips - 1, 1)
    args, specs = [pooled, mean, pick], [INVMEM, INVMEM, INSMEM]
    outs = [shape((toks,) + pooled.shape, bf16), shape((toks,) + mean.shape, bf16)]
    scratch = [
        pltpu.VMEM((heads,) + mean.shape, bf16), pltpu.VMEM(mean.shape, bf16), dma(2),
        dma(chips), dma(chips), dma(chips), dma(chips), dma(2, few), dma(2, few), dma(heads), dma(heads),
    ]
    if block is not None:
        args, specs = args + [block, *biases], specs + [ANY] + [INVMEM] * len(biases)
        (_, wa), (_, wb), (_, fa), (_, fb) = (b.shape for b in biases)
        outs = outs + [shape((heads, toks) + block.shape, bf16)]
        outs += [shape(dims, f32) for dims in ((2, heads * wa), (2, heads * wb), (heads, 1, fa), (1, heads * fb))]
        firsts = max(chips + heads - 2, 1)
        scratch += [dma(1), dma(firsts), dma(firsts), dma(few, max(heads - 1, 1)), dma(few, max(heads - 1, 1)), dma(chips, heads), dma(chips, heads)]
        scratch += [dma(max(heads - 1, 1), 4), dma(max(heads - 1, 1), 4)]
        scratch += [pltpu.VMEM((max(heads - 1, 1),) + b.shape, f32) for b in biases]
    return pl.pallas_call(
        functools.partial(share_kernel, block is not None),
        in_specs=specs,
        out_specs=[ANY] * min(len(outs), 3) + [INVMEM] * (len(outs) - 3),
        out_shape=outs,
        scratch_shapes=scratch,
        compiler_params=pltpu.CompilerParams(collective_id=number, has_side_effects=True, vmem_limit_bytes=VMEM_CAP),
        cost_estimate=about(20 if block is None else 30),
        name="share_pooled",
    )(*args)


def give_back_kernel(exchange, *refs):
    if exchange:
        part_ref, pick_ref, half_ref, piece_ref, shard_ref, own_ref, back_ref, all_ref, pieces_ref, sum_ref, *refs = refs
        *refs, half_local, half_send, half_recv, piece_send, piece_recv, shard_send, shard_recv, shard_s = refs
    else:
        part_ref, pick_ref, own_ref, back_ref, *refs = refs
    (mine_s, core_s, sum_s, chip_s, route_s, got_s,
     local_sem, core_send, core_recv, mem_send, mem_recv, own_send, own_recv, clip_send, clip_recv) = refs
    clip, head, chip, core, chips = places()
    clips, heads = lax.axis_size("clip"), lax.axis_size("head")
    share, rows = own_ref.shape[0], own_ref.shape[1]
    partner = {"tok": 2 * chip + 1 - core}
    across = [{"tok": 2 * rem(chip + k, chips) + core} for k in range(1, chips)]
    beside = [{"head": rem(head + d, heads)} for d in range(1, heads)]
    heads_of = lambda by, sign: [{"clip": clip + by, "head": rem(head + sign * d, heads)} for d in range(heads)]
    last, begun = clip < clips - 1, clip > 0
    along = [{"clip": rem(clip + k, clips)} for k in range(1, clips)]
    near = [(d, None) for d in [partner] + across + (beside + along if exchange else [])]
    greet(near + [(d, last) for d in heads_of(1, 1)], near + [(d, begun) for d in heads_of(-1, -1)])

    order = [rem(chip + k, chips) for k in list(range(1, chips)) + [0]]
    core_copies, local_copies = [], []
    for n, other in enumerate(order):
        core_copies.append(remote(part_ref.at[2 * other + 1 - core], core_s.at[n], core_send.at[n], core_recv.at[n], partner))
        core_copies[-1].start()
    for n, other in enumerate(order):
        local_copies.append(pltpu.make_async_copy(part_ref.at[2 * other + core], mine_s.at[n], local_sem.at[n]))
        local_copies[-1].start()
    halves = []
    if exchange:
        halves = [remote(half_ref, all_ref.at[head], half_send.at[k], half_recv.at[k], d) for k, d in enumerate(beside)]
        for copy in halves:
            copy.start()
        half_copy = pltpu.make_async_copy(half_ref, all_ref.at[head], half_local.at[0])
        half_copy.start()
    mem_copies, own_copies = [], []
    piece_copies, shard_copies = [], []
    for n in range(chips):
        local_copies[n].wait()
        core_copies[n].wait_recv()
        if n == chips - 1:
            break
        sum_s[n] = (mine_s[n].astype(f32) + core_s[n].astype(f32)).astype(bf16)
        low, high = pl.ds(0, rows), pl.ds(rows, sum_s.shape[2] - rows)
        mem_copies.append(remote(sum_s.at[n, :, high, :], chip_s.at[n, :, high, :], mem_send.at[n], mem_recv.at[n], across[n]))
        mem_copies[-1].start()
        own_copies.append(remote(sum_s.at[n, :, low, :], chip_s.at[n, :, low, :], own_send.at[n], own_recv.at[n], across[n]))
        own_copies[-1].start()
    base = chips - 1
    for copy in mem_copies:
        copy.wait_recv()
    memory = []
    for m in range(share):
        total = mine_s[base, m, rows:].astype(f32) + core_s[base, m, rows:].astype(f32)
        for n in range(chips - 1):
            total = total + chip_s[n, m, rows:].astype(f32)
        memory.append(total)
    clip_copies = [
        remote(route_s.at[d], got_s.at[d], clip_send.at[d], clip_recv.at[d], device) for d, device in enumerate(heads_of(-1, -1))
    ]

    @pl.when(begun)
    def _():
        for d in range(heads):
            for s in range(share):
                total = None
                for m in range(share):
                    piece = memory[m] * pick_ref[m, d * share + s]
                    total = piece if total is None else total + piece
                route_s[d, s] = total.astype(bf16)
            clip_copies[d].start()

    if exchange:
        wide = sum_ref.shape[1]
        lanes = lambda c: pl.ds(pl.multiple_of(wide * c, wide), wide)
        for k, d in enumerate(along):
            shard_copies.append(
                remote(shard_ref.at[:, lanes(rem(clip + k + 1, clips))], shard_s.at[k], shard_send.at[k], shard_recv.at[k], d))
            piece_copies.append(remote(piece_ref, pieces_ref.at[clip], piece_send.at[k], piece_recv.at[k], d))
        for copy in shard_copies + piece_copies:
            copy.start()
        piece_copy = pltpu.make_async_copy(piece_ref, pieces_ref.at[clip], half_local.at[1])
        piece_copy.start()
    for copy in own_copies:
        copy.wait_recv()
    for m in range(share):
        total = mine_s[base, m, :rows].astype(f32) + core_s[base, m, :rows].astype(f32)
        for n in range(chips - 1):
            total = total + chip_s[n, m, :rows].astype(f32)
        own_ref[m] = total

    @pl.when(last)
    def _():
        for copy in clip_copies:
            copy.wait_recv()
        total = got_s[0].astype(f32)
        for d in range(1, heads):
            total = total + got_s[d].astype(f32)
        back_ref[...] = total

    @pl.when(jnp.logical_not(last))
    def _():
        back_ref[...] = jnp.zeros_like(back_ref)

    if exchange:
        for copy in shard_copies:
            copy.wait_recv()
        total = shard_ref[:, lanes(clip)].astype(f32)
        for k in range(clips - 1):
            total = total + shard_s[k].astype(f32)
        sum_ref[...] = total.astype(bf16)
    for copy in halves + piece_copies:
        copy.wait_recv()
    for copy in core_copies + mem_copies + own_copies + halves + piece_copies + shard_copies:
        copy.wait_send()
    if exchange:
        half_copy.wait()
        piece_copy.wait()

    @pl.when(begun)
    def _():
        for copy in clip_copies:
            copy.wait_send()


def give_back(part, pick, own_rows, number, half=None, piece=None, shard=None):
    toks, heads = lax.axis_size("tok"), lax.axis_size("head")
    chips, few = toks // 2, max(toks // 2 - 1, 1)
    share, rows, d = part.shape[1:]
    args, specs = [part, pick], [ANY, INSMEM]
    outs, out_specs = [shape((share, own_rows, d), f32), shape((share, rows - own_rows, d), f32)], [INVMEM, INVMEM]
    scratch = [
        pltpu.VMEM((chips,) + part.shape[1:], bf16), pltpu.VMEM((chips,) + part.shape[1:], bf16),
        pltpu.VMEM((few,) + part.shape[1:], bf16), pltpu.VMEM((few,) + part.shape[1:], bf16),
        pltpu.VMEM((heads, share, rows - own_rows, d), bf16), pltpu.VMEM((heads, share, rows - own_rows, d), bf16),
        dma(chips), dma(chips), dma(chips), dma(few), dma(few), dma(few), dma(few), dma(heads), dma(heads),
    ]
    if half is not None:
        clips = lax.axis_size("clip")
        wide = shard.shape[1] // clips
        args, specs = args + [half, piece, shard], specs + [ANY, ANY, INVMEM]
        outs += [shape((heads,) + half.shape, half.dtype), shape((clips,) + piece.shape, bf16), shape((shard.shape[0], wide), bf16)]
        out_specs += [ANY, ANY, INVMEM]
        along = max(clips - 1, 1)
        scratch += [dma(2), dma(max(heads - 1, 1)), dma(max(heads - 1, 1)), dma(along), dma(along), dma(along), dma(along)]
        scratch += [pltpu.VMEM((along, shard.shape[0], wide), bf16)]
    return pl.pallas_call(
        functools.partial(give_back_kernel, half is not None),
        in_specs=specs,
        out_specs=out_specs,
        out_shape=outs,
        scratch_shapes=scratch,
        compiler_params=pltpu.CompilerParams(collective_id=number, has_side_effects=True, vmem_limit_bytes=VMEM_CAP),
        cost_estimate=about(25 if half is None else 35),
        name="give_back",
    )(*args)


def finish_kernel(sizes, half_ref, last_ref, qv_a_rows, a_ref, b_ref, qv_b_rows, ub_a_rows, ub_b_rows, grad_ref, rest_ref, piece_ref, all_ref, gains_a_ref, gains_b_ref, shifts_a_ref,
                  shifts_b_ref, qv_a_ref, qv_b_ref, ub_a_ref, ub_b_ref, gtotal_ref, up_ref, down_ref, out_ref,
                  q_ref, out_b_ref, skip_ref, *scratch):
    (small_ref, small_s, small_core, small_chip, small_head, small_clip, part_s, part_core, chip_s, part_chip, head_s, part_head, mine_s, part_clip,
     rest_in, rest_s, local_sem, half_send, half_recv, core_send, core_recv, chip_send, chip_recv, head_send, head_recv,
     clip_send, clip_recv, rest_send, rest_recv, back_send, back_recv, piece_s, piece_send, piece_recv) = scratch
    clip, head, chip, core, chips = places()
    clips, heads = lax.axis_size("clip"), lax.axis_size("head")
    share = half_ref.shape[0]
    partner = {"tok": 2 * chip + 1 - core}
    across = [{"tok": 2 * rem(chip + k, chips) + core} for k in range(1, chips)]
    beside = [{"head": rem(head + k, heads)} for k in range(1, heads)]
    along = [{"clip": rem(clip + k, clips)} for k in range(1, clips)]
    peers = [(d, None) for d in [partner] + across + beside + along]
    greet(peers, peers)
    pending = []
    d1 = small_ref.shape[1]
    small_ref[...] = jnp.zeros_like(small_ref)
    small_ref[0:2, :] = last_ref[0:2, :]
    small_ref[2:4, :] = qv_a_rows[0:2, :]
    for row, source in enumerate((3, 0, 5, 4, 2, 1)):
        small_ref[4 + row:5 + row, :] = a_ref[source:source + 1, :]
    row = 10
    longer = [b_ref[n:n + 1, :] for n in (3, 0, 1, 2)] + [qv_b_rows[n:n + 1, :] for n in range(2)]
    for values in longer + [ub_a_rows[h] for h in range(heads)] + [ub_b_rows[...]]:
        for low in range(0, values.shape[1], d1):
            small_ref[row:row + 1, :] = values[:, low:low + d1]
            row += 1
    wide = rest_ref.shape[1] // clips

    def lanes(c):
        return pl.ds(pl.multiple_of(wide * c, wide), wide)

    def go(copies):
        for copy in copies:
            copy.start()
        pending.extend(copies)
        return copies

    def arrived(copies):
        for copy in copies:
            copy.wait_recv()

    def in_order(index, size, own, slot):
        total = None
        for i in range(size):
            piece = jnp.where(index == i, own, jnp.zeros_like(own))
            for k in range(size - 1):
                piece = jnp.where(rem(index - k - 1, size) == i, slot(k), piece)
            total = piece if total is None else total + piece
        return total

    first = go([remote(small_ref, small_core, core_send.at[0], core_recv.at[0], partner)])
    for h in range(heads):
        for x in range(chips):
            n = h * chips + x
            first += go([remote(grad_ref.at[2 * n + 1 - core], part_core.at[n], core_send.at[n + 1], core_recv.at[n + 1], partner)])
    gather = go([remote(rest_ref.at[:, lanes(rem(clip + k + 1, clips))], rest_in.at[k], rest_send.at[k], rest_recv.at[k], d) for k, d in enumerate(along)])
    wider = piece_ref.shape[1]
    group = pl.ds(pl.multiple_of(wider * clip, wider), wider)
    piece_s[:, group] = piece_ref[...]
    pieces = go([remote(piece_ref, piece_s.at[:, group], piece_send.at[k], piece_recv.at[k], d) for k, d in enumerate(along)])
    halves = [
        [remote(half_ref.at[s], all_ref.at[head, s], half_send.at[k, s], half_recv.at[k, s], d) for k, d in enumerate(beside)]
        for s in range(share)
    ]
    for s in range(share - 1):
        go(halves[s])
    local_half = pltpu.make_async_copy(half_ref, all_ref.at[head], local_sem.at[0])
    local_half.start()
    arrived(first)
    small_s[0] = small_ref[...] + small_core[...]
    for n in range(heads * chips):
        part_s[n] = (grad_ref[2 * n + core].astype(f32) + part_core[n].astype(f32)).astype(bf16)
    copies = []
    for k, d in enumerate(across):
        copies += go([remote(small_s.at[0], small_chip.at[k], chip_send.at[k, 0], chip_recv.at[k, 0], d)])
        for h in range(heads):
            block = h * chips + rem(chip + k + 1, chips)
            copies += go([remote(part_s.at[block], part_chip.at[k, h], chip_send.at[k, h + 1], chip_recv.at[k, h + 1], d)])
    arrived(copies)
    small_s[1] = in_order(chip, chips, small_s[0], lambda k: small_chip[k])
    for h in range(heads):
        total = part_s[h * chips + chip].astype(f32)
        for k in range(chips - 1):
            total = total + part_chip[k, h].astype(f32)
        chip_s[h] = total.astype(bf16)
    copies = []
    for k, d in enumerate(beside):
        copies += go([remote(small_s.at[1], small_head.at[k], head_send.at[k, 0], head_recv.at[k, 0], d)])
        copies += go([remote(chip_s.at[rem(head + k + 1, heads)], part_head.at[k], head_send.at[k, 1], head_recv.at[k, 1], d)])
    go(halves[share - 1])
    arrived(gather)
    total = rest_ref[:, lanes(clip)].astype(f32)
    for k in range(clips - 1):
        total = total + rest_in[k].astype(f32)
    rest_s[:, lanes(clip)] = total.astype(bf16)
    spread = go([remote(rest_s.at[:, lanes(clip)], rest_s.at[:, lanes(clip)], back_send.at[k], back_recv.at[k], d) for k, d in enumerate(along)])
    arrived(copies)
    small_s[2] = in_order(head, heads, small_s[1], lambda k: small_head[k])
    total = chip_s[head].astype(f32)
    for k in range(heads - 1):
        total = total + part_head[k].astype(f32)
    mine_s[...] = total.astype(bf16)
    copies = []
    for k, d in enumerate(along):
        copies += go([remote(small_s.at[2], small_clip.at[k], clip_send.at[k, 0], clip_recv.at[k, 0], d)])
        copies += go([remote(mine_s, part_clip.at[k], clip_send.at[k, 1], clip_recv.at[k, 1], d)])
    arrived(copies)
    total = in_order(clip, clips, small_s[2], lambda k: small_clip[k])
    at = [4]

    def rows(width):
        first = at[0]
        at[0] += width // total.shape[1]
        return jnp.concatenate([total[r:r + 1] for r in range(first, at[0])], axis=1)

    def share_of(row):
        width = row.shape[1] // heads
        piece = row[:, :width]
        for h in range(1, heads):
            piece = jnp.where(head == h, row[:, width * h:width * h + width], piece)
        return piece

    gains_a_ref[0:1, :] = total[0:1]
    gains_a_ref[1:3, :] = total[4:6]
    shifts_a_ref[0:1, :] = total[1:2]
    shifts_a_ref[1:5, :] = total[6:10]
    qv_a_ref[0:1, :] = share_of(total[2:3])
    qv_a_ref[1:2, :] = share_of(total[3:4])
    at[0] = 10
    d2, fa, fb = sizes
    gains_b_ref[...] = rows(d2)
    for i in range(3):
        shifts_b_ref[i:i + 1, :] = rows(d2)
    for i in range(2):
        qv_b_ref[i:i + 1, :] = share_of(rows(d2))
    ub_a_ref[...] = share_of(rows(fa))
    ub_b_ref[...] = share_of(rows(fb))
    gtotal_ref[...] = in_order(clip, clips, mine_s[...].astype(f32), lambda k: part_clip[k].astype(f32))
    arrived(spread)
    wide = up_ref.shape[1]
    up_ref[...] = rest_s[:, :wide].astype(f32)
    down_ref[...] = rest_s[:, wide:2 * wide].astype(f32)
    out_ref[...] = rest_s[:, 2 * wide:2 * wide + out_ref.shape[1]].astype(f32)
    arrived(pieces)
    wide, rows = q_ref.shape[1], piece_s.shape[0]
    q_ref[...] = piece_s[:, :wide].astype(f32)
    for ref in (out_b_ref, skip_ref):
        for n in range(2):
            ref[rows * n:rows * n + rows, :] = piece_s[:, wide:wide + ref.shape[1]].astype(f32)
            wide += ref.shape[1]
    for copies in halves:
        arrived(copies)
    for copy in pending:
        copy.wait_send()
    local_half.wait()


def finish(half, rows, grad, rest, piece, d2, fa, fb, ha, hs, number):
    toks, heads, clips = lax.axis_size("tok"), lax.axis_size("head"), lax.axis_size("clip")
    chips = toks // 2
    across, beside, along = (max(n, 1) for n in (chips - 1, heads - 1, clips - 1))
    block, depth, d1 = grad.shape[1:], rest.shape[0], rows[0].shape[1]
    count = 4 + 6 + (6 * d2 + fa + fb) // d1
    low, full = lambda *dims: pltpu.VMEM(dims, bf16), lambda *dims: pltpu.VMEM(dims + (-(-count // 8) * 8, d1), f32)
    sums = [(3, d1), (1, d2), (5, d1), (3, d2), (2, d1 // heads), (2, d2 // heads), (1, fa // heads), (1, fb // heads),
            block, (depth, fa // heads), (depth, fa // heads), (depth, ha),
            (piece.shape[0], 3 * d2 // heads), (2 * piece.shape[0], d2 // heads), (2 * piece.shape[0], hs)]
    return pl.pallas_call(
        functools.partial(finish_kernel, (d2, fa, fb)),
        in_specs=[ANY] + [INVMEM] * (len(rows) + 3),
        out_specs=[ANY] + [INVMEM] * len(sums),
        out_shape=[shape((heads,) + half.shape, half.dtype)] + [shape(dims, f32) for dims in sums],
        scratch_shapes=[
            full(), full(3), full(), full(across), full(beside), full(along),
            low(heads * chips, *block), low(heads * chips, *block), low(heads, *block), low(across, heads, *block),
            low(heads, *block), low(beside, *block), low(*block), low(along, *block),
            low(along, depth, rest.shape[1] // clips), low(*rest.shape),
            dma(1), dma(beside, half.shape[0]), dma(beside, half.shape[0]), dma(heads * chips + 1), dma(heads * chips + 1),
            dma(across, heads + 1), dma(across, heads + 1), dma(beside, 2), dma(beside, 2), dma(along, 2), dma(along, 2),
            dma(along), dma(along), dma(along), dma(along),
            low(piece.shape[0], clips * piece.shape[1]), dma(along), dma(along),
        ],
        compiler_params=pltpu.CompilerParams(collective_id=number, has_side_effects=True, vmem_limit_bytes=VMEM_CAP),
        cost_estimate=about(40),
        name="finish",
    )(half, *rows, grad, rest, piece)


def reduce_clips(shard):
    clips, clip = lax.axis_size("clip"), lax.axis_index("clip")
    pieces = shard.reshape(clips, -1, shard.shape[-1])
    total = lax.dynamic_index_in_dim(pieces, clip, 0, keepdims=False).astype(f32)
    for k in range(1, clips):
        give = lax.dynamic_index_in_dim(pieces, (clip + k) % clips, 0, keepdims=False)
        total = total + lax.ppermute(give, "clip", [(i, (i + k) % clips) for i in range(clips)]).astype(f32)
    return total.astype(bf16)


def padded_rows(*rows):
    return jnp.concatenate([jnp.stack(rows), jnp.zeros((-len(rows) % 8, rows[0].shape[0]), f32)])


def local(
    clips_in, resets, assign, w_qkv_a, w_out_a, w_up_a, w_down_a, w_qkv_b, w_out_b, w_skip_b, w_up_b, w_down_b,
    gains_a, gains_b, shifts_a, shifts_b, qv_bias_a, qv_bias_b, up_bias_a, up_bias_b, cotangent,
):
    heads, toks, clips = lax.axis_size("head"), lax.axis_size("tok"), lax.axis_size("clip")
    head = lax.axis_index("head")
    micro, frames = clips_in.shape[1], clips_in.shape[2]
    d1, d2 = clips_in.shape[-1], cotangent.shape[-1]
    share = micro // heads
    first = head * share
    pool_np, pair_np = pool_matrix(frames), pair_matrix(frames)
    pooling, pairing = jnp.asarray(pool_np, bf16), jnp.asarray(pair_np, bf16)
    unpooling, unpairing = jnp.asarray(pool_np.T, bf16), jnp.asarray(pair_np.T, bf16)
    tokens, pooled_tokens = frames * PATCH, frames * POOLED
    own_rows, mem_rows = up16(pooled_tokens), up16(frames // 2 * POOLED)
    rows2 = share * own_rows

    cot = lax.dynamic_slice_in_dim(cotangent[0], first, share, 0).reshape(share, pooled_tokens, d2)
    cot = jnp.pad(cot, ((0, 0), (0, own_rows - pooled_tokens), (0, 0))).reshape(rows2, d2)

    source = lax.dynamic_slice_in_dim(assign[0], first, share, 0)
    flags = lax.dynamic_slice_in_dim(resets[0], first, share, 0)
    slot = ((head - source // share + heads) % heads) * share + source % share
    pick = (jnp.arange(heads * share)[None, :] == slot[:, None]).astype(f32)
    has = ((flags == 0) & (lax.axis_index("clip") > 0)).astype(jnp.int32)
    valid = (pooled_tokens, frames // 2 * POOLED)

    group = ("head", "tok")
    fa, ha = w_up_a.shape[1], w_out_a.shape[1]
    fb, hb, hs = w_up_b.shape[1], w_out_b.shape[1], w_skip_b.shape[1]
    mine = lax.dynamic_slice_in_dim(clips_in[0], first, share, 0)
    stream, low1, pooled1, mean1 = call(
        norm_pool_kernel, share,
        [(mine, 0), (padded_rows(gains_a[0], shifts_a[0]), None), (pooling, None), (pairing, None)],
        [(shape((share, tokens, d1), bf16), 0), (shape((share, tokens, d1), bf16), 0),
         (shape((share, own_rows, d1), bf16), 0), (shape((share, mem_rows, d1), bf16), 0)],
        name="norm_pool", us=5,
    )
    pooled1, w_qkv_b, w_up_b = lax.optimization_barrier((pooled1, w_qkv_b, w_up_b))
    pack_a = jnp.concatenate([w_up_a, w_down_a, w_qkv_a.reshape(w_qkv_a.shape[0], -1), w_out_a], axis=1)
    pack_q = w_qkv_b.reshape(w_qkv_b.shape[0], -1)
    pack_b = jnp.concatenate([w_up_b, w_down_b, w_out_b, w_skip_b], axis=1)
    all_q = lax.all_gather(pack_q, group).reshape(heads, d1, -1)
    all_b = lax.all_gather(pack_b, group).reshape(heads, d2, -1)
    own1, mem1, all_a, qv_a, qv_b, ub_a, ub_b = share_pooled(
        pooled1, mean1, pick, 0, pack_a, [qv_bias_a, qv_bias_b, up_bias_a[None], up_bias_b[None]])
    all_a = all_a.reshape(heads, d1, -1)

    def lanes(pack, low, width):
        return jnp.concatenate([pack[h, :, low:low + width] for h in range(heads)], axis=1)

    up_spec, down_spec, rest_spec = (pl.BlockSpec((heads, d1, fa), lambda i, n=n: (0, 0, n)) for n in range(3))
    skip_b = lanes(all_b, 2 * fb + hb, hs)

    comb1, lse1 = attend(low1, own1, mem1, (all_a, rest_spec), qv_a, has, valid, d1)
    after1, middle, pooled3, mean3 = call(
        first_mlp_kernel, share,
        [(stream, 0), (comb1, 0), (all_a, rest_spec), (all_a, up_spec), (all_a, down_spec), (ub_a, None),
         (padded_rows(shifts_a[1], gains_a[1], shifts_a[2], shifts_a[3], gains_a[2], shifts_a[4]), None),
         (pooling, None), (pairing, None)],
        [(shape((share, tokens, d1), f32), 0), (shape((share, tokens, d1), f32), 0),
         (shape((share, own_rows, d1), bf16), 0), (shape((share, mem_rows, d1), bf16), 0)],
        [((d1, d1), bf16)],
        name="first_mlp", us=13,
    )

    own2, mem2 = share_pooled(pooled3, mean3, pick, 1)
    comb2, lse2 = attend(pooled3, own2, mem2, (all_q, None), qv_b, has, valid, d2)
    chunk = 768
    per_head = fb // chunk
    steps = heads * per_head
    out_spec = pl.BlockSpec((heads, d2, hb), lambda j: (0, 0, 2 * fb // hb))
    rows_spec = pl.BlockSpec((1, d2, chunk), lambda j: (j // per_head, 0, j % per_head))
    mixed, dcomb2, dskip, g_mlp_b, g_out_b, g_skip_b, g_ub_b, rows_b = call(
        second_mlp_kernel, steps,
        [(comb2.reshape(rows2, d2), None), (pooled3.reshape(rows2, d1), None), (cot, None), (all_b, out_spec), (skip_b, None),
         (all_b, rows_spec),
         (all_b, pl.BlockSpec((1, d2, chunk), lambda j: (j // per_head, 0, per_head + j % per_head))),
         (ub_b, pl.BlockSpec((1, chunk), lambda j: (0, j))),
         (padded_rows(shifts_b[0], gains_b, shifts_b[1], shifts_b[2]), None)],
        [(shape((rows2, d2), bf16), None), (shape((rows2, d2), bf16), None), (shape((rows2, d1), f32), None),
         (shape((heads, toks, 2, d2 // toks, fb), bf16),
          pl.BlockSpec((1, toks, 2, d2 // toks, chunk), lambda j: (j // per_head, 0, 0, 0, j % per_head))),
         (shape((heads, toks, d2 // toks // 2, 2 * hb), bf16), None), (shape((heads, toks, d2 // toks // 2, 2 * hs), bf16), None),
         (shape((1, heads * fb), f32), pl.BlockSpec((1, chunk), lambda j: (0, j))), (shape((8, d2), f32), None)],
        [((rows2, d2), f32), ((rows2, d2), bf16), ((d2, rows2), bf16), ((d2, rows2), bf16), ((rows2, d2), f32), ((rows2, d2), f32)],
        name="second_mlp", us=26,
    )

    def by_owner(grad):
        return grad.reshape((heads * toks, -1) + grad.shape[2:])

    def scatter(grad):
        return lax.psum_scatter(grad, group, scatter_dimension=0, tiled=False)

    sum_mlp_b = scatter(g_mlp_b.reshape((heads * toks,) + g_mlp_b.shape[2:]))
    dcomb2 = dcomb2.reshape(share, own_rows, d2)
    dq2, dpool2, g_qkv_b, rows_qv_b = attend_back(pooled3, dcomb2, own2, mem2, (all_q, None), qv_b, has, valid, lse2, heads)
    own_back2, mem_back2 = give_back(dpool2, pick, own_rows, 2)

    merge = lambda grad: grad.reshape((heads * toks,) + grad.shape[2:])
    rest_b = jnp.concatenate([by_owner(g_qkv_b), merge(g_out_b), merge(g_skip_b)], axis=2)
    rest_b = jnp.pad(rest_b, ((0, 0), (0, 0), (0, -rest_b.shape[2] % (128 * clips))))
    sum_rest_b = scatter(rest_b)

    res1, dcomb1, g_mlp_a, g_ub_a, rows_a = call(
        first_back_kernel, share,
        [(middle, 0), (after1, 0), (comb1, 0), (dskip.reshape(share, own_rows, d1), 0), (dq2, 0), (own_back2, 0), (mem_back2, 0),
         (all_a, rest_spec), (all_a, up_spec), (all_a, down_spec), (ub_a, None),
         (padded_rows(gains_a[1], shifts_a[2], gains_a[2]), None), (unpooling, None), (unpairing, None)],
        [(shape((share, tokens, d1), f32), 0), (shape((share, tokens, d1), bf16), 0),
         (shape((heads, d1, -(-(2 * fa + ha) // (128 * clips)) * 128 * clips), bf16), None),
         (shape((heads, 1, fa), f32), None), (shape((8, d1), f32), None)],
        [((heads, d1, fa), f32), ((heads, d1, fa), f32), ((d1, d1), f32), ((d1, d1), bf16)],
        name="first_back", us=26,
    )
    rest_a = by_owner(g_mlp_a)
    dcomb1, sum_mlp_b, rest_a = lax.optimization_barrier((dcomb1, sum_mlp_b, rest_a))
    sum_rest_a = scatter(rest_a)
    sum_mlp_b = reduce_clips(sum_mlp_b)
    dx1, dpool1, g_qkv_a, rows_qv_a = attend_back(low1, dcomb1, own1, mem1, (all_a, rest_spec), qv_a, has, valid, lse1, heads)
    own_back1, mem_back1, mixed_all, mlp_b, piece_b = give_back(
        dpool1, pick, own_rows, 3, mixed.reshape(share, own_rows, d2), sum_mlp_b, sum_rest_b)
    stream_grad, rows_last = call(
        last_back_kernel, share,
        [(stream, 0), (res1, 0), (dx1, 0), (own_back1, 0), (mem_back1, 0), (padded_rows(gains_a[0]), None),
         (unpooling, None), (unpairing, None)],
        [(shape((share, frames, PATCH, d1), bf16), 0), (shape((8, d1), f32), None)],
        name="last_back", us=6,
    )

    mlp_b = mlp_b.reshape((2, -1, mlp_b.shape[-1])).astype(f32)
    rows = [rows_last, rows_qv_a, rows_a, rows_b, rows_qv_b, g_ub_a, g_ub_b]
    stream_all, *sums = finish(
        stream_grad, rows, by_owner(g_qkv_a), sum_rest_a, piece_b, d2, heads * fa, heads * fb, ha, hs, 4)
    mixed_all = mixed_all.reshape(micro, own_rows, d2)[:, :pooled_tokens]
    return (
        mixed_all.reshape(cotangent.shape),
        stream_all.astype(f32).reshape(clips_in.shape),
        sums[8].reshape(w_qkv_a.shape),
        sums[11],
        sums[9],
        sums[10],
        sums[12].reshape(w_qkv_b.shape),
        sums[13],
        sums[14],
        mlp_b[0],
        mlp_b[1],
        sums[0], sums[1][0], sums[2], sums[3], sums[4], sums[5], sums[6][0], sums[7][0],
    )


def solution(mesh):
    in_specs = (
        P("clip", None, "tok", None, None),
        P("clip", None),
        P("clip", None),
        P("tok", None, "head"),
        P("tok", "head"),
        P("tok", "head"),
        P("tok", "head"),
        P("tok", None, "head"),
        P("tok", "head"),
        P("tok", "head"),
        P("tok", "head"),
        P("tok", "head"),
        P(),
        P(),
        P(),
        P(),
        P(None, "head"),
        P(None, "head"),
        P("head"),
        P("head"),
        P("clip", None, "tok", None, None),
    )
    out_specs = (
        P("clip", None, "tok", None, None),
        P("clip", None, "tok", None, None),
        P("tok", None, "head"),
        P("tok", "head"),
        P("tok", "head"),
        P("tok", "head"),
        P("tok", None, "head"),
        P("tok", "head"),
        P("tok", "head"),
        P("tok", "head"),
        P("tok", "head"),
        P(),
        P(),
        P(),
        P(),
        P(None, "head"),
        P(None, "head"),
        P("head"),
        P("head"),
    )
    return jax.shard_map(local, mesh=mesh, in_specs=in_specs, out_specs=out_specs, check_vma=False)
```

```python
import functools
import math

import jax
import jax.numpy as jnp
import numpy as np
from jax import lax
from jax.experimental import pallas as pl
from jax.experimental.pallas import tpu as pltpu
from jax.sharding import PartitionSpec as P

GRID = 14
PATCH = GRID * GRID
POOLED = PATCH // 4
HD = 96
NEG = -1e30
VMEM_CAP = 62 * 2**20
eps = 1e-06
f32, bf16 = jnp.float32, jnp.bfloat16
NN, NT, TN = ((1,), (0,)), ((1,), (1,)), ((0,), (0,))


def up16(n):
    return -(-n // 16) * 16


def pool_matrix(frames):
    rows, cols = up16(frames * POOLED), frames * PATCH
    out = np.zeros((rows, cols), np.float32)
    half = GRID // 2
    for f in range(frames):
        for p in range(PATCH):
            r, c = divmod(p, GRID)
            out[f * POOLED + (r // 2) * half + c // 2, f * PATCH + p] = 0.25
    return out


def pair_matrix(frames):
    rows, cols = up16(frames // 2 * POOLED), up16(frames * POOLED)
    out = np.zeros((rows, cols), np.float32)
    for j in range(frames // 2):
        for p in range(POOLED):
            out[j * POOLED + p, 2 * j * POOLED + p] = 0.5
            out[j * POOLED + p, (2 * j + 1) * POOLED + p] = 0.5
    return out


def dot(a, b, dims=NN):
    return lax.dot_general(a, b, (dims, ((), ())), preferred_element_type=f32)


def exact_dot(matrix, tensor):
    high = tensor.astype(bf16)
    low = (tensor - high.astype(f32)).astype(bf16)
    return dot(matrix, high) + dot(matrix, low)


def norm(x):
    average = jnp.mean(x, axis=-1, keepdims=True)
    centred = x - average
    inverse = lax.rsqrt(jnp.mean(centred * centred, axis=-1, keepdims=True) + eps)
    return centred * inverse, inverse


def norm_back(unit, inverse, gain, gradient):
    scaled = gradient * gain
    return inverse * (
        scaled
        - jnp.mean(scaled, axis=-1, keepdims=True)
        - unit * jnp.mean(scaled * unit, axis=-1, keepdims=True)
    )


GELU_A, GELU_B = math.sqrt(2.0 / math.pi), 0.044715


def gelu(x):
    t = jnp.tanh(GELU_A * (x + GELU_B * (x * x * x)))
    return 0.5 * x * (1.0 + t)


def gelu_both(x):
    square = x * x
    t = jnp.tanh(GELU_A * x * (1.0 + GELU_B * square))
    value = 0.5 * x * (1.0 + t)
    slope = 0.5 * (1.0 + t) + 0.5 * x * (1.0 - t * t) * (GELU_A * (1.0 + 3.0 * GELU_B * square))
    return value, slope


def sum_rows(x):
    return jnp.sum(x, axis=0, keepdims=True)


def add_rows(ref, rows):
    step = pl.program_id(0)

    @pl.when(step == 0)
    def _():
        ref[...] = jnp.zeros_like(ref)

    for i, row in enumerate(rows):
        ref[i:i + 1, :] += row


def transposed(x):
    return x.astype(f32).T.astype(bf16)


def window(head):
    low = HD * head
    return low // 128 * 128, -(-(low + HD) // 128) * 128


def head_mask(head):
    start, stop = window(head)
    lane = lax.broadcasted_iota(jnp.int32, (1, stop - start), 1) + start
    return (lane >= HD * head) & (lane < HD * head + HD)


def key_rows(own_ref, mem_ref):
    row = 0
    for ref in (own_ref, mem_ref):
        for t in range(ref.shape[0]):
            yield ref, t, slice(row, row + ref.shape[2])
            row += ref.shape[2]


def key_mask(own_ref, mem_ref, valid, has):
    parts = []
    for ref, rows, there in ((own_ref, valid[0], None), (mem_ref, valid[1], has)):
        block = ref.shape[2]
        lane = lax.rem(lax.broadcasted_iota(jnp.int32, (1, ref.shape[0] * block), 1), block)
        limit = rows if there is None else jnp.where(there > 0, rows, 0)
        parts.append(jnp.where(lane < limit, 0.0, NEG))
    return jnp.concatenate(parts, axis=1)


def assemble(w_ref, w_s):
    wide = w_ref.shape[2] // 4
    for part in range(3):
        pieces = [w_ref[h, :, wide * part:wide * part + wide].astype(f32) for h in range(w_ref.shape[0])]
        w_s[0, :, 384 * part:384 * part + 384] = jnp.concatenate(pieces, axis=1).astype(bf16)


def assemble_out(w_ref, out_s):
    wide = w_ref.shape[2] // 4
    pieces = [w_ref[h, :, 3 * wide:].astype(f32) for h in range(w_ref.shape[0])]
    out_s[...] = jnp.concatenate(pieces, axis=1).astype(bf16)


def project_keys(own_ref, mem_ref, w_ref, bias_ref, x_s, k_s, v_s):
    for ref, t, rows in key_rows(own_ref, mem_ref):
        x_s[rows, :] = ref[t, 0]
    width = k_s.shape[1]
    for low in range(0, width, 384):
        k_s[:, low:low + 384] = dot(x_s[...], w_ref[low // 384, :, 384:768]).astype(bf16)
    for low in range(0, width, 384):
        value = dot(x_s[...], w_ref[low // 384, :, 768:])
        v_s[:, low:low + 384] = (value + bias_ref[1:2, low:low + 384]).astype(bf16)


def project_queries(x_ref, w_ref, bias_ref, q_s):
    width = q_s.shape[1]
    for low in range(0, width, 384):
        value = dot(x_ref[0], w_ref[low // 384, :, :384])
        q_s[:, low:low + 384] = (value + bias_ref[0:1, low:low + 384]).astype(bf16)


def norm_pool_kernel(clips_ref, vec_ref, pool_ref, pair_ref, x_ref, low_ref, pooled_ref, mean_ref):
    x = jnp.concatenate([clips_ref[0, f].astype(f32) for f in range(clips_ref.shape[1])], axis=0)
    x_ref[0] = x.astype(bf16)
    unit, _ = norm(x)
    normed = unit * vec_ref[0:1, :] + vec_ref[1:2, :]
    low_ref[0] = normed.astype(bf16)
    pooled = exact_dot(pool_ref[...], normed)
    pooled_ref[0] = pooled.astype(bf16)
    mean_ref[0] = exact_dot(pair_ref[...], pooled).astype(bf16)


def write_shares(gw_ref, h, gw_s):
    wide = gw_ref.shape[2] // 3
    for part in range(3):
        low = wide * h
        columns = gw_s[low // 384, :, 384 * part:384 * part + 384][:, low % 384:low % 384 + wide]
        gw_ref[h, :, wide * part:wide * part + wide] = columns.astype(bf16)


def attend_kernel(chunk, valid, x_ref, own_ref, mem_ref, w_ref, qv_ref, has_ref, out_ref, lse_ref, w_s, x_s, q_s, k_s, v_s, s_s, p_s):
    nq, width = q_s.shape
    columns = key_mask(own_ref, mem_ref, valid, has_ref[pl.program_id(0)])
    if width == 384:
        @pl.when(pl.program_id(0) == 0)
        def _():
            assemble(w_ref, w_s)
        w_ref = w_s
    project_queries(x_ref, w_ref, qv_ref, q_s)
    project_keys(own_ref, mem_ref, w_ref, qv_ref, x_s, k_s, v_s)
    factor = HD**-0.5 * math.log2(math.e)
    lanes = lax.broadcasted_iota(jnp.int32, (chunk, 128), 1)
    for tile in range(width // 384):
        group = slice(384 * tile, 384 * tile + 384)
        base = q_s[:, group].astype(f32)
        parts = [base[:, :128], base[:, 128:256], base[:, 256:384]]
        for head in range(4 * tile, 4 * tile + 4):
            start, stop = window(head)
            mask = head_mask(head)
            query = jnp.where(mask, q_s[:, start:stop], jnp.zeros((), bf16))
            s_s[...] = dot(query, k_s[:, start:stop], NT)

            def body(i, carry, head=head):
                rows = pl.ds(pl.multiple_of(i * chunk, chunk), chunk)
                score = s_s[rows, :] * factor + columns
                top = jnp.max(score, axis=1, keepdims=True)
                power = jnp.exp2(score - top)
                total = jnp.sum(power, axis=1, keepdims=True)
                p_s[rows, :] = (power * (1.0 / total)).astype(bf16)
                lse_ref[0, rows, :] = jnp.where(lanes == head, top + jnp.log2(total), lse_ref[0, rows, :])
                return carry

            lax.fori_loop(0, nq // chunk, body, 0, unroll=nq // chunk)
            out = jnp.where(mask, dot(p_s[...], v_s[:, start:stop]), 0.0)
            for w in range((stop - start) // 128):
                k = start // 128 - 3 * tile + w
                parts[k] = parts[k] + out[:, 128 * w:128 * w + 128]
        out_ref[0, :, group] = jnp.concatenate(parts, axis=1).astype(bf16)


def attend_back_kernel(
    chunk, valid, x_ref, g_ref, own_ref, mem_ref, w_ref, qv_ref, has_ref, lse_ref,
    dx_ref, dpool_ref, gw_ref, row_ref,
    w_s, x_s, q_s, k_s, v_s, s_s, dp_s, p_s, ds_s, dk_s, dv_s, dq_s, gw_s,
):
    nq, width = q_s.shape
    step = pl.program_id(0)
    columns = key_mask(own_ref, mem_ref, valid, has_ref[step])
    if width == 384:
        @pl.when(step == 0)
        def _():
            assemble(w_ref, w_s)
        w_ref = w_s
    project_queries(x_ref, w_ref, qv_ref, q_s)
    project_keys(own_ref, mem_ref, w_ref, qv_ref, x_s, k_s, v_s)
    scaling = HD**-0.5
    factor = scaling * math.log2(math.e)
    lanes = lax.broadcasted_iota(jnp.int32, (chunk, 128), 1)

    @pl.when(step == 0)
    def _():
        gw_s[...] = jnp.zeros_like(gw_s)

    xt = transposed(x_ref[0])
    keys_t = transposed(x_s[...])
    dx = None
    dpool = None
    row_q, row_v = [], []
    for tile in range(width // 384):
        group = slice(384 * tile, 384 * tile + 384)
        qt = transposed(q_s[:, group])
        gt = transposed(g_ref[0, :, group])
        parts = [None] * 3
        for head in range(4 * tile, 4 * tile + 4):
            start, stop = window(head)
            mask = head_mask(head)
            query = jnp.where(mask, q_s[:, start:stop], jnp.zeros((), bf16))
            grad = jnp.where(mask, g_ref[0, :, start:stop], jnp.zeros((), bf16))
            s_s[...] = dot(query, k_s[:, start:stop], NT)
            dp_s[...] = dot(grad, v_s[:, start:stop], NT)

            def body(i, carry, head=head):
                rows = pl.ds(pl.multiple_of(i * chunk, chunk), chunk)
                lse = jnp.sum(jnp.where(lanes == head, lse_ref[0, rows, :], 0.0), axis=1, keepdims=True)
                p = jnp.exp2(s_s[rows, :] * factor + columns - lse)
                dp = dp_s[rows, :]
                inner = jnp.sum(p * dp, axis=1, keepdims=True)
                p_s[rows, :] = p.astype(bf16)
                ds_s[rows, :] = (p * (dp - inner)).astype(bf16)
                return carry

            lax.fori_loop(0, nq // chunk, body, 0, unroll=nq // chunk)
            r = slice(HD * (head - 4 * tile), HD * (head - 4 * tile) + HD)
            dv_s[r, :] = dot(gt[r], p_s[...])
            dk_s[r, :] = dot(qt[r], ds_s[...]) * scaling
            dq = jnp.where(mask, dot(ds_s[...], k_s[:, start:stop]) * scaling, 0.0)
            for w in range((stop - start) // 128):
                k = start // 128 - 3 * tile + w
                part = dq[:, 128 * w:128 * w + 128]
                parts[k] = part if parts[k] is None else parts[k] + part
        total = jnp.concatenate(parts, axis=1) + g_ref[0, :, group].astype(f32)
        row_q.append(sum_rows(total))
        low = total.astype(bf16)
        gw_s[tile, :, :384] += dot(xt, low)
        add = dot(low, w_ref[tile, :, :384], NT)
        dx = add if dx is None else dx + add
        for part, src in ((1, dk_s), (2, dv_s)):
            grad = src[...].T
            if part == 2:
                row_v.append(sum_rows(grad))
            low = grad.astype(bf16)
            here = slice(384 * part, 384 * part + 384)
            gw_s[tile, :, here] += dot(keys_t, low)
            add = dot(low, w_ref[tile, :, here], NT)
            dpool = add if dpool is None else dpool + add
    dx_ref[0] = dx
    row = 0
    own, mem = own_ref.shape[2], mem_ref.shape[2]
    toks = own_ref.shape[0]
    for t in range(toks):
        dpool_ref[t, 0, :own, :] = dpool[t * own:(t + 1) * own].astype(bf16)
        dpool_ref[t, 0, own:, :] = dpool[toks * own + t * mem:toks * own + (t + 1) * mem].astype(bf16)
    add_rows(row_ref, [jnp.concatenate(row_q, axis=1), jnp.concatenate(row_v, axis=1)])

    @pl.when(step == pl.num_programs(0) - 1)
    def _():
        for h in range(gw_ref.shape[0]):
            write_shares(gw_ref, h, gw_s)


def first_mlp_kernel(x_ref, comb_ref, out_ref, up_ref, down_ref, ub_ref, vec_ref, pool_ref, pair_ref,
                     after_ref, middle_ref, pooled_ref, mean_ref, out_s):
    @pl.when(pl.program_id(0) == 0)
    def _():
        assemble_out(out_ref, out_s)

    after = x_ref[0].astype(f32) + dot(comb_ref[0], out_s[...], NT) + vec_ref[0:1, :]
    after_ref[0] = after
    unit, _ = norm(after)
    low = (unit * vec_ref[1:2, :] + vec_ref[2:3, :]).astype(bf16)
    total = after + vec_ref[3:4, :]
    for h in range(up_ref.shape[0]):
        hidden = gelu(dot(low, up_ref[h]) + ub_ref[h]).astype(bf16)
        total = total + dot(hidden, down_ref[h], NT)
    middle_ref[0] = total
    unit, _ = norm(total)
    pooled = exact_dot(pool_ref[...], unit * vec_ref[4:5, :] + vec_ref[5:6, :])
    pooled_ref[0] = pooled.astype(bf16)
    mean_ref[0] = exact_dot(pair_ref[...], pooled).astype(bf16)


def second_mlp_kernel(
    comb_ref, pooled_ref, cot_ref, out_ref, skip_ref, up_ref, down_ref, ub_ref, vec_ref,
    mixed_ref, dcomb_ref, dskip_ref, gmlp_ref, gout_ref, gskip_ref, gub_ref, row_ref,
    after_s, low_s, lowt_s, cott_s, sum_s, dlow_s, skip_s,
):
    step = pl.program_id(0)

    @pl.when(step == 0)
    def _():
        share = skip_s.shape[1] // skip_ref.shape[0]
        skip_s[...] = jnp.concatenate([skip_ref[h, :, :share].astype(f32) for h in range(skip_ref.shape[0])], axis=1).astype(bf16)
        after = dot(pooled_ref[...], skip_s[...], NT) + vec_ref[0:1, :]
        wide = out_ref.shape[2]
        for h in range(out_ref.shape[0]):
            after = after + dot(comb_ref[:, wide * h:wide * h + wide], out_ref[h], NT)
        after_s[...] = after
        unit, _ = norm(after)
        low = (unit * vec_ref[1:2, :] + vec_ref[2:3, :]).astype(bf16)
        low_s[...] = low
        lowt_s[...] = transposed(low)
        cott_s[...] = transposed(cot_ref[...])
        sum_s[...] = after + vec_ref[3:4, :]
        dlow_s[...] = jnp.zeros_like(dlow_s)

    pre = dot(low_s[...], up_ref[0]) + ub_ref[...]
    hidden, slope = gelu_both(pre)
    hidden = hidden.astype(bf16)
    dpre = dot(cot_ref[...], down_ref[0]) * slope
    gub_ref[...] = sum_rows(dpre)
    dpre = dpre.astype(bf16)
    sum_s[...] += dot(hidden, down_ref[0], NT)
    dlow_s[...] += dot(dpre, up_ref[0], NT)
    for n, grad in enumerate((dot(lowt_s[...], dpre), dot(cott_s[...], hidden))):
        rows = gmlp_ref.shape[3]
        for t in range(gmlp_ref.shape[1]):
            gmlp_ref[0, t, n] = grad[t * rows:(t + 1) * rows].astype(bf16)

    @pl.when(step == pl.num_programs(0) - 1)
    def _():
        mixed_ref[...] = sum_s[...].astype(bf16)
        unit, inverse = norm(after_s[...])
        dlow = dlow_s[...]
        cot = cot_ref[...].astype(f32)
        res = norm_back(unit, inverse, vec_ref[1:2, :], dlow) + cot
        row_ref[...] = jnp.zeros_like(row_ref)
        for i, row in enumerate((res, dlow, cot, dlow * unit)):
            row_ref[i:i + 1, :] = sum_rows(row)
        res = res.astype(bf16)
        dskip_ref[...] = dot(res, skip_s[...])
        rest = transposed(res)
        wide = out_ref.shape[2]
        for h in range(out_ref.shape[0]):
            here = slice(wide * h, wide * h + wide)
            dcomb_ref[:, here] = dot(res, out_ref[h]).astype(bf16)
            grad = dot(rest, comb_ref[:, here])
            half = gout_ref.shape[2]
            for n in range(2 * gout_ref.shape[1]):
                gout_ref[h, n // 2, :, wide * (n % 2):wide * (n % 2) + wide] = grad[half * n:half * n + half].astype(bf16)
        grad = dot(rest, pooled_ref[...])
        wide = gskip_ref.shape[3] // 2
        for h in range(gskip_ref.shape[0]):
            for t in range(gskip_ref.shape[1]):
                low, high = (grad[half * n:half * n + half, wide * h:wide * h + wide] for n in (2 * t, 2 * t + 1))
                gskip_ref[h, t] = jnp.concatenate([low, high], axis=1).astype(bf16)


def first_back_kernel(
    middle_ref, after_ref, comb_ref, dskip_ref, dq_ref, own_ref, mem_ref, out_ref, up_ref, down_ref, ub_ref, vec_ref,
    unpool_ref, unpair_ref,
    res_ref, dcomb_ref, gmlp_ref, gub_ref, row_ref,
    gup_s, gdown_s, gout_s, out_s,
):
    step = pl.program_id(0)

    @pl.when(step == 0)
    def _():
        gup_s[...] = jnp.zeros_like(gup_s)
        gdown_s[...] = jnp.zeros_like(gdown_s)
        gout_s[...] = jnp.zeros_like(gout_s)
        gub_ref[...] = jnp.zeros_like(gub_ref)
        assemble_out(out_ref, out_s)

    dpool = dskip_ref[0] + dq_ref[0] + own_ref[0] + exact_dot(unpair_ref[...], mem_ref[0])
    dnorm = exact_dot(unpool_ref[...], dpool)
    unit, inverse = norm(middle_ref[0])
    grad = norm_back(unit, inverse, vec_ref[2:3, :], dnorm)
    rows = [sum_rows(dnorm * unit), sum_rows(dnorm), sum_rows(grad)]
    low = grad.astype(bf16)
    lowt = transposed(low)
    unit, inverse = norm(after_ref[0])
    normed = (unit * vec_ref[0:1, :] + vec_ref[1:2, :]).astype(bf16)
    normedt = transposed(normed)
    dnormed = None
    for h in range(up_ref.shape[0]):
        hidden, slope = gelu_both(dot(normed, up_ref[h]) + ub_ref[h])
        hidden = hidden.astype(bf16)
        dpre = dot(low, down_ref[h]) * slope
        gub_ref[h] += sum_rows(dpre)
        dpre = dpre.astype(bf16)
        gdown_s[h] += dot(lowt, hidden)
        gup_s[h] += dot(normedt, dpre)
        add = dot(dpre, up_ref[h], NT)
        dnormed = add if dnormed is None else dnormed + add
    res = norm_back(unit, inverse, vec_ref[0:1, :], dnormed) + grad
    rows += [sum_rows(dnormed * unit), sum_rows(dnormed), sum_rows(res)]
    res_ref[0] = res
    res = res.astype(bf16)
    dcomb_ref[0] = dot(res, out_s[...]).astype(bf16)
    gout_s[...] += dot(transposed(res), comb_ref[0])
    add_rows(row_ref, rows)

    @pl.when(step == pl.num_programs(0) - 1)
    def _():
        fa, ha = gup_s.shape[2], gout_s.shape[1] // gmlp_ref.shape[0]
        for h in range(gmlp_ref.shape[0]):
            gmlp_ref[h, :, :fa] = gup_s[h].astype(bf16)
            gmlp_ref[h, :, fa:2 * fa] = gdown_s[h].astype(bf16)
            rest = gmlp_ref.shape[2] - 2 * fa - ha
            gout = jnp.concatenate([gout_s[:, ha * h:ha * h + ha], jnp.zeros((gout_s.shape[0], rest), f32)], axis=1)
            gmlp_ref[h, :, 2 * fa:] = gout.astype(bf16)


def last_back_kernel(x_ref, res_ref, dx_ref, own_ref, mem_ref, vec_ref, unpool_ref, unpair_ref, grad_ref, row_ref):
    dpool = own_ref[0] + exact_dot(unpair_ref[...], mem_ref[0])
    dnorm = dx_ref[0] + exact_dot(unpool_ref[...], dpool)
    unit, inverse = norm(x_ref[0].astype(f32))
    grad = norm_back(unit, inverse, vec_ref[0:1, :], dnorm) + res_ref[0]
    for f in range(grad_ref.shape[1]):
        grad_ref[0, f] = grad[PATCH * f:PATCH * f + PATCH].astype(bf16)
    add_rows(row_ref, [sum_rows(dnorm * unit), sum_rows(dnorm)])


def whole(array):
    return pl.BlockSpec(array.shape, lambda i: (0,) * array.ndim)


def by_micro(array, axis=0):
    block = array.shape[:axis] + (1,) + array.shape[axis + 1:]
    return pl.BlockSpec(block, lambda i: (0,) * axis + (i,) + (0,) * (array.ndim - axis - 1))


def shape(dims, dtype):
    return jax.ShapeDtypeStruct(dims, dtype)


def about(us):
    return pl.CostEstimate(flops=int(us * 1e9), bytes_accessed=0, transcendentals=0)


def call(kernel, steps, args, outs, scratch=(), name=None, us=10):
    def spec(array, how):
        if how is None:
            return whole(array)
        return by_micro(array, how) if isinstance(how, int) else how

    return pl.pallas_call(
        kernel,
        grid=(steps,),
        in_specs=[spec(a, how) for a, how in args],
        out_specs=[spec(a, how) for a, how in outs],
        out_shape=[a for a, _ in outs],
        scratch_shapes=[pltpu.VMEM(dims, dtype) for dims, dtype in scratch],
        compiler_params=pltpu.CompilerParams(vmem_limit_bytes=VMEM_CAP),
        cost_estimate=about(us),
        name=name,
    )(*[a for a, _ in args])


def chunk_of(nq):
    return 112 if nq % 112 == 0 else 16


def attend(x, own, mem, w, qv, has, valid, width):
    batches, nq, d = x.shape
    keys = own.shape[0] * own.shape[2] + mem.shape[0] * mem.shape[2]
    return call(
        functools.partial(attend_kernel, chunk_of(nq), valid), batches,
        [(x, 0), (own, 1), (mem, 1), w, (qv, None), (has, pl.BlockSpec(memory_space=pltpu.SMEM))],
        [(shape((batches, nq, width), bf16), 0), (shape((batches, nq, 128), f32), 0)],
        [((1, d, 1152 if width == 384 else 128), bf16),
         ((keys, d), bf16), ((nq, width), bf16), ((keys, width), bf16), ((keys, width), bf16), ((nq, keys), f32), ((nq, keys), bf16)],
        name="attend", us=20,
    )


def attend_back(x, grad, own, mem, w, qv, has, valid, lse, heads):
    batches, nq, d = x.shape
    width = grad.shape[2]
    keys = own.shape[0] * own.shape[2] + mem.shape[0] * mem.shape[2]
    both = (own.shape[0], batches, own.shape[2] + mem.shape[2], d)
    groups = (width // 384, d, 1152)
    return call(
        functools.partial(attend_back_kernel, chunk_of(nq), valid), batches,
        [(x, 0), (grad, 0), (own, 1), (mem, 1), w, (qv, None), (has, pl.BlockSpec(memory_space=pltpu.SMEM)), (lse, 0)],
        [(shape((batches, nq, d), f32), 0), (shape(both, bf16), 1), (shape((heads, d, 3 * width // heads), bf16), None), (shape((8, width), f32), None)],
        [((1, d, 1152 if width == 384 else 128), bf16),
         ((keys, d), bf16), ((nq, width), bf16), ((keys, width), bf16), ((keys, width), bf16),
         ((nq, keys), f32), ((nq, keys), f32), ((nq, keys), bf16), ((nq, keys), bf16),
         ((384, keys), f32), ((384, keys), f32), ((8, 128), f32), (groups, f32)],
        name="attend_back", us=36,
    )


MESH = pl.DeviceIdType.MESH


def places():
    tok, toks = lax.axis_index("tok"), lax.axis_size("tok")
    return lax.axis_index("clip"), lax.axis_index("head"), tok // 2, tok % 2, toks // 2


def greet(copies_to_me, i_copy_to):
    barrier = pltpu.get_barrier_semaphore()
    for device, condition in copies_to_me:
        if condition is None:
            pl.semaphore_signal(barrier, inc=1, device_id=device, device_id_type=MESH)
        else:
            @pl.when(condition)
            def _():
                pl.semaphore_signal(barrier, inc=1, device_id=device, device_id_type=MESH)
    count = 0
    for _, condition in i_copy_to:
        count = count + (1 if condition is None else jnp.where(condition, 1, 0))
    pl.semaphore_wait(barrier, count)


def remote(src, dst, send, recv, device):
    return pltpu.make_async_remote_copy(
        src_ref=src, dst_ref=dst, send_sem=send, recv_sem=recv, device_id=device, device_id_type=MESH
    )


def rem(a, n):
    return lax.rem(a + n, n)


class Chain:
    def __init__(self, part_s, outer_s, inner_s, pieces, in_send, in_recv, mid_send, mid_recv, out_send, out_recv):
        self.clip, clips = lax.axis_index("clip"), lax.axis_size("clip")
        clip = self.clip
        left = clip < clips // 2
        inner, outer = jnp.where(left, clip + 1, clip - 1), jnp.where(left, clip - 1, clip + 1)
        self.inner, self.outer = {"clip": inner}, {"clip": outer}
        self.end = (clip == 0) | (clip == clips - 1)
        self.middle = (clip == clips // 2 - 1) | (clip == clips // 2)
        self.part, self.from_outer, self.from_inner, self.pieces = part_s, outer_s, inner_s, pieces
        self.inward = [remote(part_s.at[p], outer_s.at[p], in_send.at[n], in_recv.at[n], self.inner) for n, p in enumerate(pieces)]
        self.across = [remote(part_s.at[p], inner_s.at[p], mid_send.at[n], mid_recv.at[n], self.inner) for n, p in enumerate(pieces)]
        self.outward = [remote(inner_s.at[p], inner_s.at[p], out_send.at[n], out_recv.at[n], self.outer) for n, p in enumerate(pieces)]

    def greets(self):
        both = [(self.inner, None), (self.outer, jnp.logical_not(self.end))]
        return both

    def send_ends(self, n):
        @pl.when(self.end & jnp.logical_not(self.middle))
        def _():
            self.inward[n].start()

    def send_parts(self, n):
        here = self.pieces[n]

        @pl.when(jnp.logical_not(self.end))
        def _():
            self.inward[n].wait_recv()
            self.part[here] = (self.part[here].astype(f32) + self.from_outer[here].astype(f32)).astype(bf16)

        @pl.when(jnp.logical_not(self.end) & jnp.logical_not(self.middle))
        def _():
            self.inward[n].start()

        @pl.when(self.middle)
        def _():
            self.across[n].start()

    def totals(self, n):
        here = self.pieces[n]

        @pl.when(self.middle)
        def _():
            self.across[n].wait_recv()
            self.across[n].wait_send()
            self.from_inner[here] = (self.part[here].astype(f32) + self.from_inner[here].astype(f32)).astype(bf16)

        @pl.when(jnp.logical_not(self.middle))
        def _():
            self.inward[n].wait_send()
            self.outward[n].wait_recv()

        @pl.when(jnp.logical_not(self.end))
        def _():
            self.outward[n].start()

    def close(self):
        @pl.when(jnp.logical_not(self.end))
        def _():
            for copy in self.outward:
                copy.wait_send()


def chain_scratch(buffer, pieces):
    return [pltpu.VMEM(buffer, bf16)] * 3 + [dma(pieces)] * 6


def share_kernel(gather, *refs):
    if gather:
        pooled_ref, mean_ref, pick_ref, w_ref, *refs = refs
        biases, (own_ref, mem_ref, all_ref, *refs) = refs[:4], refs[4:]
        (qv_a_ref, qv_b_ref, ub_a_ref, ub_b_ref), refs = refs[:4], refs[4:]
    else:
        pooled_ref, mean_ref, pick_ref, own_ref, mem_ref, *refs = refs
    (got_s, pick_s, local_sem, own_send, own_recv, mem_send, mem_recv, pass_send, pass_recv, clip_send, clip_recv, *refs) = refs
    clip, head, chip, core, chips = places()
    clips, heads = lax.axis_size("clip"), lax.axis_size("head")
    share = pooled_ref.shape[0]
    here = 2 * chip + core
    partner = {"tok": 2 * chip + 1 - core}
    across = [{"tok": 2 * rem(chip + k, chips) + core} for k in range(1, chips)]
    beside = [{"head": rem(head + d, heads)} for d in range(1, heads)]
    heads_of = lambda by, sign: [{"clip": clip + by, "head": rem(head + sign * d, heads)} for d in range(heads)]
    last, begun = clip < clips - 1, clip > 0
    near = [(d, None) for d in [partner] + across + (beside if gather else [])]
    greet(near + [(d, begun) for d in heads_of(-1, -1)], near + [(d, last) for d in heads_of(1, 1)])

    def spread(src, out, send, recv):
        copies = [remote(src, out.at[here], send.at[0], recv.at[0], partner)]
        copies += [remote(src, out.at[here], send.at[k + 1], recv.at[k + 1], across[k]) for k in range(chips - 1)]
        return copies

    def passed(out, k, row):
        block = 2 * rem(chip - k, chips) + core
        return remote(out.at[block], out.at[block], pass_send.at[row, k - 1], pass_recv.at[row, k - 1], partner)

    clip_copies = [remote(mean_ref, got_s.at[d], clip_send.at[d], clip_recv.at[d], device) for d, device in enumerate(heads_of(1, 1))]

    @pl.when(last)
    def _():
        for copy in clip_copies:
            copy.start()

    w_first, w_diagonal, w_core = {}, {}, {}
    if gather:
        w_local, w_send, w_recv, d_send, d_recv, c_send, c_recv, b_send, b_recv, *bias_got = refs
        bias_copies = [
            remote(ref, got.at[d], b_send.at[d, n], b_recv.at[d, n], device)
            for d, device in enumerate(beside)
            for n, (ref, got) in enumerate(zip(biases, bias_got))
        ]
        for copy in bias_copies:
            copy.start()
        mine = all_ref.at[head, here]
        for k in range(1, chips):
            w_first[k, 0] = remote(w_ref, mine, w_send.at[k - 1], w_recv.at[k - 1], across[k - 1])
        for d in range(1, heads):
            w_first[0, d] = remote(w_ref, mine, w_send.at[chips - 2 + d], w_recv.at[chips - 2 + d], beside[d - 1])
        w_core[0, 0] = remote(w_ref, mine, c_send.at[0, 0], c_recv.at[0, 0], partner)
        for copy in [*w_first.values(), w_core[0, 0]]:
            copy.start()
        w_copy = pltpu.make_async_copy(w_ref, mine, w_local.at[0])
        w_copy.start()

        def forward(k, d):
            block = all_ref.at[rem(head - d, heads), 2 * rem(chip - k, chips) + core]
            w_core[k, d] = remote(block, block, c_send.at[k, d], c_recv.at[k, d], partner)
            w_core[k, d].start()

    own_copies = spread(pooled_ref, own_ref, own_send, own_recv)
    for copy in own_copies[1:] + own_copies[:1]:
        copy.start()
    own_local = pltpu.make_async_copy(pooled_ref, own_ref.at[here], local_sem.at[0])
    own_local.start()
    if gather:
        for k in range(1, chips):
            w_first[k, 0].wait_recv()
            block = all_ref.at[head, 2 * rem(chip - k, chips) + core]
            for d in range(1, heads):
                w_diagonal[k, d] = remote(block, block, d_send.at[k - 1, d - 1], d_recv.at[k - 1, d - 1], beside[d - 1])
                w_diagonal[k, d].start()
            forward(k, 0)

    @pl.when(begun)
    def _():
        for copy in clip_copies:
            copy.wait_recv()
        for m in range(share):
            total = None
            for d in range(heads):
                for s in range(share):
                    piece = got_s[d, s].astype(f32) * pick_ref[m, d * share + s]
                    total = piece if total is None else total + piece
            pick_s[m] = total.astype(bf16)

    @pl.when(jnp.logical_not(begun))
    def _():
        pick_s[...] = jnp.zeros_like(pick_s)

    mem_copies = spread(pick_s, mem_ref, mem_send, mem_recv)
    for copy in mem_copies[1:] + mem_copies[:1]:
        copy.start()
    mem_local = pltpu.make_async_copy(pick_s, mem_ref.at[here], local_sem.at[1])
    mem_local.start()
    forwards = []
    for k in range(1, chips):
        own_copies[k].wait_recv()
        forwards.append(passed(own_ref, k, 0))
        forwards[-1].start()
    if gather:
        for d in range(1, heads):
            w_first[0, d].wait_recv()
            forward(0, d)
    for k in range(1, chips):
        mem_copies[k].wait_recv()
        forwards.append(passed(mem_ref, k, 1))
        forwards[-1].start()
    if gather:
        for k, d in w_diagonal:
            w_diagonal[k, d].wait_recv()
            forward(k, d)
        for copy in w_core.values():
            copy.wait_recv()
        for copy in bias_copies:
            copy.wait_recv()
        by_head = []
        for ref, got in zip(biases, bias_got):
            pieces = []
            for h in range(heads):
                piece = ref[...]
                for d in range(1, heads):
                    piece = jnp.where(rem(head - d, heads) == h, got[d - 1], piece)
                pieces.append(piece)
            by_head.append(pieces)
        qv_a_ref[...] = jnp.concatenate(by_head[0], axis=1)
        qv_b_ref[...] = jnp.concatenate(by_head[1], axis=1)
        for h in range(heads):
            ub_a_ref[h] = by_head[2][h]
        ub_b_ref[...] = jnp.concatenate(by_head[3], axis=1)
        for copy in bias_copies:
            copy.wait_send()
    own_copies[0].wait_recv()
    mem_copies[0].wait_recv()
    for copy in forwards:
        copy.wait_recv()
    for copy in own_copies + mem_copies + forwards + [*w_first.values(), *w_diagonal.values(), *w_core.values()]:
        copy.wait_send()
    own_local.wait()
    mem_local.wait()
    if gather:
        w_copy.wait()

    @pl.when(last)
    def _():
        for copy in clip_copies:
            copy.wait_send()


ANY = pl.BlockSpec(memory_space=pl.ANY)
INVMEM = pl.BlockSpec(memory_space=pltpu.VMEM)
INSMEM = pl.BlockSpec(memory_space=pltpu.SMEM)


def dma(*dims):
    return pltpu.SemaphoreType.DMA(dims)


def share_pooled(pooled, mean, pick, number, block=None, biases=()):
    toks, heads = lax.axis_size("tok"), lax.axis_size("head")
    chips = toks // 2
    few = max(chips - 1, 1)
    args, specs = [pooled, mean, pick], [INVMEM, INVMEM, INSMEM]
    outs = [shape((toks,) + pooled.shape, bf16), shape((toks,) + mean.shape, bf16)]
    scratch = [
        pltpu.VMEM((heads,) + mean.shape, bf16), pltpu.VMEM(mean.shape, bf16), dma(2),
        dma(chips), dma(chips), dma(chips), dma(chips), dma(2, few), dma(2, few), dma(heads), dma(heads),
    ]
    if block is not None:
        args, specs = args + [block, *biases], specs + [ANY] + [INVMEM] * len(biases)
        (_, wa), (_, wb), (_, fa), (_, fb) = (b.shape for b in biases)
        outs = outs + [shape((heads, toks) + block.shape, bf16)]
        outs += [shape(dims, f32) for dims in ((2, heads * wa), (2, heads * wb), (heads, 1, fa), (1, heads * fb))]
        firsts = max(chips + heads - 2, 1)
        scratch += [dma(1), dma(firsts), dma(firsts), dma(few, max(heads - 1, 1)), dma(few, max(heads - 1, 1)), dma(chips, heads), dma(chips, heads)]
        scratch += [dma(max(heads - 1, 1), 4), dma(max(heads - 1, 1), 4)]
        scratch += [pltpu.VMEM((max(heads - 1, 1),) + b.shape, f32) for b in biases]
    return pl.pallas_call(
        functools.partial(share_kernel, block is not None),
        in_specs=specs,
        out_specs=[ANY] * min(len(outs), 3) + [INVMEM] * (len(outs) - 3),
        out_shape=outs,
        scratch_shapes=scratch,
        compiler_params=pltpu.CompilerParams(collective_id=number, has_side_effects=True, vmem_limit_bytes=VMEM_CAP),
        cost_estimate=about(20 if block is None else 30),
        name="share_pooled",
    )(*args)


def give_back_kernel(exchange, *refs):
    if exchange:
        part_ref, pick_ref, half_ref, shard_ref, own_ref, back_ref, all_ref, up_ref, down_ref, *refs = refs
        refs, (half_local, half_send, half_recv), chain = refs[:-12], refs[-12:-9], refs[-9:]
        depth = chain[-1].shape[0]
        rows_each = shard_ref.shape[0] // depth
        chain = Chain(*chain[:3], [(pl.ds(rows_each * n, rows_each), slice(None)) for n in range(depth)], *chain[3:])
    else:
        part_ref, pick_ref, own_ref, back_ref, *refs = refs
    (mine_s, core_s, sum_s, chip_s, route_s, got_s,
     local_sem, core_send, core_recv, mem_send, mem_recv, own_send, own_recv, clip_send, clip_recv) = refs
    clip, head, chip, core, chips = places()
    clips, heads = lax.axis_size("clip"), lax.axis_size("head")
    share, rows = own_ref.shape[0], own_ref.shape[1]
    partner = {"tok": 2 * chip + 1 - core}
    across = [{"tok": 2 * rem(chip + k, chips) + core} for k in range(1, chips)]
    beside = [{"head": rem(head + d, heads)} for d in range(1, heads)]
    heads_of = lambda by, sign: [{"clip": clip + by, "head": rem(head + sign * d, heads)} for d in range(heads)]
    last, begun = clip < clips - 1, clip > 0
    near = [(d, None) for d in [partner] + across + (beside if exchange else [])]
    near += chain.greets() if exchange else []
    greet(near + [(d, last) for d in heads_of(1, 1)], near + [(d, begun) for d in heads_of(-1, -1)])
    if exchange:
        chain.part[...] = shard_ref[...]
        for n in range(depth):
            chain.send_ends(n)

    order = [rem(chip + k, chips) for k in list(range(1, chips)) + [0]]
    core_copies, local_copies = [], []
    for n, other in enumerate(order):
        core_copies.append(remote(part_ref.at[2 * other + 1 - core], core_s.at[n], core_send.at[n], core_recv.at[n], partner))
        core_copies[-1].start()
    for n, other in enumerate(order):
        local_copies.append(pltpu.make_async_copy(part_ref.at[2 * other + core], mine_s.at[n], local_sem.at[n]))
        local_copies[-1].start()
    halves = []
    if exchange:
        halves = [remote(half_ref, all_ref.at[head], half_send.at[k], half_recv.at[k], d) for k, d in enumerate(beside)]
        for copy in halves:
            copy.start()
        half_copy = pltpu.make_async_copy(half_ref, all_ref.at[head], half_local.at[0])
        half_copy.start()
    mem_copies, own_copies = [], []
    for n in range(chips):
        local_copies[n].wait()
        core_copies[n].wait_recv()
        if n == chips - 1:
            break
        sum_s[n] = (mine_s[n].astype(f32) + core_s[n].astype(f32)).astype(bf16)
        low, high = pl.ds(0, rows), pl.ds(rows, sum_s.shape[2] - rows)
        mem_copies.append(remote(sum_s.at[n, :, high, :], chip_s.at[n, :, high, :], mem_send.at[n], mem_recv.at[n], across[n]))
        mem_copies[-1].start()
        own_copies.append(remote(sum_s.at[n, :, low, :], chip_s.at[n, :, low, :], own_send.at[n], own_recv.at[n], across[n]))
        own_copies[-1].start()
    base = chips - 1
    for copy in mem_copies:
        copy.wait_recv()
    memory = []
    for m in range(share):
        total = mine_s[base, m, rows:].astype(f32) + core_s[base, m, rows:].astype(f32)
        for n in range(chips - 1):
            total = total + chip_s[n, m, rows:].astype(f32)
        memory.append(total)
    clip_copies = [
        remote(route_s.at[d], got_s.at[d], clip_send.at[d], clip_recv.at[d], device) for d, device in enumerate(heads_of(-1, -1))
    ]

    @pl.when(begun)
    def _():
        for d in range(heads):
            for s in range(share):
                total = None
                for m in range(share):
                    piece = memory[m] * pick_ref[m, d * share + s]
                    total = piece if total is None else total + piece
                route_s[d, s] = total.astype(bf16)
            clip_copies[d].start()

    for copy in own_copies:
        copy.wait_recv()
    for m in range(share):
        total = mine_s[base, m, :rows].astype(f32) + core_s[base, m, :rows].astype(f32)
        for n in range(chips - 1):
            total = total + chip_s[n, m, :rows].astype(f32)
        own_ref[m] = total

    @pl.when(last)
    def _():
        for copy in clip_copies:
            copy.wait_recv()
        total = got_s[0].astype(f32)
        for d in range(1, heads):
            total = total + got_s[d].astype(f32)
        back_ref[...] = total

    @pl.when(jnp.logical_not(last))
    def _():
        back_ref[...] = jnp.zeros_like(back_ref)

    if exchange:
        for n in range(depth):
            chain.send_parts(n)
            if n > 0:
                chain.totals(n - 1)
        chain.totals(depth - 1)
        total = chain.from_inner[...].astype(f32)
        up_ref[...] = total[:up_ref.shape[0]]
        down_ref[...] = total[up_ref.shape[0]:]
        chain.close()
    for copy in halves:
        copy.wait_recv()
    for copy in core_copies + mem_copies + own_copies + halves:
        copy.wait_send()
    if exchange:
        half_copy.wait()

    @pl.when(begun)
    def _():
        for copy in clip_copies:
            copy.wait_send()


def give_back(part, pick, own_rows, number, half=None, shard=None):
    toks, heads = lax.axis_size("tok"), lax.axis_size("head")
    chips, few = toks // 2, max(toks // 2 - 1, 1)
    share, rows, d = part.shape[1:]
    args, specs = [part, pick], [ANY, INSMEM]
    outs, out_specs = [shape((share, own_rows, d), f32), shape((share, rows - own_rows, d), f32)], [INVMEM, INVMEM]
    scratch = [
        pltpu.VMEM((chips,) + part.shape[1:], bf16), pltpu.VMEM((chips,) + part.shape[1:], bf16),
        pltpu.VMEM((few,) + part.shape[1:], bf16), pltpu.VMEM((few,) + part.shape[1:], bf16),
        pltpu.VMEM((heads, share, rows - own_rows, d), bf16), pltpu.VMEM((heads, share, rows - own_rows, d), bf16),
        dma(chips), dma(chips), dma(chips), dma(few), dma(few), dma(few), dma(few), dma(heads), dma(heads),
    ]
    if half is not None:
        pair, depth, lanes = shard.shape
        shard = shard.reshape(-1, lanes)
        args, specs = args + [half, shard], specs + [ANY, INVMEM]
        outs += [shape((heads,) + half.shape, half.dtype), shape((depth, lanes), f32), shape((depth, lanes), f32)]
        out_specs += [ANY, INVMEM, INVMEM]
        scratch += [dma(1), dma(max(heads - 1, 1)), dma(max(heads - 1, 1))]
        scratch += chain_scratch(shard.shape, shard.shape[0] // 48)
    return pl.pallas_call(
        functools.partial(give_back_kernel, half is not None),
        in_specs=specs,
        out_specs=out_specs,
        out_shape=outs,
        scratch_shapes=scratch,
        compiler_params=pltpu.CompilerParams(collective_id=number, has_side_effects=True, vmem_limit_bytes=VMEM_CAP),
        cost_estimate=about(25 if half is None else 35),
        name="give_back",
    )(*args)


def finish_kernel(sizes, half_ref, last_ref, qv_a_rows, a_ref, b_ref, qv_b_rows, ub_a_rows, ub_b_rows, grad_ref, rest_ref, group_ref, all_ref, gains_a_ref, gains_b_ref, shifts_a_ref,
                  shifts_b_ref, qv_a_ref, qv_b_ref, ub_a_ref, ub_b_ref, gtotal_ref, up_ref, down_ref, out_ref,
                  q_ref, out_b_ref, skip_ref, *scratch):
    (small_ref, small_s, small_core, small_chip, small_head, small_clip, part_s, part_core, chip_s, part_chip, part_head,
     local_sem, half_send, half_recv, core_send, core_recv, chip_send, chip_recv, head_send, head_recv,
     clip_send, clip_recv, *chain) = scratch
    first_lanes, next_lanes, deep = group_ref.shape[1], rest_ref.shape[1], grad_ref.shape[1]
    bounds = [0, first_lanes // 2, first_lanes, first_lanes + next_lanes // 2, first_lanes + next_lanes, chain[0].shape[1]]
    chain = Chain(*chain[:3], [(slice(None), pl.ds(low, high - low)) for low, high in zip(bounds, bounds[1:])], *chain[3:])
    clip, head, chip, core, chips = places()
    clips, heads = lax.axis_size("clip"), lax.axis_size("head")
    share = half_ref.shape[0]
    partner = {"tok": 2 * chip + 1 - core}
    across = [{"tok": 2 * rem(chip + k, chips) + core} for k in range(1, chips)]
    beside = [{"head": rem(head + k, heads)} for k in range(1, heads)]
    along = [{"clip": rem(clip + k, clips)} for k in range(1, clips)]
    peers = [(d, None) for d in [partner] + across + beside + along]
    greet(peers, peers)
    chain.part[:, :first_lanes] = group_ref[...]
    chain.part[:, first_lanes:first_lanes + next_lanes] = rest_ref[...]
    for n in range(4):
        chain.send_ends(n)
    pending = []
    d1 = small_ref.shape[1]
    small_ref[...] = jnp.zeros_like(small_ref)
    small_ref[0:2, :] = last_ref[0:2, :]
    small_ref[2:4, :] = qv_a_rows[0:2, :]
    for row, source in enumerate((3, 0, 5, 4, 2, 1)):
        small_ref[4 + row:5 + row, :] = a_ref[source:source + 1, :]
    row = 10
    longer = [b_ref[n:n + 1, :] for n in (3, 0, 1, 2)] + [qv_b_rows[n:n + 1, :] for n in range(2)]
    for values in longer + [ub_a_rows[h] for h in range(heads)] + [ub_b_rows[...]]:
        for low in range(0, values.shape[1], d1):
            small_ref[row:row + 1, :] = values[:, low:low + d1]
            row += 1
    def go(copies):
        for copy in copies:
            copy.start()
        pending.extend(copies)
        return copies

    def arrived(copies):
        for copy in copies:
            copy.wait_recv()

    def in_order(index, size, own, slot):
        total = None
        for i in range(size):
            piece = jnp.where(index == i, own, jnp.zeros_like(own))
            for k in range(size - 1):
                piece = jnp.where(rem(index - k - 1, size) == i, slot(k), piece)
            total = piece if total is None else total + piece
        return total

    first = go([remote(small_ref, small_core, core_send.at[0], core_recv.at[0], partner)])
    for h in range(heads):
        for x in range(chips):
            n = h * chips + x
            first += go([remote(grad_ref.at[2 * n + 1 - core], part_core.at[n], core_send.at[n + 1], core_recv.at[n + 1], partner)])
    halves = [
        [remote(half_ref.at[s], all_ref.at[head, s], half_send.at[k, s], half_recv.at[k, s], d) for k, d in enumerate(beside)]
        for s in range(share)
    ]
    for s in range(share - 1):
        go(halves[s])
    local_half = pltpu.make_async_copy(half_ref, all_ref.at[head], local_sem.at[0])
    local_half.start()
    arrived(first)
    small_s[0] = small_ref[...] + small_core[...]
    for n in range(heads * chips):
        part_s[n] = (grad_ref[2 * n + core].astype(f32) + part_core[n].astype(f32)).astype(bf16)
    copies = []
    for k, d in enumerate(across):
        copies += go([remote(small_s.at[0], small_chip.at[k], chip_send.at[k, 0], chip_recv.at[k, 0], d)])
        for h in range(heads):
            block = h * chips + rem(chip + k + 1, chips)
            copies += go([remote(part_s.at[block], part_chip.at[k, h], chip_send.at[k, h + 1], chip_recv.at[k, h + 1], d)])
    arrived(copies)
    small_s[1] = in_order(chip, chips, small_s[0], lambda k: small_chip[k])
    for h in range(heads):
        total = part_s[h * chips + chip].astype(f32)
        for k in range(chips - 1):
            total = total + part_chip[k, h].astype(f32)
        chip_s[h] = total.astype(bf16)
    copies = []
    for k, d in enumerate(beside):
        copies += go([remote(small_s.at[1], small_head.at[k], head_send.at[k, 0], head_recv.at[k, 0], d)])
        copies += go([remote(chip_s.at[rem(head + k + 1, heads)], part_head.at[k], head_send.at[k, 1], head_recv.at[k, 1], d)])
    go(halves[share - 1])
    for n in range(4):
        chain.send_parts(n)
    arrived(copies)
    small_s[2] = in_order(head, heads, small_s[1], lambda k: small_head[k])
    total = chip_s[head].astype(f32)
    for k in range(heads - 1):
        total = total + part_head[k].astype(f32)
    mine = first_lanes + next_lanes
    chain.part[:, mine:mine + grad_ref.shape[2]] = total.astype(bf16)
    copies = []
    for k, d in enumerate(along):
        copies += go([remote(small_s.at[2], small_clip.at[k], clip_send.at[k, 0], clip_recv.at[k, 0], d)])
    chain.send_ends(4)
    chain.totals(0)
    chain.totals(1)
    chain.send_parts(4)
    for n in range(2, 5):
        chain.totals(n)
    arrived(copies)
    total = in_order(clip, clips, small_s[2], lambda k: small_clip[k])
    at = [4]

    def rows(width):
        first = at[0]
        at[0] += width // total.shape[1]
        return jnp.concatenate([total[r:r + 1] for r in range(first, at[0])], axis=1)

    def share_of(row):
        width = row.shape[1] // heads
        piece = row[:, :width]
        for h in range(1, heads):
            piece = jnp.where(head == h, row[:, width * h:width * h + width], piece)
        return piece

    gains_a_ref[0:1, :] = total[0:1]
    gains_a_ref[1:3, :] = total[4:6]
    shifts_a_ref[0:1, :] = total[1:2]
    shifts_a_ref[1:5, :] = total[6:10]
    qv_a_ref[0:1, :] = share_of(total[2:3])
    qv_a_ref[1:2, :] = share_of(total[3:4])
    at[0] = 10
    d2, fa, fb = sizes
    gains_b_ref[...] = rows(d2)
    for i in range(3):
        shifts_b_ref[i:i + 1, :] = rows(d2)
    for i in range(2):
        qv_b_ref[i:i + 1, :] = share_of(rows(d2))
    ub_a_ref[...] = share_of(rows(fa))
    ub_b_ref[...] = share_of(rows(fb))
    wide = up_ref.shape[1]
    sums = chain.from_inner
    for ref, low in ((q_ref, 0), (up_ref, first_lanes), (down_ref, first_lanes + wide), (out_ref, first_lanes + 2 * wide), (gtotal_ref, mine)):
        ref[...] = sums[:, low:low + ref.shape[1]].astype(f32)
    low, rows = q_ref.shape[1], q_ref.shape[0]
    for ref in (out_b_ref, skip_ref):
        for n in range(2):
            ref[rows * n:rows * n + rows, :] = sums[:, low:low + ref.shape[1]].astype(f32)
            low += ref.shape[1]
    chain.close()
    for copies in halves:
        arrived(copies)
    for copy in pending:
        copy.wait_send()
    local_half.wait()


def finish(half, rows, grad, rest, first, d2, fa, fb, ha, hs, number):
    toks, heads, clips = lax.axis_size("tok"), lax.axis_size("head"), lax.axis_size("clip")
    chips = toks // 2
    across, beside, along = (max(n, 1) for n in (chips - 1, heads - 1, clips - 1))
    block, depth, d1 = grad.shape[1:], rest.shape[0], rows[0].shape[1]
    count = 4 + 6 + (6 * d2 + fa + fb) // d1
    low, full = lambda *dims: pltpu.VMEM(dims, bf16), lambda *dims: pltpu.VMEM(dims + (-(-count // 8) * 8, d1), f32)
    sums = [(3, d1), (1, d2), (5, d1), (3, d2), (2, d1 // heads), (2, d2 // heads), (1, fa // heads), (1, fb // heads),
            block, (depth, fa // heads), (depth, fa // heads), (depth, ha),
            (depth, 3 * d2 // heads), (2 * depth, d2 // heads), (2 * depth, hs)]
    buffer = (depth, first.shape[1] + rest.shape[1] + -(-block[1] // 128) * 128)
    return pl.pallas_call(
        functools.partial(finish_kernel, (d2, fa, fb)),
        in_specs=[ANY] + [INVMEM] * (len(rows) + 3),
        out_specs=[ANY] + [INVMEM] * len(sums),
        out_shape=[shape((heads,) + half.shape, half.dtype)] + [shape(dims, f32) for dims in sums],
        scratch_shapes=[
            full(), full(3), full(), full(across), full(beside), full(along),
            low(heads * chips, *block), low(heads * chips, *block), low(heads, *block), low(across, heads, *block), low(beside, *block),
            dma(1), dma(beside, half.shape[0]), dma(beside, half.shape[0]), dma(heads * chips + 1), dma(heads * chips + 1),
            dma(across, heads + 1), dma(across, heads + 1), dma(beside, 2), dma(beside, 2), dma(along, 1), dma(along, 1),
            *chain_scratch(buffer, 5),
        ],
        compiler_params=pltpu.CompilerParams(collective_id=number, has_side_effects=True, vmem_limit_bytes=VMEM_CAP),
        cost_estimate=about(40),
        name="finish",
    )(half, *rows, grad, rest, first)


def padded_rows(*rows):
    return jnp.concatenate([jnp.stack(rows), jnp.zeros((-len(rows) % 8, rows[0].shape[0]), f32)])


def local(
    clips_in, resets, assign, w_qkv_a, w_out_a, w_up_a, w_down_a, w_qkv_b, w_out_b, w_skip_b, w_up_b, w_down_b,
    gains_a, gains_b, shifts_a, shifts_b, qv_bias_a, qv_bias_b, up_bias_a, up_bias_b, cotangent,
):
    heads, toks, clips = lax.axis_size("head"), lax.axis_size("tok"), lax.axis_size("clip")
    head = lax.axis_index("head")
    micro, frames = clips_in.shape[1], clips_in.shape[2]
    d1, d2 = clips_in.shape[-1], cotangent.shape[-1]
    share = micro // heads
    first = head * share
    pool_np, pair_np = pool_matrix(frames), pair_matrix(frames)
    pooling, pairing = jnp.asarray(pool_np, bf16), jnp.asarray(pair_np, bf16)
    unpooling, unpairing = jnp.asarray(pool_np.T, bf16), jnp.asarray(pair_np.T, bf16)
    tokens, pooled_tokens = frames * PATCH, frames * POOLED
    own_rows, mem_rows = up16(pooled_tokens), up16(frames // 2 * POOLED)
    rows2 = share * own_rows

    cot = lax.dynamic_slice_in_dim(cotangent[0], first, share, 0).reshape(share, pooled_tokens, d2)

    source = lax.dynamic_slice_in_dim(assign[0], first, share, 0)
    flags = lax.dynamic_slice_in_dim(resets[0], first, share, 0)
    slot = ((head - source // share + heads) % heads) * share + source % share
    pick = (jnp.arange(heads * share)[None, :] == slot[:, None]).astype(f32)
    has = ((flags == 0) & (lax.axis_index("clip") > 0)).astype(jnp.int32)
    valid = (pooled_tokens, frames // 2 * POOLED)

    group = ("head", "tok")
    fa, ha = w_up_a.shape[1], w_out_a.shape[1]
    fb, hb, hs = w_up_b.shape[1], w_out_b.shape[1], w_skip_b.shape[1]
    pack_a = jnp.concatenate([w_up_a, w_down_a, w_qkv_a.reshape(w_qkv_a.shape[0], -1), w_out_a], axis=1)
    all_a = lax.all_gather(pack_a, group).reshape(heads, d1, -1)
    mine = lax.dynamic_slice_in_dim(clips_in[0], first, share, 0)
    stream, low1, pooled1, mean1 = call(
        norm_pool_kernel, share,
        [(mine, 0), (padded_rows(gains_a[0], shifts_a[0]), None), (pooling, None), (pairing, None)],
        [(shape((share, tokens, d1), bf16), 0), (shape((share, tokens, d1), bf16), 0),
         (shape((share, own_rows, d1), bf16), 0), (shape((share, mem_rows, d1), bf16), 0)],
        name="norm_pool", us=5,
    )
    pooled1, w_qkv_b, w_up_b = lax.optimization_barrier((pooled1, w_qkv_b, w_up_b))
    pack_q = w_qkv_b.reshape(w_qkv_b.shape[0], -1)
    own1, mem1, all_q, qv_a, qv_b, ub_a, ub_b = share_pooled(
        pooled1, mean1, pick, 0, pack_q, [qv_bias_a, qv_bias_b, up_bias_a[None], up_bias_b[None]])
    all_q = all_q.reshape(heads, d1, -1)
    own1, w_up_b, cot = lax.optimization_barrier((own1, w_up_b, cot))
    spare = jnp.zeros((w_up_b.shape[0], -(2 * fb + hb + hs) % hb), bf16)
    pack_b = jnp.concatenate([w_up_b, w_down_b, w_out_b, w_skip_b, spare], axis=1)
    all_b = lax.all_gather(pack_b, group).reshape(heads, d2, -1)
    cot = jnp.pad(cot, ((0, 0), (0, own_rows - pooled_tokens), (0, 0))).reshape(rows2, d2)

    up_spec, down_spec, rest_spec = (pl.BlockSpec((heads, d1, fa), lambda i, n=n: (0, 0, n)) for n in range(3))

    comb1, lse1 = attend(low1, own1, mem1, (all_a, rest_spec), qv_a, has, valid, d1)
    after1, middle, pooled3, mean3 = call(
        first_mlp_kernel, share,
        [(stream, 0), (comb1, 0), (all_a, rest_spec), (all_a, up_spec), (all_a, down_spec), (ub_a, None),
         (padded_rows(shifts_a[1], gains_a[1], shifts_a[2], shifts_a[3], gains_a[2], shifts_a[4]), None),
         (pooling, None), (pairing, None)],
        [(shape((share, tokens, d1), f32), 0), (shape((share, tokens, d1), f32), 0),
         (shape((share, own_rows, d1), bf16), 0), (shape((share, mem_rows, d1), bf16), 0)],
        [((d1, d1), bf16)],
        name="first_mlp", us=13,
    )

    own2, mem2 = share_pooled(pooled3, mean3, pick, 1)
    comb2, lse2 = attend(pooled3, own2, mem2, (all_q, None), qv_b, has, valid, d2)
    chunk = 768
    per_head = fb // chunk
    steps = heads * per_head
    out_spec, skip_spec = (pl.BlockSpec((heads, d2, hb), lambda j, n=n: (0, 0, 2 * fb // hb + n)) for n in range(2))
    rows_spec = pl.BlockSpec((1, d2, chunk), lambda j: (j // per_head, 0, j % per_head))
    mixed, dcomb2, dskip, g_mlp_b, g_out_b, g_skip_b, g_ub_b, rows_b = call(
        second_mlp_kernel, steps,
        [(comb2.reshape(rows2, d2), None), (pooled3.reshape(rows2, d1), None), (cot, None), (all_b, out_spec), (all_b, skip_spec),
         (all_b, rows_spec),
         (all_b, pl.BlockSpec((1, d2, chunk), lambda j: (j // per_head, 0, per_head + j % per_head))),
         (ub_b, pl.BlockSpec((1, chunk), lambda j: (0, j))),
         (padded_rows(shifts_b[0], gains_b, shifts_b[1], shifts_b[2]), None)],
        [(shape((rows2, d2), bf16), None), (shape((rows2, d2), bf16), None), (shape((rows2, d1), f32), None),
         (shape((heads, toks, 2, d2 // toks, fb), bf16),
          pl.BlockSpec((1, toks, 2, d2 // toks, chunk), lambda j: (j // per_head, 0, 0, 0, j % per_head))),
         (shape((heads, toks, d2 // toks // 2, 2 * hb), bf16), None), (shape((heads, toks, d2 // toks // 2, 2 * hs), bf16), None),
         (shape((1, heads * fb), f32), pl.BlockSpec((1, chunk), lambda j: (0, j))), (shape((8, d2), f32), None)],
        [((rows2, d2), f32), ((rows2, d2), bf16), ((d2, rows2), bf16), ((d2, rows2), bf16), ((rows2, d2), f32), ((rows2, d2), f32), ((d2, d1), bf16)],
        name="second_mlp", us=26,
    )

    def by_owner(grad):
        return grad.reshape((heads * toks, -1) + grad.shape[2:])

    def scatter(grad):
        return lax.psum_scatter(grad, group, scatter_dimension=0, tiled=False)

    sum_mlp_b = scatter(g_mlp_b.reshape((heads * toks,) + g_mlp_b.shape[2:]))
    dcomb2 = dcomb2.reshape(share, own_rows, d2)
    dq2, dpool2, g_qkv_b, rows_qv_b = attend_back(pooled3, dcomb2, own2, mem2, (all_q, None), qv_b, has, valid, lse2, heads)
    own_back2, mem_back2 = give_back(dpool2, pick, own_rows, 2)

    merge = lambda grad: grad.reshape((heads * toks,) + grad.shape[2:])
    rest_b = jnp.concatenate([by_owner(g_qkv_b), merge(g_out_b), merge(g_skip_b)], axis=2)
    sum_rest_b = scatter(rest_b)

    res1, dcomb1, g_mlp_a, g_ub_a, rows_a = call(
        first_back_kernel, share,
        [(middle, 0), (after1, 0), (comb1, 0), (dskip.reshape(share, own_rows, d1), 0), (dq2, 0), (own_back2, 0), (mem_back2, 0),
         (all_a, rest_spec), (all_a, up_spec), (all_a, down_spec), (ub_a, None),
         (padded_rows(gains_a[1], shifts_a[2], gains_a[2]), None), (unpooling, None), (unpairing, None)],
        [(shape((share, tokens, d1), f32), 0), (shape((share, tokens, d1), bf16), 0),
         (shape((heads, d1, -(-(2 * fa + ha) // 256) * 256), bf16), None),
         (shape((heads, 1, fa), f32), None), (shape((8, d1), f32), None)],
        [((heads, d1, fa), f32), ((heads, d1, fa), f32), ((d1, d1), f32), ((d1, d1), bf16)],
        name="first_back", us=26,
    )
    rest_a = by_owner(g_mlp_a)
    sum_rest_a = scatter(rest_a)
    dx1, dpool1, g_qkv_a, rows_qv_a = attend_back(low1, dcomb1, own1, mem1, (all_a, rest_spec), qv_a, has, valid, lse1, heads)
    own_back1, mem_back1, mixed_all, grad_up_b, grad_down_b = give_back(
        dpool1, pick, own_rows, 3, mixed.reshape(share, own_rows, d2), sum_mlp_b)
    stream_grad, rows_last = call(
        last_back_kernel, share,
        [(stream, 0), (res1, 0), (dx1, 0), (own_back1, 0), (mem_back1, 0), (padded_rows(gains_a[0]), None),
         (unpooling, None), (unpairing, None)],
        [(shape((share, frames, PATCH, d1), bf16), 0), (shape((8, d1), f32), None)],
        name="last_back", us=6,
    )

    rows = [rows_last, rows_qv_a, rows_a, rows_b, rows_qv_b, g_ub_a, g_ub_b]
    stream_all, *sums = finish(
        stream_grad, rows, by_owner(g_qkv_a), sum_rest_a, sum_rest_b, d2, heads * fa, heads * fb, ha, hs, 4)
    mixed_all = mixed_all.reshape(micro, own_rows, d2)[:, :pooled_tokens]
    return (
        mixed_all.reshape(cotangent.shape),
        stream_all.astype(f32).reshape(clips_in.shape),
        sums[8].reshape(w_qkv_a.shape),
        sums[11],
        sums[9],
        sums[10],
        sums[12].reshape(w_qkv_b.shape),
        sums[13],
        sums[14],
        grad_up_b,
        grad_down_b,
        sums[0], sums[1][0], sums[2], sums[3], sums[4], sums[5], sums[6][0], sums[7][0],
    )


def solution(mesh):
    in_specs = (
        P("clip", None, "tok", None, None),
        P("clip", None),
        P("clip", None),
        P("tok", None, "head"),
        P("tok", "head"),
        P("tok", "head"),
        P("tok", "head"),
        P("tok", None, "head"),
        P("tok", "head"),
        P("tok", "head"),
        P("tok", "head"),
        P("tok", "head"),
        P(),
        P(),
        P(),
        P(),
        P(None, "head"),
        P(None, "head"),
        P("head"),
        P("head"),
        P("clip", None, "tok", None, None),
    )
    out_specs = (
        P("clip", None, "tok", None, None),
        P("clip", None, "tok", None, None),
        P("tok", None, "head"),
        P("tok", "head"),
        P("tok", "head"),
        P("tok", "head"),
        P("tok", None, "head"),
        P("tok", "head"),
        P("tok", "head"),
        P("tok", "head"),
        P("tok", "head"),
        P(),
        P(),
        P(),
        P(),
        P(None, "head"),
        P(None, "head"),
        P("head"),
        P("head"),
    )
    return jax.shard_map(local, mesh=mesh, in_specs=in_specs, out_specs=out_specs, check_vma=False)
```

```python
import functools
import math

import jax
import jax.numpy as jnp
import numpy as np
from jax import lax
from jax.experimental import pallas as pl
from jax.experimental.pallas import tpu as pltpu
from jax.sharding import PartitionSpec as P

GRID = 14
PATCH = GRID * GRID
POOLED = PATCH // 4
HD = 96
NEG = -1e30
VMEM_CAP = 62 * 2**20
eps = 1e-06
f32, bf16 = jnp.float32, jnp.bfloat16
NN, NT, TN = ((1,), (0,)), ((1,), (1,)), ((0,), (0,))


def up16(n):
    return -(-n // 16) * 16


def pool_matrix(frames):
    rows, cols = up16(frames * POOLED), frames * PATCH
    out = np.zeros((rows, cols), np.float32)
    half = GRID // 2
    for f in range(frames):
        for p in range(PATCH):
            r, c = divmod(p, GRID)
            out[((r // 2) * half + c // 2) * frames + f, p * frames + f] = 0.25
    return out


def pair_matrix(frames):
    rows, cols = up16(frames // 2 * POOLED), up16(frames * POOLED)
    out = np.zeros((rows, cols), np.float32)
    for j in range(frames // 2):
        for p in range(POOLED):
            out[p * (frames // 2) + j, p * frames + 2 * j] = 0.5
            out[p * (frames // 2) + j, p * frames + 2 * j + 1] = 0.5
    return out


MESH = pl.DeviceIdType.MESH


def places():
    tok, toks = lax.axis_index("tok"), lax.axis_size("tok")
    return lax.axis_index("clip"), lax.axis_index("head"), tok // 2, tok % 2, toks // 2


def greet(copies_to_me, i_copy_to):
    barrier = pltpu.get_barrier_semaphore()
    for device, condition in copies_to_me:
        if condition is None:
            pl.semaphore_signal(barrier, inc=1, device_id=device, device_id_type=MESH)
        else:
            @pl.when(condition)
            def _():
                pl.semaphore_signal(barrier, inc=1, device_id=device, device_id_type=MESH)
    count = 0
    for _, condition in i_copy_to:
        count = count + (1 if condition is None else jnp.where(condition, 1, 0))
    pl.semaphore_wait(barrier, count)


def remote(src, dst, send, recv, device):
    return pltpu.make_async_remote_copy(
        src_ref=src, dst_ref=dst, send_sem=send, recv_sem=recv, device_id=device, device_id_type=MESH
    )


def rem(a, n):
    return lax.rem(a + n, n)


class Chain:
    def __init__(self, part_s, outer_s, inner_s, pieces, in_send, in_recv, mid_send, mid_recv, out_send, out_recv):
        self.clip, clips = lax.axis_index("clip"), lax.axis_size("clip")
        clip = self.clip
        left = clip < clips // 2
        inner, outer = jnp.where(left, clip + 1, clip - 1), jnp.where(left, clip - 1, clip + 1)
        self.inner, self.outer = {"clip": inner}, {"clip": outer}
        self.end = (clip == 0) | (clip == clips - 1)
        self.middle = (clip == clips // 2 - 1) | (clip == clips // 2)
        self.part, self.from_outer, self.from_inner, self.pieces = part_s, outer_s, inner_s, pieces
        self.inward = [remote(part_s.at[p], outer_s.at[p], in_send.at[n], in_recv.at[n], self.inner) for n, p in enumerate(pieces)]
        self.across = [remote(part_s.at[p], inner_s.at[p], mid_send.at[n], mid_recv.at[n], self.inner) for n, p in enumerate(pieces)]
        self.outward = [remote(inner_s.at[p], inner_s.at[p], out_send.at[n], out_recv.at[n], self.outer) for n, p in enumerate(pieces)]

    def greet(self):
        barrier = pltpu.get_barrier_semaphore()
        pl.semaphore_signal(barrier, inc=1, device_id=self.inner, device_id_type=MESH)

        @pl.when(jnp.logical_not(self.end))
        def _():
            pl.semaphore_signal(barrier, inc=1, device_id=self.outer, device_id_type=MESH)

        pl.semaphore_wait(barrier, jnp.where(self.end, 1, 2))

    def greets(self):
        both = [(self.inner, None), (self.outer, jnp.logical_not(self.end))]
        return both

    def send_ends(self, n):
        @pl.when(self.end & jnp.logical_not(self.middle))
        def _():
            self.inward[n].start()

    def send_parts(self, n):
        here = self.pieces[n]

        @pl.when(jnp.logical_not(self.end))
        def _():
            self.inward[n].wait_recv()
            self.part[here] = (self.part[here].astype(f32) + self.from_outer[here].astype(f32)).astype(bf16)

        @pl.when(jnp.logical_not(self.end) & jnp.logical_not(self.middle))
        def _():
            self.inward[n].start()

        @pl.when(self.middle)
        def _():
            self.across[n].start()

    def totals(self, n):
        self.middle_totals(n)
        self.other_totals(n)

    def middle_totals(self, n):
        here = self.pieces[n]

        @pl.when(self.middle)
        def _():
            self.across[n].wait_recv()
            self.across[n].wait_send()
            self.from_inner[here] = (self.part[here].astype(f32) + self.from_inner[here].astype(f32)).astype(bf16)

        @pl.when(self.middle & jnp.logical_not(self.end))
        def _():
            self.outward[n].start()

    def other_totals(self, n):
        @pl.when(jnp.logical_not(self.middle))
        def _():
            self.inward[n].wait_send()
            self.outward[n].wait_recv()

        @pl.when(jnp.logical_not(self.middle) & jnp.logical_not(self.end))
        def _():
            self.outward[n].start()

    def close(self):
        @pl.when(jnp.logical_not(self.end))
        def _():
            for copy in self.outward:
                copy.wait_send()


def chain_scratch(buffer, pieces):
    return [pltpu.VMEM(buffer, bf16)] * 3 + [dma(pieces)] * 6


ANY = pl.BlockSpec(memory_space=pl.ANY)
INVMEM = pl.BlockSpec(memory_space=pltpu.VMEM)
INSMEM = pl.BlockSpec(memory_space=pltpu.SMEM)


def dma(*dims):
    return pltpu.SemaphoreType.DMA(dims)


def dot(a, b, dims=NN):
    return lax.dot_general(a, b, (dims, ((), ())), preferred_element_type=f32)


def exact_dot(matrix, tensor):
    high = tensor.astype(bf16)
    low = (tensor - high.astype(f32)).astype(bf16)
    return dot(matrix, high) + dot(matrix, low)


def norm(x):
    average = jnp.mean(x, axis=-1, keepdims=True)
    centred = x - average
    inverse = lax.rsqrt(jnp.mean(centred * centred, axis=-1, keepdims=True) + eps)
    return centred * inverse, inverse


def norm_back(unit, inverse, gain, gradient):
    scaled = gradient * gain
    return inverse * (
        scaled
        - jnp.mean(scaled, axis=-1, keepdims=True)
        - unit * jnp.mean(scaled * unit, axis=-1, keepdims=True)
    )


GELU_A, GELU_B = math.sqrt(2.0 / math.pi), 0.044715


def gelu(x):
    t = jnp.tanh(GELU_A * (x + GELU_B * (x * x * x)))
    return 0.5 * x * (1.0 + t)


def gelu_both(x):
    square = x * x
    t = jnp.tanh(GELU_A * x * (1.0 + GELU_B * square))
    value = 0.5 * x * (1.0 + t)
    slope = 0.5 * (1.0 + t) + 0.5 * x * (1.0 - t * t) * (GELU_A * (1.0 + 3.0 * GELU_B * square))
    return value, slope


def sum_rows(x):
    return jnp.sum(x, axis=0, keepdims=True)


def add_rows(ref, rows):
    step = pl.program_id(0)

    @pl.when(step == 0)
    def _():
        ref[...] = jnp.zeros_like(ref)

    for i, row in enumerate(rows):
        ref[i:i + 1, :] += row


def transposed(x):
    return x.astype(f32).T.astype(bf16)


def window(head):
    low = HD * head
    return low // 128 * 128, -(-(low + HD) // 128) * 128


def head_mask(head):
    start, stop = window(head)
    lane = lax.broadcasted_iota(jnp.int32, (1, stop - start), 1) + start
    return (lane >= HD * head) & (lane < HD * head + HD)


def key_rows(own_ref, mem_ref):
    row = 0
    for ref in (own_ref, mem_ref):
        for t in range(ref.shape[0]):
            yield ref, t, slice(row, row + ref.shape[2])
            row += ref.shape[2]


def key_mask(own_ref, mem_ref, valid, has):
    parts = []
    for ref, rows, there in ((own_ref, valid[0], None), (mem_ref, valid[1], has)):
        block = ref.shape[2]
        lane = lax.rem(lax.broadcasted_iota(jnp.int32, (1, ref.shape[0] * block), 1), block)
        limit = rows if there is None else jnp.where(there > 0, rows, 0)
        parts.append(jnp.where(lane < limit, 0.0, NEG))
    return jnp.concatenate(parts, axis=1)


def assemble(w_ref, w_s):
    wide = w_ref.shape[2] // 4
    for part in range(3):
        pieces = [w_ref[h, :, wide * part:wide * part + wide].astype(f32) for h in range(w_ref.shape[0])]
        w_s[0, :, 384 * part:384 * part + 384] = jnp.concatenate(pieces, axis=1).astype(bf16)


def assemble_out(w_ref, out_s):
    wide = w_ref.shape[2] // 4
    pieces = [w_ref[h, :, 3 * wide:].astype(f32) for h in range(w_ref.shape[0])]
    out_s[...] = jnp.concatenate(pieces, axis=1).astype(bf16)


def project_keys(own_ref, mem_ref, w_ref, bias_ref, x_s, k_s, v_s):
    for ref, t, rows in key_rows(own_ref, mem_ref):
        x_s[rows, :] = ref[t, 0]
    width = k_s.shape[1]
    for low in range(0, width, 384):
        k_s[:, low:low + 384] = dot(x_s[...], w_ref[low // 384, :, 384:768]).astype(bf16)
    for low in range(0, width, 384):
        value = dot(x_s[...], w_ref[low // 384, :, 768:])
        v_s[:, low:low + 384] = (value + bias_ref[1:2, low:low + 384]).astype(bf16)


def project_queries(x_ref, w_ref, bias_ref, q_s):
    width = q_s.shape[1]
    for low in range(0, width, 384):
        value = dot(x_ref[0], w_ref[low // 384, :, :384])
        q_s[:, low:low + 384] = (value + bias_ref[0:1, low:low + 384]).astype(bf16)


def norm_pool_kernel(x_ref, vec_ref, pool_ref, pair_ref, low_ref, pooled_ref, mean_ref):
    unit, _ = norm(x_ref[0].astype(f32))
    normed = unit * vec_ref[0:1, :] + vec_ref[1:2, :]
    low_ref[0] = normed.astype(bf16)
    pooled = exact_dot(pool_ref[...], normed)
    pooled_ref[0] = pooled.astype(bf16)
    mean_ref[0] = exact_dot(pair_ref[...], pooled).astype(bf16)


def write_shares(gw_ref, h, gw_s):
    wide = gw_ref.shape[2] // 3
    for part in range(3):
        low = wide * h
        columns = gw_s[low // 384, :, 384 * part:384 * part + 384][:, low % 384:low % 384 + wide]
        gw_ref[h, :, wide * part:wide * part + wide] = columns.astype(bf16)


def attend_kernel(chunk, valid, x_ref, own_ref, mem_ref, w_ref, qv_ref, has_ref, out_ref, lse_ref, w_s, x_s, q_s, k_s, v_s, s_s, p_s):
    nq, width = q_s.shape
    columns = key_mask(own_ref, mem_ref, valid, has_ref[pl.program_id(0)])
    if width == 384:
        @pl.when(pl.program_id(0) == 0)
        def _():
            assemble(w_ref, w_s)
        w_ref = w_s
    project_queries(x_ref, w_ref, qv_ref, q_s)
    project_keys(own_ref, mem_ref, w_ref, qv_ref, x_s, k_s, v_s)
    factor = HD**-0.5 * math.log2(math.e)
    lanes = lax.broadcasted_iota(jnp.int32, (chunk, 128), 1)
    for tile in range(width // 384):
        group = slice(384 * tile, 384 * tile + 384)
        base = q_s[:, group].astype(f32)
        parts = [base[:, :128], base[:, 128:256], base[:, 256:384]]
        for head in range(4 * tile, 4 * tile + 4):
            start, stop = window(head)
            mask = head_mask(head)
            query = jnp.where(mask, q_s[:, start:stop], jnp.zeros((), bf16))
            s_s[...] = dot(query, k_s[:, start:stop], NT)

            def body(i, carry, head=head):
                rows = pl.ds(pl.multiple_of(i * chunk, chunk), chunk)
                score = s_s[rows, :] * factor + columns
                top = jnp.max(score, axis=1, keepdims=True)
                power = jnp.exp2(score - top)
                total = jnp.sum(power, axis=1, keepdims=True)
                p_s[rows, :] = (power * (1.0 / total)).astype(bf16)
                lse_ref[0, rows, :] = jnp.where(lanes == head, top + jnp.log2(total), lse_ref[0, rows, :])
                return carry

            lax.fori_loop(0, nq // chunk, body, 0, unroll=nq // chunk)
            out = jnp.where(mask, dot(p_s[...], v_s[:, start:stop]), 0.0)
            for w in range((stop - start) // 128):
                k = start // 128 - 3 * tile + w
                parts[k] = parts[k] + out[:, 128 * w:128 * w + 128]
        out_ref[0, :, group] = jnp.concatenate(parts, axis=1).astype(bf16)


def attend_back_kernel(chunk, valid, hosted, *refs):
    if hosted:
        *refs, copy_sem = refs
        refs, shard_ref, refs_out, sum_ref, scratch, chain = refs[:8], refs[8], refs[9:13], refs[13], refs[14:26], refs[26:]
        refs = (*refs, *refs_out, *scratch)
        each = shard_ref.shape[0] // hosted
        chain = Chain(*chain[:3], [(pl.ds(each * n, each), slice(None)) for n in range(hosted)], *chain[3:])
    (x_ref, g_ref, own_ref, mem_ref, w_ref, qv_ref, has_ref, lse_ref, dx_ref, dpool_ref, gw_ref, row_ref,
     w_s, x_s, q_s, k_s, v_s, s_s, dp_s, p_s, ds_s, dk_s, dv_s, gw_s) = refs
    nq, width = q_s.shape
    step = pl.program_id(0)
    if hosted:
        @pl.when(step == 0)
        def _():
            chain.greet()
            load = pltpu.make_async_copy(shard_ref, chain.part, copy_sem.at[0])
            load.start()
            load.wait()
            for n in range(hosted):
                chain.send_ends(n)

    def progress(head):
        if hosted:
            half = -(-hosted // 3)

            @pl.when(step == 0)
            def _():
                for n in range(max(half * (head - 1), 0), min(half * head, hosted)):
                    chain.send_parts(n)

            @pl.when(step == 1)
            def _():
                for n in range(half * head, min(half * head + half, hosted)):
                    chain.middle_totals(n)

    columns = key_mask(own_ref, mem_ref, valid, has_ref[step])
    if width == 384:
        @pl.when(step == 0)
        def _():
            assemble(w_ref, w_s)
        w_ref = w_s
    project_queries(x_ref, w_ref, qv_ref, q_s)
    project_keys(own_ref, mem_ref, w_ref, qv_ref, x_s, k_s, v_s)
    scaling = HD**-0.5
    factor = scaling * math.log2(math.e)
    lanes = lax.broadcasted_iota(jnp.int32, (chunk, 128), 1)

    @pl.when(step == 0)
    def _():
        gw_s[...] = jnp.zeros_like(gw_s)

    xt = transposed(x_ref[0])
    keys_t = transposed(x_s[...])
    dx = None
    dpool = None
    row_q, row_v = [], []
    for tile in range(width // 384):
        group = slice(384 * tile, 384 * tile + 384)
        qt = transposed(q_s[:, group])
        gt = transposed(g_ref[0, :, group])
        parts = [None] * 3
        for head in range(4 * tile, 4 * tile + 4):
            start, stop = window(head)
            mask = head_mask(head)
            query = jnp.where(mask, q_s[:, start:stop], jnp.zeros((), bf16))
            grad = jnp.where(mask, g_ref[0, :, start:stop], jnp.zeros((), bf16))
            s_s[...] = dot(query, k_s[:, start:stop], NT)
            dp_s[...] = dot(grad, v_s[:, start:stop], NT)

            def body(i, carry, head=head):
                rows = pl.ds(pl.multiple_of(i * chunk, chunk), chunk)
                lse = jnp.sum(jnp.where(lanes == head, lse_ref[0, rows, :], 0.0), axis=1, keepdims=True)
                p = jnp.exp2(s_s[rows, :] * factor + columns - lse)
                dp = dp_s[rows, :]
                inner = jnp.sum(p * dp, axis=1, keepdims=True)
                p_s[rows, :] = p.astype(bf16)
                ds_s[rows, :] = (p * (dp - inner)).astype(bf16)
                return carry

            lax.fori_loop(0, nq // chunk, body, 0, unroll=nq // chunk)
            r = slice(HD * (head - 4 * tile), HD * (head - 4 * tile) + HD)
            dv_s[r, :] = dot(gt[r], p_s[...])
            dk_s[r, :] = dot(qt[r], ds_s[...]) * scaling
            dq = jnp.where(mask, dot(ds_s[...], k_s[:, start:stop]) * scaling, 0.0)
            for w in range((stop - start) // 128):
                k = start // 128 - 3 * tile + w
                part = dq[:, 128 * w:128 * w + 128]
                parts[k] = part if parts[k] is None else parts[k] + part
            progress(head)
        total = jnp.concatenate(parts, axis=1) + g_ref[0, :, group].astype(f32)
        row_q.append(sum_rows(total))
        low = total.astype(bf16)
        gw_s[tile, :, :384] += dot(xt, low)
        add = dot(low, w_ref[tile, :, :384], NT)
        dx = add if dx is None else dx + add
        for part, src in ((1, dk_s), (2, dv_s)):
            grad = src[...].T
            if part == 2:
                row_v.append(sum_rows(grad))
            low = grad.astype(bf16)
            here = slice(384 * part, 384 * part + 384)
            gw_s[tile, :, here] += dot(keys_t, low)
            add = dot(low, w_ref[tile, :, here], NT)
            dpool = add if dpool is None else dpool + add
    dx_ref[0] = dx
    row = 0
    own, mem = own_ref.shape[2], mem_ref.shape[2]
    toks = own_ref.shape[0]
    for t in range(toks):
        dpool_ref[t, 0, :own, :] = dpool[t * own:(t + 1) * own].astype(bf16)
        dpool_ref[t, 0, own:, :] = dpool[toks * own + t * mem:toks * own + (t + 1) * mem].astype(bf16)
    add_rows(row_ref, [jnp.concatenate(row_q, axis=1), jnp.concatenate(row_v, axis=1)])

    @pl.when(step == pl.num_programs(0) - 1)
    def _():
        for h in range(gw_ref.shape[0]):
            write_shares(gw_ref, h, gw_s)
        if hosted:
            for n in range(hosted):
                chain.other_totals(n)
            chain.close()
            store = pltpu.make_async_copy(chain.from_inner, sum_ref, copy_sem.at[0])
            store.start()
            store.wait()


def first_mlp_kernel(x_ref, comb_ref, out_ref, up_ref, down_ref, ub_ref, vec_ref, pool_ref, pair_ref,
                     after_ref, middle_ref, pooled_ref, mean_ref, out_s):
    @pl.when(pl.program_id(0) == 0)
    def _():
        assemble_out(out_ref, out_s)

    after = x_ref[0].astype(f32) + dot(comb_ref[0], out_s[...], NT) + vec_ref[0:1, :]
    after_ref[0] = after
    unit, _ = norm(after)
    low = (unit * vec_ref[1:2, :] + vec_ref[2:3, :]).astype(bf16)
    total = after + vec_ref[3:4, :]
    for h in range(up_ref.shape[0]):
        hidden = gelu(dot(low, up_ref[h]) + ub_ref[h]).astype(bf16)
        total = total + dot(hidden, down_ref[h], NT)
    middle_ref[0] = total
    unit, _ = norm(total)
    pooled = exact_dot(pool_ref[...], unit * vec_ref[4:5, :] + vec_ref[5:6, :])
    pooled_ref[0] = pooled.astype(bf16)
    mean_ref[0] = exact_dot(pair_ref[...], pooled).astype(bf16)


def second_mlp_kernel(
    comb_ref, pooled_ref, cot_ref, out_ref, skip_ref, up_ref, down_ref, ub_ref, vec_ref,
    mixed_ref, dcomb_ref, dskip_ref, gmlp_ref, gout_ref, gskip_ref, gub_ref, row_ref,
    after_s, low_s, lowt_s, cott_s, sum_s, dlow_s, skip_s,
):
    step = pl.program_id(0)

    @pl.when(step == 0)
    def _():
        share = skip_s.shape[1] // skip_ref.shape[0]
        skip_s[...] = jnp.concatenate([skip_ref[h, :, :share].astype(f32) for h in range(skip_ref.shape[0])], axis=1).astype(bf16)
        after = dot(pooled_ref[...], skip_s[...], NT) + vec_ref[0:1, :]
        wide = out_ref.shape[2]
        for h in range(out_ref.shape[0]):
            after = after + dot(comb_ref[:, wide * h:wide * h + wide], out_ref[h], NT)
        after_s[...] = after
        unit, _ = norm(after)
        low = (unit * vec_ref[1:2, :] + vec_ref[2:3, :]).astype(bf16)
        low_s[...] = low
        lowt_s[...] = transposed(low)
        cott_s[...] = transposed(cot_ref[...])
        sum_s[...] = after + vec_ref[3:4, :]
        dlow_s[...] = jnp.zeros_like(dlow_s)

    pre = dot(low_s[...], up_ref[0]) + ub_ref[...]
    hidden, slope = gelu_both(pre)
    hidden = hidden.astype(bf16)
    dpre = dot(cot_ref[...], down_ref[0]) * slope
    gub_ref[...] = sum_rows(dpre)
    dpre = dpre.astype(bf16)
    sum_s[...] += dot(hidden, down_ref[0], NT)
    dlow_s[...] += dot(dpre, up_ref[0], NT)
    for n, grad in enumerate((dot(lowt_s[...], dpre), dot(cott_s[...], hidden))):
        rows = gmlp_ref.shape[3]
        for t in range(gmlp_ref.shape[1]):
            gmlp_ref[0, t, n] = grad[t * rows:(t + 1) * rows].astype(bf16)

    @pl.when(step == pl.num_programs(0) - 1)
    def _():
        mixed_ref[...] = sum_s[...].astype(bf16)
        unit, inverse = norm(after_s[...])
        dlow = dlow_s[...]
        cot = cot_ref[...].astype(f32)
        res = norm_back(unit, inverse, vec_ref[1:2, :], dlow) + cot
        row_ref[...] = jnp.zeros_like(row_ref)
        for i, row in enumerate((res, dlow, cot, dlow * unit)):
            row_ref[i:i + 1, :] = sum_rows(row)
        res = res.astype(bf16)
        dskip_ref[...] = dot(res, skip_s[...])
        rest = transposed(res)
        wide = out_ref.shape[2]
        for h in range(out_ref.shape[0]):
            here = slice(wide * h, wide * h + wide)
            dcomb_ref[:, here] = dot(res, out_ref[h]).astype(bf16)
            grad = dot(rest, comb_ref[:, here])
            half = gout_ref.shape[2]
            for n in range(2 * gout_ref.shape[1]):
                gout_ref[h, n // 2, :, wide * (n % 2):wide * (n % 2) + wide] = grad[half * n:half * n + half].astype(bf16)
        grad = dot(rest, pooled_ref[...])
        wide = gskip_ref.shape[3] // 2
        for h in range(gskip_ref.shape[0]):
            for t in range(gskip_ref.shape[1]):
                low, high = (grad[half * n:half * n + half, wide * h:wide * h + wide] for n in (2 * t, 2 * t + 1))
                gskip_ref[h, t] = jnp.concatenate([low, high], axis=1).astype(bf16)


def first_back_kernel(
    middle_ref, after_ref, comb_ref, dskip_ref, dq_ref, own_ref, mem_ref, out_ref, up_ref, down_ref, ub_ref, vec_ref,
    unpool_ref, unpair_ref,
    res_ref, dcomb_ref, gmlp_ref, gub_ref, row_ref,
    gup_s, gdown_s, gout_s, out_s,
):
    step = pl.program_id(0)

    @pl.when(step == 0)
    def _():
        gup_s[...] = jnp.zeros_like(gup_s)
        gdown_s[...] = jnp.zeros_like(gdown_s)
        gout_s[...] = jnp.zeros_like(gout_s)
        gub_ref[...] = jnp.zeros_like(gub_ref)
        assemble_out(out_ref, out_s)

    dpool = dskip_ref[0] + dq_ref[0] + own_ref[0] + exact_dot(unpair_ref[...], mem_ref[0])
    dnorm = exact_dot(unpool_ref[...], dpool)
    unit, inverse = norm(middle_ref[0])
    grad = norm_back(unit, inverse, vec_ref[2:3, :], dnorm)
    rows = [sum_rows(dnorm * unit), sum_rows(dnorm), sum_rows(grad)]
    low = grad.astype(bf16)
    lowt = transposed(low)
    unit, inverse = norm(after_ref[0])
    normed = (unit * vec_ref[0:1, :] + vec_ref[1:2, :]).astype(bf16)
    normedt = transposed(normed)
    dnormed = None
    for h in range(up_ref.shape[0]):
        hidden, slope = gelu_both(dot(normed, up_ref[h]) + ub_ref[h])
        hidden = hidden.astype(bf16)
        dpre = dot(low, down_ref[h]) * slope
        gub_ref[h] += sum_rows(dpre)
        dpre = dpre.astype(bf16)
        gdown_s[h] += dot(lowt, hidden)
        gup_s[h] += dot(normedt, dpre)
        add = dot(dpre, up_ref[h], NT)
        dnormed = add if dnormed is None else dnormed + add
    res = norm_back(unit, inverse, vec_ref[0:1, :], dnormed) + grad
    rows += [sum_rows(dnormed * unit), sum_rows(dnormed), sum_rows(res)]
    res_ref[0] = res
    res = res.astype(bf16)
    dcomb_ref[0] = dot(res, out_s[...]).astype(bf16)
    gout_s[...] += dot(transposed(res), comb_ref[0])
    add_rows(row_ref, rows)

    @pl.when(step == pl.num_programs(0) - 1)
    def _():
        fa, ha = gup_s.shape[2], gout_s.shape[1] // gmlp_ref.shape[0]
        for h in range(gmlp_ref.shape[0]):
            gmlp_ref[h, :, :fa] = gup_s[h].astype(bf16)
            gmlp_ref[h, :, fa:2 * fa] = gdown_s[h].astype(bf16)
            rest = gmlp_ref.shape[2] - 2 * fa - ha
            gout = jnp.concatenate([gout_s[:, ha * h:ha * h + ha], jnp.zeros((gout_s.shape[0], rest), f32)], axis=1)
            gmlp_ref[h, :, 2 * fa:] = gout.astype(bf16)


def last_back_kernel(x_ref, res_ref, dx_ref, own_ref, mem_ref, vec_ref, unpool_ref, unpair_ref, grad_ref, row_ref):
    dpool = own_ref[0] + exact_dot(unpair_ref[...], mem_ref[0])
    dnorm = dx_ref[0] + exact_dot(unpool_ref[...], dpool)
    unit, inverse = norm(x_ref[0].astype(f32))
    grad = norm_back(unit, inverse, vec_ref[0:1, :], dnorm) + res_ref[0]
    grad_ref[0] = grad.astype(bf16)
    add_rows(row_ref, [sum_rows(dnorm * unit), sum_rows(dnorm)])


def whole(array):
    return pl.BlockSpec(array.shape, lambda i: (0,) * array.ndim)


def by_micro(array, axis=0):
    block = array.shape[:axis] + (1,) + array.shape[axis + 1:]
    return pl.BlockSpec(block, lambda i: (0,) * axis + (i,) + (0,) * (array.ndim - axis - 1))


def shape(dims, dtype):
    return jax.ShapeDtypeStruct(dims, dtype)


def about(us):
    return pl.CostEstimate(flops=int(us * 1e9), bytes_accessed=0, transcendentals=0)


def call(kernel, steps, args, outs, scratch=(), name=None, us=10, number=None):
    def spec(array, how):
        if how is None:
            return whole(array)
        return by_micro(array, how) if isinstance(how, int) else how

    return pl.pallas_call(
        kernel,
        grid=(steps,),
        in_specs=[spec(a, how) for a, how in args],
        out_specs=[spec(a, how) for a, how in outs],
        out_shape=[a for a, _ in outs],
        scratch_shapes=[pltpu.VMEM(*one) if isinstance(one, tuple) else one for one in scratch],
        compiler_params=pltpu.CompilerParams(vmem_limit_bytes=VMEM_CAP, collective_id=number, has_side_effects=number is not None),
        cost_estimate=about(us),
        name=name,
    )(*[a for a, _ in args])


def chunk_of(nq):
    return 112 if nq % 112 == 0 else 16


def attend(x, own, mem, w, qv, has, valid, width):
    batches, nq, d = x.shape
    keys = own.shape[0] * own.shape[2] + mem.shape[0] * mem.shape[2]
    return call(
        functools.partial(attend_kernel, chunk_of(nq), valid), batches,
        [(x, 0), (own, 1), (mem, 1), w, (qv, None), (has, pl.BlockSpec(memory_space=pltpu.SMEM))],
        [(shape((batches, nq, width), bf16), 0), (shape((batches, nq, 128), f32), 0)],
        [((1, d, 1152 if width == 384 else 128), bf16),
         ((keys, d), bf16), ((nq, width), bf16), ((keys, width), bf16), ((keys, width), bf16), ((nq, keys), f32), ((nq, keys), bf16)],
        name="attend", us=20,
    )


def attend_back(x, grad, own, mem, w, qv, has, valid, lse, heads, shard=None, number=None):
    batches, nq, d = x.shape
    width = grad.shape[2]
    keys = own.shape[0] * own.shape[2] + mem.shape[0] * mem.shape[2]
    both = (own.shape[0], batches, own.shape[2] + mem.shape[2], d)
    groups = (width // 384, d, 1152)
    args = [(x, 0), (grad, 0), (own, 1), (mem, 1), w, (qv, None), (has, INSMEM), (lse, 0)]
    outs = [(shape((batches, nq, d), f32), 0), (shape(both, bf16), 1), (shape((heads, d, 3 * width // heads), bf16), None), (shape((8, width), f32), None)]
    scratch = [
        ((1, d, 1152 if width == 384 else 128), bf16),
        ((keys, d), bf16), ((nq, width), bf16), ((keys, width), bf16), ((keys, width), bf16),
        ((nq, keys), f32), ((nq, keys), f32), ((nq, keys), bf16), ((nq, keys), bf16),
        ((384, keys), f32), ((384, keys), f32), (groups, f32),
    ]
    pieces = 0
    if shard is not None:
        pieces = shard.shape[0] // 48
        args, outs = args + [(shard, ANY)], outs + [(shape(shard.shape, bf16), ANY)]
        scratch += chain_scratch(shard.shape, pieces) + [dma(1)]
    return call(
        functools.partial(attend_back_kernel, chunk_of(nq), valid, pieces), batches, args, outs, scratch,
        name="attend_back", us=36, number=number,
    )


def share_kernel(gather, *refs):
    if gather:
        pooled_ref, mean_ref, pick_ref, w_ref, *refs = refs
        biases, (own_ref, mem_ref, all_ref, *refs) = refs[:4], refs[4:]
        (qv_a_ref, qv_b_ref, ub_a_ref, ub_b_ref), refs = refs[:4], refs[4:]
    else:
        pooled_ref, mean_ref, pick_ref, own_ref, mem_ref, *refs = refs
    (got_s, pick_s, local_sem, own_send, own_recv, mem_send, mem_recv, pass_send, pass_recv, clip_send, clip_recv, *refs) = refs
    clip, head, chip, core, chips = places()
    clips, heads = lax.axis_size("clip"), lax.axis_size("head")
    share = pooled_ref.shape[0]
    here = 2 * chip + core
    partner = {"tok": 2 * chip + 1 - core}
    across = [{"tok": 2 * rem(chip + k, chips) + core} for k in range(1, chips)]
    beside = [{"head": rem(head + d, heads)} for d in range(1, heads)]
    heads_of = lambda by, sign: [{"clip": clip + by, "head": rem(head + sign * d, heads)} for d in range(heads)]
    last, begun = clip < clips - 1, clip > 0
    near = [(d, None) for d in [partner] + across + (beside if gather else [])]
    greet(near + [(d, begun) for d in heads_of(-1, -1)], near + [(d, last) for d in heads_of(1, 1)])

    def spread(src, out, send, recv):
        copies = [remote(src, out.at[here], send.at[0], recv.at[0], partner)]
        copies += [remote(src, out.at[here], send.at[k + 1], recv.at[k + 1], across[k]) for k in range(chips - 1)]
        return copies

    def passed(out, k, row):
        block = 2 * rem(chip - k, chips) + core
        return remote(out.at[block], out.at[block], pass_send.at[row, k - 1], pass_recv.at[row, k - 1], partner)

    clip_copies = [remote(mean_ref, got_s.at[d], clip_send.at[d], clip_recv.at[d], device) for d, device in enumerate(heads_of(1, 1))]

    @pl.when(last)
    def _():
        for copy in clip_copies:
            copy.start()

    w_first, w_diagonal, w_core = {}, {}, {}
    if gather:
        w_local, w_send, w_recv, d_send, d_recv, c_send, c_recv, b_send, b_recv, *bias_got = refs
        bias_copies = [
            remote(ref, got.at[d], b_send.at[d, n], b_recv.at[d, n], device)
            for d, device in enumerate(beside)
            for n, (ref, got) in enumerate(zip(biases, bias_got))
        ]
        for copy in bias_copies:
            copy.start()
        mine = all_ref.at[head, here]
        for k in range(1, chips):
            w_first[k, 0] = remote(w_ref, mine, w_send.at[k - 1], w_recv.at[k - 1], across[k - 1])
        for d in range(1, heads):
            w_first[0, d] = remote(w_ref, mine, w_send.at[chips - 2 + d], w_recv.at[chips - 2 + d], beside[d - 1])
        w_core[0, 0] = remote(w_ref, mine, c_send.at[0, 0], c_recv.at[0, 0], partner)
        for copy in [*w_first.values(), w_core[0, 0]]:
            copy.start()
        w_copy = pltpu.make_async_copy(w_ref, mine, w_local.at[0])
        w_copy.start()

        def forward(k, d):
            block = all_ref.at[rem(head - d, heads), 2 * rem(chip - k, chips) + core]
            w_core[k, d] = remote(block, block, c_send.at[k, d], c_recv.at[k, d], partner)
            w_core[k, d].start()

    own_copies = spread(pooled_ref, own_ref, own_send, own_recv)
    for copy in own_copies[1:] + own_copies[:1]:
        copy.start()
    own_local = pltpu.make_async_copy(pooled_ref, own_ref.at[here], local_sem.at[0])
    own_local.start()
    if gather:
        for k in range(1, chips):
            w_first[k, 0].wait_recv()
            block = all_ref.at[head, 2 * rem(chip - k, chips) + core]
            for d in range(1, heads):
                w_diagonal[k, d] = remote(block, block, d_send.at[k - 1, d - 1], d_recv.at[k - 1, d - 1], beside[d - 1])
                w_diagonal[k, d].start()
            forward(k, 0)

    @pl.when(begun)
    def _():
        for copy in clip_copies:
            copy.wait_recv()
        for m in range(share):
            total = None
            for d in range(heads):
                for s in range(share):
                    piece = got_s[d, s].astype(f32) * pick_ref[m, d * share + s]
                    total = piece if total is None else total + piece
            pick_s[m] = total.astype(bf16)

    @pl.when(jnp.logical_not(begun))
    def _():
        pick_s[...] = jnp.zeros_like(pick_s)

    mem_copies = spread(pick_s, mem_ref, mem_send, mem_recv)
    for copy in mem_copies[1:] + mem_copies[:1]:
        copy.start()
    mem_local = pltpu.make_async_copy(pick_s, mem_ref.at[here], local_sem.at[1])
    mem_local.start()
    forwards = []
    for k in range(1, chips):
        own_copies[k].wait_recv()
        forwards.append(passed(own_ref, k, 0))
        forwards[-1].start()
    if gather:
        for d in range(1, heads):
            w_first[0, d].wait_recv()
            forward(0, d)
    for k in range(1, chips):
        mem_copies[k].wait_recv()
        forwards.append(passed(mem_ref, k, 1))
        forwards[-1].start()
    if gather:
        for k, d in w_diagonal:
            w_diagonal[k, d].wait_recv()
            forward(k, d)
        for copy in w_core.values():
            copy.wait_recv()
        for copy in bias_copies:
            copy.wait_recv()
        by_head = []
        for ref, got in zip(biases, bias_got):
            pieces = []
            for h in range(heads):
                piece = ref[...]
                for d in range(1, heads):
                    piece = jnp.where(rem(head - d, heads) == h, got[d - 1], piece)
                pieces.append(piece)
            by_head.append(pieces)
        qv_a_ref[...] = jnp.concatenate(by_head[0], axis=1)
        qv_b_ref[...] = jnp.concatenate(by_head[1], axis=1)
        for h in range(heads):
            ub_a_ref[h] = by_head[2][h]
        ub_b_ref[...] = jnp.concatenate(by_head[3], axis=1)
        for copy in bias_copies:
            copy.wait_send()
    own_copies[0].wait_recv()
    mem_copies[0].wait_recv()
    for copy in forwards:
        copy.wait_recv()
    for copy in own_copies + mem_copies + forwards + [*w_first.values(), *w_diagonal.values(), *w_core.values()]:
        copy.wait_send()
    own_local.wait()
    mem_local.wait()
    if gather:
        w_copy.wait()

    @pl.when(last)
    def _():
        for copy in clip_copies:
            copy.wait_send()


def share_pooled(pooled, mean, pick, number, block=None, biases=()):
    toks, heads = lax.axis_size("tok"), lax.axis_size("head")
    chips = toks // 2
    few = max(chips - 1, 1)
    args, specs = [pooled, mean, pick], [INVMEM, INVMEM, INSMEM]
    outs = [shape((toks,) + pooled.shape, bf16), shape((toks,) + mean.shape, bf16)]
    scratch = [
        pltpu.VMEM((heads,) + mean.shape, bf16), pltpu.VMEM(mean.shape, bf16), dma(2),
        dma(chips), dma(chips), dma(chips), dma(chips), dma(2, few), dma(2, few), dma(heads), dma(heads),
    ]
    if block is not None:
        args, specs = args + [block, *biases], specs + [ANY] + [INVMEM] * len(biases)
        (_, wa), (_, wb), (_, fa), (_, fb) = (b.shape for b in biases)
        outs = outs + [shape((heads, toks) + block.shape, bf16)]
        outs += [shape(dims, f32) for dims in ((2, heads * wa), (2, heads * wb), (heads, 1, fa), (1, heads * fb))]
        firsts = max(chips + heads - 2, 1)
        scratch += [dma(1), dma(firsts), dma(firsts), dma(few, max(heads - 1, 1)), dma(few, max(heads - 1, 1)), dma(chips, heads), dma(chips, heads)]
        scratch += [dma(max(heads - 1, 1), 4), dma(max(heads - 1, 1), 4)]
        scratch += [pltpu.VMEM((max(heads - 1, 1),) + b.shape, f32) for b in biases]
    return pl.pallas_call(
        functools.partial(share_kernel, block is not None),
        in_specs=specs,
        out_specs=[ANY] * min(len(outs), 3) + [INVMEM] * (len(outs) - 3),
        out_shape=outs,
        scratch_shapes=scratch,
        compiler_params=pltpu.CompilerParams(collective_id=number, has_side_effects=True, vmem_limit_bytes=VMEM_CAP),
        cost_estimate=about(20 if block is None else 30),
        name="share_pooled",
    )(*args)


def give_back_kernel(exchange, *refs):
    if exchange:
        part_ref, pick_ref, half_ref, own_ref, back_ref, all_ref, *refs, half_local, half_send, half_recv = refs
    else:
        part_ref, pick_ref, own_ref, back_ref, *refs = refs
    (mine_s, core_s, sum_s, chip_s, route_s, got_s,
     local_sem, core_send, core_recv, mem_send, mem_recv, own_send, own_recv, clip_send, clip_recv) = refs
    clip, head, chip, core, chips = places()
    clips, heads = lax.axis_size("clip"), lax.axis_size("head")
    share, rows = own_ref.shape[0], own_ref.shape[1]
    partner = {"tok": 2 * chip + 1 - core}
    across = [{"tok": 2 * rem(chip + k, chips) + core} for k in range(1, chips)]
    beside = [{"head": rem(head + d, heads)} for d in range(1, heads)]
    heads_of = lambda by, sign: [{"clip": clip + by, "head": rem(head + sign * d, heads)} for d in range(heads)]
    last, begun = clip < clips - 1, clip > 0
    near = [(d, None) for d in [partner] + across + (beside if exchange else [])]
    greet(near + [(d, last) for d in heads_of(1, 1)], near + [(d, begun) for d in heads_of(-1, -1)])

    order = [rem(chip + k, chips) for k in list(range(1, chips)) + [0]]
    core_copies, local_copies = [], []
    for n, other in enumerate(order):
        core_copies.append(remote(part_ref.at[2 * other + 1 - core], core_s.at[n], core_send.at[n], core_recv.at[n], partner))
        core_copies[-1].start()
    for n, other in enumerate(order):
        local_copies.append(pltpu.make_async_copy(part_ref.at[2 * other + core], mine_s.at[n], local_sem.at[n]))
        local_copies[-1].start()
    halves = []
    if exchange:
        halves = [remote(half_ref, all_ref.at[head], half_send.at[k], half_recv.at[k], d) for k, d in enumerate(beside)]
        for copy in halves:
            copy.start()
        half_copy = pltpu.make_async_copy(half_ref, all_ref.at[head], half_local.at[0])
        half_copy.start()
    mem_copies, own_copies = [], []
    for n in range(chips):
        local_copies[n].wait()
        core_copies[n].wait_recv()
        if n == chips - 1:
            break
        sum_s[n] = (mine_s[n].astype(f32) + core_s[n].astype(f32)).astype(bf16)
        low, high = pl.ds(0, rows), pl.ds(rows, sum_s.shape[2] - rows)
        mem_copies.append(remote(sum_s.at[n, :, high, :], chip_s.at[n, :, high, :], mem_send.at[n], mem_recv.at[n], across[n]))
        mem_copies[-1].start()
        own_copies.append(remote(sum_s.at[n, :, low, :], chip_s.at[n, :, low, :], own_send.at[n], own_recv.at[n], across[n]))
        own_copies[-1].start()
    base = chips - 1
    for copy in mem_copies:
        copy.wait_recv()
    memory = []
    for m in range(share):
        total = mine_s[base, m, rows:].astype(f32) + core_s[base, m, rows:].astype(f32)
        for n in range(chips - 1):
            total = total + chip_s[n, m, rows:].astype(f32)
        memory.append(total)
    clip_copies = [
        remote(route_s.at[d], got_s.at[d], clip_send.at[d], clip_recv.at[d], device) for d, device in enumerate(heads_of(-1, -1))
    ]

    @pl.when(begun)
    def _():
        for d in range(heads):
            for s in range(share):
                total = None
                for m in range(share):
                    piece = memory[m] * pick_ref[m, d * share + s]
                    total = piece if total is None else total + piece
                route_s[d, s] = total.astype(bf16)
            clip_copies[d].start()

    for copy in own_copies:
        copy.wait_recv()
    for m in range(share):
        total = mine_s[base, m, :rows].astype(f32) + core_s[base, m, :rows].astype(f32)
        for n in range(chips - 1):
            total = total + chip_s[n, m, :rows].astype(f32)
        own_ref[m] = total

    @pl.when(last)
    def _():
        for copy in clip_copies:
            copy.wait_recv()
        total = got_s[0].astype(f32)
        for d in range(1, heads):
            total = total + got_s[d].astype(f32)
        back_ref[...] = total

    @pl.when(jnp.logical_not(last))
    def _():
        back_ref[...] = jnp.zeros_like(back_ref)

    for copy in halves:
        copy.wait_recv()
    for copy in core_copies + mem_copies + own_copies + halves:
        copy.wait_send()
    if exchange:
        half_copy.wait()

    @pl.when(begun)
    def _():
        for copy in clip_copies:
            copy.wait_send()


def give_back(part, pick, own_rows, number, half=None):
    toks, heads = lax.axis_size("tok"), lax.axis_size("head")
    chips, few = toks // 2, max(toks // 2 - 1, 1)
    share, rows, d = part.shape[1:]
    args, specs = [part, pick], [ANY, INSMEM]
    outs, out_specs = [shape((share, own_rows, d), f32), shape((share, rows - own_rows, d), f32)], [INVMEM, INVMEM]
    scratch = [
        pltpu.VMEM((chips,) + part.shape[1:], bf16), pltpu.VMEM((chips,) + part.shape[1:], bf16),
        pltpu.VMEM((few,) + part.shape[1:], bf16), pltpu.VMEM((few,) + part.shape[1:], bf16),
        pltpu.VMEM((heads, share, rows - own_rows, d), bf16), pltpu.VMEM((heads, share, rows - own_rows, d), bf16),
        dma(chips), dma(chips), dma(chips), dma(few), dma(few), dma(few), dma(few), dma(heads), dma(heads),
    ]
    if half is not None:
        args, specs = args + [half], specs + [ANY]
        outs, out_specs = outs + [shape((heads,) + half.shape, half.dtype)], out_specs + [ANY]
        scratch += [dma(1), dma(max(heads - 1, 1)), dma(max(heads - 1, 1))]
    return pl.pallas_call(
        functools.partial(give_back_kernel, half is not None),
        in_specs=specs,
        out_specs=out_specs,
        out_shape=outs,
        scratch_shapes=scratch,
        compiler_params=pltpu.CompilerParams(collective_id=number, has_side_effects=True, vmem_limit_bytes=VMEM_CAP),
        cost_estimate=about(25),
        name="give_back",
    )(*args)


def finish_kernel(half_ref, last_ref, qv_a_rows, a_ref, b_ref, qv_b_rows, ub_a_rows, ub_b_rows, grad_ref, rest_ref, group_ref,
                  all_ref, total_ref, sums_ref, *scratch):
    (small_ref, small_s, small_core, small_chip, small_head, small_clip, part_s, part_core, head_s, part_chip, part_head,
     local_sem, half_send, half_recv, core_send, core_recv, chip_send, chip_recv, head_send, head_recv,
     clip_send, clip_recv, *chain) = scratch
    first_lanes, next_lanes, deep = group_ref.shape[1], rest_ref.shape[1], grad_ref.shape[1]
    bounds = [0, first_lanes // 2, first_lanes, first_lanes + next_lanes // 2, first_lanes + next_lanes, chain[0].shape[1]]
    chain = Chain(*chain[:3], [(slice(None), pl.ds(low, high - low)) for low, high in zip(bounds, bounds[1:])], *chain[3:])
    clip, head, chip, core, chips = places()
    clips, heads = lax.axis_size("clip"), lax.axis_size("head")
    share = half_ref.shape[0]
    partner = {"tok": 2 * chip + 1 - core}
    across = [{"tok": 2 * rem(chip + k, chips) + core} for k in range(1, chips)]
    beside = [{"head": rem(head + k, heads)} for k in range(1, heads)]
    along = [{"clip": rem(clip + k, clips)} for k in range(1, clips)]
    peers = [(d, None) for d in [partner] + across + beside + along]
    greet(peers, peers)
    chain.part[:, :first_lanes] = group_ref[...]
    chain.part[:, first_lanes:first_lanes + next_lanes] = rest_ref[...]
    for n in range(4):
        chain.send_ends(n)
    pending = []
    d1 = small_ref.shape[1]
    small_ref[...] = jnp.zeros_like(small_ref)
    small_ref[0:2, :] = last_ref[0:2, :]
    small_ref[2:4, :] = qv_a_rows[0:2, :]
    for row, source in enumerate((3, 0, 5, 4, 2, 1)):
        small_ref[4 + row:5 + row, :] = a_ref[source:source + 1, :]
    row = 10
    longer = [b_ref[n:n + 1, :] for n in (3, 0, 1, 2)] + [qv_b_rows[n:n + 1, :] for n in range(2)]
    for values in longer + [ub_a_rows[h] for h in range(heads)] + [ub_b_rows[...]]:
        for low in range(0, values.shape[1], d1):
            small_ref[row:row + 1, :] = values[:, low:low + d1]
            row += 1
    def go(copies):
        for copy in copies:
            copy.start()
        pending.extend(copies)
        return copies

    def arrived(copies):
        for copy in copies:
            copy.wait_recv()

    def in_order(index, size, own, slot):
        total = None
        for i in range(size):
            piece = jnp.where(index == i, own, jnp.zeros_like(own))
            for k in range(size - 1):
                piece = jnp.where(rem(index - k - 1, size) == i, slot(k), piece)
            total = piece if total is None else total + piece
        return total

    first = go([remote(small_ref, small_core, core_send.at[0], core_recv.at[0], partner)])
    for h in range(heads):
        for x in range(chips):
            n = h * chips + x
            first += go([remote(grad_ref.at[2 * n + 1 - core], part_core.at[n], core_send.at[n + 1], core_recv.at[n + 1], partner)])
    halves = [
        [remote(half_ref.at[s], all_ref.at[head, s], half_send.at[k, s], half_recv.at[k, s], d) for k, d in enumerate(beside)]
        for s in range(share)
    ]
    local_half = pltpu.make_async_copy(half_ref, all_ref.at[head], local_sem.at[0])
    local_half.start()
    arrived(first)
    small_s[0] = small_ref[...] + small_core[...]
    for n in range(heads * chips):
        part_s[n] = (grad_ref[2 * n + core].astype(f32) + part_core[n].astype(f32)).astype(bf16)
    copies = []
    for k, d in enumerate(beside):
        copies += go([remote(small_s.at[0], small_head.at[k], head_send.at[k, 0], head_recv.at[k, 0], d)])
        for x in range(chips):
            block = rem(head + k + 1, heads) * chips + x
            copies += go([remote(part_s.at[block], part_head.at[k, x], head_send.at[k, x + 1], head_recv.at[k, x + 1], d)])
    for s in range(share):
        go(halves[s])
    chain.send_parts(0)
    chain.send_parts(1)
    arrived(copies)
    small_s[1] = in_order(head, heads, small_s[0], lambda k: small_head[k])
    for x in range(chips):
        total = part_s[head * chips + x].astype(f32)
        for k in range(heads - 1):
            total = total + part_head[k, x].astype(f32)
        head_s[x] = total.astype(bf16)
    copies = []
    for k, d in enumerate(across):
        copies += go([remote(small_s.at[1], small_chip.at[k], chip_send.at[k, 0], chip_recv.at[k, 0], d)])
        copies += go([remote(head_s.at[rem(chip + k + 1, chips)], part_chip.at[k], chip_send.at[k, 1], chip_recv.at[k, 1], d)])
    chain.send_parts(2)
    chain.middle_totals(0)
    chain.send_parts(3)
    arrived(copies)
    small_s[2] = in_order(chip, chips, small_s[1], lambda k: small_chip[k])
    total = head_s[chip].astype(f32)
    for k in range(chips - 1):
        total = total + part_chip[k].astype(f32)
    mine = first_lanes + next_lanes
    chain.part[:, mine:mine + grad_ref.shape[2]] = total.astype(bf16)
    chain.send_ends(4)
    copies = []
    for k, d in enumerate(along):
        copies += go([remote(small_s.at[2], small_clip.at[k], clip_send.at[k, 0], clip_recv.at[k, 0], d)])
    chain.middle_totals(1)
    chain.middle_totals(2)
    chain.send_parts(4)
    chain.middle_totals(3)
    chain.middle_totals(4)
    for n in range(5):
        chain.other_totals(n)
    arrived(copies)
    total_ref[...] = in_order(clip, clips, small_s[2], lambda k: small_clip[k])
    sums_ref[...] = chain.from_inner[...]
    chain.close()
    for copies in halves:
        arrived(copies)
    for copy in pending:
        copy.wait_send()
    local_half.wait()


def finish(half, rows, grad, rest, first, count, number):
    toks, heads, clips = lax.axis_size("tok"), lax.axis_size("head"), lax.axis_size("clip")
    chips = toks // 2
    across, beside, along = (max(n, 1) for n in (chips - 1, heads - 1, clips - 1))
    block, depth, d1 = grad.shape[1:], rest.shape[0], rows[0].shape[1]
    small = (-(-count // 8) * 8, d1)
    low, full = lambda *dims: pltpu.VMEM(dims, bf16), lambda *dims: pltpu.VMEM(dims + small, f32)
    buffer = (depth, first.shape[1] + rest.shape[1] + -(-block[1] // 128) * 128)
    return pl.pallas_call(
        finish_kernel,
        in_specs=[ANY] + [INVMEM] * (len(rows) + 3),
        out_specs=[ANY, INVMEM, INVMEM],
        out_shape=[shape((heads,) + half.shape, half.dtype), shape(small, f32), shape(buffer, bf16)],
        scratch_shapes=[
            full(), full(3), full(), full(across), full(beside), full(along),
            low(heads * chips, *block), low(heads * chips, *block), low(chips, *block), low(across, *block), low(beside, chips, *block),
            dma(1), dma(beside, half.shape[0]), dma(beside, half.shape[0]), dma(heads * chips + 1), dma(heads * chips + 1),
            dma(across, 2), dma(across, 2), dma(beside, chips + 1), dma(beside, chips + 1), dma(along, 1), dma(along, 1),
            *chain_scratch(buffer, 5),
        ],
        compiler_params=pltpu.CompilerParams(collective_id=number, has_side_effects=True, vmem_limit_bytes=VMEM_CAP),
        cost_estimate=about(40),
        name="finish",
    )(half, *rows, grad, rest, first)


def write_kernel(head_ref, total_ref, sums_ref, mlp_ref, qkv_a_ref, out_a_ref, up_a_ref, down_a_ref, qkv_b_ref, out_b_ref, skip_b_ref,
                 up_b_ref, down_b_ref, gains_a_ref, gains_b_ref, shifts_a_ref, shifts_b_ref, qv_a_ref, qv_b_ref, ub_a_ref, ub_b_ref):
    head, total = head_ref[0], total_ref[...]
    at = [10]

    def rows(width):
        first = at[0]
        at[0] += width // total.shape[1]
        return jnp.concatenate([total[r:r + 1] for r in range(first, at[0])], axis=1)

    def share_of(row, width):
        piece = row[:, :width]
        for h in range(1, row.shape[1] // width):
            piece = jnp.where(head == h, row[:, width * h:width * h + width], piece)
        return piece

    gains_a_ref[0:1, :] = total[0:1]
    gains_a_ref[1:3, :] = total[4:6]
    shifts_a_ref[0:1, :] = total[1:2]
    shifts_a_ref[1:5, :] = total[6:10]
    d2, fa, fb = gains_b_ref.shape[1], ub_a_ref.shape[1], ub_b_ref.shape[1]
    heads = total.shape[1] // qv_a_ref.shape[1]
    for i in range(2):
        qv_a_ref[i:i + 1, :] = share_of(total[2 + i:3 + i], qv_a_ref.shape[1])
    gains_b_ref[...] = rows(d2)
    for i in range(3):
        shifts_b_ref[i:i + 1, :] = rows(d2)
    for i in range(2):
        qv_b_ref[i:i + 1, :] = share_of(rows(d2), qv_b_ref.shape[1])
    ub_a_ref[...] = share_of(rows(heads * fa), fa)
    ub_b_ref[...] = share_of(rows(heads * fb), fb)
    low = 0
    depth = sums_ref.shape[0]

    def take(ref):
        nonlocal low
        ref[...] = sums_ref[:, low:low + ref.shape[1]].astype(f32)
        low += ref.shape[1]

    for part in range(3):
        take(qkv_b_ref.at[part])
    for ref in (out_b_ref, skip_b_ref):
        for n in range(2):
            take(ref.at[depth * n:depth * n + depth])
    for ref in (up_a_ref, down_a_ref, out_a_ref):
        take(ref)
    low = -(-low // 256) * 256
    for part in range(3):
        take(qkv_a_ref.at[part])
    up_b_ref[...] = mlp_ref[:up_b_ref.shape[0], :].astype(f32)
    down_b_ref[...] = mlp_ref[up_b_ref.shape[0]:, :].astype(f32)


def padded_rows(*rows):
    return jnp.concatenate([jnp.stack(rows), jnp.zeros((-len(rows) % 8, rows[0].shape[0]), f32)])


def local(
    clips_in, resets, assign, w_qkv_a, w_out_a, w_up_a, w_down_a, w_qkv_b, w_out_b, w_skip_b, w_up_b, w_down_b,
    gains_a, gains_b, shifts_a, shifts_b, qv_bias_a, qv_bias_b, up_bias_a, up_bias_b, cotangent,
):
    heads, toks, clips = lax.axis_size("head"), lax.axis_size("tok"), lax.axis_size("clip")
    head = lax.axis_index("head")
    micro, frames = clips_in.shape[1], clips_in.shape[2]
    d1, d2 = clips_in.shape[-1], cotangent.shape[-1]
    share = micro // heads
    first = head * share
    pool_np, pair_np = pool_matrix(frames), pair_matrix(frames)
    pooling, pairing = jnp.asarray(pool_np, bf16), jnp.asarray(pair_np, bf16)
    unpooling, unpairing = jnp.asarray(pool_np.T, bf16), jnp.asarray(pair_np.T, bf16)
    tokens, pooled_tokens = frames * PATCH, frames * POOLED
    own_rows, mem_rows = up16(pooled_tokens), up16(frames // 2 * POOLED)
    rows2 = share * own_rows


    def by_patch(tensor):
        return tensor.transpose(0, 2, 1, 3).reshape(tensor.shape[0], -1, tensor.shape[3])

    def by_frame(rows, like):
        return rows.reshape(like[:2] + (like[3], like[2], like[4])).transpose(0, 1, 3, 2, 4)

    cot = by_patch(lax.dynamic_slice_in_dim(cotangent[0], first, share, 0))

    source = lax.dynamic_slice_in_dim(assign[0], first, share, 0)
    flags = lax.dynamic_slice_in_dim(resets[0], first, share, 0)
    slot = ((head - source // share + heads) % heads) * share + source % share
    pick = (jnp.arange(heads * share)[None, :] == slot[:, None]).astype(f32)
    has = ((flags == 0) & (lax.axis_index("clip") > 0)).astype(jnp.int32)
    valid = (pooled_tokens, frames // 2 * POOLED)

    group = ("head", "tok")
    fa, ha = w_up_a.shape[1], w_out_a.shape[1]
    fb, hb, hs = w_up_b.shape[1], w_out_b.shape[1], w_skip_b.shape[1]
    pack_a = jnp.concatenate([w_up_a, w_down_a, *w_qkv_a.transpose(1, 0, 2), w_out_a], axis=1)
    all_a = lax.all_gather(pack_a, group).reshape(heads, d1, -1)
    stream = by_patch(lax.dynamic_slice_in_dim(clips_in[0], first, share, 0))
    low1, pooled1, mean1 = call(
        norm_pool_kernel, share,
        [(stream, 0), (padded_rows(gains_a[0], shifts_a[0]), None), (pooling, None), (pairing, None)],
        [(shape((share, tokens, d1), bf16), 0), (shape((share, own_rows, d1), bf16), 0), (shape((share, mem_rows, d1), bf16), 0)],
        name="norm_pool", us=5,
    )
    pooled1, w_qkv_b, w_up_b = lax.optimization_barrier((pooled1, w_qkv_b, w_up_b))
    pack_q = jnp.concatenate([*w_qkv_b.transpose(1, 0, 2)], axis=1)
    own1, mem1, all_q, qv_a, qv_b, ub_a, ub_b = share_pooled(
        pooled1, mean1, pick, 0, pack_q, [qv_bias_a, qv_bias_b, up_bias_a[None], up_bias_b[None]])
    all_q = all_q.reshape(heads, d1, -1)
    own1, w_up_b, cot = lax.optimization_barrier((own1, w_up_b, cot))
    spare = jnp.zeros((w_up_b.shape[0], -(2 * fb + hb + hs) % hb), bf16)
    pack_b = jnp.concatenate([w_up_b, w_down_b, w_out_b, w_skip_b, spare], axis=1)
    all_b = lax.all_gather(pack_b, group).reshape(heads, d2, -1)
    cot = jnp.pad(cot, ((0, 0), (0, own_rows - pooled_tokens), (0, 0))).reshape(rows2, d2)

    up_spec, down_spec, rest_spec = (pl.BlockSpec((heads, d1, fa), lambda i, n=n: (0, 0, n)) for n in range(3))

    comb1, lse1 = attend(low1, own1, mem1, (all_a, rest_spec), qv_a, has, valid, d1)
    after1, middle, pooled3, mean3 = call(
        first_mlp_kernel, share,
        [(stream, 0), (comb1, 0), (all_a, rest_spec), (all_a, up_spec), (all_a, down_spec), (ub_a, None),
         (padded_rows(shifts_a[1], gains_a[1], shifts_a[2], shifts_a[3], gains_a[2], shifts_a[4]), None),
         (pooling, None), (pairing, None)],
        [(shape((share, tokens, d1), f32), 0), (shape((share, tokens, d1), f32), 0),
         (shape((share, own_rows, d1), bf16), 0), (shape((share, mem_rows, d1), bf16), 0)],
        [((d1, d1), bf16)],
        name="first_mlp", us=13,
    )

    own2, mem2 = share_pooled(pooled3, mean3, pick, 1)
    comb2, lse2 = attend(pooled3, own2, mem2, (all_q, None), qv_b, has, valid, d2)
    chunk = 768
    per_head = fb // chunk
    steps = heads * per_head
    out_spec, skip_spec = (pl.BlockSpec((heads, d2, hb), lambda j, n=n: (0, 0, 2 * fb // hb + n)) for n in range(2))
    rows_spec = pl.BlockSpec((1, d2, chunk), lambda j: (j // per_head, 0, j % per_head))
    mixed, dcomb2, dskip, g_mlp_b, g_out_b, g_skip_b, g_ub_b, rows_b = call(
        second_mlp_kernel, steps,
        [(comb2.reshape(rows2, d2), None), (pooled3.reshape(rows2, d1), None), (cot, None), (all_b, out_spec), (all_b, skip_spec),
         (all_b, rows_spec),
         (all_b, pl.BlockSpec((1, d2, chunk), lambda j: (j // per_head, 0, per_head + j % per_head))),
         (ub_b, pl.BlockSpec((1, chunk), lambda j: (0, j))),
         (padded_rows(shifts_b[0], gains_b, shifts_b[1], shifts_b[2]), None)],
        [(shape((rows2, d2), bf16), None), (shape((rows2, d2), bf16), None), (shape((rows2, d1), f32), None),
         (shape((heads, toks, 2, d2 // toks, fb), bf16),
          pl.BlockSpec((1, toks, 2, d2 // toks, chunk), lambda j: (j // per_head, 0, 0, 0, j % per_head))),
         (shape((heads, toks, d2 // toks // 2, 2 * hb), bf16), None), (shape((heads, toks, d2 // toks // 2, 2 * hs), bf16), None),
         (shape((1, heads * fb), f32), pl.BlockSpec((1, chunk), lambda j: (0, j))), (shape((8, d2), f32), None)],
        [((rows2, d2), f32), ((rows2, d2), bf16), ((d2, rows2), bf16), ((d2, rows2), bf16), ((rows2, d2), f32), ((rows2, d2), f32), ((d2, d1), bf16)],
        name="second_mlp", us=26,
    )

    def by_owner(grad):
        return grad.reshape((heads * toks, -1) + grad.shape[2:])

    def scatter(grad):
        return lax.psum_scatter(grad, group, scatter_dimension=0, tiled=False)

    sum_mlp_b = scatter(g_mlp_b.reshape((heads * toks,) + g_mlp_b.shape[2:])).reshape(-1, fb)
    dcomb2 = dcomb2.reshape(share, own_rows, d2)
    dq2, dpool2, g_qkv_b, rows_qv_b = attend_back(pooled3, dcomb2, own2, mem2, (all_q, None), qv_b, has, valid, lse2, heads)
    own_back2, mem_back2 = give_back(dpool2, pick, own_rows, 2)

    merge = lambda grad: grad.reshape((heads * toks,) + grad.shape[2:])
    rest_b = jnp.concatenate([by_owner(g_qkv_b), merge(g_out_b), merge(g_skip_b)], axis=2)
    sum_rest_b = scatter(rest_b)

    res1, dcomb1, g_mlp_a, g_ub_a, rows_a = call(
        first_back_kernel, share,
        [(middle, 0), (after1, 0), (comb1, 0), (dskip.reshape(share, own_rows, d1), 0), (dq2, 0), (own_back2, 0), (mem_back2, 0),
         (all_a, rest_spec), (all_a, up_spec), (all_a, down_spec), (ub_a, None),
         (padded_rows(gains_a[1], shifts_a[2], gains_a[2]), None), (unpooling, None), (unpairing, None)],
        [(shape((share, tokens, d1), f32), 0), (shape((share, tokens, d1), bf16), 0),
         (shape((heads, d1, -(-(2 * fa + ha) // 256) * 256), bf16), None),
         (shape((heads, 1, fa), f32), None), (shape((8, d1), f32), None)],
        [((heads, d1, fa), f32), ((heads, d1, fa), f32), ((d1, d1), f32), ((d1, d1), bf16)],
        name="first_back", us=26,
    )
    rest_a = by_owner(g_mlp_a)
    sum_rest_a = scatter(rest_a)
    args = (low1, dcomb1, own1, mem1, (all_a, rest_spec), qv_a, has, valid, lse1, heads)
    if toks * (own_rows + mem_rows) <= 1536:
        dx1, dpool1, g_qkv_a, rows_qv_a, sum_mlp_b = attend_back(*args, sum_mlp_b, 5)
    else:
        dx1, dpool1, g_qkv_a, rows_qv_a = attend_back(*args)
        sum_mlp_b = lax.psum(sum_mlp_b, "clip")
    own_back1, mem_back1, mixed_all = give_back(dpool1, pick, own_rows, 3, mixed.reshape(share, own_rows, d2))
    stream_grad, rows_last = call(
        last_back_kernel, share,
        [(stream, 0), (res1, 0), (dx1, 0), (own_back1, 0), (mem_back1, 0), (padded_rows(gains_a[0]), None),
         (unpooling, None), (unpairing, None)],
        [(shape((share, tokens, d1), bf16), 0), (shape((8, d1), f32), None)],
        name="last_back", us=6,
    )

    rows = [rows_last, rows_qv_a, rows_a, rows_b, rows_qv_b, g_ub_a, g_ub_b]
    count = 10 + (6 * d2 + heads * (fa + fb)) // d1
    stream_all, total, sums = finish(stream_grad, rows, by_owner(g_qkv_a), sum_rest_a, sum_rest_b, count, 4)
    row1, row2 = w_up_a.shape[0], w_up_b.shape[0]
    outs = [(3, row1, ha), (row1, ha), (row1, fa), (row1, fa), (3, row1, hb), (row2, hb), (row2, hs), (row2, fb), (row2, fb),
            (3, d1), (1, d2), (5, d1), (3, d2), (2, ha), (2, hb), (1, fa), (1, fb)]
    grads = call(
        write_kernel, 1,
        [(head.astype(jnp.int32)[None], INSMEM), (total, None), (sums, None), (sum_mlp_b, None)],
        [(shape(dims, f32), None) for dims in outs],
        name="write", us=4,
    )
    mixed_all = mixed_all.reshape(micro, own_rows, d2)[:, :pooled_tokens]
    return (
        by_frame(mixed_all, cotangent.shape),
        by_frame(stream_all.astype(f32), clips_in.shape),
        grads[0].transpose(1, 0, 2), *grads[1:4], grads[4].transpose(1, 0, 2), *grads[5:10],
        grads[10][0], *grads[11:15], grads[15][0], grads[16][0],
    )


def solution(mesh):
    in_specs = (
        P("clip", None, "tok", None, None),
        P("clip", None),
        P("clip", None),
        P("tok", None, "head"),
        P("tok", "head"),
        P("tok", "head"),
        P("tok", "head"),
        P("tok", None, "head"),
        P("tok", "head"),
        P("tok", "head"),
        P("tok", "head"),
        P("tok", "head"),
        P(),
        P(),
        P(),
        P(),
        P(None, "head"),
        P(None, "head"),
        P("head"),
        P("head"),
        P("clip", None, "tok", None, None),
    )
    out_specs = (
        P("clip", None, "tok", None, None),
        P("clip", None, "tok", None, None),
        P("tok", None, "head"),
        P("tok", "head"),
        P("tok", "head"),
        P("tok", "head"),
        P("tok", None, "head"),
        P("tok", "head"),
        P("tok", "head"),
        P("tok", "head"),
        P("tok", "head"),
        P(),
        P(),
        P(),
        P(),
        P(None, "head"),
        P(None, "head"),
        P("head"),
        P("head"),
    )
    return jax.shard_map(local, mesh=mesh, in_specs=in_specs, out_specs=out_specs, check_vma=False)
```

```python
import functools
import math

import jax
import jax.numpy as jnp
import numpy as np
from jax import lax
from jax.experimental import pallas as pl
from jax.experimental.pallas import tpu as pltpu
from jax.sharding import PartitionSpec as P

GRID = 14
PATCH = GRID * GRID
POOLED = PATCH // 4
HD = 96
NEG = -1e30
VMEM_CAP = 62 * 2**20
eps = 1e-06
f32, bf16 = jnp.float32, jnp.bfloat16
NN, NT, TN = ((1,), (0,)), ((1,), (1,)), ((0,), (0,))


def up16(n):
    return -(-n // 16) * 16


def pool_matrix(frames):
    rows, cols = up16(frames * POOLED), frames * PATCH
    out = np.zeros((rows, cols), np.float32)
    half = GRID // 2
    for f in range(frames):
        for p in range(PATCH):
            r, c = divmod(p, GRID)
            out[((r // 2) * half + c // 2) * frames + f, p * frames + f] = 0.25
    return out


def pair_matrix(frames):
    rows, cols = up16(frames // 2 * POOLED), up16(frames * POOLED)
    out = np.zeros((rows, cols), np.float32)
    for j in range(frames // 2):
        for p in range(POOLED):
            out[p * (frames // 2) + j, p * frames + 2 * j] = 0.5
            out[p * (frames // 2) + j, p * frames + 2 * j + 1] = 0.5
    return out


MESH = pl.DeviceIdType.MESH


def places():
    tok, toks = lax.axis_index("tok"), lax.axis_size("tok")
    return lax.axis_index("clip"), lax.axis_index("head"), tok // 2, tok % 2, toks // 2


def greet(copies_to_me, i_copy_to):
    barrier = pltpu.get_barrier_semaphore()
    for device, condition in copies_to_me:
        if condition is None:
            pl.semaphore_signal(barrier, inc=1, device_id=device, device_id_type=MESH)
        else:
            @pl.when(condition)
            def _():
                pl.semaphore_signal(barrier, inc=1, device_id=device, device_id_type=MESH)
    count = 0
    for _, condition in i_copy_to:
        count = count + (1 if condition is None else jnp.where(condition, 1, 0))
    pl.semaphore_wait(barrier, count)


def remote(src, dst, send, recv, device):
    return pltpu.make_async_remote_copy(
        src_ref=src, dst_ref=dst, send_sem=send, recv_sem=recv, device_id=device, device_id_type=MESH
    )


def rem(a, n):
    return lax.rem(a + n, n)


class Chain:
    def __init__(self, part_s, outer_s, inner_s, pieces, in_send, in_recv, mid_send, mid_recv, out_send, out_recv):
        self.clip, clips = lax.axis_index("clip"), lax.axis_size("clip")
        clip = self.clip
        left = clip < clips // 2
        inner, outer = jnp.where(left, clip + 1, clip - 1), jnp.where(left, clip - 1, clip + 1)
        self.inner, self.outer = {"clip": inner}, {"clip": outer}
        self.end = (clip == 0) | (clip == clips - 1)
        self.middle = (clip == clips // 2 - 1) | (clip == clips // 2)
        self.part, self.from_outer, self.from_inner, self.pieces = part_s, outer_s, inner_s, pieces
        self.inward = [remote(part_s.at[p], outer_s.at[p], in_send.at[n], in_recv.at[n], self.inner) for n, p in enumerate(pieces)]
        self.across = [remote(part_s.at[p], inner_s.at[p], mid_send.at[n], mid_recv.at[n], self.inner) for n, p in enumerate(pieces)]
        self.outward = [remote(inner_s.at[p], inner_s.at[p], out_send.at[n], out_recv.at[n], self.outer) for n, p in enumerate(pieces)]

    def greet(self):
        barrier = pltpu.get_barrier_semaphore()
        pl.semaphore_signal(barrier, inc=1, device_id=self.inner, device_id_type=MESH)

        @pl.when(jnp.logical_not(self.end))
        def _():
            pl.semaphore_signal(barrier, inc=1, device_id=self.outer, device_id_type=MESH)

        pl.semaphore_wait(barrier, jnp.where(self.end, 1, 2))

    def greets(self):
        both = [(self.inner, None), (self.outer, jnp.logical_not(self.end))]
        return both

    def send_ends(self, n):
        @pl.when(self.end & jnp.logical_not(self.middle))
        def _():
            self.inward[n].start()

    def send_parts(self, n):
        here = self.pieces[n]

        @pl.when(jnp.logical_not(self.end))
        def _():
            self.inward[n].wait_recv()
            self.part[here] = (self.part[here].astype(f32) + self.from_outer[here].astype(f32)).astype(bf16)

        @pl.when(jnp.logical_not(self.end) & jnp.logical_not(self.middle))
        def _():
            self.inward[n].start()

        @pl.when(self.middle)
        def _():
            self.across[n].start()

    def totals(self, n):
        self.middle_totals(n)
        self.other_totals(n)

    def middle_totals(self, n):
        here = self.pieces[n]

        @pl.when(self.middle)
        def _():
            self.across[n].wait_recv()
            self.across[n].wait_send()
            self.from_inner[here] = (self.part[here].astype(f32) + self.from_inner[here].astype(f32)).astype(bf16)

        @pl.when(self.middle & jnp.logical_not(self.end))
        def _():
            self.outward[n].start()

    def other_totals(self, n):
        @pl.when(jnp.logical_not(self.middle))
        def _():
            self.inward[n].wait_send()
            self.outward[n].wait_recv()

        @pl.when(jnp.logical_not(self.middle) & jnp.logical_not(self.end))
        def _():
            self.outward[n].start()

    def close(self):
        @pl.when(jnp.logical_not(self.end))
        def _():
            for copy in self.outward:
                copy.wait_send()


def chain_scratch(buffer, pieces):
    return [pltpu.VMEM(buffer, bf16)] * 3 + [dma(pieces)] * 6


ANY = pl.BlockSpec(memory_space=pl.ANY)
INVMEM = pl.BlockSpec(memory_space=pltpu.VMEM)
INSMEM = pl.BlockSpec(memory_space=pltpu.SMEM)


def dma(*dims):
    return pltpu.SemaphoreType.DMA(dims)


def dot(a, b, dims=NN):
    return lax.dot_general(a, b, (dims, ((), ())), preferred_element_type=f32)


def exact_dot(matrix, tensor):
    high = tensor.astype(bf16)
    low = (tensor - high.astype(f32)).astype(bf16)
    return dot(matrix, high) + dot(matrix, low)


def norm(x):
    average = jnp.mean(x, axis=-1, keepdims=True)
    centred = x - average
    inverse = lax.rsqrt(jnp.mean(centred * centred, axis=-1, keepdims=True) + eps)
    return centred * inverse, inverse


def norm_back(unit, inverse, gain, gradient):
    scaled = gradient * gain
    return inverse * (
        scaled
        - jnp.mean(scaled, axis=-1, keepdims=True)
        - unit * jnp.mean(scaled * unit, axis=-1, keepdims=True)
    )


GELU_A, GELU_B = math.sqrt(2.0 / math.pi), 0.044715


def gelu(x):
    t = jnp.tanh(GELU_A * (x + GELU_B * (x * x * x)))
    return 0.5 * x * (1.0 + t)


def gelu_both(x):
    square = x * x
    t = jnp.tanh(GELU_A * x * (1.0 + GELU_B * square))
    value = 0.5 * x * (1.0 + t)
    slope = 0.5 * (1.0 + t) + 0.5 * x * (1.0 - t * t) * (GELU_A * (1.0 + 3.0 * GELU_B * square))
    return value, slope


def sum_rows(x):
    return jnp.sum(x, axis=0, keepdims=True)


def add_rows(ref, rows):
    step = pl.program_id(0)

    @pl.when(step == 0)
    def _():
        ref[...] = jnp.zeros_like(ref)

    for i, row in enumerate(rows):
        ref[i:i + 1, :] += row


def transposed(x):
    return x.astype(f32).T.astype(bf16)


def window(head):
    low = HD * head
    return low // 128 * 128, -(-(low + HD) // 128) * 128


def head_mask(head, start, stop):
    lane = lax.broadcasted_iota(jnp.int32, (1, stop - start), 1) + start
    return (lane >= HD * head) & (lane < HD * head + HD)


def key_rows(own_ref, mem_ref):
    row = 0
    for ref in (own_ref, mem_ref):
        for t in range(ref.shape[0]):
            yield ref, t, slice(row, row + ref.shape[2])
            row += ref.shape[2]


def key_mask(own_ref, mem_ref, valid, has):
    parts = []
    for ref, rows, there in ((own_ref, valid[0], None), (mem_ref, valid[1], has)):
        block = ref.shape[2]
        lane = lax.rem(lax.broadcasted_iota(jnp.int32, (1, ref.shape[0] * block), 1), block)
        limit = rows if there is None else jnp.where(there > 0, rows, 0)
        parts.append(jnp.where(lane < limit, 0.0, NEG))
    return jnp.concatenate(parts, axis=1)


def assemble(w_ref, w_s):
    wide = w_ref.shape[2] // 3
    for part in range(3):
        pieces = [w_ref[h, :, wide * part:wide * part + wide].astype(f32) for h in range(w_ref.shape[0])]
        w_s[0, :, 384 * part:384 * part + 384] = jnp.concatenate(pieces, axis=1).astype(bf16)


def assemble_out(w_ref, out_s):
    wide = out_s.shape[1] // w_ref.shape[0]
    pieces = [w_ref[h, :, :wide].astype(f32) for h in range(w_ref.shape[0])]
    out_s[...] = jnp.concatenate(pieces, axis=1).astype(bf16)


def project_keys(own_ref, mem_ref, w_ref, bias_ref, x_s, k_s, v_s):
    for ref, t, rows in key_rows(own_ref, mem_ref):
        x_s[rows, :] = ref[t, 0]
    width = k_s.shape[1]
    for low in range(0, width, 384):
        k_s[:, low:low + 384] = dot(x_s[...], w_ref[low // 384, :, 384:768]).astype(bf16)
    for low in range(0, width, 384):
        value = dot(x_s[...], w_ref[low // 384, :, 768:])
        v_s[:, low:low + 384] = (value + bias_ref[1:2, low:low + 384]).astype(bf16)


def project_queries(x_ref, w_ref, bias_ref, q_s):
    width = q_s.shape[1]
    for low in range(0, width, 384):
        value = dot(x_ref[0], w_ref[low // 384, :, :384])
        q_s[:, low:low + 384] = (value + bias_ref[0:1, low:low + 384]).astype(bf16)


def norm_pool_kernel(x_ref, vec_ref, pool_ref, pair_ref, low_ref, pooled_ref, mean_ref):
    unit, _ = norm(x_ref[0].astype(f32))
    normed = unit * vec_ref[0:1, :] + vec_ref[1:2, :]
    low_ref[0] = normed.astype(bf16)
    pooled = exact_dot(pool_ref[...], normed)
    pooled_ref[0] = pooled.astype(bf16)
    mean_ref[0] = exact_dot(pair_ref[...], pooled).astype(bf16)


def write_shares(gw_ref, h, gw_s):
    wide = gw_ref.shape[2] // 3
    for part in range(3):
        low = wide * h
        columns = gw_s[low // 384, :, 384 * part:384 * part + 384][:, low % 384:low % 384 + wide]
        gw_ref[h, :, wide * part:wide * part + wide] = columns.astype(bf16)


def attend_kernel(chunk, valid, x_ref, own_ref, mem_ref, w_ref, qv_ref, has_ref, out_ref, lse_ref, w_s, x_s, q_s, k_s, v_s, s_s, p_s):
    nq, width = q_s.shape
    columns = key_mask(own_ref, mem_ref, valid, has_ref[pl.program_id(0)])
    if width == 384:
        @pl.when(pl.program_id(0) == 0)
        def _():
            assemble(w_ref, w_s)
        w_ref = w_s
    project_queries(x_ref, w_ref, qv_ref, q_s)
    project_keys(own_ref, mem_ref, w_ref, qv_ref, x_s, k_s, v_s)
    factor = HD**-0.5 * math.log2(math.e)
    stack = s_s.shape[0] // nq
    lanes = lax.broadcasted_iota(jnp.int32, (chunk, 128), 1)
    for tile in range(width // 384):
        group = slice(384 * tile, 384 * tile + 384)
        base = q_s[:, group].astype(f32)
        parts = [base[:, :128], base[:, 128:256], base[:, 256:384]]
        for first in range(4 * tile, 4 * tile + 4, stack):
            start, stop = window(first)[0], window(first + stack - 1)[1]
            masks = [head_mask(first + k, start, stop) for k in range(stack)]
            base = q_s[:, start:stop]
            query = jnp.concatenate([jnp.where(mask, base, jnp.zeros((), bf16)) for mask in masks], axis=0)
            s_s[...] = dot(query, k_s[:, start:stop], NT)

            def body(i, carry, k):
                rows = pl.ds(pl.multiple_of(i * chunk, chunk), chunk)
                here = pl.ds(pl.multiple_of(k * nq + i * chunk, chunk), chunk)
                score = s_s[here, :] * factor + columns
                top = jnp.max(score, axis=1, keepdims=True)
                power = jnp.exp2(score - top)
                total = jnp.sum(power, axis=1, keepdims=True)
                p_s[here, :] = (power * (1.0 / total)).astype(bf16)
                lse_ref[0, rows, :] = jnp.where(lanes == first + k, top + jnp.log2(total), lse_ref[0, rows, :])
                return carry

            for k in range(stack):
                lax.fori_loop(0, nq // chunk, functools.partial(body, k=k), 0, unroll=nq // chunk)
            both = dot(p_s[...], v_s[:, start:stop])
            for k, mask in enumerate(masks):
                out = jnp.where(mask, both[k * nq:(k + 1) * nq], 0.0)
                for w in range((stop - start) // 128):
                    n = start // 128 - 3 * tile + w
                    parts[n] = parts[n] + out[:, 128 * w:128 * w + 128]
        out_ref[0, :, group] = jnp.concatenate(parts, axis=1).astype(bf16)


def attend_back_kernel(
    chunk, valid, x_ref, g_ref, own_ref, mem_ref, w_ref, qv_ref, has_ref, lse_ref,
    dx_ref, dpool_ref, gw_ref, row_ref,
    w_s, x_s, q_s, k_s, v_s, s_s, dp_s, p_s, ds_s, dk_s, dv_s, gw_s,
):
    nq, width = q_s.shape
    step = pl.program_id(0)
    columns = key_mask(own_ref, mem_ref, valid, has_ref[step])
    if width == 384:
        @pl.when(step == 0)
        def _():
            assemble(w_ref, w_s)
        w_ref = w_s
    project_queries(x_ref, w_ref, qv_ref, q_s)
    project_keys(own_ref, mem_ref, w_ref, qv_ref, x_s, k_s, v_s)
    scaling = HD**-0.5
    factor = scaling * math.log2(math.e)
    stack = s_s.shape[0] // nq
    lanes = lax.broadcasted_iota(jnp.int32, (chunk, 128), 1)

    @pl.when(step == 0)
    def _():
        gw_s[...] = jnp.zeros_like(gw_s)

    xt = transposed(x_ref[0])
    keys_t = transposed(x_s[...])
    dx = None
    dpool = None
    row_q, row_v = [], []
    for tile in range(width // 384):
        group = slice(384 * tile, 384 * tile + 384)
        qt = transposed(q_s[:, group])
        gt = transposed(g_ref[0, :, group])
        parts = [None] * 3
        for first in range(4 * tile, 4 * tile + 4, stack):
            start, stop = window(first)[0], window(first + stack - 1)[1]
            masks = [head_mask(first + k, start, stop) for k in range(stack)]
            zero = jnp.zeros((), bf16)
            query = jnp.concatenate([jnp.where(mask, q_s[:, start:stop], zero) for mask in masks], axis=0)
            grad = jnp.concatenate([jnp.where(mask, g_ref[0, :, start:stop], zero) for mask in masks], axis=0)
            s_s[...] = dot(query, k_s[:, start:stop], NT)
            dp_s[...] = dot(grad, v_s[:, start:stop], NT)

            def body(i, carry, k):
                rows = pl.ds(pl.multiple_of(i * chunk, chunk), chunk)
                here = pl.ds(pl.multiple_of(k * nq + i * chunk, chunk), chunk)
                lse = jnp.sum(jnp.where(lanes == first + k, lse_ref[0, rows, :], 0.0), axis=1, keepdims=True)
                p = jnp.exp2(s_s[here, :] * factor + columns - lse)
                dp = dp_s[here, :]
                inner = jnp.sum(p * dp, axis=1, keepdims=True)
                p_s[here, :] = p.astype(bf16)
                ds_s[here, :] = (p * (dp - inner)).astype(bf16)
                return carry

            for k in range(stack):
                lax.fori_loop(0, nq // chunk, functools.partial(body, k=k), 0, unroll=nq // chunk)
            dq_both = dot(ds_s[...], k_s[:, start:stop]) * scaling
            for k, mask in enumerate(masks):
                mine = slice(k * nq, (k + 1) * nq)
                r = slice(HD * (first + k - 4 * tile), HD * (first + k - 4 * tile) + HD)
                dv_s[r, :] = dot(gt[r], p_s[mine, :])
                dk_s[r, :] = dot(qt[r], ds_s[mine, :]) * scaling
                dq = jnp.where(mask, dq_both[mine], 0.0)
                for w in range((stop - start) // 128):
                    n = start // 128 - 3 * tile + w
                    part = dq[:, 128 * w:128 * w + 128]
                    parts[n] = part if parts[n] is None else parts[n] + part
        total = jnp.concatenate(parts, axis=1) + g_ref[0, :, group].astype(f32)
        row_q.append(sum_rows(total))
        low = total.astype(bf16)
        gw_s[tile, :, :384] += dot(xt, low)
        add = dot(low, w_ref[tile, :, :384], NT)
        dx = add if dx is None else dx + add
        for part, src in ((1, dk_s), (2, dv_s)):
            grad = src[...].T
            if part == 2:
                row_v.append(sum_rows(grad))
            low = grad.astype(bf16)
            here = slice(384 * part, 384 * part + 384)
            gw_s[tile, :, here] += dot(keys_t, low)
            add = dot(low, w_ref[tile, :, here], NT)
            dpool = add if dpool is None else dpool + add
    dx_ref[0] = dx
    row = 0
    own, mem = own_ref.shape[2], mem_ref.shape[2]
    toks = own_ref.shape[0]
    for t in range(toks):
        dpool_ref[t, 0, :own, :] = dpool[t * own:(t + 1) * own].astype(bf16)
        dpool_ref[t, 0, own:, :] = dpool[toks * own + t * mem:toks * own + (t + 1) * mem].astype(bf16)
    add_rows(row_ref, [jnp.concatenate(row_q, axis=1), jnp.concatenate(row_v, axis=1)])

    @pl.when(step == pl.num_programs(0) - 1)
    def _():
        for h in range(gw_ref.shape[0]):
            write_shares(gw_ref, h, gw_s)


def first_mlp_kernel(x_ref, comb_ref, out_ref, up_ref, down_ref, ub_ref, vec_ref, pool_ref, pair_ref,
                     after_ref, middle_ref, pooled_ref, mean_ref, out_s):
    @pl.when(pl.program_id(0) == 0)
    def _():
        assemble_out(out_ref, out_s)

    after = x_ref[0].astype(f32) + dot(comb_ref[0], out_s[...], NT) + vec_ref[0:1, :]
    after_ref[0] = after
    unit, _ = norm(after)
    low = (unit * vec_ref[1:2, :] + vec_ref[2:3, :]).astype(bf16)
    total = after + vec_ref[3:4, :]
    for h in range(up_ref.shape[0]):
        hidden = gelu(dot(low, up_ref[h]) + ub_ref[h]).astype(bf16)
        total = total + dot(hidden, down_ref[h], NT)
    middle_ref[0] = total
    unit, _ = norm(total)
    pooled = exact_dot(pool_ref[...], unit * vec_ref[4:5, :] + vec_ref[5:6, :])
    pooled_ref[0] = pooled.astype(bf16)
    mean_ref[0] = exact_dot(pair_ref[...], pooled).astype(bf16)


def second_mlp_kernel(
    comb_ref, pooled_ref, cot_ref, out_ref, skip_ref, up_ref, down_ref, ub_ref, vec_ref,
    mixed_ref, dcomb_ref, dskip_ref, gmlp_ref, gout_ref, gskip_ref, gub_ref, row_ref,
    after_s, low_s, lowt_s, cott_s, sum_s, dlow_s, skip_s,
):
    step = pl.program_id(0)

    @pl.when(step == 0)
    def _():
        share = skip_s.shape[1] // skip_ref.shape[0]
        skip_s[...] = jnp.concatenate([skip_ref[h, :, :share].astype(f32) for h in range(skip_ref.shape[0])], axis=1).astype(bf16)
        after = dot(pooled_ref[...], skip_s[...], NT) + vec_ref[0:1, :]
        wide = out_ref.shape[2]
        for h in range(out_ref.shape[0]):
            after = after + dot(comb_ref[:, wide * h:wide * h + wide], out_ref[h], NT)
        after_s[...] = after
        unit, _ = norm(after)
        low = (unit * vec_ref[1:2, :] + vec_ref[2:3, :]).astype(bf16)
        low_s[...] = low
        lowt_s[...] = transposed(low)
        cott_s[...] = transposed(cot_ref[...])
        sum_s[...] = after + vec_ref[3:4, :]
        dlow_s[...] = jnp.zeros_like(dlow_s)

    pre = dot(low_s[...], up_ref[0]) + ub_ref[...]
    hidden, slope = gelu_both(pre)
    hidden = hidden.astype(bf16)
    dpre = dot(cot_ref[...], down_ref[0]) * slope
    gub_ref[...] = sum_rows(dpre)
    dpre = dpre.astype(bf16)
    sum_s[...] += dot(hidden, down_ref[0], NT)
    dlow_s[...] += dot(dpre, up_ref[0], NT)
    for n, grad in enumerate((dot(lowt_s[...], dpre), dot(cott_s[...], hidden))):
        rows = gmlp_ref.shape[3]
        for t in range(gmlp_ref.shape[1]):
            gmlp_ref[0, t, n] = grad[t * rows:(t + 1) * rows].astype(bf16)

    @pl.when(step == pl.num_programs(0) - 1)
    def _():
        mixed_ref[...] = sum_s[...].astype(bf16)
        unit, inverse = norm(after_s[...])
        dlow = dlow_s[...]
        cot = cot_ref[...].astype(f32)
        res = norm_back(unit, inverse, vec_ref[1:2, :], dlow) + cot
        row_ref[...] = jnp.zeros_like(row_ref)
        for i, row in enumerate((res, dlow, cot, dlow * unit)):
            row_ref[i:i + 1, :] = sum_rows(row)
        res = res.astype(bf16)
        dskip_ref[...] = dot(res, skip_s[...])
        rest = transposed(res)
        wide = out_ref.shape[2]
        for h in range(out_ref.shape[0]):
            here = slice(wide * h, wide * h + wide)
            dcomb_ref[:, here] = dot(res, out_ref[h]).astype(bf16)
            grad = dot(rest, comb_ref[:, here])
            half = gout_ref.shape[2]
            for n in range(2 * gout_ref.shape[1]):
                gout_ref[h, n // 2, :, wide * (n % 2):wide * (n % 2) + wide] = grad[half * n:half * n + half].astype(bf16)
        grad = dot(rest, pooled_ref[...])
        wide = gskip_ref.shape[3] // 2
        for h in range(gskip_ref.shape[0]):
            for t in range(gskip_ref.shape[1]):
                low, high = (grad[half * n:half * n + half, wide * h:wide * h + wide] for n in (2 * t, 2 * t + 1))
                gskip_ref[h, t] = jnp.concatenate([low, high], axis=1).astype(bf16)


def first_back_kernel(
    middle_ref, after_ref, comb_ref, dskip_ref, dq_ref, own_ref, mem_ref, out_ref, up_ref, down_ref, ub_ref, vec_ref,
    unpool_ref, unpair_ref,
    res_ref, dcomb_ref, gmlp_ref, gub_ref, row_ref,
    gup_s, gdown_s, gout_s, out_s,
):
    step = pl.program_id(0)

    @pl.when(step == 0)
    def _():
        gup_s[...] = jnp.zeros_like(gup_s)
        gdown_s[...] = jnp.zeros_like(gdown_s)
        gout_s[...] = jnp.zeros_like(gout_s)
        gub_ref[...] = jnp.zeros_like(gub_ref)
        assemble_out(out_ref, out_s)

    dpool = dskip_ref[0] + dq_ref[0] + own_ref[0] + exact_dot(unpair_ref[...], mem_ref[0])
    dnorm = exact_dot(unpool_ref[...], dpool)
    unit, inverse = norm(middle_ref[0])
    grad = norm_back(unit, inverse, vec_ref[2:3, :], dnorm)
    rows = [sum_rows(dnorm * unit), sum_rows(dnorm), sum_rows(grad)]
    low = grad.astype(bf16)
    lowt = transposed(low)
    unit, inverse = norm(after_ref[0])
    normed = (unit * vec_ref[0:1, :] + vec_ref[1:2, :]).astype(bf16)
    normedt = transposed(normed)
    dnormed = None
    for h in range(up_ref.shape[0]):
        hidden, slope = gelu_both(dot(normed, up_ref[h]) + ub_ref[h])
        hidden = hidden.astype(bf16)
        dpre = dot(low, down_ref[h]) * slope
        gub_ref[h] += sum_rows(dpre)
        dpre = dpre.astype(bf16)
        gdown_s[h] += dot(lowt, hidden)
        gup_s[h] += dot(normedt, dpre)
        add = dot(dpre, up_ref[h], NT)
        dnormed = add if dnormed is None else dnormed + add
    res = norm_back(unit, inverse, vec_ref[0:1, :], dnormed) + grad
    rows += [sum_rows(dnormed * unit), sum_rows(dnormed), sum_rows(res)]
    res_ref[0] = res
    res = res.astype(bf16)
    dcomb_ref[0] = dot(res, out_s[...]).astype(bf16)
    gout_s[...] += dot(transposed(res), comb_ref[0])
    add_rows(row_ref, rows)

    @pl.when(step == pl.num_programs(0) - 1)
    def _():
        fa, ha = gup_s.shape[2], gout_s.shape[1] // gmlp_ref.shape[0]
        for h in range(gmlp_ref.shape[0]):
            gmlp_ref[h, :, :fa] = gup_s[h].astype(bf16)
            gmlp_ref[h, :, fa:2 * fa] = gdown_s[h].astype(bf16)
            rest = gmlp_ref.shape[2] - 2 * fa - ha
            gout = jnp.concatenate([gout_s[:, ha * h:ha * h + ha], jnp.zeros((gout_s.shape[0], rest), f32)], axis=1)
            gmlp_ref[h, :, 2 * fa:] = gout.astype(bf16)


def last_back_kernel(x_ref, res_ref, dx_ref, own_ref, mem_ref, vec_ref, unpool_ref, unpair_ref, grad_ref, row_ref):
    dpool = own_ref[0] + exact_dot(unpair_ref[...], mem_ref[0])
    dnorm = dx_ref[0] + exact_dot(unpool_ref[...], dpool)
    unit, inverse = norm(x_ref[0].astype(f32))
    grad = norm_back(unit, inverse, vec_ref[0:1, :], dnorm) + res_ref[0]
    grad_ref[0] = grad.astype(bf16)
    add_rows(row_ref, [sum_rows(dnorm * unit), sum_rows(dnorm)])


def whole(array):
    return pl.BlockSpec(array.shape, lambda i: (0,) * array.ndim)


def by_micro(array, axis=0):
    block = array.shape[:axis] + (1,) + array.shape[axis + 1:]
    return pl.BlockSpec(block, lambda i: (0,) * axis + (i,) + (0,) * (array.ndim - axis - 1))


def shape(dims, dtype):
    return jax.ShapeDtypeStruct(dims, dtype)


def about(us):
    return pl.CostEstimate(flops=int(us * 1e9), bytes_accessed=0, transcendentals=0)


def call(kernel, steps, args, outs, scratch=(), name=None, us=10, number=None):
    def spec(array, how):
        if how is None:
            return whole(array)
        return by_micro(array, how) if isinstance(how, int) else how

    return pl.pallas_call(
        kernel,
        grid=(steps,),
        in_specs=[spec(a, how) for a, how in args],
        out_specs=[spec(a, how) for a, how in outs],
        out_shape=[a for a, _ in outs],
        scratch_shapes=[pltpu.VMEM(*one) if isinstance(one, tuple) else one for one in scratch],
        compiler_params=pltpu.CompilerParams(vmem_limit_bytes=VMEM_CAP, collective_id=number, has_side_effects=number is not None),
        cost_estimate=about(us),
        name=name,
    )(*[a for a, _ in args])


def stacked(nq):
    return 2 if nq < 512 else 1


def chunk_of(nq):
    return 112 if nq % 112 == 0 else 16


def attend(x, own, mem, w, qv, has, valid, width):
    batches, nq, d = x.shape
    keys = own.shape[0] * own.shape[2] + mem.shape[0] * mem.shape[2]
    return call(
        functools.partial(attend_kernel, chunk_of(nq), valid), batches,
        [(x, 0), (own, 1), (mem, 1), w, (qv, None), (has, pl.BlockSpec(memory_space=pltpu.SMEM))],
        [(shape((batches, nq, width), bf16), 0), (shape((batches, nq, 128), f32), 0)],
        [((1, d, 1152 if width == 384 else 128), bf16),
         ((keys, d), bf16), ((nq, width), bf16), ((keys, width), bf16), ((keys, width), bf16),
         ((stacked(nq) * nq, keys), f32), ((stacked(nq) * nq, keys), bf16)],
        name="attend", us=20,
    )


def attend_back(x, grad, own, mem, w, qv, has, valid, lse, heads):
    batches, nq, d = x.shape
    width = grad.shape[2]
    keys = own.shape[0] * own.shape[2] + mem.shape[0] * mem.shape[2]
    both = (own.shape[0], batches, own.shape[2] + mem.shape[2], d)
    groups = (width // 384, d, 1152)
    rows = stacked(nq) * nq
    return call(
        functools.partial(attend_back_kernel, chunk_of(nq), valid), batches,
        [(x, 0), (grad, 0), (own, 1), (mem, 1), w, (qv, None), (has, INSMEM), (lse, 0)],
        [(shape((batches, nq, d), f32), 0), (shape(both, bf16), 1), (shape((heads, d, 3 * width // heads), bf16), None), (shape((8, width), f32), None)],
        [((1, d, 1152 if width == 384 else 128), bf16),
         ((keys, d), bf16), ((nq, width), bf16), ((keys, width), bf16), ((keys, width), bf16),
         ((rows, keys), f32), ((rows, keys), f32), ((rows, keys), bf16), ((rows, keys), bf16),
         ((384, keys), f32), ((384, keys), f32), (groups, f32)],
        name="attend_back", us=36,
    )


def share_kernel(gather, count, *refs):
    if gather:
        pooled_ref, mean_ref, pick_ref, w_ref, *refs = refs
        biases, (own_ref, mem_ref, all_ref, *refs) = refs[:count], refs[count:]
        if count:
            (qv_a_ref, qv_b_ref, ub_a_ref, ub_b_ref), refs = refs[:4], refs[4:]
    else:
        pooled_ref, mean_ref, pick_ref, own_ref, mem_ref, *refs = refs
    (got_s, pick_s, local_sem, own_send, own_recv, mem_send, mem_recv, pass_send, pass_recv, clip_send, clip_recv, *refs) = refs
    clip, head, chip, core, chips = places()
    clips, heads = lax.axis_size("clip"), lax.axis_size("head")
    share = pooled_ref.shape[0]
    here = 2 * chip + core
    partner = {"tok": 2 * chip + 1 - core}
    across = [{"tok": 2 * rem(chip + k, chips) + core} for k in range(1, chips)]
    beside = [{"head": rem(head + d, heads)} for d in range(1, heads)]
    heads_of = lambda by, sign: [{"clip": clip + by, "head": rem(head + sign * d, heads)} for d in range(heads)]
    last, begun = clip < clips - 1, clip > 0
    near = [(d, None) for d in [partner] + across + (beside if gather else [])]
    greet(near + [(d, begun) for d in heads_of(-1, -1)], near + [(d, last) for d in heads_of(1, 1)])

    def spread(src, out, send, recv):
        copies = [remote(src, out.at[here], send.at[0], recv.at[0], partner)]
        copies += [remote(src, out.at[here], send.at[k + 1], recv.at[k + 1], across[k]) for k in range(chips - 1)]
        return copies

    def passed(out, k, row):
        block = 2 * rem(chip - k, chips) + core
        return remote(out.at[block], out.at[block], pass_send.at[row, k - 1], pass_recv.at[row, k - 1], partner)

    clip_copies = [remote(mean_ref, got_s.at[d], clip_send.at[d], clip_recv.at[d], device) for d, device in enumerate(heads_of(1, 1))]

    @pl.when(last)
    def _():
        for copy in clip_copies:
            copy.start()

    w_first, w_diagonal, w_core = {}, {}, {}
    if gather:
        w_local, w_send, w_recv, d_send, d_recv, c_send, c_recv, b_send, b_recv, *bias_got = refs
        bias_copies = [
            remote(ref, got.at[d], b_send.at[d, n], b_recv.at[d, n], device)
            for d, device in enumerate(beside)
            for n, (ref, got) in enumerate(zip(biases, bias_got))
        ]
        for copy in bias_copies:
            copy.start()
        mine = all_ref.at[head, here]
        for k in range(1, chips):
            w_first[k, 0] = remote(w_ref, mine, w_send.at[k - 1], w_recv.at[k - 1], across[k - 1])
        for d in range(1, heads):
            w_first[0, d] = remote(w_ref, mine, w_send.at[chips - 2 + d], w_recv.at[chips - 2 + d], beside[d - 1])
        w_core[0, 0] = remote(w_ref, mine, c_send.at[0, 0], c_recv.at[0, 0], partner)
        for copy in [*w_first.values(), w_core[0, 0]]:
            copy.start()
        w_copy = pltpu.make_async_copy(w_ref, mine, w_local.at[0])
        w_copy.start()

        def forward(k, d):
            block = all_ref.at[rem(head - d, heads), 2 * rem(chip - k, chips) + core]
            w_core[k, d] = remote(block, block, c_send.at[k, d], c_recv.at[k, d], partner)
            w_core[k, d].start()

    own_copies = spread(pooled_ref, own_ref, own_send, own_recv)
    for copy in own_copies[1:] + own_copies[:1]:
        copy.start()
    own_local = pltpu.make_async_copy(pooled_ref, own_ref.at[here], local_sem.at[0])
    own_local.start()
    if gather:
        for k in range(1, chips):
            w_first[k, 0].wait_recv()
            block = all_ref.at[head, 2 * rem(chip - k, chips) + core]
            for d in range(1, heads):
                w_diagonal[k, d] = remote(block, block, d_send.at[k - 1, d - 1], d_recv.at[k - 1, d - 1], beside[d - 1])
                w_diagonal[k, d].start()
            forward(k, 0)

    @pl.when(begun)
    def _():
        for copy in clip_copies:
            copy.wait_recv()
        for m in range(share):
            total = None
            for d in range(heads):
                for s in range(share):
                    piece = got_s[d, s].astype(f32) * pick_ref[m, d * share + s]
                    total = piece if total is None else total + piece
            pick_s[m] = total.astype(bf16)

    @pl.when(jnp.logical_not(begun))
    def _():
        pick_s[...] = jnp.zeros_like(pick_s)

    mem_copies = spread(pick_s, mem_ref, mem_send, mem_recv)
    for copy in mem_copies[1:] + mem_copies[:1]:
        copy.start()
    mem_local = pltpu.make_async_copy(pick_s, mem_ref.at[here], local_sem.at[1])
    mem_local.start()
    forwards = []
    for k in range(1, chips):
        own_copies[k].wait_recv()
        forwards.append(passed(own_ref, k, 0))
        forwards[-1].start()
    if gather:
        for d in range(1, heads):
            w_first[0, d].wait_recv()
            forward(0, d)
    for k in range(1, chips):
        mem_copies[k].wait_recv()
        forwards.append(passed(mem_ref, k, 1))
        forwards[-1].start()
    if gather:
        for k, d in w_diagonal:
            w_diagonal[k, d].wait_recv()
            forward(k, d)
        for copy in w_core.values():
            copy.wait_recv()
        for copy in bias_copies:
            copy.wait_recv()
    if count:
        by_head = []
        for ref, got in zip(biases, bias_got):
            pieces = []
            for h in range(heads):
                piece = ref[...]
                for d in range(1, heads):
                    piece = jnp.where(rem(head - d, heads) == h, got[d - 1], piece)
                pieces.append(piece)
            by_head.append(pieces)
        qv_a_ref[...] = jnp.concatenate(by_head[0], axis=1)
        qv_b_ref[...] = jnp.concatenate(by_head[1], axis=1)
        fa = ub_a_ref.shape[2]
        for h in range(heads):
            ub_a_ref[h] = by_head[2][h][:, :fa]
        ub_b_ref[...] = jnp.concatenate([piece[:, fa:] for piece in by_head[2]], axis=1)
        for copy in bias_copies:
            copy.wait_send()
    own_copies[0].wait_recv()
    mem_copies[0].wait_recv()
    for copy in forwards:
        copy.wait_recv()
    for copy in own_copies + mem_copies + forwards + [*w_first.values(), *w_diagonal.values(), *w_core.values()]:
        copy.wait_send()
    own_local.wait()
    mem_local.wait()
    if gather:
        w_copy.wait()

    @pl.when(last)
    def _():
        for copy in clip_copies:
            copy.wait_send()


def share_pooled(pooled, mean, pick, number, block=None, biases=(), fa=0):
    toks, heads = lax.axis_size("tok"), lax.axis_size("head")
    chips = toks // 2
    few = max(chips - 1, 1)
    args, specs = [pooled, mean, pick], [INVMEM, INVMEM, INSMEM]
    outs = [shape((toks,) + pooled.shape, bf16), shape((toks,) + mean.shape, bf16)]
    scratch = [
        pltpu.VMEM((heads,) + mean.shape, bf16), pltpu.VMEM(mean.shape, bf16), dma(2),
        dma(chips), dma(chips), dma(chips), dma(chips), dma(2, few), dma(2, few), dma(heads), dma(heads),
    ]
    if block is not None:
        args, specs = args + [block, *biases], specs + [ANY] + [INVMEM] * len(biases)
        outs = outs + [shape((heads, toks) + block.shape, bf16)]
        if biases:
            (_, wa), (_, wb), (_, wide) = (b.shape for b in biases)
            outs += [shape(dims, f32) for dims in ((2, heads * wa), (2, heads * wb), (heads, 1, fa), (1, heads * (wide - fa)))]
        firsts = max(chips + heads - 2, 1)
        scratch += [dma(1), dma(firsts), dma(firsts), dma(few, max(heads - 1, 1)), dma(few, max(heads - 1, 1)), dma(chips, heads), dma(chips, heads)]
        scratch += [dma(max(heads - 1, 1), max(len(biases), 1)), dma(max(heads - 1, 1), max(len(biases), 1))]
        scratch += [pltpu.VMEM((max(heads - 1, 1),) + b.shape, f32) for b in biases]
    return pl.pallas_call(
        functools.partial(share_kernel, block is not None, len(biases)),
        in_specs=specs,
        out_specs=[ANY] * min(len(outs), 3) + [INVMEM] * (len(outs) - 3),
        out_shape=outs,
        scratch_shapes=scratch,
        compiler_params=pltpu.CompilerParams(collective_id=number, has_side_effects=True, vmem_limit_bytes=VMEM_CAP),
        cost_estimate=about(20 if block is None else 30),
        name="share_pooled",
    )(*args)


def give_back_kernel(exchange, *refs):
    if exchange:
        part_ref, pick_ref, half_ref, own_ref, back_ref, all_ref, *refs, half_local, half_send, half_recv = refs
    else:
        part_ref, pick_ref, own_ref, back_ref, *refs = refs
    (mine_s, core_s, sum_s, chip_s, route_s, got_s,
     local_sem, core_send, core_recv, mem_send, mem_recv, own_send, own_recv, clip_send, clip_recv) = refs
    clip, head, chip, core, chips = places()
    clips, heads = lax.axis_size("clip"), lax.axis_size("head")
    share, rows = own_ref.shape[0], own_ref.shape[1]
    partner = {"tok": 2 * chip + 1 - core}
    across = [{"tok": 2 * rem(chip + k, chips) + core} for k in range(1, chips)]
    beside = [{"head": rem(head + d, heads)} for d in range(1, heads)]
    heads_of = lambda by, sign: [{"clip": clip + by, "head": rem(head + sign * d, heads)} for d in range(heads)]
    last, begun = clip < clips - 1, clip > 0
    near = [(d, None) for d in [partner] + across + (beside if exchange else [])]
    greet(near + [(d, last) for d in heads_of(1, 1)], near + [(d, begun) for d in heads_of(-1, -1)])

    order = [rem(chip + k, chips) for k in list(range(1, chips)) + [0]]
    core_copies, local_copies = [], []
    for n, other in enumerate(order):
        core_copies.append(remote(part_ref.at[2 * other + 1 - core], core_s.at[n], core_send.at[n], core_recv.at[n], partner))
        core_copies[-1].start()
    for n, other in enumerate(order):
        local_copies.append(pltpu.make_async_copy(part_ref.at[2 * other + core], mine_s.at[n], local_sem.at[n]))
        local_copies[-1].start()
    halves = []
    if exchange:
        halves = [remote(half_ref, all_ref.at[head], half_send.at[k], half_recv.at[k], d) for k, d in enumerate(beside)]
        for copy in halves:
            copy.start()
        half_copy = pltpu.make_async_copy(half_ref, all_ref.at[head], half_local.at[0])
        half_copy.start()
    mem_copies, own_copies = [], []
    for n in range(chips):
        local_copies[n].wait()
        core_copies[n].wait_recv()
        if n == chips - 1:
            break
        sum_s[n] = (mine_s[n].astype(f32) + core_s[n].astype(f32)).astype(bf16)
        low, high = pl.ds(0, rows), pl.ds(rows, sum_s.shape[2] - rows)
        mem_copies.append(remote(sum_s.at[n, :, high, :], chip_s.at[n, :, high, :], mem_send.at[n], mem_recv.at[n], across[n]))
        mem_copies[-1].start()
        own_copies.append(remote(sum_s.at[n, :, low, :], chip_s.at[n, :, low, :], own_send.at[n], own_recv.at[n], across[n]))
        own_copies[-1].start()
    base = chips - 1
    for copy in mem_copies:
        copy.wait_recv()
    memory = []
    for m in range(share):
        total = mine_s[base, m, rows:].astype(f32) + core_s[base, m, rows:].astype(f32)
        for n in range(chips - 1):
            total = total + chip_s[n, m, rows:].astype(f32)
        memory.append(total)
    clip_copies = [
        remote(route_s.at[d], got_s.at[d], clip_send.at[d], clip_recv.at[d], device) for d, device in enumerate(heads_of(-1, -1))
    ]

    @pl.when(begun)
    def _():
        for d in range(heads):
            for s in range(share):
                total = None
                for m in range(share):
                    piece = memory[m] * pick_ref[m, d * share + s]
                    total = piece if total is None else total + piece
                route_s[d, s] = total.astype(bf16)
            clip_copies[d].start()

    for copy in own_copies:
        copy.wait_recv()
    for m in range(share):
        total = mine_s[base, m, :rows].astype(f32) + core_s[base, m, :rows].astype(f32)
        for n in range(chips - 1):
            total = total + chip_s[n, m, :rows].astype(f32)
        own_ref[m] = total

    @pl.when(last)
    def _():
        for copy in clip_copies:
            copy.wait_recv()
        total = got_s[0].astype(f32)
        for d in range(1, heads):
            total = total + got_s[d].astype(f32)
        back_ref[...] = total

    @pl.when(jnp.logical_not(last))
    def _():
        back_ref[...] = jnp.zeros_like(back_ref)

    for copy in halves:
        copy.wait_recv()
    for copy in core_copies + mem_copies + own_copies + halves:
        copy.wait_send()
    if exchange:
        half_copy.wait()

    @pl.when(begun)
    def _():
        for copy in clip_copies:
            copy.wait_send()


def give_back(part, pick, own_rows, number, half=None):
    toks, heads = lax.axis_size("tok"), lax.axis_size("head")
    chips, few = toks // 2, max(toks // 2 - 1, 1)
    share, rows, d = part.shape[1:]
    args, specs = [part, pick], [ANY, INSMEM]
    outs, out_specs = [shape((share, own_rows, d), f32), shape((share, rows - own_rows, d), f32)], [INVMEM, INVMEM]
    scratch = [
        pltpu.VMEM((chips,) + part.shape[1:], bf16), pltpu.VMEM((chips,) + part.shape[1:], bf16),
        pltpu.VMEM((few,) + part.shape[1:], bf16), pltpu.VMEM((few,) + part.shape[1:], bf16),
        pltpu.VMEM((heads, share, rows - own_rows, d), bf16), pltpu.VMEM((heads, share, rows - own_rows, d), bf16),
        dma(chips), dma(chips), dma(chips), dma(few), dma(few), dma(few), dma(few), dma(heads), dma(heads),
    ]
    if half is not None:
        args, specs = args + [half], specs + [ANY]
        outs, out_specs = outs + [shape((heads,) + half.shape, half.dtype)], out_specs + [ANY]
        scratch += [dma(1), dma(max(heads - 1, 1)), dma(max(heads - 1, 1))]
    return pl.pallas_call(
        functools.partial(give_back_kernel, half is not None),
        in_specs=specs,
        out_specs=out_specs,
        out_shape=outs,
        scratch_shapes=scratch,
        compiler_params=pltpu.CompilerParams(collective_id=number, has_side_effects=True, vmem_limit_bytes=VMEM_CAP),
        cost_estimate=about(25),
        name="give_back",
    )(*args)


def finish_kernel(half_ref, last_ref, qv_a_rows, a_ref, b_ref, qv_b_rows, ub_a_rows, ub_b_rows, grad_ref, rest_ref, group_ref,
                  all_ref, total_ref, sums_ref, *scratch):
    (small_ref, small_s, small_core, small_chip, small_head, small_clip, part_s, part_core, head_s, part_chip, part_head,
     local_sem, half_send, half_recv, core_send, core_recv, chip_send, chip_recv, head_send, head_recv,
     clip_send, clip_recv, *chain) = scratch
    first_lanes, next_lanes, deep = group_ref.shape[1], rest_ref.shape[1], grad_ref.shape[1]
    bounds = [0, first_lanes // 2, first_lanes, first_lanes + next_lanes // 2, first_lanes + next_lanes, chain[0].shape[1]]
    chain = Chain(*chain[:3], [(slice(None), pl.ds(low, high - low)) for low, high in zip(bounds, bounds[1:])], *chain[3:])
    clip, head, chip, core, chips = places()
    clips, heads = lax.axis_size("clip"), lax.axis_size("head")
    share = half_ref.shape[0]
    partner = {"tok": 2 * chip + 1 - core}
    across = [{"tok": 2 * rem(chip + k, chips) + core} for k in range(1, chips)]
    beside = [{"head": rem(head + k, heads)} for k in range(1, heads)]
    along = [{"clip": rem(clip + k, clips)} for k in range(1, clips)]
    peers = [(d, None) for d in [partner] + across + beside + along]
    greet(peers, peers)
    chain.part[:, :first_lanes] = group_ref[...]
    chain.part[:, first_lanes:first_lanes + next_lanes] = rest_ref[...]
    for n in range(4):
        chain.send_ends(n)
    pending = []
    d1 = small_ref.shape[1]
    small_ref[...] = jnp.zeros_like(small_ref)
    small_ref[0:2, :] = last_ref[0:2, :]
    small_ref[2:4, :] = qv_a_rows[0:2, :]
    for row, source in enumerate((3, 0, 5, 4, 2, 1)):
        small_ref[4 + row:5 + row, :] = a_ref[source:source + 1, :]
    row = 10
    longer = [b_ref[n:n + 1, :] for n in (3, 0, 1, 2)] + [qv_b_rows[n:n + 1, :] for n in range(2)]
    for values in longer + [ub_a_rows[h] for h in range(heads)] + [ub_b_rows[...]]:
        for low in range(0, values.shape[1], d1):
            small_ref[row:row + 1, :] = values[:, low:low + d1]
            row += 1
    def go(copies):
        for copy in copies:
            copy.start()
        pending.extend(copies)
        return copies

    def arrived(copies):
        for copy in copies:
            copy.wait_recv()

    def in_order(index, size, own, slot):
        total = None
        for i in range(size):
            piece = jnp.where(index == i, own, jnp.zeros_like(own))
            for k in range(size - 1):
                piece = jnp.where(rem(index - k - 1, size) == i, slot(k), piece)
            total = piece if total is None else total + piece
        return total

    first = go([remote(small_ref, small_core, core_send.at[0], core_recv.at[0], partner)])
    for h in range(heads):
        for x in range(chips):
            n = h * chips + x
            first += go([remote(grad_ref.at[2 * n + 1 - core], part_core.at[n], core_send.at[n + 1], core_recv.at[n + 1], partner)])
    halves = [
        [remote(half_ref.at[s], all_ref.at[head, s], half_send.at[k, s], half_recv.at[k, s], d) for k, d in enumerate(beside)]
        for s in range(share)
    ]
    local_half = pltpu.make_async_copy(half_ref, all_ref.at[head], local_sem.at[0])
    local_half.start()
    arrived(first)
    small_s[0] = small_ref[...] + small_core[...]
    for n in range(heads * chips):
        part_s[n] = (grad_ref[2 * n + core].astype(f32) + part_core[n].astype(f32)).astype(bf16)
    copies = []
    for k, d in enumerate(beside):
        copies += go([remote(small_s.at[0], small_head.at[k], head_send.at[k, 0], head_recv.at[k, 0], d)])
        for x in range(chips):
            block = rem(head + k + 1, heads) * chips + x
            copies += go([remote(part_s.at[block], part_head.at[k, x], head_send.at[k, x + 1], head_recv.at[k, x + 1], d)])
    for s in range(share):
        go(halves[s])
    chain.send_parts(0)
    chain.send_parts(1)
    arrived(copies)
    small_s[1] = in_order(head, heads, small_s[0], lambda k: small_head[k])
    for x in range(chips):
        total = part_s[head * chips + x].astype(f32)
        for k in range(heads - 1):
            total = total + part_head[k, x].astype(f32)
        head_s[x] = total.astype(bf16)
    copies = []
    for k, d in enumerate(across):
        copies += go([remote(small_s.at[1], small_chip.at[k], chip_send.at[k, 0], chip_recv.at[k, 0], d)])
        copies += go([remote(head_s.at[rem(chip + k + 1, chips)], part_chip.at[k], chip_send.at[k, 1], chip_recv.at[k, 1], d)])
    chain.send_parts(2)
    chain.middle_totals(0)
    chain.send_parts(3)
    arrived(copies)
    small_s[2] = in_order(chip, chips, small_s[1], lambda k: small_chip[k])
    total = head_s[chip].astype(f32)
    for k in range(chips - 1):
        total = total + part_chip[k].astype(f32)
    mine = first_lanes + next_lanes
    chain.part[:, mine:mine + grad_ref.shape[2]] = total.astype(bf16)
    chain.send_ends(4)
    copies = []
    for k, d in enumerate(along):
        copies += go([remote(small_s.at[2], small_clip.at[k], clip_send.at[k, 0], clip_recv.at[k, 0], d)])
    chain.middle_totals(1)
    chain.middle_totals(2)
    chain.send_parts(4)
    chain.middle_totals(3)
    chain.middle_totals(4)
    for n in range(5):
        chain.other_totals(n)
    arrived(copies)
    total_ref[...] = in_order(clip, clips, small_s[2], lambda k: small_clip[k])
    sums_ref[...] = chain.from_inner[...]
    chain.close()
    for copies in halves:
        arrived(copies)
    for copy in pending:
        copy.wait_send()
    local_half.wait()


def finish(half, rows, grad, rest, first, count, number):
    toks, heads, clips = lax.axis_size("tok"), lax.axis_size("head"), lax.axis_size("clip")
    chips = toks // 2
    across, beside, along = (max(n, 1) for n in (chips - 1, heads - 1, clips - 1))
    block, depth, d1 = grad.shape[1:], rest.shape[0], rows[0].shape[1]
    small = (-(-count // 8) * 8, d1)
    low, full = lambda *dims: pltpu.VMEM(dims, bf16), lambda *dims: pltpu.VMEM(dims + small, f32)
    buffer = (depth, first.shape[1] + rest.shape[1] + -(-block[1] // 128) * 128)
    return pl.pallas_call(
        finish_kernel,
        in_specs=[ANY] + [INVMEM] * (len(rows) + 3),
        out_specs=[ANY, INVMEM, INVMEM],
        out_shape=[shape((heads,) + half.shape, half.dtype), shape(small, f32), shape(buffer, bf16)],
        scratch_shapes=[
            full(), full(3), full(), full(across), full(beside), full(along),
            low(heads * chips, *block), low(heads * chips, *block), low(chips, *block), low(across, *block), low(beside, chips, *block),
            dma(1), dma(beside, half.shape[0]), dma(beside, half.shape[0]), dma(heads * chips + 1), dma(heads * chips + 1),
            dma(across, 2), dma(across, 2), dma(beside, chips + 1), dma(beside, chips + 1), dma(along, 1), dma(along, 1),
            *chain_scratch(buffer, 5),
        ],
        compiler_params=pltpu.CompilerParams(collective_id=number, has_side_effects=True, vmem_limit_bytes=VMEM_CAP),
        cost_estimate=about(40),
        name="finish",
    )(half, *rows, grad, rest, first)


def write_kernel(head_ref, total_ref, sums_ref, mlp_ref, qkv_a_ref, out_a_ref, up_a_ref, down_a_ref, qkv_b_ref, out_b_ref, skip_b_ref,
                 up_b_ref, down_b_ref, gains_a_ref, gains_b_ref, shifts_a_ref, shifts_b_ref, qv_a_ref, qv_b_ref, ub_a_ref, ub_b_ref):
    head, total = head_ref[0], total_ref[...]
    at = [10]

    def rows(width):
        first = at[0]
        at[0] += width // total.shape[1]
        return jnp.concatenate([total[r:r + 1] for r in range(first, at[0])], axis=1)

    def share_of(row, width):
        piece = row[:, :width]
        for h in range(1, row.shape[1] // width):
            piece = jnp.where(head == h, row[:, width * h:width * h + width], piece)
        return piece

    gains_a_ref[0:1, :] = total[0:1]
    gains_a_ref[1:3, :] = total[4:6]
    shifts_a_ref[0:1, :] = total[1:2]
    shifts_a_ref[1:5, :] = total[6:10]
    d2, fa, fb = gains_b_ref.shape[1], ub_a_ref.shape[1], ub_b_ref.shape[1]
    heads = total.shape[1] // qv_a_ref.shape[1]
    for i in range(2):
        qv_a_ref[i:i + 1, :] = share_of(total[2 + i:3 + i], qv_a_ref.shape[1])
    gains_b_ref[...] = rows(d2)
    for i in range(3):
        shifts_b_ref[i:i + 1, :] = rows(d2)
    for i in range(2):
        qv_b_ref[i:i + 1, :] = share_of(rows(d2), qv_b_ref.shape[1])
    ub_a_ref[...] = share_of(rows(heads * fa), fa)
    ub_b_ref[...] = share_of(rows(heads * fb), fb)
    low = 0
    depth = sums_ref.shape[0]

    def take(ref):
        nonlocal low
        ref[...] = sums_ref[:, low:low + ref.shape[1]].astype(f32)
        low += ref.shape[1]

    for part in range(3):
        take(qkv_b_ref.at[part])
    for ref in (out_b_ref, skip_b_ref):
        for n in range(2):
            take(ref.at[depth * n:depth * n + depth])
    for ref in (up_a_ref, down_a_ref, out_a_ref):
        take(ref)
    low = -(-low // 256) * 256
    for part in range(3):
        take(qkv_a_ref.at[part])
    up_b_ref[...] = mlp_ref[:up_b_ref.shape[0], :].astype(f32)
    down_b_ref[...] = mlp_ref[up_b_ref.shape[0]:, :].astype(f32)


def reduce_clips(shard):
    clips, clip = lax.axis_size("clip"), lax.axis_index("clip")
    pieces = shard.reshape(clips, -1, shard.shape[-1])
    total = lax.dynamic_index_in_dim(pieces, clip, 0, keepdims=False).astype(f32)
    for k in range(1, clips):
        give = lax.dynamic_index_in_dim(pieces, (clip + k) % clips, 0, keepdims=False)
        total = total + lax.ppermute(give, "clip", [(i, (i + k) % clips) for i in range(clips)]).astype(f32)
    return total.astype(bf16)


def spread_clips(piece):
    clips, clip = lax.axis_size("clip"), lax.axis_index("clip")
    out = jnp.zeros((clips,) + piece.shape, piece.dtype)
    out = lax.dynamic_update_index_in_dim(out, piece, clip, 0)
    for k in range(1, clips):
        got = lax.ppermute(piece, "clip", [(i, (i + k) % clips) for i in range(clips)])
        out = lax.dynamic_update_index_in_dim(out, got, (clip - k + clips) % clips, 0)
    return out.reshape((-1,) + piece.shape[1:])


def padded_rows(*rows):
    return jnp.concatenate([jnp.stack(rows), jnp.zeros((-len(rows) % 8, rows[0].shape[0]), f32)])


def local(
    clips_in, resets, assign, w_qkv_a, w_out_a, w_up_a, w_down_a, w_qkv_b, w_out_b, w_skip_b, w_up_b, w_down_b,
    gains_a, gains_b, shifts_a, shifts_b, qv_bias_a, qv_bias_b, up_bias_a, up_bias_b, cotangent,
):
    heads, toks, clips = lax.axis_size("head"), lax.axis_size("tok"), lax.axis_size("clip")
    head = lax.axis_index("head")
    micro, frames = clips_in.shape[1], clips_in.shape[2]
    d1, d2 = clips_in.shape[-1], cotangent.shape[-1]
    share = micro // heads
    first = head * share
    pool_np, pair_np = pool_matrix(frames), pair_matrix(frames)
    pooling, pairing = jnp.asarray(pool_np, bf16), jnp.asarray(pair_np, bf16)
    unpooling, unpairing = jnp.asarray(pool_np.T, bf16), jnp.asarray(pair_np.T, bf16)
    tokens, pooled_tokens = frames * PATCH, frames * POOLED
    own_rows, mem_rows = up16(pooled_tokens), up16(frames // 2 * POOLED)
    rows2 = share * own_rows


    def by_patch(tensor):
        return tensor.transpose(0, 2, 1, 3).reshape(tensor.shape[0], -1, tensor.shape[3])

    def by_frame(rows, like):
        return rows.reshape(like[:2] + (like[3], like[2], like[4])).transpose(0, 1, 3, 2, 4)

    cot = by_patch(lax.dynamic_slice_in_dim(cotangent[0], first, share, 0))

    source = lax.dynamic_slice_in_dim(assign[0], first, share, 0)
    flags = lax.dynamic_slice_in_dim(resets[0], first, share, 0)
    slot = ((head - source // share + heads) % heads) * share + source % share
    pick = (jnp.arange(heads * share)[None, :] == slot[:, None]).astype(f32)
    has = ((flags == 0) & (lax.axis_index("clip") > 0)).astype(jnp.int32)
    valid = (pooled_tokens, frames // 2 * POOLED)

    group = ("head", "tok")
    fa, ha = w_up_a.shape[1], w_out_a.shape[1]
    fb, hb, hs = w_up_b.shape[1], w_out_b.shape[1], w_skip_b.shape[1]
    spare_a = jnp.zeros((w_out_a.shape[0], -w_out_a.shape[1] % 256), bf16)
    pack_a = jnp.concatenate([w_up_a, w_down_a, w_out_a, spare_a], axis=1)
    all_a = lax.all_gather(pack_a, group).reshape(heads, d1, -1)
    stream = by_patch(lax.dynamic_slice_in_dim(clips_in[0], first, share, 0))
    low1, pooled1, mean1 = call(
        norm_pool_kernel, share,
        [(stream, 0), (padded_rows(gains_a[0], shifts_a[0]), None), (pooling, None), (pairing, None)],
        [(shape((share, tokens, d1), bf16), 0), (shape((share, own_rows, d1), bf16), 0), (shape((share, mem_rows, d1), bf16), 0)],
        name="norm_pool", us=5,
    )
    pack_w = jnp.concatenate([*w_qkv_a.transpose(1, 0, 2)], axis=1)
    own1, mem1, all_w, qv_a, qv_b, ub_a, ub_b = share_pooled(
        pooled1, mean1, pick, 0, pack_w, [qv_bias_a, qv_bias_b, jnp.concatenate([up_bias_a, up_bias_b])[None]], fa)
    all_w = all_w.reshape(heads, d1, -1)
    pack_q = jnp.concatenate([*w_qkv_b.transpose(1, 0, 2)], axis=1)
    own1, w_up_b, cot = lax.optimization_barrier((own1, w_up_b, cot))
    spare = jnp.zeros((w_up_b.shape[0], -(2 * fb + hb + hs) % hb), bf16)
    pack_b = jnp.concatenate([w_up_b, w_down_b, w_out_b, w_skip_b, spare], axis=1)
    all_b = lax.all_gather(pack_b, group).reshape(heads, d2, -1)
    cot = jnp.pad(cot, ((0, 0), (0, own_rows - pooled_tokens), (0, 0))).reshape(rows2, d2)

    up_spec, down_spec = (pl.BlockSpec((heads, d1, fa), lambda i, n=n: (0, 0, n)) for n in range(2))
    out_a_spec = pl.BlockSpec((heads, d1, 256), lambda i: (0, 0, 2 * fa // 256))

    comb1, lse1 = attend(low1, own1, mem1, (all_w, None), qv_a, has, valid, d1)
    after1, middle, pooled3, mean3 = call(
        first_mlp_kernel, share,
        [(stream, 0), (comb1, 0), (all_a, out_a_spec), (all_a, up_spec), (all_a, down_spec), (ub_a, None),
         (padded_rows(shifts_a[1], gains_a[1], shifts_a[2], shifts_a[3], gains_a[2], shifts_a[4]), None),
         (pooling, None), (pairing, None)],
        [(shape((share, tokens, d1), f32), 0), (shape((share, tokens, d1), f32), 0),
         (shape((share, own_rows, d1), bf16), 0), (shape((share, mem_rows, d1), bf16), 0)],
        [((d1, d1), bf16)],
        name="first_mlp", us=13,
    )

    own2, mem2, all_q = share_pooled(pooled3, mean3, pick, 1, pack_q)
    all_q = all_q.reshape(heads, d1, -1)
    comb2, lse2 = attend(pooled3, own2, mem2, (all_q, None), qv_b, has, valid, d2)
    chunk = 768
    per_head = fb // chunk
    steps = heads * per_head
    out_spec, skip_spec = (pl.BlockSpec((heads, d2, hb), lambda j, n=n: (0, 0, 2 * fb // hb + n)) for n in range(2))
    rows_spec = pl.BlockSpec((1, d2, chunk), lambda j: (j // per_head, 0, j % per_head))
    mixed, dcomb2, dskip, g_mlp_b, g_out_b, g_skip_b, g_ub_b, rows_b = call(
        second_mlp_kernel, steps,
        [(comb2.reshape(rows2, d2), None), (pooled3.reshape(rows2, d1), None), (cot, None), (all_b, out_spec), (all_b, skip_spec),
         (all_b, rows_spec),
         (all_b, pl.BlockSpec((1, d2, chunk), lambda j: (j // per_head, 0, per_head + j % per_head))),
         (ub_b, pl.BlockSpec((1, chunk), lambda j: (0, j))),
         (padded_rows(shifts_b[0], gains_b, shifts_b[1], shifts_b[2]), None)],
        [(shape((rows2, d2), bf16), None), (shape((rows2, d2), bf16), None), (shape((rows2, d1), f32), None),
         (shape((heads, toks, 2, d2 // toks, fb), bf16),
          pl.BlockSpec((1, toks, 2, d2 // toks, chunk), lambda j: (j // per_head, 0, 0, 0, j % per_head))),
         (shape((heads, toks, d2 // toks // 2, 2 * hb), bf16), None), (shape((heads, toks, d2 // toks // 2, 2 * hs), bf16), None),
         (shape((1, heads * fb), f32), pl.BlockSpec((1, chunk), lambda j: (0, j))), (shape((8, d2), f32), None)],
        [((rows2, d2), f32), ((rows2, d2), bf16), ((d2, rows2), bf16), ((d2, rows2), bf16), ((rows2, d2), f32), ((rows2, d2), f32), ((d2, d1), bf16)],
        name="second_mlp", us=26,
    )

    def by_owner(grad):
        return grad.reshape((heads * toks, -1) + grad.shape[2:])

    def scatter(grad):
        return lax.psum_scatter(grad, group, scatter_dimension=0, tiled=False)

    sum_mlp_b = scatter(g_mlp_b.reshape((heads * toks,) + g_mlp_b.shape[2:])).reshape(-1, fb)
    dcomb2 = dcomb2.reshape(share, own_rows, d2)
    dq2, dpool2, g_qkv_b, rows_qv_b = attend_back(pooled3, dcomb2, own2, mem2, (all_q, None), qv_b, has, valid, lse2, heads)
    own_back2, mem_back2 = give_back(dpool2, pick, own_rows, 2)

    merge = lambda grad: grad.reshape((heads * toks,) + grad.shape[2:])
    rest_b = jnp.concatenate([by_owner(g_qkv_b), merge(g_out_b), merge(g_skip_b)], axis=2)
    sum_rest_b = scatter(rest_b)

    res1, dcomb1, g_mlp_a, g_ub_a, rows_a = call(
        first_back_kernel, share,
        [(middle, 0), (after1, 0), (comb1, 0), (dskip.reshape(share, own_rows, d1), 0), (dq2, 0), (own_back2, 0), (mem_back2, 0),
         (all_a, out_a_spec), (all_a, up_spec), (all_a, down_spec), (ub_a, None),
         (padded_rows(gains_a[1], shifts_a[2], gains_a[2]), None), (unpooling, None), (unpairing, None)],
        [(shape((share, tokens, d1), f32), 0), (shape((share, tokens, d1), bf16), 0),
         (shape((heads, d1, -(-(2 * fa + ha) // 256) * 256), bf16), None),
         (shape((heads, 1, fa), f32), None), (shape((8, d1), f32), None)],
        [((heads, d1, fa), f32), ((heads, d1, fa), f32), ((d1, d1), f32), ((d1, d1), bf16)],
        name="first_back", us=26,
    )
    rest_a = by_owner(g_mlp_a)
    dcomb1, sum_mlp_b, rest_a = lax.optimization_barrier((dcomb1, sum_mlp_b, rest_a))
    sum_rest_a = scatter(rest_a)
    sum_mlp_b = reduce_clips(sum_mlp_b)
    dx1, dpool1, g_qkv_a, rows_qv_a = attend_back(low1, dcomb1, own1, mem1, (all_w, None), qv_a, has, valid, lse1, heads)
    dpool1, sum_mlp_b = lax.optimization_barrier((dpool1, sum_mlp_b))
    sum_mlp_b = spread_clips(sum_mlp_b)
    own_back1, mem_back1, mixed_all = give_back(dpool1, pick, own_rows, 3, mixed.reshape(share, own_rows, d2))
    stream_grad, rows_last = call(
        last_back_kernel, share,
        [(stream, 0), (res1, 0), (dx1, 0), (own_back1, 0), (mem_back1, 0), (padded_rows(gains_a[0]), None),
         (unpooling, None), (unpairing, None)],
        [(shape((share, tokens, d1), bf16), 0), (shape((8, d1), f32), None)],
        name="last_back", us=6,
    )

    rows = [rows_last, rows_qv_a, rows_a, rows_b, rows_qv_b, g_ub_a, g_ub_b]
    count = 10 + (6 * d2 + heads * (fa + fb)) // d1
    stream_all, total, sums = finish(stream_grad, rows, by_owner(g_qkv_a), sum_rest_a, sum_rest_b, count, 4)
    row1, row2 = w_up_a.shape[0], w_up_b.shape[0]
    outs = [(3, row1, ha), (row1, ha), (row1, fa), (row1, fa), (3, row1, hb), (row2, hb), (row2, hs), (row2, fb), (row2, fb),
            (3, d1), (1, d2), (5, d1), (3, d2), (2, ha), (2, hb), (1, fa), (1, fb)]
    grads = call(
        write_kernel, 1,
        [(head.astype(jnp.int32)[None], INSMEM), (total, None), (sums, None), (sum_mlp_b, None)],
        [(shape(dims, f32), None) for dims in outs],
        name="write", us=4,
    )
    mixed_all = mixed_all.reshape(micro, own_rows, d2)[:, :pooled_tokens]
    return (
        by_frame(mixed_all, cotangent.shape),
        by_frame(stream_all.astype(f32), clips_in.shape),
        grads[0].transpose(1, 0, 2), *grads[1:4], grads[4].transpose(1, 0, 2), *grads[5:10],
        grads[10][0], *grads[11:15], grads[15][0], grads[16][0],
    )


def solution(mesh):
    in_specs = (
        P("clip", None, "tok", None, None),
        P("clip", None),
        P("clip", None),
        P("tok", None, "head"),
        P("tok", "head"),
        P("tok", "head"),
        P("tok", "head"),
        P("tok", None, "head"),
        P("tok", "head"),
        P("tok", "head"),
        P("tok", "head"),
        P("tok", "head"),
        P(),
        P(),
        P(),
        P(),
        P(None, "head"),
        P(None, "head"),
        P("head"),
        P("head"),
        P("clip", None, "tok", None, None),
    )
    out_specs = (
        P("clip", None, "tok", None, None),
        P("clip", None, "tok", None, None),
        P("tok", None, "head"),
        P("tok", "head"),
        P("tok", "head"),
        P("tok", "head"),
        P("tok", None, "head"),
        P("tok", "head"),
        P("tok", "head"),
        P("tok", "head"),
        P("tok", "head"),
        P(),
        P(),
        P(),
        P(),
        P(None, "head"),
        P(None, "head"),
        P("head"),
        P("head"),
    )
    return jax.shard_map(local, mesh=mesh, in_specs=in_specs, out_specs=out_specs, check_vma=False)
```

```python
import functools
import math

import jax
import jax.numpy as jnp
import numpy as np
from jax import lax
from jax.experimental import pallas as pl
from jax.experimental.pallas import tpu as pltpu
from jax.sharding import PartitionSpec as P

GRID = 14
PATCH = GRID * GRID
POOLED = PATCH // 4
HD = 96
NEG = -1e30
VMEM_CAP = 62 * 2**20
eps = 1e-06
f32, bf16 = jnp.float32, jnp.bfloat16
NN, NT, TN = ((1,), (0,)), ((1,), (1,)), ((0,), (0,))


def up16(n):
    return -(-n // 16) * 16


def pool_matrix(frames):
    rows, cols = up16(frames * POOLED), frames * PATCH
    out = np.zeros((rows, cols), np.float32)
    half = GRID // 2
    for f in range(frames):
        for p in range(PATCH):
            r, c = divmod(p, GRID)
            out[((r // 2) * half + c // 2) * frames + f, p * frames + f] = 0.25
    return out


def pair_matrix(frames):
    rows, cols = up16(frames // 2 * POOLED), up16(frames * POOLED)
    out = np.zeros((rows, cols), np.float32)
    for j in range(frames // 2):
        for p in range(POOLED):
            out[p * (frames // 2) + j, p * frames + 2 * j] = 0.5
            out[p * (frames // 2) + j, p * frames + 2 * j + 1] = 0.5
    return out


MESH = pl.DeviceIdType.MESH


def places():
    tok, toks = lax.axis_index("tok"), lax.axis_size("tok")
    return lax.axis_index("clip"), lax.axis_index("head"), tok // 2, tok % 2, toks // 2


def greet(copies_to_me, i_copy_to):
    barrier = pltpu.get_barrier_semaphore()
    for device, condition in copies_to_me:
        if condition is None:
            pl.semaphore_signal(barrier, inc=1, device_id=device, device_id_type=MESH)
        else:
            @pl.when(condition)
            def _():
                pl.semaphore_signal(barrier, inc=1, device_id=device, device_id_type=MESH)
    count = 0
    for _, condition in i_copy_to:
        count = count + (1 if condition is None else jnp.where(condition, 1, 0))
    pl.semaphore_wait(barrier, count)


def remote(src, dst, send, recv, device):
    return pltpu.make_async_remote_copy(
        src_ref=src, dst_ref=dst, send_sem=send, recv_sem=recv, device_id=device, device_id_type=MESH
    )


def rem(a, n):
    return lax.rem(a + n, n)


class Chain:
    def __init__(self, part_s, outer_s, inner_s, pieces, in_send, in_recv, mid_send, mid_recv, out_send, out_recv):
        self.clip, clips = lax.axis_index("clip"), lax.axis_size("clip")
        clip = self.clip
        left = clip < clips // 2
        inner, outer = jnp.where(left, clip + 1, clip - 1), jnp.where(left, clip - 1, clip + 1)
        self.inner, self.outer = {"clip": inner}, {"clip": outer}
        self.end = (clip == 0) | (clip == clips - 1)
        self.middle = (clip == clips // 2 - 1) | (clip == clips // 2)
        self.part, self.from_outer, self.from_inner, self.pieces = part_s, outer_s, inner_s, pieces
        self.inward = [remote(part_s.at[p], outer_s.at[p], in_send.at[n], in_recv.at[n], self.inner) for n, p in enumerate(pieces)]
        self.across = [remote(part_s.at[p], inner_s.at[p], mid_send.at[n], mid_recv.at[n], self.inner) for n, p in enumerate(pieces)]
        self.outward = [remote(inner_s.at[p], inner_s.at[p], out_send.at[n], out_recv.at[n], self.outer) for n, p in enumerate(pieces)]

    def greet(self):
        barrier = pltpu.get_barrier_semaphore()
        pl.semaphore_signal(barrier, inc=1, device_id=self.inner, device_id_type=MESH)

        @pl.when(jnp.logical_not(self.end))
        def _():
            pl.semaphore_signal(barrier, inc=1, device_id=self.outer, device_id_type=MESH)

        pl.semaphore_wait(barrier, jnp.where(self.end, 1, 2))

    def greets(self):
        both = [(self.inner, None), (self.outer, jnp.logical_not(self.end))]
        return both

    def send_ends(self, n):
        @pl.when(self.end & jnp.logical_not(self.middle))
        def _():
            self.inward[n].start()

    def send_parts(self, n):
        here = self.pieces[n]

        @pl.when(jnp.logical_not(self.end))
        def _():
            self.inward[n].wait_recv()
            self.part[here] = (self.part[here].astype(f32) + self.from_outer[here].astype(f32)).astype(bf16)

        @pl.when(jnp.logical_not(self.end) & jnp.logical_not(self.middle))
        def _():
            self.inward[n].start()

        @pl.when(self.middle)
        def _():
            self.across[n].start()

    def totals(self, n):
        self.middle_totals(n)
        self.other_totals(n)

    def middle_totals(self, n):
        here = self.pieces[n]

        @pl.when(self.middle)
        def _():
            self.across[n].wait_recv()
            self.across[n].wait_send()
            self.from_inner[here] = (self.part[here].astype(f32) + self.from_inner[here].astype(f32)).astype(bf16)

        @pl.when(self.middle & jnp.logical_not(self.end))
        def _():
            self.outward[n].start()

    def other_totals(self, n):
        @pl.when(jnp.logical_not(self.middle))
        def _():
            self.inward[n].wait_send()
            self.outward[n].wait_recv()

        @pl.when(jnp.logical_not(self.middle) & jnp.logical_not(self.end))
        def _():
            self.outward[n].start()

    def close(self):
        @pl.when(jnp.logical_not(self.end))
        def _():
            for copy in self.outward:
                copy.wait_send()


def chain_scratch(buffer, pieces):
    return [pltpu.VMEM(buffer, bf16)] * 3 + [dma(pieces)] * 6


ANY = pl.BlockSpec(memory_space=pl.ANY)
INVMEM = pl.BlockSpec(memory_space=pltpu.VMEM)
INSMEM = pl.BlockSpec(memory_space=pltpu.SMEM)


def dma(*dims):
    return pltpu.SemaphoreType.DMA(dims)


def dot(a, b, dims=NN):
    return lax.dot_general(a, b, (dims, ((), ())), preferred_element_type=f32)


def exact_dot(matrix, tensor):
    high = tensor.astype(bf16)
    low = (tensor - high.astype(f32)).astype(bf16)
    return dot(matrix, high) + dot(matrix, low)


def norm(x):
    average = jnp.mean(x, axis=-1, keepdims=True)
    centred = x - average
    inverse = lax.rsqrt(jnp.mean(centred * centred, axis=-1, keepdims=True) + eps)
    return centred * inverse, inverse


def norm_back(unit, inverse, gain, gradient):
    scaled = gradient * gain
    return inverse * (
        scaled
        - jnp.mean(scaled, axis=-1, keepdims=True)
        - unit * jnp.mean(scaled * unit, axis=-1, keepdims=True)
    )


GELU_A, GELU_B = math.sqrt(2.0 / math.pi), 0.044715


def gelu(x):
    t = jnp.tanh(GELU_A * (x + GELU_B * (x * x * x)))
    return 0.5 * x * (1.0 + t)


def gelu_both(x):
    square = x * x
    t = jnp.tanh(GELU_A * x * (1.0 + GELU_B * square))
    value = 0.5 * x * (1.0 + t)
    slope = 0.5 * (1.0 + t) + 0.5 * x * (1.0 - t * t) * (GELU_A * (1.0 + 3.0 * GELU_B * square))
    return value, slope


def sum_rows(x):
    return jnp.sum(x, axis=0, keepdims=True)


def add_rows(ref, rows):
    step = pl.program_id(0)

    @pl.when(step == 0)
    def _():
        ref[...] = jnp.zeros_like(ref)

    for i, row in enumerate(rows):
        ref[i:i + 1, :] += row


def transposed(x):
    return x.astype(f32).T.astype(bf16)


def window(head):
    low = HD * head
    return low // 128 * 128, -(-(low + HD) // 128) * 128


def head_mask(head, start, stop):
    lane = lax.broadcasted_iota(jnp.int32, (1, stop - start), 1) + start
    return (lane >= HD * head) & (lane < HD * head + HD)


def key_rows(own_ref, mem_ref):
    row = 0
    for ref in (own_ref, mem_ref):
        for t in range(ref.shape[0]):
            yield ref, t, slice(row, row + ref.shape[2])
            row += ref.shape[2]


def key_mask(own_ref, mem_ref, valid, has):
    parts = []
    for ref, rows, there in ((own_ref, valid[0], None), (mem_ref, valid[1], has)):
        block = ref.shape[2]
        lane = lax.rem(lax.broadcasted_iota(jnp.int32, (1, ref.shape[0] * block), 1), block)
        limit = rows if there is None else jnp.where(there > 0, rows, 0)
        parts.append(jnp.where(lane < limit, 0.0, NEG))
    return jnp.concatenate(parts, axis=1)


def assemble(w_ref, w_s):
    wide = w_ref.shape[2] // 3
    for part in range(3):
        pieces = [w_ref[h, :, wide * part:wide * part + wide].astype(f32) for h in range(w_ref.shape[0])]
        w_s[0, :, 384 * part:384 * part + 384] = jnp.concatenate(pieces, axis=1).astype(bf16)


def assemble_out(w_ref, out_s):
    wide = out_s.shape[1] // w_ref.shape[0]
    pieces = [w_ref[h, :, :wide].astype(f32) for h in range(w_ref.shape[0])]
    out_s[...] = jnp.concatenate(pieces, axis=1).astype(bf16)


def project_keys(own_ref, mem_ref, w_ref, bias_ref, x_s, k_s, v_s):
    for ref, t, rows in key_rows(own_ref, mem_ref):
        x_s[rows, :] = ref[t, 0]
    width = k_s.shape[1]
    for low in range(0, width, 384):
        k_s[:, low:low + 384] = dot(x_s[...], w_ref[low // 384, :, 384:768]).astype(bf16)
    for low in range(0, width, 384):
        value = dot(x_s[...], w_ref[low // 384, :, 768:])
        v_s[:, low:low + 384] = (value + bias_ref[1:2, low:low + 384]).astype(bf16)


def project_queries(x_ref, w_ref, bias_ref, q_s):
    width = q_s.shape[1]
    for low in range(0, width, 384):
        value = dot(x_ref[0], w_ref[low // 384, :, :384])
        q_s[:, low:low + 384] = (value + bias_ref[0:1, low:low + 384]).astype(bf16)


def norm_pool_kernel(x_ref, gains_ref, shifts_ref, pool_ref, pair_ref, low_ref, pooled_ref, mean_ref):
    unit, _ = norm(x_ref[0].astype(f32))
    normed = unit * gains_ref[0:1, :] + shifts_ref[0:1, :]
    low_ref[0] = normed.astype(bf16)
    pooled = exact_dot(pool_ref[...], normed)
    pooled_ref[0] = pooled.astype(bf16)
    mean_ref[0] = exact_dot(pair_ref[...], pooled).astype(bf16)


def write_shares(gw_ref, h, gw_s):
    wide = gw_ref.shape[2] // 3
    for part in range(3):
        low = wide * h
        columns = gw_s[low // 384, :, 384 * part:384 * part + 384][:, low % 384:low % 384 + wide]
        gw_ref[h, :, wide * part:wide * part + wide] = columns.astype(bf16)


def attend_kernel(chunk, valid, x_ref, own_ref, mem_ref, w_ref, qv_ref, has_ref, out_ref, lse_ref, w_s, x_s, q_s, k_s, v_s, s_s, p_s):
    nq, width = q_s.shape
    columns = key_mask(own_ref, mem_ref, valid, has_ref[pl.program_id(0)])
    if width == 384:
        @pl.when(pl.program_id(0) == 0)
        def _():
            assemble(w_ref, w_s)
        w_ref = w_s
    project_queries(x_ref, w_ref, qv_ref, q_s)
    project_keys(own_ref, mem_ref, w_ref, qv_ref, x_s, k_s, v_s)
    factor = HD**-0.5 * math.log2(math.e)
    stack = s_s.shape[0] // nq
    lanes = lax.broadcasted_iota(jnp.int32, (chunk, 128), 1)
    for tile in range(width // 384):
        group = slice(384 * tile, 384 * tile + 384)
        base = q_s[:, group].astype(f32)
        parts = [base[:, :128], base[:, 128:256], base[:, 256:384]]
        for first in range(4 * tile, 4 * tile + 4, stack):
            start, stop = window(first)[0], window(first + stack - 1)[1]
            masks = [head_mask(first + k, start, stop) for k in range(stack)]
            base = q_s[:, start:stop]
            query = jnp.concatenate([jnp.where(mask, base, jnp.zeros((), bf16)) for mask in masks], axis=0)
            s_s[...] = dot(query, k_s[:, start:stop], NT)

            def body(i, carry, k):
                rows = pl.ds(pl.multiple_of(i * chunk, chunk), chunk)
                here = pl.ds(pl.multiple_of(k * nq + i * chunk, chunk), chunk)
                score = s_s[here, :] * factor + columns
                top = jnp.max(score, axis=1, keepdims=True)
                power = jnp.exp2(score - top)
                total = jnp.sum(power, axis=1, keepdims=True)
                p_s[here, :] = (power * (1.0 / total)).astype(bf16)
                lse_ref[0, rows, :] = jnp.where(lanes == first + k, top + jnp.log2(total), lse_ref[0, rows, :])
                return carry

            for k in range(stack):
                lax.fori_loop(0, nq // chunk, functools.partial(body, k=k), 0, unroll=nq // chunk)
            both = dot(p_s[...], v_s[:, start:stop])
            for k, mask in enumerate(masks):
                out = jnp.where(mask, both[k * nq:(k + 1) * nq], 0.0)
                for w in range((stop - start) // 128):
                    n = start // 128 - 3 * tile + w
                    parts[n] = parts[n] + out[:, 128 * w:128 * w + 128]
        out_ref[0, :, group] = jnp.concatenate(parts, axis=1).astype(bf16)


def attend_back_kernel(
    chunk, valid, x_ref, g_ref, own_ref, mem_ref, w_ref, qv_ref, has_ref, lse_ref,
    dx_ref, dpool_ref, gw_ref, row_ref,
    w_s, x_s, q_s, k_s, v_s, s_s, dp_s, p_s, ds_s, dk_s, dv_s, gw_s,
):
    nq, width = q_s.shape
    step = pl.program_id(0)
    columns = key_mask(own_ref, mem_ref, valid, has_ref[step])
    if width == 384:
        @pl.when(step == 0)
        def _():
            assemble(w_ref, w_s)
        w_ref = w_s
    project_queries(x_ref, w_ref, qv_ref, q_s)
    project_keys(own_ref, mem_ref, w_ref, qv_ref, x_s, k_s, v_s)
    scaling = HD**-0.5
    factor = scaling * math.log2(math.e)
    stack = s_s.shape[0] // nq
    lanes = lax.broadcasted_iota(jnp.int32, (chunk, 128), 1)

    @pl.when(step == 0)
    def _():
        gw_s[...] = jnp.zeros_like(gw_s)

    xt = transposed(x_ref[0])
    keys_t = transposed(x_s[...])
    dx = None
    dpool = None
    row_q, row_v = [], []
    for tile in range(width // 384):
        group = slice(384 * tile, 384 * tile + 384)
        qt = transposed(q_s[:, group])
        gt = transposed(g_ref[0, :, group])
        parts = [None] * 3
        for first in range(4 * tile, 4 * tile + 4, stack):
            start, stop = window(first)[0], window(first + stack - 1)[1]
            masks = [head_mask(first + k, start, stop) for k in range(stack)]
            zero = jnp.zeros((), bf16)
            query = jnp.concatenate([jnp.where(mask, q_s[:, start:stop], zero) for mask in masks], axis=0)
            grad = jnp.concatenate([jnp.where(mask, g_ref[0, :, start:stop], zero) for mask in masks], axis=0)
            s_s[...] = dot(query, k_s[:, start:stop], NT)
            dp_s[...] = dot(grad, v_s[:, start:stop], NT)

            def body(i, carry, k):
                rows = pl.ds(pl.multiple_of(i * chunk, chunk), chunk)
                here = pl.ds(pl.multiple_of(k * nq + i * chunk, chunk), chunk)
                lse = jnp.sum(jnp.where(lanes == first + k, lse_ref[0, rows, :], 0.0), axis=1, keepdims=True)
                p = jnp.exp2(s_s[here, :] * factor + columns - lse)
                dp = dp_s[here, :]
                inner = jnp.sum(p * dp, axis=1, keepdims=True)
                p_s[here, :] = p.astype(bf16)
                ds_s[here, :] = (p * (dp - inner)).astype(bf16)
                return carry

            for k in range(stack):
                lax.fori_loop(0, nq // chunk, functools.partial(body, k=k), 0, unroll=nq // chunk)
            dq_both = dot(ds_s[...], k_s[:, start:stop]) * scaling
            for k, mask in enumerate(masks):
                mine = slice(k * nq, (k + 1) * nq)
                r = slice(HD * (first + k - 4 * tile), HD * (first + k - 4 * tile) + HD)
                dv_s[r, :] = dot(gt[r], p_s[mine, :])
                dk_s[r, :] = dot(qt[r], ds_s[mine, :]) * scaling
                dq = jnp.where(mask, dq_both[mine], 0.0)
                for w in range((stop - start) // 128):
                    n = start // 128 - 3 * tile + w
                    part = dq[:, 128 * w:128 * w + 128]
                    parts[n] = part if parts[n] is None else parts[n] + part
        total = jnp.concatenate(parts, axis=1) + g_ref[0, :, group].astype(f32)
        row_q.append(sum_rows(total))
        low = total.astype(bf16)
        gw_s[tile, :, :384] += dot(xt, low)
        add = dot(low, w_ref[tile, :, :384], NT)
        dx = add if dx is None else dx + add
        for part, src in ((1, dk_s), (2, dv_s)):
            grad = src[...].T
            if part == 2:
                row_v.append(sum_rows(grad))
            low = grad.astype(bf16)
            here = slice(384 * part, 384 * part + 384)
            gw_s[tile, :, here] += dot(keys_t, low)
            add = dot(low, w_ref[tile, :, here], NT)
            dpool = add if dpool is None else dpool + add
    dx_ref[0] = dx
    row = 0
    own, mem = own_ref.shape[2], mem_ref.shape[2]
    toks = own_ref.shape[0]
    for t in range(toks):
        dpool_ref[t, 0, :own, :] = dpool[t * own:(t + 1) * own].astype(bf16)
        dpool_ref[t, 0, own:, :] = dpool[toks * own + t * mem:toks * own + (t + 1) * mem].astype(bf16)
    add_rows(row_ref, [jnp.concatenate(row_q, axis=1), jnp.concatenate(row_v, axis=1)])

    @pl.when(step == pl.num_programs(0) - 1)
    def _():
        for h in range(gw_ref.shape[0]):
            write_shares(gw_ref, h, gw_s)


def first_mlp_kernel(x_ref, comb_ref, out_ref, up_ref, down_ref, ub_ref, gains_ref, shifts_ref, pool_ref, pair_ref,
                     after_ref, middle_ref, pooled_ref, mean_ref, out_s):
    @pl.when(pl.program_id(0) == 0)
    def _():
        assemble_out(out_ref, out_s)

    after = x_ref[0].astype(f32) + dot(comb_ref[0], out_s[...], NT) + shifts_ref[1:2, :]
    after_ref[0] = after
    unit, _ = norm(after)
    low = (unit * gains_ref[1:2, :] + shifts_ref[2:3, :]).astype(bf16)
    total = after + shifts_ref[3:4, :]
    for h in range(up_ref.shape[0]):
        hidden = gelu(dot(low, up_ref[h]) + ub_ref[h]).astype(bf16)
        total = total + dot(hidden, down_ref[h], NT)
    middle_ref[0] = total
    unit, _ = norm(total)
    pooled = exact_dot(pool_ref[...], unit * gains_ref[2:3, :] + shifts_ref[4:5, :])
    pooled_ref[0] = pooled.astype(bf16)
    mean_ref[0] = exact_dot(pair_ref[...], pooled).astype(bf16)


def second_mlp_kernel(
    comb_ref, pooled_ref, cot_ref, out_ref, skip_ref, up_ref, down_ref, ub_ref, gains_ref, shifts_ref,
    mixed_ref, dcomb_ref, dskip_ref, gmlp_ref, gout_ref, gskip_ref, gub_ref, row_ref,
    after_s, low_s, lowt_s, cott_s, sum_s, dlow_s, skip_s,
):
    step = pl.program_id(0)

    @pl.when(step == 0)
    def _():
        share = skip_s.shape[1] // skip_ref.shape[0]
        skip_s[...] = jnp.concatenate([skip_ref[h, :, :share].astype(f32) for h in range(skip_ref.shape[0])], axis=1).astype(bf16)
        after = dot(pooled_ref[...], skip_s[...], NT) + shifts_ref[0:1, :]
        wide = out_ref.shape[2]
        for h in range(out_ref.shape[0]):
            after = after + dot(comb_ref[:, wide * h:wide * h + wide], out_ref[h], NT)
        after_s[...] = after
        unit, _ = norm(after)
        low = (unit * gains_ref[...] + shifts_ref[1:2, :]).astype(bf16)
        low_s[...] = low
        lowt_s[...] = transposed(low)
        cott_s[...] = transposed(cot_ref[...])
        sum_s[...] = after + shifts_ref[2:3, :]
        dlow_s[...] = jnp.zeros_like(dlow_s)

    pre = dot(low_s[...], up_ref[0]) + ub_ref[...]
    hidden, slope = gelu_both(pre)
    hidden = hidden.astype(bf16)
    dpre = dot(cot_ref[...], down_ref[0]) * slope
    gub_ref[...] = sum_rows(dpre)
    dpre = dpre.astype(bf16)
    sum_s[...] += dot(hidden, down_ref[0], NT)
    dlow_s[...] += dot(dpre, up_ref[0], NT)
    for n, grad in enumerate((dot(lowt_s[...], dpre), dot(cott_s[...], hidden))):
        rows = gmlp_ref.shape[3]
        for t in range(gmlp_ref.shape[1]):
            gmlp_ref[0, t, n] = grad[t * rows:(t + 1) * rows].astype(bf16)

    @pl.when(step == pl.num_programs(0) - 1)
    def _():
        mixed_ref[...] = sum_s[...].astype(bf16)
        unit, inverse = norm(after_s[...])
        dlow = dlow_s[...]
        cot = cot_ref[...].astype(f32)
        res = norm_back(unit, inverse, gains_ref[...], dlow) + cot
        row_ref[...] = jnp.zeros_like(row_ref)
        for i, row in enumerate((res, dlow, cot, dlow * unit)):
            row_ref[i:i + 1, :] = sum_rows(row)
        res = res.astype(bf16)
        dskip_ref[...] = dot(res, skip_s[...])
        rest = transposed(res)
        wide = out_ref.shape[2]
        for h in range(out_ref.shape[0]):
            here = slice(wide * h, wide * h + wide)
            dcomb_ref[:, here] = dot(res, out_ref[h]).astype(bf16)
            grad = dot(rest, comb_ref[:, here])
            half = gout_ref.shape[2]
            for n in range(2 * gout_ref.shape[1]):
                gout_ref[h, n // 2, :, wide * (n % 2):wide * (n % 2) + wide] = grad[half * n:half * n + half].astype(bf16)
        grad = dot(rest, pooled_ref[...])
        wide = gskip_ref.shape[3] // 2
        for h in range(gskip_ref.shape[0]):
            for t in range(gskip_ref.shape[1]):
                low, high = (grad[half * n:half * n + half, wide * h:wide * h + wide] for n in (2 * t, 2 * t + 1))
                gskip_ref[h, t] = jnp.concatenate([low, high], axis=1).astype(bf16)


def first_back_kernel(
    middle_ref, after_ref, comb_ref, dskip_ref, dq_ref, own_ref, mem_ref, out_ref, up_ref, down_ref, ub_ref, gains_ref, shifts_ref,
    unpool_ref, unpair_ref,
    res_ref, dcomb_ref, gmlp_ref, gub_ref, row_ref,
    gup_s, gdown_s, gout_s, out_s,
):
    step = pl.program_id(0)

    @pl.when(step == 0)
    def _():
        gup_s[...] = jnp.zeros_like(gup_s)
        gdown_s[...] = jnp.zeros_like(gdown_s)
        gout_s[...] = jnp.zeros_like(gout_s)
        gub_ref[...] = jnp.zeros_like(gub_ref)
        assemble_out(out_ref, out_s)

    dpool = dskip_ref[0] + dq_ref[0] + own_ref[0] + exact_dot(unpair_ref[...], mem_ref[0])
    dnorm = exact_dot(unpool_ref[...], dpool)
    unit, inverse = norm(middle_ref[0])
    grad = norm_back(unit, inverse, gains_ref[2:3, :], dnorm)
    rows = [sum_rows(dnorm * unit), sum_rows(dnorm), sum_rows(grad)]
    low = grad.astype(bf16)
    lowt = transposed(low)
    unit, inverse = norm(after_ref[0])
    normed = (unit * gains_ref[1:2, :] + shifts_ref[2:3, :]).astype(bf16)
    normedt = transposed(normed)
    dnormed = None
    for h in range(up_ref.shape[0]):
        hidden, slope = gelu_both(dot(normed, up_ref[h]) + ub_ref[h])
        hidden = hidden.astype(bf16)
        dpre = dot(low, down_ref[h]) * slope
        gub_ref[h] += sum_rows(dpre)
        dpre = dpre.astype(bf16)
        gdown_s[h] += dot(lowt, hidden)
        gup_s[h] += dot(normedt, dpre)
        add = dot(dpre, up_ref[h], NT)
        dnormed = add if dnormed is None else dnormed + add
    res = norm_back(unit, inverse, gains_ref[1:2, :], dnormed) + grad
    rows += [sum_rows(dnormed * unit), sum_rows(dnormed), sum_rows(res)]
    res_ref[0] = res
    res = res.astype(bf16)
    dcomb_ref[0] = dot(res, out_s[...]).astype(bf16)
    gout_s[...] += dot(transposed(res), comb_ref[0])
    add_rows(row_ref, rows)

    @pl.when(step == pl.num_programs(0) - 1)
    def _():
        fa, ha = gup_s.shape[2], gout_s.shape[1] // gmlp_ref.shape[0]
        for h in range(gmlp_ref.shape[0]):
            gmlp_ref[h, :, :fa] = gup_s[h].astype(bf16)
            gmlp_ref[h, :, fa:2 * fa] = gdown_s[h].astype(bf16)
            rest = gmlp_ref.shape[2] - 2 * fa - ha
            gout = jnp.concatenate([gout_s[:, ha * h:ha * h + ha], jnp.zeros((gout_s.shape[0], rest), f32)], axis=1)
            gmlp_ref[h, :, 2 * fa:] = gout.astype(bf16)


def last_back_kernel(x_ref, res_ref, dx_ref, own_ref, mem_ref, gains_ref, unpool_ref, unpair_ref, grad_ref, row_ref):
    dpool = own_ref[0] + exact_dot(unpair_ref[...], mem_ref[0])
    dnorm = dx_ref[0] + exact_dot(unpool_ref[...], dpool)
    unit, inverse = norm(x_ref[0].astype(f32))
    grad = norm_back(unit, inverse, gains_ref[0:1, :], dnorm) + res_ref[0]
    grad_ref[0] = grad.astype(bf16)
    add_rows(row_ref, [sum_rows(dnorm * unit), sum_rows(dnorm)])


def whole(array):
    return pl.BlockSpec(array.shape, lambda i: (0,) * array.ndim)


def by_micro(array, axis=0):
    block = array.shape[:axis] + (1,) + array.shape[axis + 1:]
    return pl.BlockSpec(block, lambda i: (0,) * axis + (i,) + (0,) * (array.ndim - axis - 1))


def shape(dims, dtype):
    return jax.ShapeDtypeStruct(dims, dtype)


def about(us):
    return pl.CostEstimate(flops=int(us * 1e9), bytes_accessed=0, transcendentals=0)


def call(kernel, steps, args, outs, scratch=(), name=None, us=10, number=None):
    def spec(array, how):
        if how is None:
            return whole(array)
        return by_micro(array, how) if isinstance(how, int) else how

    return pl.pallas_call(
        kernel,
        grid=(steps,),
        in_specs=[spec(a, how) for a, how in args],
        out_specs=[spec(a, how) for a, how in outs],
        out_shape=[a for a, _ in outs],
        scratch_shapes=[pltpu.VMEM(*one) if isinstance(one, tuple) else one for one in scratch],
        compiler_params=pltpu.CompilerParams(vmem_limit_bytes=VMEM_CAP, collective_id=number, has_side_effects=number is not None),
        cost_estimate=about(us),
        name=name,
    )(*[a for a, _ in args])


def stacked(nq):
    return 2 if nq < 512 else 1


def chunk_of(nq):
    return 112 if nq % 112 == 0 else 16


def attend(x, own, mem, w, qv, has, valid, width):
    batches, nq, d = x.shape
    keys = own.shape[0] * own.shape[2] + mem.shape[0] * mem.shape[2]
    return call(
        functools.partial(attend_kernel, chunk_of(nq), valid), batches,
        [(x, 0), (own, 1), (mem, 1), w, (qv, None), (has, pl.BlockSpec(memory_space=pltpu.SMEM))],
        [(shape((batches, nq, width), bf16), 0), (shape((batches, nq, 128), f32), 0)],
        [((1, d, 1152 if width == 384 else 128), bf16),
         ((keys, d), bf16), ((nq, width), bf16), ((keys, width), bf16), ((keys, width), bf16),
         ((stacked(nq) * nq, keys), f32), ((stacked(nq) * nq, keys), bf16)],
        name="attend", us=20,
    )


def attend_back(x, grad, own, mem, w, qv, has, valid, lse, heads):
    batches, nq, d = x.shape
    width = grad.shape[2]
    keys = own.shape[0] * own.shape[2] + mem.shape[0] * mem.shape[2]
    both = (own.shape[0], batches, own.shape[2] + mem.shape[2], d)
    groups = (width // 384, d, 1152)
    rows = stacked(nq) * nq
    return call(
        functools.partial(attend_back_kernel, chunk_of(nq), valid), batches,
        [(x, 0), (grad, 0), (own, 1), (mem, 1), w, (qv, None), (has, INSMEM), (lse, 0)],
        [(shape((batches, nq, d), f32), 0), (shape(both, bf16), 1), (shape((heads, d, 3 * width // heads), bf16), None), (shape((8, width), f32), None)],
        [((1, d, 1152 if width == 384 else 128), bf16),
         ((keys, d), bf16), ((nq, width), bf16), ((keys, width), bf16), ((keys, width), bf16),
         ((rows, keys), f32), ((rows, keys), f32), ((rows, keys), bf16), ((rows, keys), bf16),
         ((384, keys), f32), ((384, keys), f32), (groups, f32)],
        name="attend_back", us=36,
    )


def share_kernel(gather, count, *refs):
    if gather:
        pooled_ref, mean_ref, pick_ref, w_ref, *refs = refs
        biases, (own_ref, mem_ref, all_ref, *refs) = refs[:count], refs[count:]
        if count:
            (qv_a_ref, qv_b_ref, ub_a_ref, ub_b_ref), refs = refs[:4], refs[4:]
    else:
        pooled_ref, mean_ref, pick_ref, own_ref, mem_ref, *refs = refs
    (got_s, pick_s, local_sem, own_send, own_recv, mem_send, mem_recv, pass_send, pass_recv, clip_send, clip_recv, *refs) = refs
    clip, head, chip, core, chips = places()
    clips, heads = lax.axis_size("clip"), lax.axis_size("head")
    share = pooled_ref.shape[0]
    here = 2 * chip + core
    partner = {"tok": 2 * chip + 1 - core}
    across = [{"tok": 2 * rem(chip + k, chips) + core} for k in range(1, chips)]
    beside = [{"head": rem(head + d, heads)} for d in range(1, heads)]
    heads_of = lambda by, sign: [{"clip": clip + by, "head": rem(head + sign * d, heads)} for d in range(heads)]
    last, begun = clip < clips - 1, clip > 0
    near = [(d, None) for d in [partner] + across + (beside if gather else [])]
    greet(near + [(d, begun) for d in heads_of(-1, -1)], near + [(d, last) for d in heads_of(1, 1)])

    def spread(src, out, send, recv):
        copies = [remote(src, out.at[here], send.at[0], recv.at[0], partner)]
        copies += [remote(src, out.at[here], send.at[k + 1], recv.at[k + 1], across[k]) for k in range(chips - 1)]
        return copies

    def passed(out, k, row):
        block = 2 * rem(chip - k, chips) + core
        return remote(out.at[block], out.at[block], pass_send.at[row, k - 1], pass_recv.at[row, k - 1], partner)

    clip_copies = [remote(mean_ref, got_s.at[d], clip_send.at[d], clip_recv.at[d], device) for d, device in enumerate(heads_of(1, 1))]

    @pl.when(last)
    def _():
        for copy in clip_copies:
            copy.start()

    w_first, w_diagonal, w_core = {}, {}, {}
    if gather:
        w_local, w_send, w_recv, d_send, d_recv, c_send, c_recv, b_send, b_recv, *bias_got = refs
        bias_copies = [
            remote(ref, got.at[d], b_send.at[d, n], b_recv.at[d, n], device)
            for d, device in enumerate(beside)
            for n, (ref, got) in enumerate(zip(biases, bias_got))
        ]
        for copy in bias_copies:
            copy.start()
        mine = all_ref.at[head, here]
        for k in range(1, chips):
            w_first[k, 0] = remote(w_ref, mine, w_send.at[k - 1], w_recv.at[k - 1], across[k - 1])
        for d in range(1, heads):
            w_first[0, d] = remote(w_ref, mine, w_send.at[chips - 2 + d], w_recv.at[chips - 2 + d], beside[d - 1])
        w_core[0, 0] = remote(w_ref, mine, c_send.at[0, 0], c_recv.at[0, 0], partner)
        for copy in [*w_first.values(), w_core[0, 0]]:
            copy.start()
        w_copy = pltpu.make_async_copy(w_ref, mine, w_local.at[0])
        w_copy.start()

        def forward(k, d):
            block = all_ref.at[rem(head - d, heads), 2 * rem(chip - k, chips) + core]
            w_core[k, d] = remote(block, block, c_send.at[k, d], c_recv.at[k, d], partner)
            w_core[k, d].start()

    own_copies = spread(pooled_ref, own_ref, own_send, own_recv)
    for copy in own_copies[1:] + own_copies[:1]:
        copy.start()
    own_local = pltpu.make_async_copy(pooled_ref, own_ref.at[here], local_sem.at[0])
    own_local.start()
    if gather:
        for k in range(1, chips):
            w_first[k, 0].wait_recv()
            block = all_ref.at[head, 2 * rem(chip - k, chips) + core]
            for d in range(1, heads):
                w_diagonal[k, d] = remote(block, block, d_send.at[k - 1, d - 1], d_recv.at[k - 1, d - 1], beside[d - 1])
                w_diagonal[k, d].start()
            forward(k, 0)

    @pl.when(begun)
    def _():
        for copy in clip_copies:
            copy.wait_recv()
        for m in range(share):
            total = None
            for d in range(heads):
                for s in range(share):
                    piece = got_s[d, s].astype(f32) * pick_ref[m, d * share + s]
                    total = piece if total is None else total + piece
            pick_s[m] = total.astype(bf16)

    @pl.when(jnp.logical_not(begun))
    def _():
        pick_s[...] = jnp.zeros_like(pick_s)

    mem_copies = spread(pick_s, mem_ref, mem_send, mem_recv)
    for copy in mem_copies[1:] + mem_copies[:1]:
        copy.start()
    mem_local = pltpu.make_async_copy(pick_s, mem_ref.at[here], local_sem.at[1])
    mem_local.start()
    forwards = []
    for k in range(1, chips):
        own_copies[k].wait_recv()
        forwards.append(passed(own_ref, k, 0))
        forwards[-1].start()
    if gather:
        for d in range(1, heads):
            w_first[0, d].wait_recv()
            forward(0, d)
    for k in range(1, chips):
        mem_copies[k].wait_recv()
        forwards.append(passed(mem_ref, k, 1))
        forwards[-1].start()
    if gather:
        for k, d in w_diagonal:
            w_diagonal[k, d].wait_recv()
            forward(k, d)
        for copy in w_core.values():
            copy.wait_recv()
        for copy in bias_copies:
            copy.wait_recv()
    if count:
        by_head = []
        for ref, got in zip(biases, bias_got):
            pieces = []
            for h in range(heads):
                piece = ref[...]
                for d in range(1, heads):
                    piece = jnp.where(rem(head - d, heads) == h, got[d - 1], piece)
                pieces.append(piece)
            by_head.append(pieces)
        qv_a_ref[...] = jnp.concatenate(by_head[0], axis=1)
        qv_b_ref[...] = jnp.concatenate(by_head[1], axis=1)
        fa = ub_a_ref.shape[2]
        for h in range(heads):
            ub_a_ref[h] = by_head[2][h][:, :fa]
        ub_b_ref[...] = jnp.concatenate([piece[:, fa:] for piece in by_head[2]], axis=1)
        for copy in bias_copies:
            copy.wait_send()
    own_copies[0].wait_recv()
    mem_copies[0].wait_recv()
    for copy in forwards:
        copy.wait_recv()
    for copy in own_copies + mem_copies + forwards + [*w_first.values(), *w_diagonal.values(), *w_core.values()]:
        copy.wait_send()
    own_local.wait()
    mem_local.wait()
    if gather:
        w_copy.wait()

    @pl.when(last)
    def _():
        for copy in clip_copies:
            copy.wait_send()


def share_pooled(pooled, mean, pick, number, block=None, biases=(), fa=0):
    toks, heads = lax.axis_size("tok"), lax.axis_size("head")
    chips = toks // 2
    few = max(chips - 1, 1)
    args, specs = [pooled, mean, pick], [INVMEM, INVMEM, INSMEM]
    outs = [shape((toks,) + pooled.shape, bf16), shape((toks,) + mean.shape, bf16)]
    scratch = [
        pltpu.VMEM((heads,) + mean.shape, bf16), pltpu.VMEM(mean.shape, bf16), dma(2),
        dma(chips), dma(chips), dma(chips), dma(chips), dma(2, few), dma(2, few), dma(heads), dma(heads),
    ]
    if block is not None:
        args, specs = args + [block, *biases], specs + [INVMEM] * (1 + len(biases))
        outs = outs + [shape((heads, toks) + block.shape, bf16)]
        if biases:
            (_, wa), (_, wb), (_, wide) = (b.shape for b in biases)
            outs += [shape(dims, f32) for dims in ((2, heads * wa), (2, heads * wb), (heads, 1, fa), (1, heads * (wide - fa)))]
        firsts = max(chips + heads - 2, 1)
        scratch += [dma(1), dma(firsts), dma(firsts), dma(few, max(heads - 1, 1)), dma(few, max(heads - 1, 1)), dma(chips, heads), dma(chips, heads)]
        scratch += [dma(max(heads - 1, 1), max(len(biases), 1)), dma(max(heads - 1, 1), max(len(biases), 1))]
        scratch += [pltpu.VMEM((max(heads - 1, 1),) + b.shape, f32) for b in biases]
    return pl.pallas_call(
        functools.partial(share_kernel, block is not None, len(biases)),
        in_specs=specs,
        out_specs=[ANY] * min(len(outs), 3) + [INVMEM] * (len(outs) - 3),
        out_shape=outs,
        scratch_shapes=scratch,
        compiler_params=pltpu.CompilerParams(collective_id=number, has_side_effects=True, vmem_limit_bytes=VMEM_CAP),
        cost_estimate=about(20 if block is None else 30),
        name="share_pooled",
    )(*args)


def give_back_kernel(exchange, *refs):
    if exchange:
        part_ref, pick_ref, half_ref, grad_ref, own_ref, back_ref, all_ref, sum_ref, *refs = refs
        refs, hosted = refs[:-14], refs[-14:]
        (half_local, half_send, half_recv, block_s, block_core, head_s, block_head, block_chip,
         bc_send, bc_recv, bh_send, bh_recv, bx_send, bx_recv) = hosted
    else:
        part_ref, pick_ref, own_ref, back_ref, *refs = refs
    (mine_s, core_s, sum_s, chip_s, route_s, got_s,
     local_sem, core_send, core_recv, mem_send, mem_recv, own_send, own_recv, clip_send, clip_recv) = refs
    clip, head, chip, core, chips = places()
    clips, heads = lax.axis_size("clip"), lax.axis_size("head")
    share, rows = own_ref.shape[0], own_ref.shape[1]
    partner = {"tok": 2 * chip + 1 - core}
    across = [{"tok": 2 * rem(chip + k, chips) + core} for k in range(1, chips)]
    beside = [{"head": rem(head + d, heads)} for d in range(1, heads)]
    heads_of = lambda by, sign: [{"clip": clip + by, "head": rem(head + sign * d, heads)} for d in range(heads)]
    last, begun = clip < clips - 1, clip > 0
    near = [(d, None) for d in [partner] + across + (beside if exchange else [])]
    greet(near + [(d, last) for d in heads_of(1, 1)], near + [(d, begun) for d in heads_of(-1, -1)])

    order = [rem(chip + k, chips) for k in list(range(1, chips)) + [0]]
    core_copies, local_copies = [], []
    for n, other in enumerate(order):
        core_copies.append(remote(part_ref.at[2 * other + 1 - core], core_s.at[n], core_send.at[n], core_recv.at[n], partner))
        core_copies[-1].start()
    for n, other in enumerate(order):
        local_copies.append(pltpu.make_async_copy(part_ref.at[2 * other + core], mine_s.at[n], local_sem.at[n]))
        local_copies[-1].start()
    halves, block_copies = [], []
    if exchange:
        for n in range(heads * chips):
            block_copies.append(remote(grad_ref.at[2 * n + 1 - core], block_core.at[n], bc_send.at[n], bc_recv.at[n], partner))
            block_copies[-1].start()
        for n, copy in enumerate(block_copies):
            copy.wait_recv()
            block_s[n] = (grad_ref[2 * n + core].astype(f32) + block_core[n].astype(f32)).astype(bf16)
        head_copies = [
            remote(block_s.at[rem(head + k + 1, heads) * chips + x], block_head.at[k, x], bh_send.at[k, x], bh_recv.at[k, x], d)
            for k, d in enumerate(beside) for x in range(chips)
        ]
        for copy in head_copies:
            copy.start()
        halves = [remote(half_ref, all_ref.at[head], half_send.at[k], half_recv.at[k], d) for k, d in enumerate(beside)]
        for copy in halves:
            copy.start()
        half_copy = pltpu.make_async_copy(half_ref, all_ref.at[head], half_local.at[0])
        half_copy.start()
    mem_copies, own_copies = [], []
    for n in range(chips):
        local_copies[n].wait()
        core_copies[n].wait_recv()
        if n == chips - 1:
            break
        sum_s[n] = (mine_s[n].astype(f32) + core_s[n].astype(f32)).astype(bf16)
        low, high = pl.ds(0, rows), pl.ds(rows, sum_s.shape[2] - rows)
        mem_copies.append(remote(sum_s.at[n, :, high, :], chip_s.at[n, :, high, :], mem_send.at[n], mem_recv.at[n], across[n]))
        mem_copies[-1].start()
        own_copies.append(remote(sum_s.at[n, :, low, :], chip_s.at[n, :, low, :], own_send.at[n], own_recv.at[n], across[n]))
        own_copies[-1].start()
    base = chips - 1
    for copy in mem_copies:
        copy.wait_recv()
    memory = []
    for m in range(share):
        total = mine_s[base, m, rows:].astype(f32) + core_s[base, m, rows:].astype(f32)
        for n in range(chips - 1):
            total = total + chip_s[n, m, rows:].astype(f32)
        memory.append(total)
    clip_copies = [
        remote(route_s.at[d], got_s.at[d], clip_send.at[d], clip_recv.at[d], device) for d, device in enumerate(heads_of(-1, -1))
    ]

    @pl.when(begun)
    def _():
        for d in range(heads):
            for s in range(share):
                total = None
                for m in range(share):
                    piece = memory[m] * pick_ref[m, d * share + s]
                    total = piece if total is None else total + piece
                route_s[d, s] = total.astype(bf16)
            clip_copies[d].start()

    if exchange:
        for copy in head_copies:
            copy.wait_recv()
        for x in range(chips):
            total = block_s[head * chips + x].astype(f32)
            for k in range(heads - 1):
                total = total + block_head[k, x].astype(f32)
            head_s[x] = total.astype(bf16)
        chip_copies = [
            remote(head_s.at[rem(chip + k + 1, chips)], block_chip.at[k], bx_send.at[k], bx_recv.at[k], d) for k, d in enumerate(across)
        ]
        for copy in chip_copies:
            copy.start()
    for copy in own_copies:
        copy.wait_recv()
    for m in range(share):
        total = mine_s[base, m, :rows].astype(f32) + core_s[base, m, :rows].astype(f32)
        for n in range(chips - 1):
            total = total + chip_s[n, m, :rows].astype(f32)
        own_ref[m] = total

    @pl.when(last)
    def _():
        for copy in clip_copies:
            copy.wait_recv()
        total = got_s[0].astype(f32)
        for d in range(1, heads):
            total = total + got_s[d].astype(f32)
        back_ref[...] = total

    @pl.when(jnp.logical_not(last))
    def _():
        back_ref[...] = jnp.zeros_like(back_ref)

    for copy in halves:
        copy.wait_recv()
    if exchange:
        for copy in chip_copies:
            copy.wait_recv()
        total = head_s[chip].astype(f32)
        for k in range(chips - 1):
            total = total + block_chip[k].astype(f32)
        sum_ref[...] = jnp.zeros_like(sum_ref)
        sum_ref[:, :grad_ref.shape[2]] = total.astype(bf16)
        for copy in block_copies + head_copies + chip_copies:
            copy.wait_send()
    for copy in core_copies + mem_copies + own_copies + halves:
        copy.wait_send()
    if exchange:
        half_copy.wait()

    @pl.when(begun)
    def _():
        for copy in clip_copies:
            copy.wait_send()


def give_back(part, pick, own_rows, number, half=None, grad=None):
    toks, heads = lax.axis_size("tok"), lax.axis_size("head")
    chips, few = toks // 2, max(toks // 2 - 1, 1)
    share, rows, d = part.shape[1:]
    args, specs = [part, pick], [ANY, INSMEM]
    outs, out_specs = [shape((share, own_rows, d), f32), shape((share, rows - own_rows, d), f32)], [INVMEM, INVMEM]
    scratch = [
        pltpu.VMEM((chips,) + part.shape[1:], bf16), pltpu.VMEM((chips,) + part.shape[1:], bf16),
        pltpu.VMEM((few,) + part.shape[1:], bf16), pltpu.VMEM((few,) + part.shape[1:], bf16),
        pltpu.VMEM((heads, share, rows - own_rows, d), bf16), pltpu.VMEM((heads, share, rows - own_rows, d), bf16),
        dma(chips), dma(chips), dma(chips), dma(few), dma(few), dma(few), dma(few), dma(heads), dma(heads),
    ]
    if half is not None:
        block = grad.shape[1:]
        beside = max(heads - 1, 1)
        args, specs = args + [half, grad], specs + [INVMEM, INVMEM]
        outs += [shape((heads,) + half.shape, half.dtype), shape((block[0], -(-block[1] // 128) * 128), bf16)]
        out_specs += [ANY, INVMEM]
        low = lambda *dims: pltpu.VMEM(dims + block, bf16)
        scratch += [dma(1), dma(beside), dma(beside), low(heads * chips), low(heads * chips), low(chips), low(beside, chips), low(few)]
        scratch += [dma(heads * chips), dma(heads * chips), dma(beside, chips), dma(beside, chips), dma(few), dma(few)]
    return pl.pallas_call(
        functools.partial(give_back_kernel, half is not None),
        in_specs=specs,
        out_specs=out_specs,
        out_shape=outs,
        scratch_shapes=scratch,
        compiler_params=pltpu.CompilerParams(collective_id=number, has_side_effects=True, vmem_limit_bytes=VMEM_CAP),
        cost_estimate=about(1),
        name="give_back",
    )(*args)


def finish_kernel(half_ref, last_ref, qv_a_rows, a_ref, b_ref, qv_b_rows, ub_a_rows, ub_b_rows, grad_ref, rest_ref, group_ref,
                  all_ref, total_ref, sums_ref, *scratch):
    (small_ref, small_s, small_core, small_chip, small_head, small_clip,
     local_sem, half_send, half_recv, core_send, core_recv, chip_send, chip_recv, head_send, head_recv,
     clip_send, clip_recv, *chain) = scratch
    first_lanes, next_lanes = group_ref.shape[1], rest_ref.shape[1]
    bounds = [0, first_lanes // 2, first_lanes, first_lanes + next_lanes // 2, first_lanes + next_lanes, chain[0].shape[1]]
    chain = Chain(*chain[:3], [(slice(None), pl.ds(low, high - low)) for low, high in zip(bounds, bounds[1:])], *chain[3:])
    clip, head, chip, core, chips = places()
    clips, heads = lax.axis_size("clip"), lax.axis_size("head")
    share = half_ref.shape[0]
    partner = {"tok": 2 * chip + 1 - core}
    across = [{"tok": 2 * rem(chip + k, chips) + core} for k in range(1, chips)]
    beside = [{"head": rem(head + k, heads)} for k in range(1, heads)]
    along = [{"clip": rem(clip + k, clips)} for k in range(1, clips)]
    peers = [(d, None) for d in [partner] + across + beside + along]
    greet(peers, peers)
    chain.part[:, :first_lanes] = group_ref[...]
    chain.part[:, first_lanes:first_lanes + next_lanes] = rest_ref[...]
    chain.part[:, first_lanes + next_lanes:] = grad_ref[...]
    for n in range(5):
        chain.send_ends(n)
    pending = []
    d1 = small_ref.shape[1]
    small_ref[...] = jnp.zeros_like(small_ref)
    small_ref[0:2, :] = last_ref[0:2, :]
    small_ref[2:4, :] = qv_a_rows[0:2, :]
    for row, source in enumerate((3, 0, 5, 4, 2, 1)):
        small_ref[4 + row:5 + row, :] = a_ref[source:source + 1, :]
    row = 10
    longer = [b_ref[n:n + 1, :] for n in (3, 0, 1, 2)] + [qv_b_rows[n:n + 1, :] for n in range(2)]
    for values in longer + [ub_a_rows[h] for h in range(heads)] + [ub_b_rows[...]]:
        for low in range(0, values.shape[1], d1):
            small_ref[row:row + 1, :] = values[:, low:low + d1]
            row += 1
    def go(copies):
        for copy in copies:
            copy.start()
        pending.extend(copies)
        return copies

    def arrived(copies):
        for copy in copies:
            copy.wait_recv()

    def in_order(index, size, own, slot):
        total = None
        for i in range(size):
            piece = jnp.where(index == i, own, jnp.zeros_like(own))
            for k in range(size - 1):
                piece = jnp.where(rem(index - k - 1, size) == i, slot(k), piece)
            total = piece if total is None else total + piece
        return total

    first = go([remote(small_ref, small_core, core_send.at[0], core_recv.at[0], partner)])
    cuts, tokens = [], half_ref.shape[1]
    for s in range(share):
        early = tokens // 4 // 16 * 16 if s == 0 else 0
        cuts += [(s, low, high) for low, high in ((0, early), (early, tokens)) if high > low]
    halves = [
        [remote(half_ref.at[s, pl.ds(low, high - low)], all_ref.at[head, s, pl.ds(low, high - low)], half_send.at[k, n], half_recv.at[k, n], d)
         for k, d in enumerate(beside)]
        for n, (s, low, high) in enumerate(cuts)
    ]
    go(halves[0])
    local_half = pltpu.make_async_copy(half_ref, all_ref.at[head], local_sem.at[0])
    local_half.start()
    arrived(first)
    small_s[0] = small_ref[...] + small_core[...]
    copies = go([remote(small_s.at[0], small_head.at[k], head_send.at[k, 0], head_recv.at[k, 0], d) for k, d in enumerate(beside)])
    for s in range(1, len(halves)):
        go(halves[s])
    chain.send_parts(0)
    arrived(copies)
    small_s[1] = in_order(head, heads, small_s[0], lambda k: small_head[k])
    copies = go([remote(small_s.at[1], small_chip.at[k], chip_send.at[k, 0], chip_recv.at[k, 0], d) for k, d in enumerate(across)])
    chain.send_parts(1)
    arrived(copies)
    small_s[2] = in_order(chip, chips, small_s[1], lambda k: small_chip[k])
    copies = []
    for k, d in enumerate(along):
        copies += go([remote(small_s.at[2], small_clip.at[k], clip_send.at[k, 0], clip_recv.at[k, 0], d)])
    chain.send_parts(2)
    chain.middle_totals(0)
    chain.send_parts(3)
    chain.middle_totals(1)
    chain.send_parts(4)
    for n in range(2, 5):
        chain.middle_totals(n)
    for n in range(5):
        chain.other_totals(n)
    arrived(copies)
    total_ref[...] = in_order(clip, clips, small_s[2], lambda k: small_clip[k])
    sums_ref[...] = chain.from_inner[...]
    chain.close()
    for copies in halves:
        arrived(copies)
    for copy in pending:
        copy.wait_send()
    local_half.wait()


def finish(half, rows, grad, rest, first, count, number):
    toks, heads, clips = lax.axis_size("tok"), lax.axis_size("head"), lax.axis_size("clip")
    chips = toks // 2
    across, beside, along = (max(n, 1) for n in (chips - 1, heads - 1, clips - 1))
    depth, d1 = rest.shape[0], rows[0].shape[1]
    small = (-(-count // 8) * 8, d1)
    full = lambda *dims: pltpu.VMEM(dims + small, f32)
    buffer = (depth, first.shape[1] + rest.shape[1] + grad.shape[1])
    return pl.pallas_call(
        finish_kernel,
        in_specs=[INVMEM] * (len(rows) + 4),
        out_specs=[ANY, INVMEM, INVMEM],
        out_shape=[shape((heads,) + half.shape, half.dtype), shape(small, f32), shape(buffer, bf16)],
        scratch_shapes=[
            full(), full(3), full(), full(across), full(beside), full(along),
            dma(1), dma(beside, half.shape[0] + 1), dma(beside, half.shape[0] + 1), dma(1), dma(1),
            dma(across, 1), dma(across, 1), dma(beside, 1), dma(beside, 1), dma(along, 1), dma(along, 1),
            *chain_scratch(buffer, 5),
        ],
        compiler_params=pltpu.CompilerParams(collective_id=number, has_side_effects=True, vmem_limit_bytes=VMEM_CAP),
        cost_estimate=about(40),
        name="finish",
    )(half, *rows, grad, rest, first)


def write_kernel(head_ref, total_ref, sums_ref, mlp_ref, qkv_a_ref, out_a_ref, up_a_ref, down_a_ref, qkv_b_ref, out_b_ref, skip_b_ref,
                 up_b_ref, down_b_ref, gains_a_ref, gains_b_ref, shifts_a_ref, shifts_b_ref, qv_a_ref, qv_b_ref, ub_a_ref, ub_b_ref):
    head, total = head_ref[0], total_ref[...]
    at = [10]

    def rows(width):
        first = at[0]
        at[0] += width // total.shape[1]
        return jnp.concatenate([total[r:r + 1] for r in range(first, at[0])], axis=1)

    def share_of(row, width):
        piece = row[:, :width]
        for h in range(1, row.shape[1] // width):
            piece = jnp.where(head == h, row[:, width * h:width * h + width], piece)
        return piece

    gains_a_ref[0:1, :] = total[0:1]
    gains_a_ref[1:3, :] = total[4:6]
    shifts_a_ref[0:1, :] = total[1:2]
    shifts_a_ref[1:5, :] = total[6:10]
    d2, fa, fb = gains_b_ref.shape[1], ub_a_ref.shape[1], ub_b_ref.shape[1]
    heads = total.shape[1] // qv_a_ref.shape[1]
    for i in range(2):
        qv_a_ref[i:i + 1, :] = share_of(total[2 + i:3 + i], qv_a_ref.shape[1])
    gains_b_ref[...] = rows(d2)
    for i in range(3):
        shifts_b_ref[i:i + 1, :] = rows(d2)
    for i in range(2):
        qv_b_ref[i:i + 1, :] = share_of(rows(d2), qv_b_ref.shape[1])
    ub_a_ref[...] = share_of(rows(heads * fa), fa)
    ub_b_ref[...] = share_of(rows(heads * fb), fb)
    low = 0
    depth = sums_ref.shape[0]

    def take(ref):
        nonlocal low
        ref[...] = sums_ref[:, low:low + ref.shape[1]].astype(f32)
        low += ref.shape[1]

    for part in range(3):
        take(qkv_b_ref.at[part])
    for ref in (out_b_ref, skip_b_ref):
        for n in range(2):
            take(ref.at[depth * n:depth * n + depth])
    for ref in (up_a_ref, down_a_ref, out_a_ref):
        take(ref)
    low = -(-low // 256) * 256
    for part in range(3):
        take(qkv_a_ref.at[part])
    up_b_ref[...] = mlp_ref[:up_b_ref.shape[0], :].astype(f32)
    down_b_ref[...] = mlp_ref[up_b_ref.shape[0]:, :].astype(f32)


def reduce_clips(shard):
    clips, clip = lax.axis_size("clip"), lax.axis_index("clip")
    pieces = shard.reshape(clips, -1, shard.shape[-1])
    total = lax.dynamic_index_in_dim(pieces, clip, 0, keepdims=False).astype(f32)
    for k in range(1, clips):
        give = lax.dynamic_index_in_dim(pieces, (clip + k) % clips, 0, keepdims=False)
        total = total + lax.ppermute(give, "clip", [(i, (i + k) % clips) for i in range(clips)]).astype(f32)
    return total.astype(bf16)


def spread_clips(piece):
    clips, clip = lax.axis_size("clip"), lax.axis_index("clip")
    out = jnp.zeros((clips,) + piece.shape, piece.dtype)
    out = lax.dynamic_update_index_in_dim(out, piece, clip, 0)
    for k in range(1, clips):
        got = lax.ppermute(piece, "clip", [(i, (i + k) % clips) for i in range(clips)])
        out = lax.dynamic_update_index_in_dim(out, got, (clip - k + clips) % clips, 0)
    return out.reshape((-1,) + piece.shape[1:])


def local(
    clips_in, resets, assign, w_qkv_a, w_out_a, w_up_a, w_down_a, w_qkv_b, w_out_b, w_skip_b, w_up_b, w_down_b,
    gains_a, gains_b, shifts_a, shifts_b, qv_bias_a, qv_bias_b, up_bias_a, up_bias_b, cotangent,
):
    heads, toks, clips = lax.axis_size("head"), lax.axis_size("tok"), lax.axis_size("clip")
    head = lax.axis_index("head")
    micro, frames = clips_in.shape[1], clips_in.shape[2]
    d1, d2 = clips_in.shape[-1], cotangent.shape[-1]
    share = micro // heads
    first = head * share
    pool_np, pair_np = pool_matrix(frames), pair_matrix(frames)
    pooling, pairing = jnp.asarray(pool_np, bf16), jnp.asarray(pair_np, bf16)
    unpooling, unpairing = jnp.asarray(pool_np.T, bf16), jnp.asarray(pair_np.T, bf16)
    tokens, pooled_tokens = frames * PATCH, frames * POOLED
    own_rows, mem_rows = up16(pooled_tokens), up16(frames // 2 * POOLED)
    rows2 = share * own_rows


    def by_patch(tensor):
        return tensor.transpose(0, 2, 1, 3).reshape(tensor.shape[0], -1, tensor.shape[3])

    def by_frame(rows, like):
        return rows.reshape(like[:2] + (like[3], like[2], like[4])).transpose(0, 1, 3, 2, 4)

    cot = by_patch(lax.dynamic_slice_in_dim(cotangent[0], first, share, 0))

    source = lax.dynamic_slice_in_dim(assign[0], first, share, 0)
    flags = lax.dynamic_slice_in_dim(resets[0], first, share, 0)
    slot = ((head - source // share + heads) % heads) * share + source % share
    pick = (jnp.arange(heads * share)[None, :] == slot[:, None]).astype(f32)
    has = ((flags == 0) & (lax.axis_index("clip") > 0)).astype(jnp.int32)
    valid = (pooled_tokens, frames // 2 * POOLED)

    group = ("head", "tok")
    fa, ha = w_up_a.shape[1], w_out_a.shape[1]
    fb, hb, hs = w_up_b.shape[1], w_out_b.shape[1], w_skip_b.shape[1]
    spare_a = jnp.zeros((w_out_a.shape[0], -w_out_a.shape[1] % 256), bf16)
    pack_a = jnp.concatenate([w_up_a, w_down_a, w_out_a, spare_a], axis=1)
    all_a = lax.all_gather(pack_a, group).reshape(heads, d1, -1)
    stream = by_patch(lax.dynamic_slice_in_dim(clips_in[0], first, share, 0))
    low1, pooled1, mean1 = call(
        norm_pool_kernel, share,
        [(stream, 0), (gains_a, None), (shifts_a, None), (pooling, None), (pairing, None)],
        [(shape((share, tokens, d1), bf16), 0), (shape((share, own_rows, d1), bf16), 0), (shape((share, mem_rows, d1), bf16), 0)],
        name="norm_pool", us=5,
    )
    pack_w = jnp.concatenate([*w_qkv_b.transpose(1, 0, 2), *w_qkv_a.transpose(1, 0, 2)], axis=1)
    own1, mem1, all_w, qv_a, qv_b, ub_a, ub_b = share_pooled(
        pooled1, mean1, pick, 0, pack_w, [qv_bias_a, qv_bias_b, jnp.concatenate([up_bias_a, up_bias_b])[None]], fa)
    all_q = all_w.reshape(heads, d1, -1)
    all_w = all_q[:, :, 3 * hb:]
    q_spec = pl.BlockSpec((heads, d1, 3 * hb), lambda i: (0, 0, 0))
    own1, w_up_b, cot = lax.optimization_barrier((own1, w_up_b, cot))
    spare = jnp.zeros((w_up_b.shape[0], -(2 * fb + hb + hs) % hb), bf16)
    pack_b = jnp.concatenate([w_up_b, w_down_b, w_out_b, w_skip_b, spare], axis=1)
    all_b = lax.all_gather(pack_b, group).reshape(heads, d2, -1)
    cot = jnp.pad(cot, ((0, 0), (0, own_rows - pooled_tokens), (0, 0))).reshape(rows2, d2)

    up_spec, down_spec = (pl.BlockSpec((heads, d1, fa), lambda i, n=n: (0, 0, n)) for n in range(2))
    out_a_spec = pl.BlockSpec((heads, d1, 256), lambda i: (0, 0, 2 * fa // 256))

    comb1, lse1 = attend(low1, own1, mem1, (all_w, None), qv_a, has, valid, d1)
    after1, middle, pooled3, mean3 = call(
        first_mlp_kernel, share,
        [(stream, 0), (comb1, 0), (all_a, out_a_spec), (all_a, up_spec), (all_a, down_spec), (ub_a, None),
         (gains_a, None), (shifts_a, None),
         (pooling, None), (pairing, None)],
        [(shape((share, tokens, d1), f32), 0), (shape((share, tokens, d1), f32), 0),
         (shape((share, own_rows, d1), bf16), 0), (shape((share, mem_rows, d1), bf16), 0)],
        [((d1, d1), bf16)],
        name="first_mlp", us=13,
    )

    own2, mem2 = share_pooled(pooled3, mean3, pick, 1)
    comb2, lse2 = attend(pooled3, own2, mem2, (all_q, q_spec), qv_b, has, valid, d2)
    chunk = 768
    per_head = fb // chunk
    steps = heads * per_head
    out_spec, skip_spec = (pl.BlockSpec((heads, d2, hb), lambda j, n=n: (0, 0, 2 * fb // hb + n)) for n in range(2))
    rows_spec = pl.BlockSpec((1, d2, chunk), lambda j: (j // per_head, 0, j % per_head))
    mixed, dcomb2, dskip, g_mlp_b, g_out_b, g_skip_b, g_ub_b, rows_b = call(
        second_mlp_kernel, steps,
        [(comb2.reshape(rows2, d2), None), (pooled3.reshape(rows2, d1), None), (cot, None), (all_b, out_spec), (all_b, skip_spec),
         (all_b, rows_spec),
         (all_b, pl.BlockSpec((1, d2, chunk), lambda j: (j // per_head, 0, per_head + j % per_head))),
         (ub_b, pl.BlockSpec((1, chunk), lambda j: (0, j))),
         (gains_b[None], None), (shifts_b, None)],
        [(shape((rows2, d2), bf16), None), (shape((rows2, d2), bf16), None), (shape((rows2, d1), f32), None),
         (shape((heads, toks, 2, d2 // toks, fb), bf16),
          pl.BlockSpec((1, toks, 2, d2 // toks, chunk), lambda j: (j // per_head, 0, 0, 0, j % per_head))),
         (shape((heads, toks, d2 // toks // 2, 2 * hb), bf16), None), (shape((heads, toks, d2 // toks // 2, 2 * hs), bf16), None),
         (shape((1, heads * fb), f32), pl.BlockSpec((1, chunk), lambda j: (0, j))), (shape((8, d2), f32), None)],
        [((rows2, d2), f32), ((rows2, d2), bf16), ((d2, rows2), bf16), ((d2, rows2), bf16), ((rows2, d2), f32), ((rows2, d2), f32), ((d2, d1), bf16)],
        name="second_mlp", us=26,
    )

    def by_owner(grad):
        return grad.reshape((heads * toks, -1) + grad.shape[2:])

    def scatter(grad):
        return lax.psum_scatter(grad, group, scatter_dimension=0, tiled=False)

    sum_mlp_b = scatter(g_mlp_b.reshape((heads * toks,) + g_mlp_b.shape[2:])).reshape(-1, fb)
    dcomb2 = dcomb2.reshape(share, own_rows, d2)
    dq2, dpool2, g_qkv_b, rows_qv_b = attend_back(pooled3, dcomb2, own2, mem2, (all_q, q_spec), qv_b, has, valid, lse2, heads)
    own_back2, mem_back2 = give_back(dpool2, pick, own_rows, 2)

    merge = lambda grad: grad.reshape((heads * toks,) + grad.shape[2:])
    rest_b = jnp.concatenate([by_owner(g_qkv_b), merge(g_out_b), merge(g_skip_b)], axis=2)
    sum_rest_b = scatter(rest_b)

    res1, dcomb1, g_mlp_a, g_ub_a, rows_a = call(
        first_back_kernel, share,
        [(middle, 0), (after1, 0), (comb1, 0), (dskip.reshape(share, own_rows, d1), 0), (dq2, 0), (own_back2, 0), (mem_back2, 0),
         (all_a, out_a_spec), (all_a, up_spec), (all_a, down_spec), (ub_a, None),
         (gains_a, None), (shifts_a, None), (unpooling, None), (unpairing, None)],
        [(shape((share, tokens, d1), f32), 0), (shape((share, tokens, d1), bf16), 0),
         (shape((heads, d1, -(-(2 * fa + ha) // 256) * 256), bf16), None),
         (shape((heads, 1, fa), f32), None), (shape((8, d1), f32), None)],
        [((heads, d1, fa), f32), ((heads, d1, fa), f32), ((d1, d1), f32), ((d1, d1), bf16)],
        name="first_back", us=26,
    )
    rest_a = by_owner(g_mlp_a)
    dcomb1, sum_mlp_b, rest_a = lax.optimization_barrier((dcomb1, sum_mlp_b, rest_a))
    sum_rest_a = scatter(rest_a)
    sum_mlp_b = reduce_clips(sum_mlp_b)
    dx1, dpool1, g_qkv_a, rows_qv_a = attend_back(low1, dcomb1, own1, mem1, (all_w, None), qv_a, has, valid, lse1, heads)
    dpool1, sum_mlp_b = lax.optimization_barrier((dpool1, sum_mlp_b))
    sum_mlp_b = spread_clips(sum_mlp_b)
    own_back1, mem_back1, mixed_all, sum_qkv_a = give_back(
        dpool1, pick, own_rows, 3, mixed.reshape(share, own_rows, d2), by_owner(g_qkv_a))
    stream_grad, rows_last = call(
        last_back_kernel, share,
        [(stream, 0), (res1, 0), (dx1, 0), (own_back1, 0), (mem_back1, 0), (gains_a, None),
         (unpooling, None), (unpairing, None)],
        [(shape((share, tokens, d1), bf16), 0), (shape((8, d1), f32), None)],
        name="last_back", us=1,
    )

    rows = [rows_last, rows_qv_a, rows_a, rows_b, rows_qv_b, g_ub_a, g_ub_b]
    count = 10 + (6 * d2 + heads * (fa + fb)) // d1
    stream_all, total, sums = finish(stream_grad, rows, sum_qkv_a, sum_rest_a, sum_rest_b, count, 4)
    row1, row2 = w_up_a.shape[0], w_up_b.shape[0]
    outs = [(3, row1, ha), (row1, ha), (row1, fa), (row1, fa), (3, row1, hb), (row2, hb), (row2, hs), (row2, fb), (row2, fb),
            (3, d1), (1, d2), (5, d1), (3, d2), (2, ha), (2, hb), (1, fa), (1, fb)]
    grads = call(
        write_kernel, 1,
        [(head.astype(jnp.int32)[None], INSMEM), (total, None), (sums, None), (sum_mlp_b, None)],
        [(shape(dims, f32), None) for dims in outs],
        name="write", us=4,
    )
    mixed_all = mixed_all.reshape(micro, own_rows, d2)[:, :pooled_tokens]
    return (
        by_frame(mixed_all, cotangent.shape),
        by_frame(stream_all.astype(f32), clips_in.shape),
        grads[0].transpose(1, 0, 2), *grads[1:4], grads[4].transpose(1, 0, 2), *grads[5:10],
        grads[10][0], *grads[11:15], grads[15][0], grads[16][0],
    )


def solution(mesh):
    in_specs = (
        P("clip", None, "tok", None, None),
        P("clip", None),
        P("clip", None),
        P("tok", None, "head"),
        P("tok", "head"),
        P("tok", "head"),
        P("tok", "head"),
        P("tok", None, "head"),
        P("tok", "head"),
        P("tok", "head"),
        P("tok", "head"),
        P("tok", "head"),
        P(),
        P(),
        P(),
        P(),
        P(None, "head"),
        P(None, "head"),
        P("head"),
        P("head"),
        P("clip", None, "tok", None, None),
    )
    out_specs = (
        P("clip", None, "tok", None, None),
        P("clip", None, "tok", None, None),
        P("tok", None, "head"),
        P("tok", "head"),
        P("tok", "head"),
        P("tok", "head"),
        P("tok", None, "head"),
        P("tok", "head"),
        P("tok", "head"),
        P("tok", "head"),
        P("tok", "head"),
        P(),
        P(),
        P(),
        P(),
        P(None, "head"),
        P(None, "head"),
        P("head"),
        P("head"),
    )
    return jax.shard_map(local, mesh=mesh, in_specs=in_specs, out_specs=out_specs, check_vma=False)
```

```python
import functools
import math

import jax
import jax.numpy as jnp
import numpy as np
from jax import lax
from jax.experimental import pallas as pl
from jax.experimental.pallas import tpu as pltpu
from jax.sharding import PartitionSpec as P

GRID = 14
PATCH = GRID * GRID
POOLED = PATCH // 4
HD = 96
NEG = -1e30
VMEM_CAP = 62 * 2**20
PIECES = 9
eps = 1e-06
f32, bf16 = jnp.float32, jnp.bfloat16
NN, NT, TN = ((1,), (0,)), ((1,), (1,)), ((0,), (0,))


def up16(n):
    return -(-n // 16) * 16


def pool_matrix(frames):
    rows, cols = up16(frames * POOLED), frames * PATCH
    out = np.zeros((rows, cols), np.float32)
    half = GRID // 2
    for f in range(frames):
        for p in range(PATCH):
            r, c = divmod(p, GRID)
            out[((r // 2) * half + c // 2) * frames + f, p * frames + f] = 0.25
    return out


def pair_matrix(frames):
    rows, cols = up16(frames // 2 * POOLED), up16(frames * POOLED)
    out = np.zeros((rows, cols), np.float32)
    for j in range(frames // 2):
        for p in range(POOLED):
            out[p * (frames // 2) + j, p * frames + 2 * j] = 0.5
            out[p * (frames // 2) + j, p * frames + 2 * j + 1] = 0.5
    return out


MESH = pl.DeviceIdType.MESH


def places():
    tok, toks = lax.axis_index("tok"), lax.axis_size("tok")
    return lax.axis_index("clip"), lax.axis_index("head"), tok // 2, tok % 2, toks // 2


def greet(copies_to_me, i_copy_to):
    barrier = pltpu.get_barrier_semaphore()
    for device, condition in copies_to_me:
        if condition is None:
            pl.semaphore_signal(barrier, inc=1, device_id=device, device_id_type=MESH)
        else:
            @pl.when(condition)
            def _():
                pl.semaphore_signal(barrier, inc=1, device_id=device, device_id_type=MESH)
    count = 0
    for _, condition in i_copy_to:
        count = count + (1 if condition is None else jnp.where(condition, 1, 0))
    pl.semaphore_wait(barrier, count)


def remote(src, dst, send, recv, device):
    return pltpu.make_async_remote_copy(
        src_ref=src, dst_ref=dst, send_sem=send, recv_sem=recv, device_id=device, device_id_type=MESH
    )


def rem(a, n):
    return lax.rem(a + n, n)


class Chain:
    def __init__(self, part_s, outer_s, inner_s, pieces, in_send, in_recv, mid_send, mid_recv, out_send, out_recv):
        self.clip, clips = lax.axis_index("clip"), lax.axis_size("clip")
        clip = self.clip
        left = clip < clips // 2
        inner, outer = jnp.where(left, clip + 1, clip - 1), jnp.where(left, clip - 1, clip + 1)
        self.inner, self.outer = {"clip": inner}, {"clip": outer}
        self.end = (clip == 0) | (clip == clips - 1)
        self.middle = (clip == clips // 2 - 1) | (clip == clips // 2)
        self.part, self.from_outer, self.from_inner, self.pieces = part_s, outer_s, inner_s, pieces
        self.inward = [remote(part_s.at[p], outer_s.at[p], in_send.at[n], in_recv.at[n], self.inner) for n, p in enumerate(pieces)]
        self.across = [remote(part_s.at[p], inner_s.at[p], mid_send.at[n], mid_recv.at[n], self.inner) for n, p in enumerate(pieces)]
        self.outward = [remote(inner_s.at[p], inner_s.at[p], out_send.at[n], out_recv.at[n], self.outer) for n, p in enumerate(pieces)]

    def greet(self):
        barrier = pltpu.get_barrier_semaphore()
        pl.semaphore_signal(barrier, inc=1, device_id=self.inner, device_id_type=MESH)

        @pl.when(jnp.logical_not(self.end))
        def _():
            pl.semaphore_signal(barrier, inc=1, device_id=self.outer, device_id_type=MESH)

        pl.semaphore_wait(barrier, jnp.where(self.end, 1, 2))

    def greets(self):
        both = [(self.inner, None), (self.outer, jnp.logical_not(self.end))]
        return both

    def send_ends(self, n):
        @pl.when(self.end & jnp.logical_not(self.middle))
        def _():
            self.inward[n].start()

    def send_parts(self, n):
        here = self.pieces[n]

        @pl.when(jnp.logical_not(self.end))
        def _():
            self.inward[n].wait_recv()
            self.part[here] = (self.part[here].astype(f32) + self.from_outer[here].astype(f32)).astype(bf16)

        @pl.when(jnp.logical_not(self.end) & jnp.logical_not(self.middle))
        def _():
            self.inward[n].start()

        @pl.when(self.middle)
        def _():
            self.across[n].start()

    def totals(self, n):
        self.middle_totals(n)
        self.other_totals(n)

    def middle_totals(self, n):
        here = self.pieces[n]

        @pl.when(self.middle)
        def _():
            self.across[n].wait_recv()
            self.across[n].wait_send()
            self.from_inner[here] = (self.part[here].astype(f32) + self.from_inner[here].astype(f32)).astype(bf16)

        @pl.when(self.middle & jnp.logical_not(self.end))
        def _():
            self.outward[n].start()

    def other_totals(self, n):
        @pl.when(jnp.logical_not(self.middle))
        def _():
            self.inward[n].wait_send()
            self.outward[n].wait_recv()

        @pl.when(jnp.logical_not(self.middle) & jnp.logical_not(self.end))
        def _():
            self.outward[n].start()

    def close(self):
        @pl.when(jnp.logical_not(self.end))
        def _():
            for copy in self.outward:
                copy.wait_send()


def chain_scratch(buffer, pieces):
    return [pltpu.VMEM(buffer, bf16)] * 3 + [dma(pieces)] * 6


ANY = pl.BlockSpec(memory_space=pl.ANY)
INVMEM = pl.BlockSpec(memory_space=pltpu.VMEM)
INSMEM = pl.BlockSpec(memory_space=pltpu.SMEM)


def dma(*dims):
    return pltpu.SemaphoreType.DMA(dims)


def dot(a, b, dims=NN):
    return lax.dot_general(a, b, (dims, ((), ())), preferred_element_type=f32)


def exact_dot(matrix, tensor):
    high = tensor.astype(bf16)
    low = (tensor - high.astype(f32)).astype(bf16)
    return dot(matrix, high) + dot(matrix, low)


def norm(x):
    average = jnp.mean(x, axis=-1, keepdims=True)
    centred = x - average
    inverse = lax.rsqrt(jnp.mean(centred * centred, axis=-1, keepdims=True) + eps)
    return centred * inverse, inverse


def norm_back(unit, inverse, gain, gradient):
    scaled = gradient * gain
    return inverse * (
        scaled
        - jnp.mean(scaled, axis=-1, keepdims=True)
        - unit * jnp.mean(scaled * unit, axis=-1, keepdims=True)
    )


GELU_A, GELU_B = math.sqrt(2.0 / math.pi), 0.044715


def gelu(x):
    t = jnp.tanh(GELU_A * (x + GELU_B * (x * x * x)))
    return 0.5 * x * (1.0 + t)


def gelu_both(x):
    square = x * x
    t = jnp.tanh(GELU_A * x * (1.0 + GELU_B * square))
    value = 0.5 * x * (1.0 + t)
    slope = 0.5 * (1.0 + t) + 0.5 * x * (1.0 - t * t) * (GELU_A * (1.0 + 3.0 * GELU_B * square))
    return value, slope


def sum_rows(x):
    return jnp.sum(x, axis=0, keepdims=True)


def add_rows(ref, rows):
    step = pl.program_id(0)

    @pl.when(step == 0)
    def _():
        ref[...] = jnp.zeros_like(ref)

    for i, row in enumerate(rows):
        ref[i:i + 1, :] += row


def transposed(x):
    return x.astype(f32).T.astype(bf16)


def window(head):
    low = HD * head
    return low // 128 * 128, -(-(low + HD) // 128) * 128


def head_mask(head, start, stop):
    lane = lax.broadcasted_iota(jnp.int32, (1, stop - start), 1) + start
    return (lane >= HD * head) & (lane < HD * head + HD)


def key_rows(own_ref, mem_ref):
    row = 0
    for ref in (own_ref, mem_ref):
        for t in range(ref.shape[0]):
            yield ref, t, slice(row, row + ref.shape[2])
            row += ref.shape[2]


def key_mask(own_ref, mem_ref, valid, has):
    parts = []
    for ref, rows, there in ((own_ref, valid[0], None), (mem_ref, valid[1], has)):
        block = ref.shape[2]
        lane = lax.rem(lax.broadcasted_iota(jnp.int32, (1, ref.shape[0] * block), 1), block)
        limit = rows if there is None else jnp.where(there > 0, rows, 0)
        parts.append(jnp.where(lane < limit, 0.0, NEG))
    return jnp.concatenate(parts, axis=1)


def assemble(w_ref, w_s):
    wide = w_ref.shape[2] // 3
    for part in range(3):
        pieces = [w_ref[h, :, wide * part:wide * part + wide].astype(f32) for h in range(w_ref.shape[0])]
        w_s[0, :, 384 * part:384 * part + 384] = jnp.concatenate(pieces, axis=1).astype(bf16)


def assemble_out(w_ref, out_s):
    wide = out_s.shape[1] // w_ref.shape[0]
    pieces = [w_ref[h, :, :wide].astype(f32) for h in range(w_ref.shape[0])]
    out_s[...] = jnp.concatenate(pieces, axis=1).astype(bf16)


def project_keys(own_ref, mem_ref, w_ref, bias_ref, x_s, k_s, v_s):
    for ref, t, rows in key_rows(own_ref, mem_ref):
        x_s[rows, :] = ref[t, 0]
    width = k_s.shape[1]
    for low in range(0, width, 384):
        k_s[:, low:low + 384] = dot(x_s[...], w_ref[low // 384, :, 384:768]).astype(bf16)
    for low in range(0, width, 384):
        value = dot(x_s[...], w_ref[low // 384, :, 768:])
        v_s[:, low:low + 384] = (value + bias_ref[1:2, low:low + 384]).astype(bf16)


def project_queries(x_ref, w_ref, bias_ref, q_s):
    width = q_s.shape[1]
    for low in range(0, width, 384):
        value = dot(x_ref[0], w_ref[low // 384, :, :384])
        q_s[:, low:low + 384] = (value + bias_ref[0:1, low:low + 384]).astype(bf16)


def norm_pool_kernel(x_ref, gains_ref, shifts_ref, pool_ref, pair_ref, low_ref, pooled_ref, mean_ref):
    unit, _ = norm(x_ref[0].astype(f32))
    normed = unit * gains_ref[0:1, :] + shifts_ref[0:1, :]
    low_ref[0] = normed.astype(bf16)
    pooled = exact_dot(pool_ref[...], normed)
    pooled_ref[0] = pooled.astype(bf16)
    mean_ref[0] = exact_dot(pair_ref[...], pooled).astype(bf16)


def write_shares(gw_ref, h, gw_s):
    wide = gw_ref.shape[2] // 3
    for part in range(3):
        low = wide * h
        columns = gw_s[low // 384, :, 384 * part:384 * part + 384][:, low % 384:low % 384 + wide]
        gw_ref[h, :, wide * part:wide * part + wide] = columns.astype(bf16)


def attend_kernel(chunk, valid, x_ref, own_ref, mem_ref, w_ref, qv_ref, has_ref, out_ref, lse_ref, w_s, x_s, q_s, k_s, v_s, s_s, p_s):
    nq, width = q_s.shape
    columns = key_mask(own_ref, mem_ref, valid, has_ref[pl.program_id(0)])
    if width == 384:
        @pl.when(pl.program_id(0) == 0)
        def _():
            assemble(w_ref, w_s)
        w_ref = w_s
    project_queries(x_ref, w_ref, qv_ref, q_s)
    project_keys(own_ref, mem_ref, w_ref, qv_ref, x_s, k_s, v_s)
    factor = HD**-0.5 * math.log2(math.e)
    stack = s_s.shape[0] // nq
    lanes = lax.broadcasted_iota(jnp.int32, (chunk, 128), 1)
    for tile in range(width // 384):
        group = slice(384 * tile, 384 * tile + 384)
        base = q_s[:, group].astype(f32)
        parts = [base[:, :128], base[:, 128:256], base[:, 256:384]]
        for first in range(4 * tile, 4 * tile + 4, stack):
            start, stop = window(first)[0], window(first + stack - 1)[1]
            masks = [head_mask(first + k, start, stop) for k in range(stack)]
            base = q_s[:, start:stop]
            query = jnp.concatenate([jnp.where(mask, base, jnp.zeros((), bf16)) for mask in masks], axis=0)
            s_s[...] = dot(query, k_s[:, start:stop], NT)

            def body(i, carry, k):
                rows = pl.ds(pl.multiple_of(i * chunk, chunk), chunk)
                here = pl.ds(pl.multiple_of(k * nq + i * chunk, chunk), chunk)
                score = s_s[here, :] * factor + columns
                top = jnp.max(score, axis=1, keepdims=True)
                power = jnp.exp2(score - top)
                total = jnp.sum(power, axis=1, keepdims=True)
                p_s[here, :] = (power * (1.0 / total)).astype(bf16)
                lse_ref[0, rows, :] = jnp.where(lanes == first + k, top + jnp.log2(total), lse_ref[0, rows, :])
                return carry

            for k in range(stack):
                lax.fori_loop(0, nq // chunk, functools.partial(body, k=k), 0, unroll=nq // chunk)
            both = dot(p_s[...], v_s[:, start:stop])
            for k, mask in enumerate(masks):
                out = jnp.where(mask, both[k * nq:(k + 1) * nq], 0.0)
                for w in range((stop - start) // 128):
                    n = start // 128 - 3 * tile + w
                    parts[n] = parts[n] + out[:, 128 * w:128 * w + 128]
        out_ref[0, :, group] = jnp.concatenate(parts, axis=1).astype(bf16)


def attend_back_kernel(
    chunk, valid, x_ref, g_ref, own_ref, mem_ref, w_ref, qv_ref, has_ref, lse_ref,
    dx_ref, dpool_ref, gw_ref, row_ref,
    w_s, x_s, q_s, k_s, v_s, s_s, dp_s, p_s, ds_s, dk_s, dv_s, gw_s,
):
    nq, width = q_s.shape
    step = pl.program_id(0)
    columns = key_mask(own_ref, mem_ref, valid, has_ref[step])
    if width == 384:
        @pl.when(step == 0)
        def _():
            assemble(w_ref, w_s)
        w_ref = w_s
    project_queries(x_ref, w_ref, qv_ref, q_s)
    project_keys(own_ref, mem_ref, w_ref, qv_ref, x_s, k_s, v_s)
    scaling = HD**-0.5
    factor = scaling * math.log2(math.e)
    stack = s_s.shape[0] // nq
    lanes = lax.broadcasted_iota(jnp.int32, (chunk, 128), 1)

    @pl.when(step == 0)
    def _():
        gw_s[...] = jnp.zeros_like(gw_s)

    xt = transposed(x_ref[0])
    keys_t = transposed(x_s[...])
    dx = None
    dpool = None
    row_q, row_v = [], []
    for tile in range(width // 384):
        group = slice(384 * tile, 384 * tile + 384)
        qt = transposed(q_s[:, group])
        gt = transposed(g_ref[0, :, group])
        parts = [None] * 3
        for first in range(4 * tile, 4 * tile + 4, stack):
            start, stop = window(first)[0], window(first + stack - 1)[1]
            masks = [head_mask(first + k, start, stop) for k in range(stack)]
            zero = jnp.zeros((), bf16)
            query = jnp.concatenate([jnp.where(mask, q_s[:, start:stop], zero) for mask in masks], axis=0)
            grad = jnp.concatenate([jnp.where(mask, g_ref[0, :, start:stop], zero) for mask in masks], axis=0)
            s_s[...] = dot(query, k_s[:, start:stop], NT)
            dp_s[...] = dot(grad, v_s[:, start:stop], NT)

            def body(i, carry, k):
                rows = pl.ds(pl.multiple_of(i * chunk, chunk), chunk)
                here = pl.ds(pl.multiple_of(k * nq + i * chunk, chunk), chunk)
                lse = jnp.sum(jnp.where(lanes == first + k, lse_ref[0, rows, :], 0.0), axis=1, keepdims=True)
                p = jnp.exp2(s_s[here, :] * factor + columns - lse)
                dp = dp_s[here, :]
                inner = jnp.sum(p * dp, axis=1, keepdims=True)
                p_s[here, :] = p.astype(bf16)
                ds_s[here, :] = (p * (dp - inner)).astype(bf16)
                return carry

            for k in range(stack):
                lax.fori_loop(0, nq // chunk, functools.partial(body, k=k), 0, unroll=nq // chunk)
            dq_both = dot(ds_s[...], k_s[:, start:stop]) * scaling
            for k, mask in enumerate(masks):
                mine = slice(k * nq, (k + 1) * nq)
                r = slice(HD * (first + k - 4 * tile), HD * (first + k - 4 * tile) + HD)
                dv_s[r, :] = dot(gt[r], p_s[mine, :])
                dk_s[r, :] = dot(qt[r], ds_s[mine, :]) * scaling
                dq = jnp.where(mask, dq_both[mine], 0.0)
                for w in range((stop - start) // 128):
                    n = start // 128 - 3 * tile + w
                    part = dq[:, 128 * w:128 * w + 128]
                    parts[n] = part if parts[n] is None else parts[n] + part
        total = jnp.concatenate(parts, axis=1) + g_ref[0, :, group].astype(f32)
        row_q.append(sum_rows(total))
        low = total.astype(bf16)
        gw_s[tile, :, :384] += dot(xt, low)
        add = dot(low, w_ref[tile, :, :384], NT)
        dx = add if dx is None else dx + add
        for part, src in ((1, dk_s), (2, dv_s)):
            grad = src[...].T
            if part == 2:
                row_v.append(sum_rows(grad))
            low = grad.astype(bf16)
            here = slice(384 * part, 384 * part + 384)
            gw_s[tile, :, here] += dot(keys_t, low)
            add = dot(low, w_ref[tile, :, here], NT)
            dpool = add if dpool is None else dpool + add
    dx_ref[0] = dx
    row = 0
    own, mem = own_ref.shape[2], mem_ref.shape[2]
    toks = own_ref.shape[0]
    for t in range(toks):
        dpool_ref[t, 0, :own, :] = dpool[t * own:(t + 1) * own].astype(bf16)
        dpool_ref[t, 0, own:, :] = dpool[toks * own + t * mem:toks * own + (t + 1) * mem].astype(bf16)
    add_rows(row_ref, [jnp.concatenate(row_q, axis=1), jnp.concatenate(row_v, axis=1)])

    @pl.when(step == pl.num_programs(0) - 1)
    def _():
        for h in range(gw_ref.shape[0]):
            write_shares(gw_ref, h, gw_s)


def first_mlp_kernel(x_ref, comb_ref, out_ref, up_ref, down_ref, ub_ref, gains_ref, shifts_ref, pool_ref, pair_ref,
                     after_ref, middle_ref, pooled_ref, mean_ref, out_s):
    @pl.when(pl.program_id(0) == 0)
    def _():
        assemble_out(out_ref, out_s)

    after = x_ref[0].astype(f32) + dot(comb_ref[0], out_s[...], NT) + shifts_ref[1:2, :]
    after_ref[0] = after
    unit, _ = norm(after)
    low = (unit * gains_ref[1:2, :] + shifts_ref[2:3, :]).astype(bf16)
    total = after + shifts_ref[3:4, :]
    for h in range(up_ref.shape[0]):
        hidden = gelu(dot(low, up_ref[h]) + ub_ref[h]).astype(bf16)
        total = total + dot(hidden, down_ref[h], NT)
    middle_ref[0] = total
    unit, _ = norm(total)
    pooled = exact_dot(pool_ref[...], unit * gains_ref[2:3, :] + shifts_ref[4:5, :])
    pooled_ref[0] = pooled.astype(bf16)
    mean_ref[0] = exact_dot(pair_ref[...], pooled).astype(bf16)


def second_mlp_kernel(
    comb_ref, pooled_ref, cot_ref, out_ref, skip_ref, up_ref, down_ref, ub_ref, gains_ref, shifts_ref,
    mixed_ref, dcomb_ref, dskip_ref, gmlp_ref, gout_ref, gskip_ref, gub_ref, row_ref,
    after_s, low_s, lowt_s, cott_s, sum_s, dlow_s, skip_s,
):
    step = pl.program_id(0)

    @pl.when(step == 0)
    def _():
        share = skip_s.shape[1] // skip_ref.shape[0]
        skip_s[...] = jnp.concatenate([skip_ref[h, :, :share].astype(f32) for h in range(skip_ref.shape[0])], axis=1).astype(bf16)
        after = dot(pooled_ref[...], skip_s[...], NT) + shifts_ref[0:1, :]
        wide = out_ref.shape[2]
        for h in range(out_ref.shape[0]):
            after = after + dot(comb_ref[:, wide * h:wide * h + wide], out_ref[h], NT)
        after_s[...] = after
        unit, _ = norm(after)
        low = (unit * gains_ref[...] + shifts_ref[1:2, :]).astype(bf16)
        low_s[...] = low
        lowt_s[...] = transposed(low)
        cott_s[...] = transposed(cot_ref[...])
        sum_s[...] = after + shifts_ref[2:3, :]
        dlow_s[...] = jnp.zeros_like(dlow_s)

    pre = dot(low_s[...], up_ref[0]) + ub_ref[...]
    hidden, slope = gelu_both(pre)
    hidden = hidden.astype(bf16)
    dpre = dot(cot_ref[...], down_ref[0]) * slope
    gub_ref[...] = sum_rows(dpre)
    dpre = dpre.astype(bf16)
    sum_s[...] += dot(hidden, down_ref[0], NT)
    dlow_s[...] += dot(dpre, up_ref[0], NT)
    for n, grad in enumerate((dot(lowt_s[...], dpre), dot(cott_s[...], hidden))):
        rows = gmlp_ref.shape[3]
        for t in range(gmlp_ref.shape[1]):
            gmlp_ref[0, t, n] = grad[t * rows:(t + 1) * rows].astype(bf16)

    @pl.when(step == pl.num_programs(0) - 1)
    def _():
        padded = sum_s.shape[0] // mixed_ref.shape[0]
        for m in range(mixed_ref.shape[0]):
            mixed_ref[m] = sum_s[padded * m:padded * m + mixed_ref.shape[1], :].astype(bf16)
        unit, inverse = norm(after_s[...])
        dlow = dlow_s[...]
        cot = cot_ref[...].astype(f32)
        res = norm_back(unit, inverse, gains_ref[...], dlow) + cot
        row_ref[...] = jnp.zeros_like(row_ref)
        for i, row in enumerate((res, dlow, cot, dlow * unit)):
            row_ref[i:i + 1, :] = sum_rows(row)
        res = res.astype(bf16)
        dskip_ref[...] = dot(res, skip_s[...])
        rest = transposed(res)
        wide = out_ref.shape[2]
        for h in range(out_ref.shape[0]):
            here = slice(wide * h, wide * h + wide)
            dcomb_ref[:, here] = dot(res, out_ref[h]).astype(bf16)
            grad = dot(rest, comb_ref[:, here])
            half = gout_ref.shape[2]
            for n in range(2 * gout_ref.shape[1]):
                gout_ref[h, n // 2, :, wide * (n % 2):wide * (n % 2) + wide] = grad[half * n:half * n + half].astype(bf16)
        grad = dot(rest, pooled_ref[...])
        wide = gskip_ref.shape[3] // 2
        for h in range(gskip_ref.shape[0]):
            for t in range(gskip_ref.shape[1]):
                low, high = (grad[half * n:half * n + half, wide * h:wide * h + wide] for n in (2 * t, 2 * t + 1))
                gskip_ref[h, t] = jnp.concatenate([low, high], axis=1).astype(bf16)


def first_back_kernel(
    middle_ref, after_ref, comb_ref, dskip_ref, dq_ref, own_ref, mem_ref, out_ref, up_ref, down_ref, ub_ref, gains_ref, shifts_ref,
    unpool_ref, unpair_ref,
    res_ref, dcomb_ref, gmlp_ref, gub_ref, row_ref,
    gup_s, gdown_s, gout_s, out_s,
):
    step = pl.program_id(0)

    @pl.when(step == 0)
    def _():
        gup_s[...] = jnp.zeros_like(gup_s)
        gdown_s[...] = jnp.zeros_like(gdown_s)
        gout_s[...] = jnp.zeros_like(gout_s)
        gub_ref[...] = jnp.zeros_like(gub_ref)
        assemble_out(out_ref, out_s)

    dpool = dskip_ref[0] + dq_ref[0] + own_ref[0] + exact_dot(unpair_ref[...], mem_ref[0])
    dnorm = exact_dot(unpool_ref[...], dpool)
    unit, inverse = norm(middle_ref[0])
    grad = norm_back(unit, inverse, gains_ref[2:3, :], dnorm)
    rows = [sum_rows(dnorm * unit), sum_rows(dnorm), sum_rows(grad)]
    low = grad.astype(bf16)
    lowt = transposed(low)
    unit, inverse = norm(after_ref[0])
    normed = (unit * gains_ref[1:2, :] + shifts_ref[2:3, :]).astype(bf16)
    normedt = transposed(normed)
    dnormed = None
    for h in range(up_ref.shape[0]):
        hidden, slope = gelu_both(dot(normed, up_ref[h]) + ub_ref[h])
        hidden = hidden.astype(bf16)
        dpre = dot(low, down_ref[h]) * slope
        gub_ref[h] += sum_rows(dpre)
        dpre = dpre.astype(bf16)
        gdown_s[h] += dot(lowt, hidden)
        gup_s[h] += dot(normedt, dpre)
        add = dot(dpre, up_ref[h], NT)
        dnormed = add if dnormed is None else dnormed + add
    res = norm_back(unit, inverse, gains_ref[1:2, :], dnormed) + grad
    rows += [sum_rows(dnormed * unit), sum_rows(dnormed), sum_rows(res)]
    res_ref[0] = res
    res = res.astype(bf16)
    dcomb_ref[0] = dot(res, out_s[...]).astype(bf16)
    gout_s[...] += dot(transposed(res), comb_ref[0])
    add_rows(row_ref, rows)

    @pl.when(step == pl.num_programs(0) - 1)
    def _():
        fa, ha = gup_s.shape[2], gout_s.shape[1] // gmlp_ref.shape[0]
        for h in range(gmlp_ref.shape[0]):
            gmlp_ref[h, :, :fa] = gup_s[h].astype(bf16)
            gmlp_ref[h, :, fa:2 * fa] = gdown_s[h].astype(bf16)
            rest = gmlp_ref.shape[2] - 2 * fa - ha
            gout = jnp.concatenate([gout_s[:, ha * h:ha * h + ha], jnp.zeros((gout_s.shape[0], rest), f32)], axis=1)
            gmlp_ref[h, :, 2 * fa:] = gout.astype(bf16)


def last_back_kernel(x_ref, res_ref, dx_ref, own_ref, mem_ref, gains_ref, unpool_ref, unpair_ref, grad_ref, row_ref):
    dpool = own_ref[0] + exact_dot(unpair_ref[...], mem_ref[0])
    dnorm = dx_ref[0] + exact_dot(unpool_ref[...], dpool)
    unit, inverse = norm(x_ref[0].astype(f32))
    grad = norm_back(unit, inverse, gains_ref[0:1, :], dnorm) + res_ref[0]
    grad_ref[0] = grad.astype(bf16)
    add_rows(row_ref, [sum_rows(dnorm * unit), sum_rows(dnorm)])


def whole(array):
    return pl.BlockSpec(array.shape, lambda i: (0,) * array.ndim)


def by_micro(array, axis=0):
    block = array.shape[:axis] + (1,) + array.shape[axis + 1:]
    return pl.BlockSpec(block, lambda i: (0,) * axis + (i,) + (0,) * (array.ndim - axis - 1))


def shape(dims, dtype):
    return jax.ShapeDtypeStruct(dims, dtype)


def about(us):
    return pl.CostEstimate(flops=int(us * 1e9), bytes_accessed=0, transcendentals=0)


def call(kernel, steps, args, outs, scratch=(), name=None, us=10, number=None):
    def spec(array, how):
        if how is None:
            return whole(array)
        return by_micro(array, how) if isinstance(how, int) else how

    return pl.pallas_call(
        kernel,
        grid=(steps,),
        in_specs=[spec(a, how) for a, how in args],
        out_specs=[spec(a, how) for a, how in outs],
        out_shape=[a for a, _ in outs],
        scratch_shapes=[pltpu.VMEM(*one) if isinstance(one, tuple) else one for one in scratch],
        compiler_params=pltpu.CompilerParams(vmem_limit_bytes=VMEM_CAP, collective_id=number, has_side_effects=number is not None),
        cost_estimate=about(us),
        name=name,
    )(*[a for a, _ in args])


def stacked(nq):
    return 2 if nq < 512 else 1


def chunk_of(nq):
    return 112 if nq % 112 == 0 else 16


def attend(x, own, mem, w, qv, has, valid, width):
    batches, nq, d = x.shape
    keys = own.shape[0] * own.shape[2] + mem.shape[0] * mem.shape[2]
    return call(
        functools.partial(attend_kernel, chunk_of(nq), valid), batches,
        [(x, 0), (own, 1), (mem, 1), w, (qv, None), (has, pl.BlockSpec(memory_space=pltpu.SMEM))],
        [(shape((batches, nq, width), bf16), 0), (shape((batches, nq, 128), f32), 0)],
        [((1, d, 1152 if width == 384 else 128), bf16),
         ((keys, d), bf16), ((nq, width), bf16), ((keys, width), bf16), ((keys, width), bf16),
         ((stacked(nq) * nq, keys), f32), ((stacked(nq) * nq, keys), bf16)],
        name="attend", us=20,
    )


def attend_back(x, grad, own, mem, w, qv, has, valid, lse, heads):
    batches, nq, d = x.shape
    width = grad.shape[2]
    keys = own.shape[0] * own.shape[2] + mem.shape[0] * mem.shape[2]
    both = (own.shape[0], batches, own.shape[2] + mem.shape[2], d)
    groups = (width // 384, d, 1152)
    rows = stacked(nq) * nq
    return call(
        functools.partial(attend_back_kernel, chunk_of(nq), valid), batches,
        [(x, 0), (grad, 0), (own, 1), (mem, 1), w, (qv, None), (has, INSMEM), (lse, 0)],
        [(shape((batches, nq, d), f32), 0), (shape(both, bf16), 1), (shape((heads, d, 3 * width // heads), bf16), None), (shape((8, width), f32), None)],
        [((1, d, 1152 if width == 384 else 128), bf16),
         ((keys, d), bf16), ((nq, width), bf16), ((keys, width), bf16), ((keys, width), bf16),
         ((rows, keys), f32), ((rows, keys), f32), ((rows, keys), bf16), ((rows, keys), bf16),
         ((384, keys), f32), ((384, keys), f32), (groups, f32)],
        name="attend_back", us=36,
    )


def share_kernel(gather, count, *refs):
    if gather:
        pooled_ref, mean_ref, pick_ref, w_ref, *refs = refs
        biases, (own_ref, mem_ref, all_ref, *refs) = refs[:count], refs[count:]
        if count:
            (qv_a_ref, qv_b_ref, ub_a_ref, ub_b_ref), refs = refs[:4], refs[4:]
    else:
        pooled_ref, mean_ref, pick_ref, own_ref, mem_ref, *refs = refs
    (got_s, pick_s, local_sem, own_send, own_recv, mem_send, mem_recv, pass_send, pass_recv, clip_send, clip_recv, *refs) = refs
    clip, head, chip, core, chips = places()
    clips, heads = lax.axis_size("clip"), lax.axis_size("head")
    share = pooled_ref.shape[0]
    here = 2 * chip + core
    partner = {"tok": 2 * chip + 1 - core}
    across = [{"tok": 2 * rem(chip + k, chips) + core} for k in range(1, chips)]
    beside = [{"head": rem(head + d, heads)} for d in range(1, heads)]
    heads_of = lambda by, sign: [{"clip": clip + by, "head": rem(head + sign * d, heads)} for d in range(heads)]
    last, begun = clip < clips - 1, clip > 0
    near = [(d, None) for d in [partner] + across + (beside if gather else [])]
    greet(near + [(d, begun) for d in heads_of(-1, -1)], near + [(d, last) for d in heads_of(1, 1)])

    def spread(src, out, send, recv):
        copies = [remote(src, out.at[here], send.at[0], recv.at[0], partner)]
        copies += [remote(src, out.at[here], send.at[k + 1], recv.at[k + 1], across[k]) for k in range(chips - 1)]
        return copies

    def passed(out, k, row):
        block = 2 * rem(chip - k, chips) + core
        return remote(out.at[block], out.at[block], pass_send.at[row, k - 1], pass_recv.at[row, k - 1], partner)

    clip_copies = [remote(mean_ref, got_s.at[d], clip_send.at[d], clip_recv.at[d], device) for d, device in enumerate(heads_of(1, 1))]

    @pl.when(last)
    def _():
        for copy in clip_copies:
            copy.start()

    w_first, w_diagonal, w_core = {}, {}, {}
    if gather:
        w_local, w_send, w_recv, d_send, d_recv, c_send, c_recv, b_send, b_recv, *bias_got = refs
        bias_copies = [
            remote(ref, got.at[d], b_send.at[d, n], b_recv.at[d, n], device)
            for d, device in enumerate(beside)
            for n, (ref, got) in enumerate(zip(biases, bias_got))
        ]
        for copy in bias_copies:
            copy.start()
        mine = all_ref.at[head, here]
        for k in range(1, chips):
            w_first[k, 0] = remote(w_ref, mine, w_send.at[k - 1], w_recv.at[k - 1], across[k - 1])
        for d in range(1, heads):
            w_first[0, d] = remote(w_ref, mine, w_send.at[chips - 2 + d], w_recv.at[chips - 2 + d], beside[d - 1])
        w_core[0, 0] = remote(w_ref, mine, c_send.at[0, 0], c_recv.at[0, 0], partner)
        for copy in [*w_first.values(), w_core[0, 0]]:
            copy.start()
        w_copy = pltpu.make_async_copy(w_ref, mine, w_local.at[0])
        w_copy.start()

        def forward(k, d):
            block = all_ref.at[rem(head - d, heads), 2 * rem(chip - k, chips) + core]
            w_core[k, d] = remote(block, block, c_send.at[k, d], c_recv.at[k, d], partner)
            w_core[k, d].start()

    own_copies = spread(pooled_ref, own_ref, own_send, own_recv)
    for copy in own_copies[1:] + own_copies[:1]:
        copy.start()
    own_local = pltpu.make_async_copy(pooled_ref, own_ref.at[here], local_sem.at[0])
    own_local.start()
    if gather:
        for k in range(1, chips):
            w_first[k, 0].wait_recv()
            block = all_ref.at[head, 2 * rem(chip - k, chips) + core]
            for d in range(1, heads):
                w_diagonal[k, d] = remote(block, block, d_send.at[k - 1, d - 1], d_recv.at[k - 1, d - 1], beside[d - 1])
                w_diagonal[k, d].start()
            forward(k, 0)

    @pl.when(begun)
    def _():
        for copy in clip_copies:
            copy.wait_recv()
        for m in range(share):
            total = None
            for d in range(heads):
                for s in range(share):
                    piece = got_s[d, s].astype(f32) * pick_ref[m, d * share + s]
                    total = piece if total is None else total + piece
            pick_s[m] = total.astype(bf16)

    @pl.when(jnp.logical_not(begun))
    def _():
        pick_s[...] = jnp.zeros_like(pick_s)

    mem_copies = spread(pick_s, mem_ref, mem_send, mem_recv)
    for copy in mem_copies[1:] + mem_copies[:1]:
        copy.start()
    mem_local = pltpu.make_async_copy(pick_s, mem_ref.at[here], local_sem.at[1])
    mem_local.start()
    forwards = []
    for k in range(1, chips):
        own_copies[k].wait_recv()
        forwards.append(passed(own_ref, k, 0))
        forwards[-1].start()
    if gather:
        for d in range(1, heads):
            w_first[0, d].wait_recv()
            forward(0, d)
    for k in range(1, chips):
        mem_copies[k].wait_recv()
        forwards.append(passed(mem_ref, k, 1))
        forwards[-1].start()
    if gather:
        for k, d in w_diagonal:
            w_diagonal[k, d].wait_recv()
            forward(k, d)
        for copy in w_core.values():
            copy.wait_recv()
        for copy in bias_copies:
            copy.wait_recv()
    if count:
        by_head = []
        for ref, got in zip(biases, bias_got):
            pieces = []
            for h in range(heads):
                piece = ref[...]
                for d in range(1, heads):
                    piece = jnp.where(rem(head - d, heads) == h, got[d - 1], piece)
                pieces.append(piece)
            by_head.append(pieces)
        qv_a_ref[...] = jnp.concatenate(by_head[0], axis=1)
        qv_b_ref[...] = jnp.concatenate(by_head[1], axis=1)
        fa = ub_a_ref.shape[2]
        for h in range(heads):
            ub_a_ref[h] = by_head[2][h][:, :fa]
        ub_b_ref[...] = jnp.concatenate([piece[:, fa:] for piece in by_head[2]], axis=1)
        for copy in bias_copies:
            copy.wait_send()
    own_copies[0].wait_recv()
    mem_copies[0].wait_recv()
    for copy in forwards:
        copy.wait_recv()
    for copy in own_copies + mem_copies + forwards + [*w_first.values(), *w_diagonal.values(), *w_core.values()]:
        copy.wait_send()
    own_local.wait()
    mem_local.wait()
    if gather:
        w_copy.wait()

    @pl.when(last)
    def _():
        for copy in clip_copies:
            copy.wait_send()


def share_pooled(pooled, mean, pick, number, block=None, biases=(), fa=0):
    toks, heads = lax.axis_size("tok"), lax.axis_size("head")
    chips = toks // 2
    few = max(chips - 1, 1)
    args, specs = [pooled, mean, pick], [INVMEM, INVMEM, INSMEM]
    outs = [shape((toks,) + pooled.shape, bf16), shape((toks,) + mean.shape, bf16)]
    scratch = [
        pltpu.VMEM((heads,) + mean.shape, bf16), pltpu.VMEM(mean.shape, bf16), dma(2),
        dma(chips), dma(chips), dma(chips), dma(chips), dma(2, few), dma(2, few), dma(heads), dma(heads),
    ]
    if block is not None:
        args, specs = args + [block, *biases], specs + [INVMEM] * (1 + len(biases))
        outs = outs + [shape((heads, toks) + block.shape, bf16)]
        if biases:
            (_, wa), (_, wb), (_, wide) = (b.shape for b in biases)
            outs += [shape(dims, f32) for dims in ((2, heads * wa), (2, heads * wb), (heads, 1, fa), (1, heads * (wide - fa)))]
        firsts = max(chips + heads - 2, 1)
        scratch += [dma(1), dma(firsts), dma(firsts), dma(few, max(heads - 1, 1)), dma(few, max(heads - 1, 1)), dma(chips, heads), dma(chips, heads)]
        scratch += [dma(max(heads - 1, 1), max(len(biases), 1)), dma(max(heads - 1, 1), max(len(biases), 1))]
        scratch += [pltpu.VMEM((max(heads - 1, 1),) + b.shape, f32) for b in biases]
    return pl.pallas_call(
        functools.partial(share_kernel, block is not None, len(biases)),
        in_specs=specs,
        out_specs=[ANY] * min(len(outs), 3) + [INVMEM] * (len(outs) - 3),
        out_shape=outs,
        scratch_shapes=scratch,
        compiler_params=pltpu.CompilerParams(collective_id=number, has_side_effects=True, vmem_limit_bytes=VMEM_CAP),
        cost_estimate=about(20 if block is None else 30),
        name="share_pooled",
    )(*args)


def give_back_kernel(exchange, *refs):
    if exchange:
        part_ref, pick_ref, half_ref, grad_ref, own_ref, back_ref, all_ref, sum_ref, *refs = refs
        refs, hosted = refs[:-14], refs[-14:]
        (half_local, half_send, half_recv, block_s, block_core, head_s, block_head, block_chip,
         bc_send, bc_recv, bh_send, bh_recv, bx_send, bx_recv) = hosted
    else:
        part_ref, pick_ref, own_ref, back_ref, *refs = refs
    (mine_s, core_s, sum_s, chip_s, route_s, got_s,
     local_sem, core_send, core_recv, mem_send, mem_recv, own_send, own_recv, clip_send, clip_recv) = refs
    clip, head, chip, core, chips = places()
    clips, heads = lax.axis_size("clip"), lax.axis_size("head")
    share, rows = own_ref.shape[0], own_ref.shape[1]
    partner = {"tok": 2 * chip + 1 - core}
    across = [{"tok": 2 * rem(chip + k, chips) + core} for k in range(1, chips)]
    beside = [{"head": rem(head + d, heads)} for d in range(1, heads)]
    heads_of = lambda by, sign: [{"clip": clip + by, "head": rem(head + sign * d, heads)} for d in range(heads)]
    last, begun = clip < clips - 1, clip > 0
    near = [(d, None) for d in [partner] + across + (beside if exchange else [])]
    greet(near + [(d, last) for d in heads_of(1, 1)], near + [(d, begun) for d in heads_of(-1, -1)])

    order = [rem(chip + k, chips) for k in list(range(1, chips)) + [0]]
    core_copies, local_copies = [], []
    for n, other in enumerate(order):
        core_copies.append(remote(part_ref.at[2 * other + 1 - core], core_s.at[n], core_send.at[n], core_recv.at[n], partner))
        core_copies[-1].start()
    for n, other in enumerate(order):
        local_copies.append(pltpu.make_async_copy(part_ref.at[2 * other + core], mine_s.at[n], local_sem.at[n]))
        local_copies[-1].start()
    halves, block_copies = [], []
    if exchange:
        for n in range(heads * chips):
            block_copies.append(remote(grad_ref.at[2 * n + 1 - core], block_core.at[n], bc_send.at[n], bc_recv.at[n], partner))
            block_copies[-1].start()
        for n, copy in enumerate(block_copies):
            copy.wait_recv()
            block_s[n] = (grad_ref[2 * n + core].astype(f32) + block_core[n].astype(f32)).astype(bf16)
        head_copies = [
            remote(block_s.at[rem(head + k + 1, heads) * chips + x], block_head.at[k, x], bh_send.at[k, x], bh_recv.at[k, x], d)
            for k, d in enumerate(beside) for x in range(chips)
        ]
        for copy in head_copies:
            copy.start()
        halves = [remote(half_ref, all_ref.at[head], half_send.at[k], half_recv.at[k], d) for k, d in enumerate(beside)]
        for copy in halves:
            copy.start()
        half_copy = pltpu.make_async_copy(half_ref, all_ref.at[head], half_local.at[0])
        half_copy.start()
    mem_copies, own_copies = [], []
    for n in range(chips):
        local_copies[n].wait()
        core_copies[n].wait_recv()
        if n == chips - 1:
            break
        sum_s[n] = (mine_s[n].astype(f32) + core_s[n].astype(f32)).astype(bf16)
        low, high = pl.ds(0, rows), pl.ds(rows, sum_s.shape[2] - rows)
        mem_copies.append(remote(sum_s.at[n, :, high, :], chip_s.at[n, :, high, :], mem_send.at[n], mem_recv.at[n], across[n]))
        mem_copies[-1].start()
        own_copies.append(remote(sum_s.at[n, :, low, :], chip_s.at[n, :, low, :], own_send.at[n], own_recv.at[n], across[n]))
        own_copies[-1].start()
    base = chips - 1
    for copy in mem_copies:
        copy.wait_recv()
    memory = []
    for m in range(share):
        total = mine_s[base, m, rows:].astype(f32) + core_s[base, m, rows:].astype(f32)
        for n in range(chips - 1):
            total = total + chip_s[n, m, rows:].astype(f32)
        memory.append(total)
    clip_copies = [
        remote(route_s.at[d], got_s.at[d], clip_send.at[d], clip_recv.at[d], device) for d, device in enumerate(heads_of(-1, -1))
    ]

    @pl.when(begun)
    def _():
        for d in range(heads):
            for s in range(share):
                total = None
                for m in range(share):
                    piece = memory[m] * pick_ref[m, d * share + s]
                    total = piece if total is None else total + piece
                route_s[d, s] = total.astype(bf16)
            clip_copies[d].start()

    if exchange:
        for copy in head_copies:
            copy.wait_recv()
        for x in range(chips):
            total = block_s[head * chips + x].astype(f32)
            for k in range(heads - 1):
                total = total + block_head[k, x].astype(f32)
            head_s[x] = total.astype(bf16)
        chip_copies = [
            remote(head_s.at[rem(chip + k + 1, chips)], block_chip.at[k], bx_send.at[k], bx_recv.at[k], d) for k, d in enumerate(across)
        ]
        for copy in chip_copies:
            copy.start()
    for copy in own_copies:
        copy.wait_recv()
    for m in range(share):
        total = mine_s[base, m, :rows].astype(f32) + core_s[base, m, :rows].astype(f32)
        for n in range(chips - 1):
            total = total + chip_s[n, m, :rows].astype(f32)
        own_ref[m] = total

    @pl.when(last)
    def _():
        for copy in clip_copies:
            copy.wait_recv()
        total = got_s[0].astype(f32)
        for d in range(1, heads):
            total = total + got_s[d].astype(f32)
        back_ref[...] = total

    @pl.when(jnp.logical_not(last))
    def _():
        back_ref[...] = jnp.zeros_like(back_ref)

    for copy in halves:
        copy.wait_recv()
    if exchange:
        for copy in chip_copies:
            copy.wait_recv()
        total = head_s[chip].astype(f32)
        for k in range(chips - 1):
            total = total + block_chip[k].astype(f32)
        sum_ref[...] = jnp.zeros_like(sum_ref)
        sum_ref[:, :grad_ref.shape[2]] = total.astype(bf16)
        for copy in block_copies + head_copies + chip_copies:
            copy.wait_send()
    for copy in core_copies + mem_copies + own_copies + halves:
        copy.wait_send()
    if exchange:
        half_copy.wait()

    @pl.when(begun)
    def _():
        for copy in clip_copies:
            copy.wait_send()


def give_back(part, pick, own_rows, number, half=None, grad=None):
    toks, heads = lax.axis_size("tok"), lax.axis_size("head")
    chips, few = toks // 2, max(toks // 2 - 1, 1)
    share, rows, d = part.shape[1:]
    args, specs = [part, pick], [ANY, INSMEM]
    outs, out_specs = [shape((share, own_rows, d), f32), shape((share, rows - own_rows, d), f32)], [INVMEM, INVMEM]
    scratch = [
        pltpu.VMEM((chips,) + part.shape[1:], bf16), pltpu.VMEM((chips,) + part.shape[1:], bf16),
        pltpu.VMEM((few,) + part.shape[1:], bf16), pltpu.VMEM((few,) + part.shape[1:], bf16),
        pltpu.VMEM((heads, share, rows - own_rows, d), bf16), pltpu.VMEM((heads, share, rows - own_rows, d), bf16),
        dma(chips), dma(chips), dma(chips), dma(few), dma(few), dma(few), dma(few), dma(heads), dma(heads),
    ]
    if half is not None:
        block = grad.shape[1:]
        beside = max(heads - 1, 1)
        args, specs = args + [half, grad], specs + [INVMEM, INVMEM]
        outs += [shape((heads,) + half.shape, half.dtype), shape((block[0], -(-block[1] // 128) * 128), bf16)]
        out_specs += [ANY, INVMEM]
        low = lambda *dims: pltpu.VMEM(dims + block, bf16)
        scratch += [dma(1), dma(beside), dma(beside), low(heads * chips), low(heads * chips), low(chips), low(beside, chips), low(few)]
        scratch += [dma(heads * chips), dma(heads * chips), dma(beside, chips), dma(beside, chips), dma(few), dma(few)]
    return pl.pallas_call(
        functools.partial(give_back_kernel, half is not None),
        in_specs=specs,
        out_specs=out_specs,
        out_shape=outs,
        scratch_shapes=scratch,
        compiler_params=pltpu.CompilerParams(collective_id=number, has_side_effects=True, vmem_limit_bytes=VMEM_CAP),
        cost_estimate=about(1),
        name="give_back",
    )(*args)


def finish_kernel(half_ref, last_ref, qv_a_rows, a_ref, b_ref, qv_b_rows, ub_a_rows, ub_b_rows, grad_ref, rest_ref, group_ref,
                  all_ref, total_ref, sums_ref, *scratch):
    (small_ref, small_s, small_core, small_chip, small_head, small_clip,
     local_sem, half_send, half_recv, core_send, core_recv, chip_send, chip_recv, head_send, head_recv,
     clip_send, clip_recv, *chain) = scratch
    first_lanes, next_lanes = group_ref.shape[1], rest_ref.shape[1]
    tiles, count = chain[0].shape[1] // 128, chain[-1].shape[0]
    bounds = [tiles * n // count * 128 for n in range(count + 1)]
    chain = Chain(*chain[:3], [(slice(None), pl.ds(low, high - low)) for low, high in zip(bounds, bounds[1:])], *chain[3:])
    clip, head, chip, core, chips = places()
    clips, heads = lax.axis_size("clip"), lax.axis_size("head")
    share = half_ref.shape[0]
    partner = {"tok": 2 * chip + 1 - core}
    across = [{"tok": 2 * rem(chip + k, chips) + core} for k in range(1, chips)]
    beside = [{"head": rem(head + k, heads)} for k in range(1, heads)]
    along = [{"clip": rem(clip + k, clips)} for k in range(1, clips)]
    peers = [(d, None) for d in [partner] + across + beside + along]
    greet(peers, peers)
    chain.part[:, :first_lanes] = group_ref[...]
    chain.part[:, first_lanes:first_lanes + next_lanes] = rest_ref[...]
    chain.part[:, first_lanes + next_lanes:] = grad_ref[...]
    for n in range(count):
        chain.send_ends(n)
    pending = []
    d1 = small_ref.shape[1]
    small_ref[...] = jnp.zeros_like(small_ref)
    small_ref[0:2, :] = last_ref[0:2, :]
    small_ref[2:4, :] = qv_a_rows[0:2, :]
    for row, source in enumerate((3, 0, 5, 4, 2, 1)):
        small_ref[4 + row:5 + row, :] = a_ref[source:source + 1, :]
    row = 10
    longer = [b_ref[n:n + 1, :] for n in (3, 0, 1, 2)] + [qv_b_rows[n:n + 1, :] for n in range(2)]
    for values in longer + [ub_a_rows[h] for h in range(heads)] + [ub_b_rows[...]]:
        for low in range(0, values.shape[1], d1):
            small_ref[row:row + 1, :] = values[:, low:low + d1]
            row += 1
    def go(copies):
        for copy in copies:
            copy.start()
        pending.extend(copies)
        return copies

    def arrived(copies):
        for copy in copies:
            copy.wait_recv()

    def in_order(index, size, own, slot):
        total = None
        for i in range(size):
            piece = jnp.where(index == i, own, jnp.zeros_like(own))
            for k in range(size - 1):
                piece = jnp.where(rem(index - k - 1, size) == i, slot(k), piece)
            total = piece if total is None else total + piece
        return total

    first = go([remote(small_ref, small_core, core_send.at[0], core_recv.at[0], partner)])
    cuts, tokens = [], half_ref.shape[1]
    for s in range(share):
        early = tokens // 4 // 16 * 16 if s == 0 else 0
        cuts += [(s, low, high) for low, high in ((0, early), (early, tokens)) if high > low]
    halves = [
        [remote(half_ref.at[s, pl.ds(low, high - low)], all_ref.at[head, s, pl.ds(low, high - low)], half_send.at[k, n], half_recv.at[k, n], d)
         for k, d in enumerate(beside)]
        for n, (s, low, high) in enumerate(cuts)
    ]
    go(halves[0])
    local_half = pltpu.make_async_copy(half_ref, all_ref.at[head], local_sem.at[0])
    local_half.start()
    arrived(first)
    small_s[0] = small_ref[...] + small_core[...]
    copies = go([remote(small_s.at[0], small_head.at[k], head_send.at[k, 0], head_recv.at[k, 0], d) for k, d in enumerate(beside)])
    for s in range(1, len(halves)):
        go(halves[s])
    chain.send_parts(0)
    arrived(copies)
    small_s[1] = in_order(head, heads, small_s[0], lambda k: small_head[k])
    copies = go([remote(small_s.at[1], small_chip.at[k], chip_send.at[k, 0], chip_recv.at[k, 0], d) for k, d in enumerate(across)])
    chain.send_parts(1)
    arrived(copies)
    small_s[2] = in_order(chip, chips, small_s[1], lambda k: small_chip[k])
    copies = []
    for k, d in enumerate(along):
        copies += go([remote(small_s.at[2], small_clip.at[k], clip_send.at[k, 0], clip_recv.at[k, 0], d)])
    for n in range(2, count):
        chain.send_parts(n)
        chain.middle_totals(n - 2)
    for n in range(count - 2, count):
        chain.middle_totals(n)
    for n in range(count):
        chain.other_totals(n)
    arrived(copies)
    total_ref[...] = in_order(clip, clips, small_s[2], lambda k: small_clip[k])
    sums_ref[...] = chain.from_inner[...]
    chain.close()
    for copies in halves:
        arrived(copies)
    for copy in pending:
        copy.wait_send()
    local_half.wait()


def finish(half, rows, grad, rest, first, count, number):
    toks, heads, clips = lax.axis_size("tok"), lax.axis_size("head"), lax.axis_size("clip")
    chips = toks // 2
    across, beside, along = (max(n, 1) for n in (chips - 1, heads - 1, clips - 1))
    depth, d1 = rest.shape[0], rows[0].shape[1]
    small = (-(-count // 8) * 8, d1)
    full = lambda *dims: pltpu.VMEM(dims + small, f32)
    buffer = (depth, first.shape[1] + rest.shape[1] + grad.shape[1])
    return pl.pallas_call(
        finish_kernel,
        in_specs=[INVMEM] * (len(rows) + 4),
        out_specs=[ANY, INVMEM, INVMEM],
        out_shape=[shape((heads,) + half.shape, half.dtype), shape(small, f32), shape(buffer, bf16)],
        scratch_shapes=[
            full(), full(3), full(), full(across), full(beside), full(along),
            dma(1), dma(beside, half.shape[0] + 1), dma(beside, half.shape[0] + 1), dma(1), dma(1),
            dma(across, 1), dma(across, 1), dma(beside, 1), dma(beside, 1), dma(along, 1), dma(along, 1),
            *chain_scratch(buffer, PIECES),
        ],
        compiler_params=pltpu.CompilerParams(collective_id=number, has_side_effects=True, vmem_limit_bytes=VMEM_CAP),
        cost_estimate=about(40),
        name="finish",
    )(half, *rows, grad, rest, first)


def write_kernel(head_ref, total_ref, sums_ref, mlp_ref, qkv_a_ref, out_a_ref, up_a_ref, down_a_ref, qkv_b_ref, out_b_ref, skip_b_ref,
                 up_b_ref, down_b_ref, gains_a_ref, gains_b_ref, shifts_a_ref, shifts_b_ref, qv_a_ref, qv_b_ref, ub_a_ref, ub_b_ref):
    head, total = head_ref[0], total_ref[...]
    at = [10]

    def rows(width):
        first = at[0]
        at[0] += width // total.shape[1]
        return jnp.concatenate([total[r:r + 1] for r in range(first, at[0])], axis=1)

    def share_of(row, width):
        piece = row[:, :width]
        for h in range(1, row.shape[1] // width):
            piece = jnp.where(head == h, row[:, width * h:width * h + width], piece)
        return piece

    gains_a_ref[0:1, :] = total[0:1]
    gains_a_ref[1:3, :] = total[4:6]
    shifts_a_ref[0:1, :] = total[1:2]
    shifts_a_ref[1:5, :] = total[6:10]
    d2, fa, fb = gains_b_ref.shape[0], ub_a_ref.shape[0], ub_b_ref.shape[0]
    heads = total.shape[1] // qv_a_ref.shape[1]
    for i in range(2):
        qv_a_ref[i:i + 1, :] = share_of(total[2 + i:3 + i], qv_a_ref.shape[1])
    gains_b_ref[...] = rows(d2).reshape(d2)
    for i in range(3):
        shifts_b_ref[i:i + 1, :] = rows(d2)
    for i in range(2):
        qv_b_ref[i:i + 1, :] = share_of(rows(d2), qv_b_ref.shape[1])
    ub_a_ref[...] = share_of(rows(heads * fa), fa).reshape(fa)
    ub_b_ref[...] = share_of(rows(heads * fb), fb).reshape(fb)
    low = 0
    depth = sums_ref.shape[0]

    def take(ref):
        nonlocal low
        ref[...] = sums_ref[:, low:low + ref.shape[1]].astype(f32)
        low += ref.shape[1]

    for part in range(3):
        take(qkv_b_ref.at[part])
    for ref in (out_b_ref, skip_b_ref):
        for n in range(2):
            take(ref.at[depth * n:depth * n + depth])
    for ref in (up_a_ref, down_a_ref, out_a_ref):
        take(ref)
    low = -(-low // 256) * 256
    for part in range(3):
        take(qkv_a_ref.at[part])
    up_b_ref[...] = mlp_ref[:up_b_ref.shape[0], :].astype(f32)
    down_b_ref[...] = mlp_ref[up_b_ref.shape[0]:, :].astype(f32)


def reduce_clips(shard):
    clips, clip = lax.axis_size("clip"), lax.axis_index("clip")
    pieces = shard.reshape(clips, -1, shard.shape[-1])
    total = lax.dynamic_index_in_dim(pieces, clip, 0, keepdims=False).astype(f32)
    for k in range(1, clips):
        give = lax.dynamic_index_in_dim(pieces, (clip + k) % clips, 0, keepdims=False)
        total = total + lax.ppermute(give, "clip", [(i, (i + k) % clips) for i in range(clips)]).astype(f32)
    return total.astype(bf16)


def spread_clips(piece):
    clips, clip = lax.axis_size("clip"), lax.axis_index("clip")
    out = jnp.zeros((clips,) + piece.shape, piece.dtype)
    out = lax.dynamic_update_index_in_dim(out, piece, clip, 0)
    for k in range(1, clips):
        got = lax.ppermute(piece, "clip", [(i, (i + k) % clips) for i in range(clips)])
        out = lax.dynamic_update_index_in_dim(out, got, (clip - k + clips) % clips, 0)
    return out.reshape((-1,) + piece.shape[1:])


def local(
    clips_in, resets, assign, w_qkv_a, w_out_a, w_up_a, w_down_a, w_qkv_b, w_out_b, w_skip_b, w_up_b, w_down_b,
    gains_a, gains_b, shifts_a, shifts_b, qv_bias_a, qv_bias_b, up_bias_a, up_bias_b, cotangent,
):
    heads, toks, clips = lax.axis_size("head"), lax.axis_size("tok"), lax.axis_size("clip")
    head = lax.axis_index("head")
    micro, frames = clips_in.shape[1], clips_in.shape[2]
    d1, d2 = clips_in.shape[-1], cotangent.shape[-1]
    share = micro // heads
    first = head * share
    pool_np, pair_np = pool_matrix(frames), pair_matrix(frames)
    pooling, pairing = jnp.asarray(pool_np, bf16), jnp.asarray(pair_np, bf16)
    unpooling, unpairing = jnp.asarray(pool_np.T, bf16), jnp.asarray(pair_np.T, bf16)
    tokens, pooled_tokens = frames * PATCH, frames * POOLED
    own_rows, mem_rows = up16(pooled_tokens), up16(frames // 2 * POOLED)
    rows2 = share * own_rows


    def by_patch(tensor):
        return tensor.transpose(0, 2, 1, 3).reshape(tensor.shape[0], -1, tensor.shape[3])

    def by_frame(rows, like):
        return rows.reshape(like[:2] + (like[3], like[2], like[4])).transpose(0, 1, 3, 2, 4)

    cot = by_patch(lax.dynamic_slice_in_dim(cotangent[0], first, share, 0))

    source = lax.dynamic_slice_in_dim(assign[0], first, share, 0)
    flags = lax.dynamic_slice_in_dim(resets[0], first, share, 0)
    slot = ((head - source // share + heads) % heads) * share + source % share
    pick = (jnp.arange(heads * share)[None, :] == slot[:, None]).astype(f32)
    has = ((flags == 0) & (lax.axis_index("clip") > 0)).astype(jnp.int32)
    valid = (pooled_tokens, frames // 2 * POOLED)

    group = ("head", "tok")
    fa, ha = w_up_a.shape[1], w_out_a.shape[1]
    fb, hb, hs = w_up_b.shape[1], w_out_b.shape[1], w_skip_b.shape[1]
    spare_a = jnp.zeros((w_out_a.shape[0], -w_out_a.shape[1] % 256), bf16)
    pack_a = jnp.concatenate([w_up_a, w_down_a, w_out_a, spare_a], axis=1)
    all_a = lax.all_gather(pack_a, group).reshape(heads, d1, -1)
    stream = by_patch(lax.dynamic_slice_in_dim(clips_in[0], first, share, 0))
    low1, pooled1, mean1 = call(
        norm_pool_kernel, share,
        [(stream, 0), (gains_a, None), (shifts_a, None), (pooling, None), (pairing, None)],
        [(shape((share, tokens, d1), bf16), 0), (shape((share, own_rows, d1), bf16), 0), (shape((share, mem_rows, d1), bf16), 0)],
        name="norm_pool", us=5,
    )
    pack_w = jnp.concatenate([*w_qkv_b.transpose(1, 0, 2), *w_qkv_a.transpose(1, 0, 2)], axis=1)
    own1, mem1, all_w, qv_a, qv_b, ub_a, ub_b = share_pooled(
        pooled1, mean1, pick, 0, pack_w, [qv_bias_a, qv_bias_b, jnp.concatenate([up_bias_a, up_bias_b])[None]], fa)
    all_q = all_w.reshape(heads, d1, -1)
    all_w = all_q[:, :, 3 * hb:]
    q_spec = pl.BlockSpec((heads, d1, 3 * hb), lambda i: (0, 0, 0))
    own1, w_up_b, cot = lax.optimization_barrier((own1, w_up_b, cot))
    spare = jnp.zeros((w_up_b.shape[0], -(2 * fb + hb + hs) % hb), bf16)
    pack_b = jnp.concatenate([w_up_b, w_down_b, w_out_b, w_skip_b, spare], axis=1)
    all_b = lax.all_gather(pack_b, group).reshape(heads, d2, -1)
    cot = jnp.pad(cot, ((0, 0), (0, own_rows - pooled_tokens), (0, 0))).reshape(rows2, d2)

    up_spec, down_spec = (pl.BlockSpec((heads, d1, fa), lambda i, n=n: (0, 0, n)) for n in range(2))
    out_a_spec = pl.BlockSpec((heads, d1, 256), lambda i: (0, 0, 2 * fa // 256))

    comb1, lse1 = attend(low1, own1, mem1, (all_w, None), qv_a, has, valid, d1)
    after1, middle, pooled3, mean3 = call(
        first_mlp_kernel, share,
        [(stream, 0), (comb1, 0), (all_a, out_a_spec), (all_a, up_spec), (all_a, down_spec), (ub_a, None),
         (gains_a, None), (shifts_a, None),
         (pooling, None), (pairing, None)],
        [(shape((share, tokens, d1), f32), 0), (shape((share, tokens, d1), f32), 0),
         (shape((share, own_rows, d1), bf16), 0), (shape((share, mem_rows, d1), bf16), 0)],
        [((d1, d1), bf16)],
        name="first_mlp", us=13,
    )

    own2, mem2 = share_pooled(pooled3, mean3, pick, 1)
    comb2, lse2 = attend(pooled3, own2, mem2, (all_q, q_spec), qv_b, has, valid, d2)
    chunk = 768
    per_head = fb // chunk
    steps = heads * per_head
    out_spec, skip_spec = (pl.BlockSpec((heads, d2, hb), lambda j, n=n: (0, 0, 2 * fb // hb + n)) for n in range(2))
    rows_spec = pl.BlockSpec((1, d2, chunk), lambda j: (j // per_head, 0, j % per_head))
    mixed, dcomb2, dskip, g_mlp_b, g_out_b, g_skip_b, g_ub_b, rows_b = call(
        second_mlp_kernel, steps,
        [(comb2.reshape(rows2, d2), None), (pooled3.reshape(rows2, d1), None), (cot, None), (all_b, out_spec), (all_b, skip_spec),
         (all_b, rows_spec),
         (all_b, pl.BlockSpec((1, d2, chunk), lambda j: (j // per_head, 0, per_head + j % per_head))),
         (ub_b, pl.BlockSpec((1, chunk), lambda j: (0, j))),
         (gains_b[None], None), (shifts_b, None)],
        [(shape((share, pooled_tokens, d2), bf16), None), (shape((rows2, d2), bf16), None), (shape((rows2, d1), f32), None),
         (shape((heads, toks, 2, d2 // toks, fb), bf16),
          pl.BlockSpec((1, toks, 2, d2 // toks, chunk), lambda j: (j // per_head, 0, 0, 0, j % per_head))),
         (shape((heads, toks, d2 // toks // 2, 2 * hb), bf16), None), (shape((heads, toks, d2 // toks // 2, 2 * hs), bf16), None),
         (shape((1, heads * fb), f32), pl.BlockSpec((1, chunk), lambda j: (0, j))), (shape((8, d2), f32), None)],
        [((rows2, d2), f32), ((rows2, d2), bf16), ((d2, rows2), bf16), ((d2, rows2), bf16), ((rows2, d2), f32), ((rows2, d2), f32), ((d2, d1), bf16)],
        name="second_mlp", us=26,
    )

    def by_owner(grad):
        return grad.reshape((heads * toks, -1) + grad.shape[2:])

    def scatter(grad):
        return lax.psum_scatter(grad, group, scatter_dimension=0, tiled=False)

    sum_mlp_b = scatter(g_mlp_b.reshape((heads * toks,) + g_mlp_b.shape[2:])).reshape(-1, fb)
    dcomb2 = dcomb2.reshape(share, own_rows, d2)
    dq2, dpool2, g_qkv_b, rows_qv_b = attend_back(pooled3, dcomb2, own2, mem2, (all_q, q_spec), qv_b, has, valid, lse2, heads)
    own_back2, mem_back2 = give_back(dpool2, pick, own_rows, 2)

    merge = lambda grad: grad.reshape((heads * toks,) + grad.shape[2:])
    rest_b = jnp.concatenate([by_owner(g_qkv_b), merge(g_out_b), merge(g_skip_b)], axis=2)
    sum_rest_b = scatter(rest_b)

    res1, dcomb1, g_mlp_a, g_ub_a, rows_a = call(
        first_back_kernel, share,
        [(middle, 0), (after1, 0), (comb1, 0), (dskip.reshape(share, own_rows, d1), 0), (dq2, 0), (own_back2, 0), (mem_back2, 0),
         (all_a, out_a_spec), (all_a, up_spec), (all_a, down_spec), (ub_a, None),
         (gains_a, None), (shifts_a, None), (unpooling, None), (unpairing, None)],
        [(shape((share, tokens, d1), f32), 0), (shape((share, tokens, d1), bf16), 0),
         (shape((heads, d1, -(-(2 * fa + ha) // 256) * 256), bf16), None),
         (shape((heads, 1, fa), f32), None), (shape((8, d1), f32), None)],
        [((heads, d1, fa), f32), ((heads, d1, fa), f32), ((d1, d1), f32), ((d1, d1), bf16)],
        name="first_back", us=26,
    )
    rest_a = by_owner(g_mlp_a)
    dcomb1, sum_mlp_b, rest_a = lax.optimization_barrier((dcomb1, sum_mlp_b, rest_a))
    sum_rest_a = scatter(rest_a)
    sum_mlp_b = reduce_clips(sum_mlp_b)
    dx1, dpool1, g_qkv_a, rows_qv_a = attend_back(low1, dcomb1, own1, mem1, (all_w, None), qv_a, has, valid, lse1, heads)
    dpool1, sum_mlp_b = lax.optimization_barrier((dpool1, sum_mlp_b))
    sum_mlp_b = spread_clips(sum_mlp_b)
    own_back1, mem_back1, mixed_all, sum_qkv_a = give_back(
        dpool1, pick, own_rows, 3, mixed, by_owner(g_qkv_a))
    stream_grad, rows_last = call(
        last_back_kernel, share,
        [(stream, 0), (res1, 0), (dx1, 0), (own_back1, 0), (mem_back1, 0), (gains_a, None),
         (unpooling, None), (unpairing, None)],
        [(shape((share, tokens, d1), bf16), 0), (shape((8, d1), f32), None)],
        name="last_back", us=1,
    )

    rows = [rows_last, rows_qv_a, rows_a, rows_b, rows_qv_b, g_ub_a, g_ub_b]
    count = 10 + (6 * d2 + heads * (fa + fb)) // d1
    stream_all, total, sums = finish(stream_grad, rows, sum_qkv_a, sum_rest_a, sum_rest_b, count, 4)
    row1, row2 = w_up_a.shape[0], w_up_b.shape[0]
    outs = [(3, row1, ha), (row1, ha), (row1, fa), (row1, fa), (3, row1, hb), (row2, hb), (row2, hs), (row2, fb), (row2, fb),
            (3, d1), (d2,), (5, d1), (3, d2), (2, ha), (2, hb), (fa,), (fb,)]
    grads = call(
        write_kernel, 1,
        [(head.astype(jnp.int32)[None], INSMEM), (total, None), (sums, None), (sum_mlp_b, None)],
        [(shape(dims, f32), None) for dims in outs],
        name="write", us=4,
    )
    mixed_all = mixed_all.reshape(micro, pooled_tokens, d2)
    return (
        by_frame(mixed_all, cotangent.shape),
        by_frame(stream_all.astype(f32), clips_in.shape),
        grads[0].transpose(1, 0, 2), *grads[1:4], grads[4].transpose(1, 0, 2), *grads[5:10],
        *grads[10:],
    )


def solution(mesh):
    in_specs = (
        P("clip", None, "tok", None, None),
        P("clip", None),
        P("clip", None),
        P("tok", None, "head"),
        P("tok", "head"),
        P("tok", "head"),
        P("tok", "head"),
        P("tok", None, "head"),
        P("tok", "head"),
        P("tok", "head"),
        P("tok", "head"),
        P("tok", "head"),
        P(),
        P(),
        P(),
        P(),
        P(None, "head"),
        P(None, "head"),
        P("head"),
        P("head"),
        P("clip", None, "tok", None, None),
    )
    out_specs = (
        P("clip", None, "tok", None, None),
        P("clip", None, "tok", None, None),
        P("tok", None, "head"),
        P("tok", "head"),
        P("tok", "head"),
        P("tok", "head"),
        P("tok", None, "head"),
        P("tok", "head"),
        P("tok", "head"),
        P("tok", "head"),
        P("tok", "head"),
        P(),
        P(),
        P(),
        P(),
        P(None, "head"),
        P(None, "head"),
        P("head"),
        P("head"),
    )
    return jax.shard_map(local, mesh=mesh, in_specs=in_specs, out_specs=out_specs, check_vma=False)
```

```python
import functools
import math

import jax
import jax.numpy as jnp
import numpy as np
from jax import lax
from jax.experimental import pallas as pl
from jax.experimental.pallas import tpu as pltpu
from jax.sharding import PartitionSpec as P

GRID = 14
PATCH = GRID * GRID
POOLED = PATCH // 4
HD = 96
NEG = -1e30
VMEM_CAP = 62 * 2**20
PIECES = 9
eps = 1e-06
f32, bf16 = jnp.float32, jnp.bfloat16
NN, NT, TN = ((1,), (0,)), ((1,), (1,)), ((0,), (0,))


def up16(n):
    return -(-n // 16) * 16


def pool_matrix(frames):
    rows, cols = up16(frames * POOLED), frames * PATCH
    out = np.zeros((rows, cols), np.float32)
    half = GRID // 2
    for f in range(frames):
        for p in range(PATCH):
            r, c = divmod(p, GRID)
            out[((r // 2) * half + c // 2) * frames + f, p * frames + f] = 0.25
    return out


def pair_matrix(frames):
    rows, cols = up16(frames // 2 * POOLED), up16(frames * POOLED)
    out = np.zeros((rows, cols), np.float32)
    for j in range(frames // 2):
        for p in range(POOLED):
            out[p * (frames // 2) + j, p * frames + 2 * j] = 0.5
            out[p * (frames // 2) + j, p * frames + 2 * j + 1] = 0.5
    return out


MESH = pl.DeviceIdType.MESH


def places():
    tok, toks = lax.axis_index("tok"), lax.axis_size("tok")
    return lax.axis_index("clip"), lax.axis_index("head"), tok // 2, tok % 2, toks // 2


def greet(copies_to_me, i_copy_to):
    barrier = pltpu.get_barrier_semaphore()
    for device, condition in copies_to_me:
        if condition is None:
            pl.semaphore_signal(barrier, inc=1, device_id=device, device_id_type=MESH)
        else:
            @pl.when(condition)
            def _():
                pl.semaphore_signal(barrier, inc=1, device_id=device, device_id_type=MESH)
    count = 0
    for _, condition in i_copy_to:
        count = count + (1 if condition is None else jnp.where(condition, 1, 0))
    pl.semaphore_wait(barrier, count)


def remote(src, dst, send, recv, device):
    return pltpu.make_async_remote_copy(
        src_ref=src, dst_ref=dst, send_sem=send, recv_sem=recv, device_id=device, device_id_type=MESH
    )


def rem(a, n):
    return lax.rem(a + n, n)


class Chain:
    def __init__(self, part_s, outer_s, inner_s, pieces, in_send, in_recv, mid_send, mid_recv, out_send, out_recv):
        self.clip, clips = lax.axis_index("clip"), lax.axis_size("clip")
        clip = self.clip
        left = clip < clips // 2
        inner, outer = jnp.where(left, clip + 1, clip - 1), jnp.where(left, clip - 1, clip + 1)
        self.inner, self.outer = {"clip": inner}, {"clip": outer}
        self.end = (clip == 0) | (clip == clips - 1)
        self.middle = (clip == clips // 2 - 1) | (clip == clips // 2)
        self.part, self.from_outer, self.from_inner, self.pieces = part_s, outer_s, inner_s, pieces
        self.inward = [remote(part_s.at[p], outer_s.at[p], in_send.at[n], in_recv.at[n], self.inner) for n, p in enumerate(pieces)]
        self.across = [remote(part_s.at[p], inner_s.at[p], mid_send.at[n], mid_recv.at[n], self.inner) for n, p in enumerate(pieces)]
        self.outward = [remote(inner_s.at[p], inner_s.at[p], out_send.at[n], out_recv.at[n], self.outer) for n, p in enumerate(pieces)]

    def greet(self):
        barrier = pltpu.get_barrier_semaphore()
        pl.semaphore_signal(barrier, inc=1, device_id=self.inner, device_id_type=MESH)

        @pl.when(jnp.logical_not(self.end))
        def _():
            pl.semaphore_signal(barrier, inc=1, device_id=self.outer, device_id_type=MESH)

        pl.semaphore_wait(barrier, jnp.where(self.end, 1, 2))

    def greets(self):
        both = [(self.inner, None), (self.outer, jnp.logical_not(self.end))]
        return both

    def send_ends(self, n):
        @pl.when(self.end & jnp.logical_not(self.middle))
        def _():
            self.inward[n].start()

    def send_parts(self, n):
        here = self.pieces[n]

        @pl.when(jnp.logical_not(self.end))
        def _():
            self.inward[n].wait_recv()
            self.part[here] = (self.part[here].astype(f32) + self.from_outer[here].astype(f32)).astype(bf16)

        @pl.when(jnp.logical_not(self.end) & jnp.logical_not(self.middle))
        def _():
            self.inward[n].start()

        @pl.when(self.middle)
        def _():
            self.across[n].start()

    def totals(self, n):
        self.middle_totals(n)
        self.other_totals(n)

    def middle_totals(self, n):
        here = self.pieces[n]

        @pl.when(self.middle)
        def _():
            self.across[n].wait_recv()
            self.across[n].wait_send()
            self.from_inner[here] = (self.part[here].astype(f32) + self.from_inner[here].astype(f32)).astype(bf16)

        @pl.when(self.middle & jnp.logical_not(self.end))
        def _():
            self.outward[n].start()

    def other_totals(self, n):
        @pl.when(jnp.logical_not(self.middle))
        def _():
            self.inward[n].wait_send()
            self.outward[n].wait_recv()

        @pl.when(jnp.logical_not(self.middle) & jnp.logical_not(self.end))
        def _():
            self.outward[n].start()

    def close(self):
        @pl.when(jnp.logical_not(self.end))
        def _():
            for copy in self.outward:
                copy.wait_send()


def chain_scratch(buffer, pieces):
    return [pltpu.VMEM(buffer, bf16)] * 3 + [dma(pieces)] * 6


ANY = pl.BlockSpec(memory_space=pl.ANY)
INVMEM = pl.BlockSpec(memory_space=pltpu.VMEM)
INSMEM = pl.BlockSpec(memory_space=pltpu.SMEM)


def dma(*dims):
    return pltpu.SemaphoreType.DMA(dims)


def dot(a, b, dims=NN):
    return lax.dot_general(a, b, (dims, ((), ())), preferred_element_type=f32)


def exact_dot(matrix, tensor):
    high = tensor.astype(bf16)
    low = (tensor - high.astype(f32)).astype(bf16)
    return dot(matrix, high) + dot(matrix, low)


def norm(x):
    average = jnp.mean(x, axis=-1, keepdims=True)
    centred = x - average
    inverse = lax.rsqrt(jnp.mean(centred * centred, axis=-1, keepdims=True) + eps)
    return centred * inverse, inverse


def norm_back(unit, inverse, gain, gradient):
    scaled = gradient * gain
    return inverse * (
        scaled
        - jnp.mean(scaled, axis=-1, keepdims=True)
        - unit * jnp.mean(scaled * unit, axis=-1, keepdims=True)
    )


GELU_A, GELU_B = math.sqrt(2.0 / math.pi), 0.044715


def gelu(x):
    t = jnp.tanh(GELU_A * (x + GELU_B * (x * x * x)))
    return 0.5 * x * (1.0 + t)


def gelu_both(x):
    square = x * x
    t = jnp.tanh(GELU_A * x * (1.0 + GELU_B * square))
    value = 0.5 * x * (1.0 + t)
    slope = 0.5 * (1.0 + t) + 0.5 * x * (1.0 - t * t) * (GELU_A * (1.0 + 3.0 * GELU_B * square))
    return value, slope


def sum_rows(x):
    return jnp.sum(x, axis=0, keepdims=True)


def add_rows(ref, rows):
    step = pl.program_id(0)

    @pl.when(step == 0)
    def _():
        ref[...] = jnp.zeros_like(ref)

    for i, row in enumerate(rows):
        ref[i:i + 1, :] += row


def transposed(x):
    return x.astype(f32).T.astype(bf16)


def window(head):
    low = HD * head
    return low // 128 * 128, -(-(low + HD) // 128) * 128


def head_mask(head, start, stop):
    lane = lax.broadcasted_iota(jnp.int32, (1, stop - start), 1) + start
    return (lane >= HD * head) & (lane < HD * head + HD)


def key_rows(own_ref, mem_ref):
    row = 0
    for ref in (own_ref, mem_ref):
        for t in range(ref.shape[0]):
            yield ref, t, slice(row, row + ref.shape[2])
            row += ref.shape[2]


def key_mask(own_ref, mem_ref, valid, has):
    parts = []
    for ref, rows, there in ((own_ref, valid[0], None), (mem_ref, valid[1], has)):
        block = ref.shape[2]
        lane = lax.rem(lax.broadcasted_iota(jnp.int32, (1, ref.shape[0] * block), 1), block)
        limit = rows if there is None else jnp.where(there > 0, rows, 0)
        parts.append(jnp.where(lane < limit, 0.0, NEG))
    return jnp.concatenate(parts, axis=1)


def assemble(w_ref, w_s):
    wide = w_ref.shape[2] // 3
    for part in range(3):
        pieces = [w_ref[h, :, wide * part:wide * part + wide].astype(f32) for h in range(w_ref.shape[0])]
        w_s[0, :, 384 * part:384 * part + 384] = jnp.concatenate(pieces, axis=1).astype(bf16)


def assemble_out(w_ref, out_s):
    wide = out_s.shape[1] // w_ref.shape[0]
    pieces = [w_ref[h, :, :wide].astype(f32) for h in range(w_ref.shape[0])]
    out_s[...] = jnp.concatenate(pieces, axis=1).astype(bf16)


def project_keys(own_ref, mem_ref, w_ref, bias_ref, x_s, k_s, v_s):
    for ref, t, rows in key_rows(own_ref, mem_ref):
        x_s[rows, :] = ref[t, 0]
    width = k_s.shape[1]
    for low in range(0, width, 384):
        k_s[:, low:low + 384] = dot(x_s[...], w_ref[low // 384, :, 384:768]).astype(bf16)
    for low in range(0, width, 384):
        value = dot(x_s[...], w_ref[low // 384, :, 768:])
        v_s[:, low:low + 384] = (value + bias_ref[1:2, low:low + 384]).astype(bf16)


def project_queries(x_ref, w_ref, bias_ref, q_s):
    width = q_s.shape[1]
    for low in range(0, width, 384):
        value = dot(x_ref[0], w_ref[low // 384, :, :384])
        q_s[:, low:low + 384] = (value + bias_ref[0:1, low:low + 384]).astype(bf16)


def norm_pool_kernel(x_ref, gains_ref, shifts_ref, pool_ref, pair_ref, low_ref, pooled_ref, mean_ref):
    unit, _ = norm(x_ref[0].astype(f32))
    normed = unit * gains_ref[0:1, :] + shifts_ref[0:1, :]
    low_ref[0] = normed.astype(bf16)
    pooled = exact_dot(pool_ref[...], normed)
    pooled_ref[0] = pooled.astype(bf16)
    mean_ref[0] = exact_dot(pair_ref[...], pooled).astype(bf16)


def write_shares(gw_ref, h, gw_s):
    wide = gw_ref.shape[2] // 3
    for part in range(3):
        low = wide * h
        columns = gw_s[low // 384, :, 384 * part:384 * part + 384][:, low % 384:low % 384 + wide]
        gw_ref[h, :, wide * part:wide * part + wide] = columns.astype(bf16)


def attend_kernel(chunk, valid, x_ref, own_ref, mem_ref, w_ref, qv_ref, has_ref, out_ref, lse_ref, w_s, x_s, q_s, k_s, v_s, s_s, p_s):
    nq, width = q_s.shape
    columns = key_mask(own_ref, mem_ref, valid, has_ref[pl.program_id(0)])
    if width == 384:
        @pl.when(pl.program_id(0) == 0)
        def _():
            assemble(w_ref, w_s)
        w_ref = w_s
    project_queries(x_ref, w_ref, qv_ref, q_s)
    project_keys(own_ref, mem_ref, w_ref, qv_ref, x_s, k_s, v_s)
    factor = HD**-0.5 * math.log2(math.e)
    stack = s_s.shape[0] // nq
    lanes = lax.broadcasted_iota(jnp.int32, (chunk, 128), 1)
    for tile in range(width // 384):
        group = slice(384 * tile, 384 * tile + 384)
        base = q_s[:, group].astype(f32)
        parts = [base[:, :128], base[:, 128:256], base[:, 256:384]]
        for first in range(4 * tile, 4 * tile + 4, stack):
            start, stop = window(first)[0], window(first + stack - 1)[1]
            masks = [head_mask(first + k, start, stop) for k in range(stack)]
            base = q_s[:, start:stop]
            query = jnp.concatenate([jnp.where(mask, base, jnp.zeros((), bf16)) for mask in masks], axis=0)
            s_s[...] = dot(query, k_s[:, start:stop], NT)

            def body(i, carry, k):
                rows = pl.ds(pl.multiple_of(i * chunk, chunk), chunk)
                here = pl.ds(pl.multiple_of(k * nq + i * chunk, chunk), chunk)
                score = s_s[here, :] * factor + columns
                top = jnp.max(score, axis=1, keepdims=True)
                power = jnp.exp2(score - top)
                total = jnp.sum(power, axis=1, keepdims=True)
                p_s[here, :] = (power * (1.0 / total)).astype(bf16)
                lse_ref[0, rows, :] = jnp.where(lanes == first + k, top + jnp.log2(total), lse_ref[0, rows, :])
                return carry

            for k in range(stack):
                lax.fori_loop(0, nq // chunk, functools.partial(body, k=k), 0, unroll=nq // chunk)
            both = dot(p_s[...], v_s[:, start:stop])
            for k, mask in enumerate(masks):
                out = jnp.where(mask, both[k * nq:(k + 1) * nq], 0.0)
                for w in range((stop - start) // 128):
                    n = start // 128 - 3 * tile + w
                    parts[n] = parts[n] + out[:, 128 * w:128 * w + 128]
        out_ref[0, :, group] = jnp.concatenate(parts, axis=1).astype(bf16)


def attend_back_kernel(
    chunk, valid, x_ref, g_ref, own_ref, mem_ref, w_ref, qv_ref, has_ref, lse_ref,
    dx_ref, dpool_ref, gw_ref, row_ref,
    w_s, x_s, q_s, k_s, v_s, s_s, dp_s, p_s, ds_s, dk_s, dv_s, gw_s,
):
    nq, width = q_s.shape
    step = pl.program_id(0)
    columns = key_mask(own_ref, mem_ref, valid, has_ref[step])
    if width == 384:
        @pl.when(step == 0)
        def _():
            assemble(w_ref, w_s)
        w_ref = w_s
    project_queries(x_ref, w_ref, qv_ref, q_s)
    project_keys(own_ref, mem_ref, w_ref, qv_ref, x_s, k_s, v_s)
    scaling = HD**-0.5
    factor = scaling * math.log2(math.e)
    stack = s_s.shape[0] // nq
    lanes = lax.broadcasted_iota(jnp.int32, (chunk, 128), 1)

    @pl.when(step == 0)
    def _():
        gw_s[...] = jnp.zeros_like(gw_s)

    xt = transposed(x_ref[0])
    keys_t = transposed(x_s[...])
    dx = None
    dpool = None
    row_q, row_v = [], []
    for tile in range(width // 384):
        group = slice(384 * tile, 384 * tile + 384)
        qt = transposed(q_s[:, group])
        gt = transposed(g_ref[0, :, group])
        parts = [None] * 3
        for first in range(4 * tile, 4 * tile + 4, stack):
            start, stop = window(first)[0], window(first + stack - 1)[1]
            masks = [head_mask(first + k, start, stop) for k in range(stack)]
            zero = jnp.zeros((), bf16)
            query = jnp.concatenate([jnp.where(mask, q_s[:, start:stop], zero) for mask in masks], axis=0)
            grad = jnp.concatenate([jnp.where(mask, g_ref[0, :, start:stop], zero) for mask in masks], axis=0)
            s_s[...] = dot(query, k_s[:, start:stop], NT)
            dp_s[...] = dot(grad, v_s[:, start:stop], NT)

            def body(i, carry, k):
                rows = pl.ds(pl.multiple_of(i * chunk, chunk), chunk)
                here = pl.ds(pl.multiple_of(k * nq + i * chunk, chunk), chunk)
                lse = jnp.sum(jnp.where(lanes == first + k, lse_ref[0, rows, :], 0.0), axis=1, keepdims=True)
                p = jnp.exp2(s_s[here, :] * factor + columns - lse)
                dp = dp_s[here, :]
                inner = jnp.sum(p * dp, axis=1, keepdims=True)
                p_s[here, :] = p.astype(bf16)
                ds_s[here, :] = (p * (dp - inner)).astype(bf16)
                return carry

            for k in range(stack):
                lax.fori_loop(0, nq // chunk, functools.partial(body, k=k), 0, unroll=nq // chunk)
            dq_both = dot(ds_s[...], k_s[:, start:stop]) * scaling
            for k, mask in enumerate(masks):
                mine = slice(k * nq, (k + 1) * nq)
                r = slice(HD * (first + k - 4 * tile), HD * (first + k - 4 * tile) + HD)
                dv_s[r, :] = dot(gt[r], p_s[mine, :])
                dk_s[r, :] = dot(qt[r], ds_s[mine, :]) * scaling
                dq = jnp.where(mask, dq_both[mine], 0.0)
                for w in range((stop - start) // 128):
                    n = start // 128 - 3 * tile + w
                    part = dq[:, 128 * w:128 * w + 128]
                    parts[n] = part if parts[n] is None else parts[n] + part
        total = jnp.concatenate(parts, axis=1) + g_ref[0, :, group].astype(f32)
        row_q.append(sum_rows(total))
        low = total.astype(bf16)
        gw_s[tile, :, :384] += dot(xt, low)
        add = dot(low, w_ref[tile, :, :384], NT)
        dx = add if dx is None else dx + add
        for part, src in ((1, dk_s), (2, dv_s)):
            grad = src[...].T
            if part == 2:
                row_v.append(sum_rows(grad))
            low = grad.astype(bf16)
            here = slice(384 * part, 384 * part + 384)
            gw_s[tile, :, here] += dot(keys_t, low)
            add = dot(low, w_ref[tile, :, here], NT)
            dpool = add if dpool is None else dpool + add
    dx_ref[0] = dx
    row = 0
    own, mem = own_ref.shape[2], mem_ref.shape[2]
    toks = own_ref.shape[0]
    for t in range(toks):
        dpool_ref[t, 0, :own, :] = dpool[t * own:(t + 1) * own].astype(bf16)
        dpool_ref[t, 0, own:, :] = dpool[toks * own + t * mem:toks * own + (t + 1) * mem].astype(bf16)
    add_rows(row_ref, [jnp.concatenate(row_q, axis=1), jnp.concatenate(row_v, axis=1)])

    @pl.when(step == pl.num_programs(0) - 1)
    def _():
        for h in range(gw_ref.shape[0]):
            write_shares(gw_ref, h, gw_s)


def first_mlp_kernel(x_ref, comb_ref, out_ref, up_ref, down_ref, ub_ref, gains_ref, shifts_ref, pool_ref, pair_ref,
                     after_ref, middle_ref, pooled_ref, mean_ref, out_s):
    @pl.when(pl.program_id(0) == 0)
    def _():
        assemble_out(out_ref, out_s)

    after = x_ref[0].astype(f32) + dot(comb_ref[0], out_s[...], NT) + shifts_ref[1:2, :]
    after_ref[0] = after
    unit, _ = norm(after)
    low = (unit * gains_ref[1:2, :] + shifts_ref[2:3, :]).astype(bf16)
    total = after + shifts_ref[3:4, :]
    for h in range(up_ref.shape[0]):
        hidden = gelu(dot(low, up_ref[h]) + ub_ref[h]).astype(bf16)
        total = total + dot(hidden, down_ref[h], NT)
    middle_ref[0] = total
    unit, _ = norm(total)
    pooled = exact_dot(pool_ref[...], unit * gains_ref[2:3, :] + shifts_ref[4:5, :])
    pooled_ref[0] = pooled.astype(bf16)
    mean_ref[0] = exact_dot(pair_ref[...], pooled).astype(bf16)


def second_mlp_kernel(
    comb_ref, pooled_ref, cot_ref, out_ref, skip_ref, up_ref, down_ref, ub_ref, gains_ref, shifts_ref,
    mixed_ref, dcomb_ref, dskip_ref, gmlp_ref, gout_ref, gskip_ref, gub_ref, row_ref,
    after_s, low_s, lowt_s, cott_s, sum_s, dlow_s, skip_s,
):
    step = pl.program_id(0)

    @pl.when(step == 0)
    def _():
        share = skip_s.shape[1] // skip_ref.shape[0]
        skip_s[...] = jnp.concatenate([skip_ref[h, :, :share].astype(f32) for h in range(skip_ref.shape[0])], axis=1).astype(bf16)
        after = dot(pooled_ref[...], skip_s[...], NT) + shifts_ref[0:1, :]
        wide = out_ref.shape[2]
        for h in range(out_ref.shape[0]):
            after = after + dot(comb_ref[:, wide * h:wide * h + wide], out_ref[h], NT)
        after_s[...] = after
        unit, _ = norm(after)
        low = (unit * gains_ref[...] + shifts_ref[1:2, :]).astype(bf16)
        low_s[...] = low
        lowt_s[...] = transposed(low)
        cott_s[...] = transposed(cot_ref[...])
        sum_s[...] = after + shifts_ref[2:3, :]
        dlow_s[...] = jnp.zeros_like(dlow_s)

    pre = dot(low_s[...], up_ref[0]) + ub_ref[...]
    hidden, slope = gelu_both(pre)
    hidden = hidden.astype(bf16)
    dpre = dot(cot_ref[...], down_ref[0]) * slope
    gub_ref[...] = sum_rows(dpre)
    dpre = dpre.astype(bf16)
    sum_s[...] += dot(hidden, down_ref[0], NT)
    dlow_s[...] += dot(dpre, up_ref[0], NT)
    for n, grad in enumerate((dot(lowt_s[...], dpre), dot(cott_s[...], hidden))):
        rows = gmlp_ref.shape[3]
        for t in range(gmlp_ref.shape[1]):
            gmlp_ref[0, t, n] = grad[t * rows:(t + 1) * rows].astype(bf16)

    @pl.when(step == pl.num_programs(0) - 1)
    def _():
        mixed_ref[...] = sum_s[...].astype(bf16)
        unit, inverse = norm(after_s[...])
        dlow = dlow_s[...]
        cot = cot_ref[...].astype(f32)
        res = norm_back(unit, inverse, gains_ref[...], dlow) + cot
        row_ref[...] = jnp.zeros_like(row_ref)
        for i, row in enumerate((res, dlow, cot, dlow * unit)):
            row_ref[i:i + 1, :] = sum_rows(row)
        res = res.astype(bf16)
        dskip_ref[...] = dot(res, skip_s[...])
        rest = transposed(res)
        wide = out_ref.shape[2]
        for h in range(out_ref.shape[0]):
            here = slice(wide * h, wide * h + wide)
            dcomb_ref[:, here] = dot(res, out_ref[h]).astype(bf16)
            grad = dot(rest, comb_ref[:, here])
            half = gout_ref.shape[2]
            for n in range(2 * gout_ref.shape[1]):
                gout_ref[h, n // 2, :, wide * (n % 2):wide * (n % 2) + wide] = grad[half * n:half * n + half].astype(bf16)
        grad = dot(rest, pooled_ref[...])
        wide = gskip_ref.shape[3] // 2
        for h in range(gskip_ref.shape[0]):
            for t in range(gskip_ref.shape[1]):
                low, high = (grad[half * n:half * n + half, wide * h:wide * h + wide] for n in (2 * t, 2 * t + 1))
                gskip_ref[h, t] = jnp.concatenate([low, high], axis=1).astype(bf16)


def first_back_kernel(
    middle_ref, after_ref, comb_ref, dskip_ref, dq_ref, own_ref, mem_ref, out_ref, up_ref, down_ref, ub_ref, gains_ref, shifts_ref,
    unpool_ref, unpair_ref,
    res_ref, dcomb_ref, gmlp_ref, gub_ref, row_ref,
    gup_s, gdown_s, gout_s, out_s,
):
    step = pl.program_id(0)

    @pl.when(step == 0)
    def _():
        gup_s[...] = jnp.zeros_like(gup_s)
        gdown_s[...] = jnp.zeros_like(gdown_s)
        gout_s[...] = jnp.zeros_like(gout_s)
        gub_ref[...] = jnp.zeros_like(gub_ref)
        assemble_out(out_ref, out_s)

    dpool = dskip_ref[0] + dq_ref[0] + own_ref[0] + exact_dot(unpair_ref[...], mem_ref[0])
    dnorm = exact_dot(unpool_ref[...], dpool)
    unit, inverse = norm(middle_ref[0])
    grad = norm_back(unit, inverse, gains_ref[2:3, :], dnorm)
    rows = [sum_rows(dnorm * unit), sum_rows(dnorm), sum_rows(grad)]
    low = grad.astype(bf16)
    lowt = transposed(low)
    unit, inverse = norm(after_ref[0])
    normed = (unit * gains_ref[1:2, :] + shifts_ref[2:3, :]).astype(bf16)
    normedt = transposed(normed)
    dnormed = None
    for h in range(up_ref.shape[0]):
        hidden, slope = gelu_both(dot(normed, up_ref[h]) + ub_ref[h])
        hidden = hidden.astype(bf16)
        dpre = dot(low, down_ref[h]) * slope
        gub_ref[h] += sum_rows(dpre)
        dpre = dpre.astype(bf16)
        gdown_s[h] += dot(lowt, hidden)
        gup_s[h] += dot(normedt, dpre)
        add = dot(dpre, up_ref[h], NT)
        dnormed = add if dnormed is None else dnormed + add
    res = norm_back(unit, inverse, gains_ref[1:2, :], dnormed) + grad
    rows += [sum_rows(dnormed * unit), sum_rows(dnormed), sum_rows(res)]
    res_ref[0] = res
    res = res.astype(bf16)
    dcomb_ref[0] = dot(res, out_s[...]).astype(bf16)
    gout_s[...] += dot(transposed(res), comb_ref[0])
    add_rows(row_ref, rows)

    @pl.when(step == pl.num_programs(0) - 1)
    def _():
        fa, ha = gup_s.shape[2], gout_s.shape[1] // gmlp_ref.shape[0]
        for h in range(gmlp_ref.shape[0]):
            gmlp_ref[h, :, :fa] = gup_s[h].astype(bf16)
            gmlp_ref[h, :, fa:2 * fa] = gdown_s[h].astype(bf16)
            rest = gmlp_ref.shape[2] - 2 * fa - ha
            gout = jnp.concatenate([gout_s[:, ha * h:ha * h + ha], jnp.zeros((gout_s.shape[0], rest), f32)], axis=1)
            gmlp_ref[h, :, 2 * fa:] = gout.astype(bf16)


def last_back_kernel(x_ref, res_ref, dx_ref, own_ref, mem_ref, gains_ref, unpool_ref, unpair_ref, grad_ref, row_ref):
    dpool = own_ref[0] + exact_dot(unpair_ref[...], mem_ref[0])
    dnorm = dx_ref[0] + exact_dot(unpool_ref[...], dpool)
    unit, inverse = norm(x_ref[0].astype(f32))
    grad = norm_back(unit, inverse, gains_ref[0:1, :], dnorm) + res_ref[0]
    grad_ref[0] = grad.astype(bf16)
    add_rows(row_ref, [sum_rows(dnorm * unit), sum_rows(dnorm)])


def whole(array):
    return pl.BlockSpec(array.shape, lambda i: (0,) * array.ndim)


def by_micro(array, axis=0):
    block = array.shape[:axis] + (1,) + array.shape[axis + 1:]
    return pl.BlockSpec(block, lambda i: (0,) * axis + (i,) + (0,) * (array.ndim - axis - 1))


def shape(dims, dtype):
    return jax.ShapeDtypeStruct(dims, dtype)


def about(us):
    return pl.CostEstimate(flops=int(us * 1e9), bytes_accessed=0, transcendentals=0)


def call(kernel, steps, args, outs, scratch=(), name=None, us=10, number=None):
    def spec(array, how):
        if how is None:
            return whole(array)
        return by_micro(array, how) if isinstance(how, int) else how

    return pl.pallas_call(
        kernel,
        grid=(steps,),
        in_specs=[spec(a, how) for a, how in args],
        out_specs=[spec(a, how) for a, how in outs],
        out_shape=[a for a, _ in outs],
        scratch_shapes=[pltpu.VMEM(*one) if isinstance(one, tuple) else one for one in scratch],
        compiler_params=pltpu.CompilerParams(vmem_limit_bytes=VMEM_CAP, collective_id=number, has_side_effects=number is not None),
        cost_estimate=about(us),
        name=name,
    )(*[a for a, _ in args])


def stacked(nq):
    return 2 if nq < 512 else 1


def chunk_of(nq):
    return 112 if nq % 112 == 0 else 16


def attend(x, own, mem, w, qv, has, valid, width):
    batches, nq, d = x.shape
    keys = own.shape[0] * own.shape[2] + mem.shape[0] * mem.shape[2]
    return call(
        functools.partial(attend_kernel, chunk_of(nq), valid), batches,
        [(x, 0), (own, 1), (mem, 1), w, (qv, None), (has, pl.BlockSpec(memory_space=pltpu.SMEM))],
        [(shape((batches, nq, width), bf16), 0), (shape((batches, nq, 128), f32), 0)],
        [((1, d, 1152 if width == 384 else 128), bf16),
         ((keys, d), bf16), ((nq, width), bf16), ((keys, width), bf16), ((keys, width), bf16),
         ((stacked(nq) * nq, keys), f32), ((stacked(nq) * nq, keys), bf16)],
        name="attend", us=20,
    )


def attend_back(x, grad, own, mem, w, qv, has, valid, lse, heads):
    batches, nq, d = x.shape
    width = grad.shape[2]
    keys = own.shape[0] * own.shape[2] + mem.shape[0] * mem.shape[2]
    both = (own.shape[0], batches, own.shape[2] + mem.shape[2], d)
    groups = (width // 384, d, 1152)
    rows = stacked(nq) * nq
    return call(
        functools.partial(attend_back_kernel, chunk_of(nq), valid), batches,
        [(x, 0), (grad, 0), (own, 1), (mem, 1), w, (qv, None), (has, INSMEM), (lse, 0)],
        [(shape((batches, nq, d), f32), 0), (shape(both, bf16), 1), (shape((heads, d, 3 * width // heads), bf16), None), (shape((8, width), f32), None)],
        [((1, d, 1152 if width == 384 else 128), bf16),
         ((keys, d), bf16), ((nq, width), bf16), ((keys, width), bf16), ((keys, width), bf16),
         ((rows, keys), f32), ((rows, keys), f32), ((rows, keys), bf16), ((rows, keys), bf16),
         ((384, keys), f32), ((384, keys), f32), (groups, f32)],
        name="attend_back", us=36,
    )


def share_kernel(gather, count, *refs):
    if gather:
        pooled_ref, mean_ref, pick_ref, w_ref, *refs = refs
        biases, (own_ref, mem_ref, all_ref, *refs) = refs[:count], refs[count:]
        if count:
            (qv_a_ref, qv_b_ref, ub_a_ref, ub_b_ref), refs = refs[:4], refs[4:]
    else:
        pooled_ref, mean_ref, pick_ref, own_ref, mem_ref, *refs = refs
    (got_s, pick_s, local_sem, own_send, own_recv, mem_send, mem_recv, pass_send, pass_recv, clip_send, clip_recv, *refs) = refs
    clip, head, chip, core, chips = places()
    clips, heads = lax.axis_size("clip"), lax.axis_size("head")
    share = pooled_ref.shape[0]
    here = 2 * chip + core
    partner = {"tok": 2 * chip + 1 - core}
    across = [{"tok": 2 * rem(chip + k, chips) + core} for k in range(1, chips)]
    beside = [{"head": rem(head + d, heads)} for d in range(1, heads)]
    heads_of = lambda by, sign: [{"clip": clip + by, "head": rem(head + sign * d, heads)} for d in range(heads)]
    last, begun = clip < clips - 1, clip > 0
    near = [(d, None) for d in [partner] + across + (beside if gather else [])]
    greet(near + [(d, begun) for d in heads_of(-1, -1)], near + [(d, last) for d in heads_of(1, 1)])

    def spread(src, out, send, recv):
        copies = [remote(src, out.at[here], send.at[0], recv.at[0], partner)]
        copies += [remote(src, out.at[here], send.at[k + 1], recv.at[k + 1], across[k]) for k in range(chips - 1)]
        return copies

    def passed(out, k, row):
        block = 2 * rem(chip - k, chips) + core
        return remote(out.at[block], out.at[block], pass_send.at[row, k - 1], pass_recv.at[row, k - 1], partner)

    clip_copies = [remote(mean_ref, got_s.at[d], clip_send.at[d], clip_recv.at[d], device) for d, device in enumerate(heads_of(1, 1))]

    @pl.when(last)
    def _():
        for copy in clip_copies:
            copy.start()

    w_first, w_diagonal, w_core = {}, {}, {}
    if gather:
        w_local, w_send, w_recv, d_send, d_recv, c_send, c_recv, b_send, b_recv, *bias_got = refs
        bias_copies = [
            remote(ref, got.at[d], b_send.at[d, n], b_recv.at[d, n], device)
            for d, device in enumerate(beside)
            for n, (ref, got) in enumerate(zip(biases, bias_got))
        ]
        for copy in bias_copies:
            copy.start()
        mine = all_ref.at[head, here]
        for k in range(1, chips):
            w_first[k, 0] = remote(w_ref, mine, w_send.at[k - 1], w_recv.at[k - 1], across[k - 1])
        for d in range(1, heads):
            w_first[0, d] = remote(w_ref, mine, w_send.at[chips - 2 + d], w_recv.at[chips - 2 + d], beside[d - 1])
        w_core[0, 0] = remote(w_ref, mine, c_send.at[0, 0], c_recv.at[0, 0], partner)
        for copy in [*w_first.values(), w_core[0, 0]]:
            copy.start()
        w_copy = pltpu.make_async_copy(w_ref, mine, w_local.at[0])
        w_copy.start()

        def forward(k, d):
            block = all_ref.at[rem(head - d, heads), 2 * rem(chip - k, chips) + core]
            w_core[k, d] = remote(block, block, c_send.at[k, d], c_recv.at[k, d], partner)
            w_core[k, d].start()

    own_copies = spread(pooled_ref, own_ref, own_send, own_recv)
    for copy in own_copies[1:] + own_copies[:1]:
        copy.start()
    own_local = pltpu.make_async_copy(pooled_ref, own_ref.at[here], local_sem.at[0])
    own_local.start()
    if gather:
        for k in range(1, chips):
            w_first[k, 0].wait_recv()
            block = all_ref.at[head, 2 * rem(chip - k, chips) + core]
            for d in range(1, heads):
                w_diagonal[k, d] = remote(block, block, d_send.at[k - 1, d - 1], d_recv.at[k - 1, d - 1], beside[d - 1])
                w_diagonal[k, d].start()
            forward(k, 0)

    @pl.when(begun)
    def _():
        for copy in clip_copies:
            copy.wait_recv()
        for m in range(share):
            total = None
            for d in range(heads):
                for s in range(share):
                    piece = got_s[d, s].astype(f32) * pick_ref[m, d * share + s]
                    total = piece if total is None else total + piece
            pick_s[m] = total.astype(bf16)

    @pl.when(jnp.logical_not(begun))
    def _():
        pick_s[...] = jnp.zeros_like(pick_s)

    mem_copies = spread(pick_s, mem_ref, mem_send, mem_recv)
    for copy in mem_copies[1:] + mem_copies[:1]:
        copy.start()
    mem_local = pltpu.make_async_copy(pick_s, mem_ref.at[here], local_sem.at[1])
    mem_local.start()
    forwards = []
    for k in range(1, chips):
        own_copies[k].wait_recv()
        forwards.append(passed(own_ref, k, 0))
        forwards[-1].start()
    if gather:
        for d in range(1, heads):
            w_first[0, d].wait_recv()
            forward(0, d)
    for k in range(1, chips):
        mem_copies[k].wait_recv()
        forwards.append(passed(mem_ref, k, 1))
        forwards[-1].start()
    if gather:
        for k, d in w_diagonal:
            w_diagonal[k, d].wait_recv()
            forward(k, d)
        for copy in w_core.values():
            copy.wait_recv()
        for copy in bias_copies:
            copy.wait_recv()
    if count:
        by_head = []
        for ref, got in zip(biases, bias_got):
            pieces = []
            for h in range(heads):
                piece = ref[...]
                for d in range(1, heads):
                    piece = jnp.where(rem(head - d, heads) == h, got[d - 1], piece)
                pieces.append(piece)
            by_head.append(pieces)
        qv_a_ref[...] = jnp.concatenate(by_head[0], axis=1)
        qv_b_ref[...] = jnp.concatenate(by_head[1], axis=1)
        fa = ub_a_ref.shape[2]
        for h in range(heads):
            ub_a_ref[h] = by_head[2][h][:, :fa]
        ub_b_ref[...] = jnp.concatenate([piece[:, fa:] for piece in by_head[2]], axis=1)
        for copy in bias_copies:
            copy.wait_send()
    own_copies[0].wait_recv()
    mem_copies[0].wait_recv()
    for copy in forwards:
        copy.wait_recv()
    for copy in own_copies + mem_copies + forwards + [*w_first.values(), *w_diagonal.values(), *w_core.values()]:
        copy.wait_send()
    own_local.wait()
    mem_local.wait()
    if gather:
        w_copy.wait()

    @pl.when(last)
    def _():
        for copy in clip_copies:
            copy.wait_send()


def share_pooled(pooled, mean, pick, number, block=None, biases=(), fa=0):
    toks, heads = lax.axis_size("tok"), lax.axis_size("head")
    chips = toks // 2
    few = max(chips - 1, 1)
    args, specs = [pooled, mean, pick], [INVMEM, INVMEM, INSMEM]
    outs = [shape((toks,) + pooled.shape, bf16), shape((toks,) + mean.shape, bf16)]
    scratch = [
        pltpu.VMEM((heads,) + mean.shape, bf16), pltpu.VMEM(mean.shape, bf16), dma(2),
        dma(chips), dma(chips), dma(chips), dma(chips), dma(2, few), dma(2, few), dma(heads), dma(heads),
    ]
    if block is not None:
        args, specs = args + [block, *biases], specs + [INVMEM] * (1 + len(biases))
        outs = outs + [shape((heads, toks) + block.shape, bf16)]
        if biases:
            (_, wa), (_, wb), (_, wide) = (b.shape for b in biases)
            outs += [shape(dims, f32) for dims in ((2, heads * wa), (2, heads * wb), (heads, 1, fa), (1, heads * (wide - fa)))]
        firsts = max(chips + heads - 2, 1)
        scratch += [dma(1), dma(firsts), dma(firsts), dma(few, max(heads - 1, 1)), dma(few, max(heads - 1, 1)), dma(chips, heads), dma(chips, heads)]
        scratch += [dma(max(heads - 1, 1), max(len(biases), 1)), dma(max(heads - 1, 1), max(len(biases), 1))]
        scratch += [pltpu.VMEM((max(heads - 1, 1),) + b.shape, f32) for b in biases]
    return pl.pallas_call(
        functools.partial(share_kernel, block is not None, len(biases)),
        in_specs=specs,
        out_specs=[ANY] * min(len(outs), 3) + [INVMEM] * (len(outs) - 3),
        out_shape=outs,
        scratch_shapes=scratch,
        compiler_params=pltpu.CompilerParams(collective_id=number, has_side_effects=True, vmem_limit_bytes=VMEM_CAP),
        cost_estimate=about(20 if block is None else 30),
        name="share_pooled",
    )(*args)


def give_back_kernel(exchange, *refs):
    if exchange:
        part_ref, pick_ref, half_ref, grad_ref, own_ref, back_ref, all_ref, sum_ref, *refs = refs
        refs, hosted = refs[:-14], refs[-14:]
        (half_local, half_send, half_recv, block_s, block_core, head_s, block_head, block_chip,
         bc_send, bc_recv, bh_send, bh_recv, bx_send, bx_recv) = hosted
    else:
        part_ref, pick_ref, own_ref, back_ref, *refs = refs
    (mine_s, core_s, sum_s, chip_s, route_s, got_s,
     local_sem, core_send, core_recv, mem_send, mem_recv, own_send, own_recv, clip_send, clip_recv) = refs
    clip, head, chip, core, chips = places()
    clips, heads = lax.axis_size("clip"), lax.axis_size("head")
    share, rows = own_ref.shape[0], own_ref.shape[1]
    partner = {"tok": 2 * chip + 1 - core}
    across = [{"tok": 2 * rem(chip + k, chips) + core} for k in range(1, chips)]
    beside = [{"head": rem(head + d, heads)} for d in range(1, heads)]
    heads_of = lambda by, sign: [{"clip": clip + by, "head": rem(head + sign * d, heads)} for d in range(heads)]
    last, begun = clip < clips - 1, clip > 0
    near = [(d, None) for d in [partner] + across + (beside if exchange else [])]
    greet(near + [(d, last) for d in heads_of(1, 1)], near + [(d, begun) for d in heads_of(-1, -1)])

    order = [rem(chip + k, chips) for k in list(range(1, chips)) + [0]]
    core_copies, local_copies = [], []
    for n, other in enumerate(order):
        core_copies.append(remote(part_ref.at[2 * other + 1 - core], core_s.at[n], core_send.at[n], core_recv.at[n], partner))
        core_copies[-1].start()
    for n, other in enumerate(order):
        local_copies.append(pltpu.make_async_copy(part_ref.at[2 * other + core], mine_s.at[n], local_sem.at[n]))
        local_copies[-1].start()
    halves, block_copies = [], []
    if exchange:
        for n in range(heads * chips):
            block_copies.append(remote(grad_ref.at[2 * n + 1 - core], block_core.at[n], bc_send.at[n], bc_recv.at[n], partner))
            block_copies[-1].start()
        for n, copy in enumerate(block_copies):
            copy.wait_recv()
            block_s[n] = (grad_ref[2 * n + core].astype(f32) + block_core[n].astype(f32)).astype(bf16)
        head_copies = [
            remote(block_s.at[rem(head + k + 1, heads) * chips + x], block_head.at[k, x], bh_send.at[k, x], bh_recv.at[k, x], d)
            for k, d in enumerate(beside) for x in range(chips)
        ]
        for copy in head_copies:
            copy.start()
        halves = [remote(half_ref, all_ref.at[head], half_send.at[k], half_recv.at[k], d) for k, d in enumerate(beside)]
        for copy in halves:
            copy.start()
        half_copy = pltpu.make_async_copy(half_ref, all_ref.at[head], half_local.at[0])
        half_copy.start()
    mem_copies, own_copies = [], []
    for n in range(chips):
        local_copies[n].wait()
        core_copies[n].wait_recv()
        if n == chips - 1:
            break
        sum_s[n] = (mine_s[n].astype(f32) + core_s[n].astype(f32)).astype(bf16)
        low, high = pl.ds(0, rows), pl.ds(rows, sum_s.shape[2] - rows)
        mem_copies.append(remote(sum_s.at[n, :, high, :], chip_s.at[n, :, high, :], mem_send.at[n], mem_recv.at[n], across[n]))
        mem_copies[-1].start()
        own_copies.append(remote(sum_s.at[n, :, low, :], chip_s.at[n, :, low, :], own_send.at[n], own_recv.at[n], across[n]))
        own_copies[-1].start()
    base = chips - 1
    for copy in mem_copies:
        copy.wait_recv()
    memory = []
    for m in range(share):
        total = mine_s[base, m, rows:].astype(f32) + core_s[base, m, rows:].astype(f32)
        for n in range(chips - 1):
            total = total + chip_s[n, m, rows:].astype(f32)
        memory.append(total)
    clip_copies = [
        remote(route_s.at[d], got_s.at[d], clip_send.at[d], clip_recv.at[d], device) for d, device in enumerate(heads_of(-1, -1))
    ]

    @pl.when(begun)
    def _():
        for d in range(heads):
            for s in range(share):
                total = None
                for m in range(share):
                    piece = memory[m] * pick_ref[m, d * share + s]
                    total = piece if total is None else total + piece
                route_s[d, s] = total.astype(bf16)
            clip_copies[d].start()

    if exchange:
        for copy in head_copies:
            copy.wait_recv()
        for x in range(chips):
            total = block_s[head * chips + x].astype(f32)
            for k in range(heads - 1):
                total = total + block_head[k, x].astype(f32)
            head_s[x] = total.astype(bf16)
        chip_copies = [
            remote(head_s.at[rem(chip + k + 1, chips)], block_chip.at[k], bx_send.at[k], bx_recv.at[k], d) for k, d in enumerate(across)
        ]
        for copy in chip_copies:
            copy.start()
    for copy in own_copies:
        copy.wait_recv()
    for m in range(share):
        total = mine_s[base, m, :rows].astype(f32) + core_s[base, m, :rows].astype(f32)
        for n in range(chips - 1):
            total = total + chip_s[n, m, :rows].astype(f32)
        own_ref[m] = total

    @pl.when(last)
    def _():
        for copy in clip_copies:
            copy.wait_recv()
        total = got_s[0].astype(f32)
        for d in range(1, heads):
            total = total + got_s[d].astype(f32)
        back_ref[...] = total

    @pl.when(jnp.logical_not(last))
    def _():
        back_ref[...] = jnp.zeros_like(back_ref)

    for copy in halves:
        copy.wait_recv()
    if exchange:
        for copy in chip_copies:
            copy.wait_recv()
        total = head_s[chip].astype(f32)
        for k in range(chips - 1):
            total = total + block_chip[k].astype(f32)
        sum_ref[...] = jnp.zeros_like(sum_ref)
        sum_ref[:, :grad_ref.shape[2]] = total.astype(bf16)
        for copy in block_copies + head_copies + chip_copies:
            copy.wait_send()
    for copy in core_copies + mem_copies + own_copies + halves:
        copy.wait_send()
    if exchange:
        half_copy.wait()

    @pl.when(begun)
    def _():
        for copy in clip_copies:
            copy.wait_send()


def give_back(part, pick, own_rows, number, half=None, grad=None):
    toks, heads = lax.axis_size("tok"), lax.axis_size("head")
    chips, few = toks // 2, max(toks // 2 - 1, 1)
    share, rows, d = part.shape[1:]
    args, specs = [part, pick], [ANY, INSMEM]
    outs, out_specs = [shape((share, own_rows, d), f32), shape((share, rows - own_rows, d), f32)], [INVMEM, INVMEM]
    scratch = [
        pltpu.VMEM((chips,) + part.shape[1:], bf16), pltpu.VMEM((chips,) + part.shape[1:], bf16),
        pltpu.VMEM((few,) + part.shape[1:], bf16), pltpu.VMEM((few,) + part.shape[1:], bf16),
        pltpu.VMEM((heads, share, rows - own_rows, d), bf16), pltpu.VMEM((heads, share, rows - own_rows, d), bf16),
        dma(chips), dma(chips), dma(chips), dma(few), dma(few), dma(few), dma(few), dma(heads), dma(heads),
    ]
    if half is not None:
        block = grad.shape[1:]
        beside = max(heads - 1, 1)
        args, specs = args + [half, grad], specs + [INVMEM, INVMEM]
        outs += [shape((heads,) + half.shape, half.dtype), shape((block[0], -(-block[1] // 128) * 128), bf16)]
        out_specs += [ANY, INVMEM]
        low = lambda *dims: pltpu.VMEM(dims + block, bf16)
        scratch += [dma(1), dma(beside), dma(beside), low(heads * chips), low(heads * chips), low(chips), low(beside, chips), low(few)]
        scratch += [dma(heads * chips), dma(heads * chips), dma(beside, chips), dma(beside, chips), dma(few), dma(few)]
    return pl.pallas_call(
        functools.partial(give_back_kernel, half is not None),
        in_specs=specs,
        out_specs=out_specs,
        out_shape=outs,
        scratch_shapes=scratch,
        compiler_params=pltpu.CompilerParams(collective_id=number, has_side_effects=True, vmem_limit_bytes=VMEM_CAP),
        cost_estimate=about(1),
        name="give_back",
    )(*args)


def finish_kernel(half_ref, last_ref, qv_a_rows, a_ref, b_ref, qv_b_rows, ub_a_rows, ub_b_rows, grad_ref, rest_ref, group_ref,
                  all_ref, total_ref, sums_ref, *scratch):
    (small_ref, small_s, small_core, small_chip, small_head, small_clip,
     local_sem, half_send, half_recv, core_send, core_recv, chip_send, chip_recv, head_send, head_recv,
     clip_send, clip_recv, *chain) = scratch
    first_lanes, next_lanes = group_ref.shape[1], rest_ref.shape[1]
    tiles, count = chain[0].shape[1] // 128, chain[-1].shape[0]
    bounds = [tiles * n // count * 128 for n in range(count + 1)]
    chain = Chain(*chain[:3], [(slice(None), pl.ds(low, high - low)) for low, high in zip(bounds, bounds[1:])], *chain[3:])
    clip, head, chip, core, chips = places()
    clips, heads = lax.axis_size("clip"), lax.axis_size("head")
    share = half_ref.shape[0]
    partner = {"tok": 2 * chip + 1 - core}
    across = [{"tok": 2 * rem(chip + k, chips) + core} for k in range(1, chips)]
    beside = [{"head": rem(head + k, heads)} for k in range(1, heads)]
    along = [{"clip": rem(clip + k, clips)} for k in range(1, clips)]
    peers = [(d, None) for d in [partner] + across + beside + along]
    greet(peers, peers)
    chain.part[:, :first_lanes] = group_ref[...]
    chain.part[:, first_lanes:first_lanes + next_lanes] = rest_ref[...]
    chain.part[:, first_lanes + next_lanes:] = grad_ref[...]
    for n in range(count):
        chain.send_ends(n)
    pending = []
    d1 = small_ref.shape[1]
    small_ref[...] = jnp.zeros_like(small_ref)
    small_ref[0:2, :] = last_ref[0:2, :]
    small_ref[2:4, :] = qv_a_rows[0:2, :]
    for row, source in enumerate((3, 0, 5, 4, 2, 1)):
        small_ref[4 + row:5 + row, :] = a_ref[source:source + 1, :]
    row = 10
    longer = [b_ref[n:n + 1, :] for n in (3, 0, 1, 2)] + [qv_b_rows[n:n + 1, :] for n in range(2)]
    for values in longer + [ub_a_rows[h] for h in range(heads)] + [ub_b_rows[...]]:
        for low in range(0, values.shape[1], d1):
            small_ref[row:row + 1, :] = values[:, low:low + d1]
            row += 1
    def go(copies):
        for copy in copies:
            copy.start()
        pending.extend(copies)
        return copies

    def arrived(copies):
        for copy in copies:
            copy.wait_recv()

    def in_order(index, size, own, slot):
        total = None
        for i in range(size):
            piece = jnp.where(index == i, own, jnp.zeros_like(own))
            for k in range(size - 1):
                piece = jnp.where(rem(index - k - 1, size) == i, slot(k), piece)
            total = piece if total is None else total + piece
        return total

    first = go([remote(small_ref, small_core, core_send.at[0], core_recv.at[0], partner)])
    cuts, tokens = [], half_ref.shape[1]
    for s in range(share):
        early = tokens // 4 // 16 * 16 if s == 0 else 0
        cuts += [(s, low, high) for low, high in ((0, early), (early, tokens)) if high > low]
    halves = [
        [remote(half_ref.at[s, pl.ds(low, high - low)], all_ref.at[head, s, pl.ds(low, high - low)], half_send.at[k, n], half_recv.at[k, n], d)
         for k, d in enumerate(beside)]
        for n, (s, low, high) in enumerate(cuts)
    ]
    go(halves[0])
    local_half = pltpu.make_async_copy(half_ref, all_ref.at[head], local_sem.at[0])
    local_half.start()
    arrived(first)
    small_s[0] = small_ref[...] + small_core[...]
    copies = go([remote(small_s.at[0], small_head.at[k], head_send.at[k, 0], head_recv.at[k, 0], d) for k, d in enumerate(beside)])
    for s in range(1, len(halves)):
        go(halves[s])
    chain.send_parts(0)
    arrived(copies)
    small_s[1] = in_order(head, heads, small_s[0], lambda k: small_head[k])
    copies = go([remote(small_s.at[1], small_chip.at[k], chip_send.at[k, 0], chip_recv.at[k, 0], d) for k, d in enumerate(across)])
    chain.send_parts(1)
    arrived(copies)
    small_s[2] = in_order(chip, chips, small_s[1], lambda k: small_chip[k])
    copies = []
    for k, d in enumerate(along):
        copies += go([remote(small_s.at[2], small_clip.at[k], clip_send.at[k, 0], clip_recv.at[k, 0], d)])
    for n in range(2, count):
        chain.send_parts(n)
        chain.middle_totals(n - 2)
    for n in range(count - 2, count):
        chain.middle_totals(n)
    for n in range(count):
        chain.other_totals(n)
    arrived(copies)
    total_ref[...] = in_order(clip, clips, small_s[2], lambda k: small_clip[k])
    sums_ref[...] = chain.from_inner[...]
    chain.close()
    for copies in halves:
        arrived(copies)
    for copy in pending:
        copy.wait_send()
    local_half.wait()


def finish(half, rows, grad, rest, first, count, number):
    toks, heads, clips = lax.axis_size("tok"), lax.axis_size("head"), lax.axis_size("clip")
    chips = toks // 2
    across, beside, along = (max(n, 1) for n in (chips - 1, heads - 1, clips - 1))
    depth, d1 = rest.shape[0], rows[0].shape[1]
    small = (-(-count // 8) * 8, d1)
    full = lambda *dims: pltpu.VMEM(dims + small, f32)
    buffer = (depth, first.shape[1] + rest.shape[1] + grad.shape[1])
    return pl.pallas_call(
        finish_kernel,
        in_specs=[INVMEM] * (len(rows) + 4),
        out_specs=[ANY, INVMEM, INVMEM],
        out_shape=[shape((heads,) + half.shape, half.dtype), shape(small, f32), shape(buffer, bf16)],
        scratch_shapes=[
            full(), full(3), full(), full(across), full(beside), full(along),
            dma(1), dma(beside, half.shape[0] + 1), dma(beside, half.shape[0] + 1), dma(1), dma(1),
            dma(across, 1), dma(across, 1), dma(beside, 1), dma(beside, 1), dma(along, 1), dma(along, 1),
            *chain_scratch(buffer, PIECES),
        ],
        compiler_params=pltpu.CompilerParams(collective_id=number, has_side_effects=True, vmem_limit_bytes=VMEM_CAP),
        cost_estimate=about(40),
        name="finish",
    )(half, *rows, grad, rest, first)


def write_kernel(head_ref, total_ref, sums_ref, mlp_ref, qkv_a_ref, out_a_ref, up_a_ref, down_a_ref, qkv_b_ref, out_b_ref, skip_b_ref,
                 up_b_ref, down_b_ref, gains_a_ref, gains_b_ref, shifts_a_ref, shifts_b_ref, qv_a_ref, qv_b_ref, ub_a_ref, ub_b_ref):
    head, total = head_ref[0], total_ref[...]
    at = [10]

    def rows(width):
        first = at[0]
        at[0] += width // total.shape[1]
        return jnp.concatenate([total[r:r + 1] for r in range(first, at[0])], axis=1)

    def share_of(row, width):
        piece = row[:, :width]
        for h in range(1, row.shape[1] // width):
            piece = jnp.where(head == h, row[:, width * h:width * h + width], piece)
        return piece

    gains_a_ref[0:1, :] = total[0:1]
    gains_a_ref[1:3, :] = total[4:6]
    shifts_a_ref[0:1, :] = total[1:2]
    shifts_a_ref[1:5, :] = total[6:10]
    d2, fa, fb = gains_b_ref.shape[0], ub_a_ref.shape[0], ub_b_ref.shape[0]
    heads = total.shape[1] // qv_a_ref.shape[1]
    for i in range(2):
        qv_a_ref[i:i + 1, :] = share_of(total[2 + i:3 + i], qv_a_ref.shape[1])
    gains_b_ref[...] = rows(d2).reshape(d2)
    for i in range(3):
        shifts_b_ref[i:i + 1, :] = rows(d2)
    for i in range(2):
        qv_b_ref[i:i + 1, :] = share_of(rows(d2), qv_b_ref.shape[1])
    ub_a_ref[...] = share_of(rows(heads * fa), fa).reshape(fa)
    ub_b_ref[...] = share_of(rows(heads * fb), fb).reshape(fb)
    low = 0
    depth = sums_ref.shape[0]

    def take(ref):
        nonlocal low
        ref[...] = sums_ref[:, low:low + ref.shape[1]].astype(f32)
        low += ref.shape[1]

    for part in range(3):
        take(qkv_b_ref.at[part])
    for ref in (out_b_ref, skip_b_ref):
        for n in range(2):
            take(ref.at[depth * n:depth * n + depth])
    for ref in (up_a_ref, down_a_ref, out_a_ref):
        take(ref)
    low = -(-low // 256) * 256
    for part in range(3):
        take(qkv_a_ref.at[part])
    up_b_ref[...] = mlp_ref[:up_b_ref.shape[0], :].astype(f32)
    down_b_ref[...] = mlp_ref[up_b_ref.shape[0]:, :].astype(f32)


def reduce_clips(shard):
    clips, clip = lax.axis_size("clip"), lax.axis_index("clip")
    pieces = shard.reshape(clips, -1, shard.shape[-1])
    total = lax.dynamic_index_in_dim(pieces, clip, 0, keepdims=False).astype(f32)
    for k in range(1, clips):
        give = lax.dynamic_index_in_dim(pieces, (clip + k) % clips, 0, keepdims=False)
        total = total + lax.ppermute(give, "clip", [(i, (i + k) % clips) for i in range(clips)]).astype(f32)
    return total.astype(bf16)


def spread_clips(piece):
    clips, clip = lax.axis_size("clip"), lax.axis_index("clip")
    out = jnp.zeros((clips,) + piece.shape, piece.dtype)
    out = lax.dynamic_update_index_in_dim(out, piece, clip, 0)
    for k in range(1, clips):
        got = lax.ppermute(piece, "clip", [(i, (i + k) % clips) for i in range(clips)])
        out = lax.dynamic_update_index_in_dim(out, got, (clip - k + clips) % clips, 0)
    return out.reshape((-1,) + piece.shape[1:])


def local(
    clips_in, resets, assign, w_qkv_a, w_out_a, w_up_a, w_down_a, w_qkv_b, w_out_b, w_skip_b, w_up_b, w_down_b,
    gains_a, gains_b, shifts_a, shifts_b, qv_bias_a, qv_bias_b, up_bias_a, up_bias_b, cotangent,
):
    heads, toks, clips = lax.axis_size("head"), lax.axis_size("tok"), lax.axis_size("clip")
    head = lax.axis_index("head")
    micro, frames = clips_in.shape[1], clips_in.shape[2]
    d1, d2 = clips_in.shape[-1], cotangent.shape[-1]
    share = micro // heads
    first = head * share
    pool_np, pair_np = pool_matrix(frames), pair_matrix(frames)
    pooling, pairing = jnp.asarray(pool_np, bf16), jnp.asarray(pair_np, bf16)
    unpooling, unpairing = jnp.asarray(pool_np.T, bf16), jnp.asarray(pair_np.T, bf16)
    tokens, pooled_tokens = frames * PATCH, frames * POOLED
    own_rows, mem_rows = up16(pooled_tokens), up16(frames // 2 * POOLED)
    rows2 = share * own_rows


    def by_patch(tensor):
        return tensor.transpose(0, 2, 1, 3).reshape(tensor.shape[0], -1, tensor.shape[3])

    def by_frame(rows, like):
        return rows.reshape(like[:2] + (like[3], like[2], like[4])).transpose(0, 1, 3, 2, 4)

    cot = by_patch(lax.dynamic_slice_in_dim(cotangent[0], first, share, 0))

    source = lax.dynamic_slice_in_dim(assign[0], first, share, 0)
    flags = lax.dynamic_slice_in_dim(resets[0], first, share, 0)
    slot = ((head - source // share + heads) % heads) * share + source % share
    pick = (jnp.arange(heads * share)[None, :] == slot[:, None]).astype(f32)
    has = ((flags == 0) & (lax.axis_index("clip") > 0)).astype(jnp.int32)
    valid = (pooled_tokens, frames // 2 * POOLED)

    group = ("head", "tok")
    fa, ha = w_up_a.shape[1], w_out_a.shape[1]
    fb, hb, hs = w_up_b.shape[1], w_out_b.shape[1], w_skip_b.shape[1]
    spare_a = jnp.zeros((w_out_a.shape[0], -w_out_a.shape[1] % 256), bf16)
    pack_a = jnp.concatenate([w_up_a, w_down_a, w_out_a, spare_a], axis=1)
    all_a = lax.all_gather(pack_a, group).reshape(heads, d1, -1)
    stream = by_patch(lax.dynamic_slice_in_dim(clips_in[0], first, share, 0))
    low1, pooled1, mean1 = call(
        norm_pool_kernel, share,
        [(stream, 0), (gains_a, None), (shifts_a, None), (pooling, None), (pairing, None)],
        [(shape((share, tokens, d1), bf16), 0), (shape((share, own_rows, d1), bf16), 0), (shape((share, mem_rows, d1), bf16), 0)],
        name="norm_pool", us=5,
    )
    pack_w = jnp.concatenate([*w_qkv_b.transpose(1, 0, 2), *w_qkv_a.transpose(1, 0, 2)], axis=1)
    own1, mem1, all_w, qv_a, qv_b, ub_a, ub_b = share_pooled(
        pooled1, mean1, pick, 0, pack_w, [qv_bias_a, qv_bias_b, jnp.concatenate([up_bias_a, up_bias_b])[None]], fa)
    all_q = all_w.reshape(heads, d1, -1)
    all_w = all_q[:, :, 3 * hb:]
    q_spec = pl.BlockSpec((heads, d1, 3 * hb), lambda i: (0, 0, 0))
    own1, w_up_b, cot = lax.optimization_barrier((own1, w_up_b, cot))
    spare = jnp.zeros((w_up_b.shape[0], -(2 * fb + hb + hs) % hb), bf16)
    pack_b = jnp.concatenate([w_up_b, w_down_b, w_out_b, w_skip_b, spare], axis=1)
    all_b = lax.all_gather(pack_b, group).reshape(heads, d2, -1)
    cot = jnp.pad(cot, ((0, 0), (0, own_rows - pooled_tokens), (0, 0))).reshape(rows2, d2)

    up_spec, down_spec = (pl.BlockSpec((heads, d1, fa), lambda i, n=n: (0, 0, n)) for n in range(2))
    out_a_spec = pl.BlockSpec((heads, d1, 256), lambda i: (0, 0, 2 * fa // 256))

    comb1, lse1 = attend(low1, own1, mem1, (all_w, None), qv_a, has, valid, d1)
    after1, middle, pooled3, mean3 = call(
        first_mlp_kernel, share,
        [(stream, 0), (comb1, 0), (all_a, out_a_spec), (all_a, up_spec), (all_a, down_spec), (ub_a, None),
         (gains_a, None), (shifts_a, None),
         (pooling, None), (pairing, None)],
        [(shape((share, tokens, d1), f32), 0), (shape((share, tokens, d1), f32), 0),
         (shape((share, own_rows, d1), bf16), 0), (shape((share, mem_rows, d1), bf16), 0)],
        [((d1, d1), bf16)],
        name="first_mlp", us=13,
    )

    own2, mem2 = share_pooled(pooled3, mean3, pick, 1)
    comb2, lse2 = attend(pooled3, own2, mem2, (all_q, q_spec), qv_b, has, valid, d2)
    chunk = 768
    per_head = fb // chunk
    steps = heads * per_head
    out_spec, skip_spec = (pl.BlockSpec((heads, d2, hb), lambda j, n=n: (0, 0, 2 * fb // hb + n)) for n in range(2))
    rows_spec = pl.BlockSpec((1, d2, chunk), lambda j: (j // per_head, 0, j % per_head))
    mixed, dcomb2, dskip, g_mlp_b, g_out_b, g_skip_b, g_ub_b, rows_b = call(
        second_mlp_kernel, steps,
        [(comb2.reshape(rows2, d2), None), (pooled3.reshape(rows2, d1), None), (cot, None), (all_b, out_spec), (all_b, skip_spec),
         (all_b, rows_spec),
         (all_b, pl.BlockSpec((1, d2, chunk), lambda j: (j // per_head, 0, per_head + j % per_head))),
         (ub_b, pl.BlockSpec((1, chunk), lambda j: (0, j))),
         (gains_b[None], None), (shifts_b, None)],
        [(shape((rows2, d2), bf16), None), (shape((rows2, d2), bf16), None), (shape((rows2, d1), f32), None),
         (shape((heads, toks, 2, d2 // toks, fb), bf16),
          pl.BlockSpec((1, toks, 2, d2 // toks, chunk), lambda j: (j // per_head, 0, 0, 0, j % per_head))),
         (shape((heads, toks, d2 // toks // 2, 2 * hb), bf16), None), (shape((heads, toks, d2 // toks // 2, 2 * hs), bf16), None),
         (shape((1, heads * fb), f32), pl.BlockSpec((1, chunk), lambda j: (0, j))), (shape((8, d2), f32), None)],
        [((rows2, d2), f32), ((rows2, d2), bf16), ((d2, rows2), bf16), ((d2, rows2), bf16), ((rows2, d2), f32), ((rows2, d2), f32), ((d2, d1), bf16)],
        name="second_mlp", us=26,
    )

    def by_owner(grad):
        return grad.reshape((heads * toks, -1) + grad.shape[2:])

    def scatter(grad):
        return lax.psum_scatter(grad, group, scatter_dimension=0, tiled=False)

    sum_mlp_b = scatter(g_mlp_b.reshape((heads * toks,) + g_mlp_b.shape[2:])).reshape(-1, fb)
    dcomb2 = dcomb2.reshape(share, own_rows, d2)
    dq2, dpool2, g_qkv_b, rows_qv_b = attend_back(pooled3, dcomb2, own2, mem2, (all_q, q_spec), qv_b, has, valid, lse2, heads)
    own_back2, mem_back2 = give_back(dpool2, pick, own_rows, 2)

    merge = lambda grad: grad.reshape((heads * toks,) + grad.shape[2:])
    rest_b = jnp.concatenate([by_owner(g_qkv_b), merge(g_out_b), merge(g_skip_b)], axis=2)
    sum_rest_b = scatter(rest_b)

    res1, dcomb1, g_mlp_a, g_ub_a, rows_a = call(
        first_back_kernel, share,
        [(middle, 0), (after1, 0), (comb1, 0), (dskip.reshape(share, own_rows, d1), 0), (dq2, 0), (own_back2, 0), (mem_back2, 0),
         (all_a, out_a_spec), (all_a, up_spec), (all_a, down_spec), (ub_a, None),
         (gains_a, None), (shifts_a, None), (unpooling, None), (unpairing, None)],
        [(shape((share, tokens, d1), f32), 0), (shape((share, tokens, d1), bf16), 0),
         (shape((heads, d1, -(-(2 * fa + ha) // 256) * 256), bf16), None),
         (shape((heads, 1, fa), f32), None), (shape((8, d1), f32), None)],
        [((heads, d1, fa), f32), ((heads, d1, fa), f32), ((d1, d1), f32), ((d1, d1), bf16)],
        name="first_back", us=26,
    )
    rest_a = by_owner(g_mlp_a)
    dcomb1, sum_mlp_b, rest_a = lax.optimization_barrier((dcomb1, sum_mlp_b, rest_a))
    sum_rest_a = scatter(rest_a)
    sum_mlp_b = reduce_clips(sum_mlp_b)
    dx1, dpool1, g_qkv_a, rows_qv_a = attend_back(low1, dcomb1, own1, mem1, (all_w, None), qv_a, has, valid, lse1, heads)
    dpool1, sum_mlp_b = lax.optimization_barrier((dpool1, sum_mlp_b))
    sum_mlp_b = spread_clips(sum_mlp_b)
    own_back1, mem_back1, mixed_all, sum_qkv_a = give_back(
        dpool1, pick, own_rows, 3, mixed.reshape(share, own_rows, d2), by_owner(g_qkv_a))
    stream_grad, rows_last = call(
        last_back_kernel, share,
        [(stream, 0), (res1, 0), (dx1, 0), (own_back1, 0), (mem_back1, 0), (gains_a, None),
         (unpooling, None), (unpairing, None)],
        [(shape((share, tokens, d1), bf16), 0), (shape((8, d1), f32), None)],
        name="last_back", us=1,
    )

    rows = [rows_last, rows_qv_a, rows_a, rows_b, rows_qv_b, g_ub_a, g_ub_b]
    count = 10 + (6 * d2 + heads * (fa + fb)) // d1
    stream_all, total, sums = finish(stream_grad, rows, sum_qkv_a, sum_rest_a, sum_rest_b, count, 4)
    row1, row2 = w_up_a.shape[0], w_up_b.shape[0]
    outs = [(3, row1, ha), (row1, ha), (row1, fa), (row1, fa), (3, row1, hb), (row2, hb), (row2, hs), (row2, fb), (row2, fb),
            (3, d1), (d2,), (5, d1), (3, d2), (2, ha), (2, hb), (fa,), (fb,)]
    grads = call(
        write_kernel, 1,
        [(head.astype(jnp.int32)[None], INSMEM), (total, None), (sums, None), (sum_mlp_b, None)],
        [(shape(dims, f32), None) for dims in outs],
        name="write", us=4,
    )
    mixed_all = mixed_all.reshape(micro, own_rows, d2)[:, :pooled_tokens]
    return (
        by_frame(mixed_all, cotangent.shape),
        by_frame(stream_all.astype(f32), clips_in.shape),
        grads[0].transpose(1, 0, 2), *grads[1:4], grads[4].transpose(1, 0, 2), *grads[5:10],
        *grads[10:],
    )


def solution(mesh):
    in_specs = (
        P("clip", None, "tok", None, None),
        P("clip", None),
        P("clip", None),
        P("tok", None, "head"),
        P("tok", "head"),
        P("tok", "head"),
        P("tok", "head"),
        P("tok", None, "head"),
        P("tok", "head"),
        P("tok", "head"),
        P("tok", "head"),
        P("tok", "head"),
        P(),
        P(),
        P(),
        P(),
        P(None, "head"),
        P(None, "head"),
        P("head"),
        P("head"),
        P("clip", None, "tok", None, None),
    )
    out_specs = (
        P("clip", None, "tok", None, None),
        P("clip", None, "tok", None, None),
        P("tok", None, "head"),
        P("tok", "head"),
        P("tok", "head"),
        P("tok", "head"),
        P("tok", None, "head"),
        P("tok", "head"),
        P("tok", "head"),
        P("tok", "head"),
        P("tok", "head"),
        P(),
        P(),
        P(),
        P(),
        P(None, "head"),
        P(None, "head"),
        P("head"),
        P("head"),
    )
    return jax.shard_map(local, mesh=mesh, in_specs=in_specs, out_specs=out_specs, check_vma=False)
```
